32 devices in a mesh: dp: 8 (over z, y), tensor: 4 (over x, core).
Axes of the slice: x: 2, y: 2, z: 4, core: 2. Of those that a mesh axis runs over, the one named last changes fastest.
Arguments:
- inputs: bfloat16 [5632, 1280], P('dp'), may hold values from -24 to 24
- targets: bfloat16 [5632, 1280], P('dp'), may hold values from -6 to 6
- w_in: bfloat16 [1280, 5120], P(None, 'tensor'), may hold values from -0.15625 to 0.15625
- w_out: bfloat16 [5120, 1280], P('tensor'), may hold values from -0.078125 to 0.078125
Outputs:
- merged_in: float32 [1280, 5120], P('dp', 'tensor')
- merged_out: float32 [1280, 5120], P('dp', 'tensor')
The draws below stay inside these ranges and needn't reach their ends.
All inputs are finite; a program needn't handle non-finite values.
Results may differ from the reference program's by a relative error of at most 0.0033.
Values may be sent and summed in bfloat16 or wider, within the bound.
No kernel may reach another device: no remote copies, remote signals or barrier semaphores. Data moves between devices by JAX's collectives and lax.ppermute only.
A program may use at most 128 MiB of HBM per device.

```python
import jax
import jax.numpy as jnp

D = 1280
FF = 5120
ROWS_DEV = 704
ROWS = 5632
N_DP = 8


def draw_inputs(key, part):
    first_key = jax.random.fold_in(jax.random.fold_in(key, 17), 0)
    base = jnp.clip(jax.random.normal(first_key, (ROWS, D), jnp.float32), -4.0, 4.0)
    blocks = ROWS // ROWS_DEV
    block_of = jnp.arange(ROWS) // ROWS_DEV
    row_scale = 1.0 + 2.0 * block_of.astype(jnp.float32) / max(blocks - 1, 1)
    return (base * row_scale[:, None]).astype(jnp.bfloat16)


def steps_of(own_key, dims, cuts, low, high):
    def one(axis_at, blocks):
        steps = jax.random.uniform(jax.random.fold_in(jax.random.fold_in(own_key, 6), axis_at), (blocks,), jnp.float32, low / len(cuts), high / len(cuts))
        return jnp.repeat(jnp.exp(steps), dims[axis_at] // blocks).reshape((-1,) + (1,) * (len(dims) - axis_at - 1))

    level = one(*cuts[0])
    for cut in cuts[1:]:
        level = level * one(*cut)
    return level


def scatter_about(key, extent, width, reach, shards=(), kind=jnp.bfloat16):
    entries = jax.random.normal(key, extent, jnp.float32) * width
    if len(shards) > 0:
        entries = steps_of(key, extent, shards, -0.22, 0.18) * entries
    return jnp.clip(entries, min=-reach, max=reach).astype(kind)


def setup_inputs(seed: int = 0) -> dict:
    key_of = jax.random.split(jax.random.key(seed), 5)
    return {
        "inputs": draw_inputs(jax.random.fold_in(key_of[4], 71), 0),
        "targets": scatter_about(key_of[1], (ROWS, D), 1.0, 6.0, ((0, 8),)),
        "w_in": scatter_about(key_of[2], (D, FF), D ** -0.5, 0.15625, ((1, 4),)),
        "w_out": scatter_about(key_of[3], (FF, D), FF ** -0.5, 0.078125, ((0, 4),)),
    }


def activate(values):
    return jax.nn.gelu(values, approximate=True)

def worker_grads(inputs, targets, w_in, w_out):
    preact = jnp.dot(inputs, w_in, preferred_element_type=jnp.float32)
    hidden = activate(preact).astype(jnp.bfloat16)
    output = jnp.dot(hidden, w_out, preferred_element_type=jnp.float32)
    error = ((output - targets.astype(jnp.float32)) / ROWS_DEV).astype(jnp.bfloat16)
    back = jnp.dot(error, w_out.T, preferred_element_type=jnp.float32)
    _, pullback = jax.vjp(activate, preact)
    dpre = pullback(back)[0].astype(jnp.bfloat16)
    first = jnp.dot(inputs.T, dpre, preferred_element_type=jnp.float32)
    second = jnp.dot(error.T, hidden, preferred_element_type=jnp.float32)
    return (first, second)

def merge_pair(lower, higher):
    product = jnp.sum(lower[0] * higher[0]) + jnp.sum(lower[1] * higher[1])
    norm_low = jnp.sum(lower[0] * lower[0]) + jnp.sum(lower[1] * lower[1])
    norm_high = jnp.sum(higher[0] * higher[0]) + jnp.sum(higher[1] * higher[1])
    coef_low = 1.0 - product / (2.0 * (norm_low + 1e-06))
    coef_high = 1.0 - product / (2.0 * (norm_high + 1e-06))
    return (coef_low * lower[0] + coef_high * higher[0], coef_low * lower[1] + coef_high * higher[1])

def subtree(residue, stride, inputs, targets, w_in, w_out):
    if stride == N_DP:
        start = residue * ROWS_DEV
        return worker_grads(inputs[start:start + ROWS_DEV], targets[start:start + ROWS_DEV], w_in, w_out)
    lower = subtree(residue, 2 * stride, inputs, targets, w_in, w_out)
    higher = subtree(residue + stride, 2 * stride, inputs, targets, w_in, w_out)
    return merge_pair(lower, higher)

def reference(inputs, targets, w_in, w_out):
    merged = subtree(0, 1, inputs, targets, w_in, w_out)
    return (merged[0], merged[1])
```

```python
import functools

import jax
import jax.numpy as jnp
from jax import lax
from jax.experimental import pallas as pl
from jax.experimental.pallas import tpu as pltpu
from jax.sharding import PartitionSpec as P

epsilon = 1e-06
gather_levels_limit = 3


def from_partner(value, axis, distance):
    mask = 2**distance
    pairs = [(source, source ^ mask) for source in range(lax.axis_size(axis))]
    return lax.ppermute(value, axis, pairs)


def activate(values):
    return jax.nn.gelu(values, approximate=True)


def split_piece(piece, upper_flag):
    half = piece.shape[0] // 2
    keep = lax.dynamic_slice_in_dim(piece, upper_flag * half, half, 0)
    send = lax.dynamic_slice_in_dim(piece, (1 - upper_flag) * half, half, 0)
    return (keep, send)


def group_total(values, section, levels):
    if section + 1 == levels:
        return lax.psum(values, ("dp", "tensor"))
    summed = lax.psum(values, "tensor")
    for offset in range(section + 1):
        summed = summed + from_partner(summed, "dp", levels - 1 - offset)
    return summed


def combine(own, incoming, upper_flag, section, levels):
    product = jnp.sum(own[0] * incoming[0]) + jnp.sum(own[1] * incoming[1])
    norm_own = jnp.sum(own[0] * own[0]) + jnp.sum(own[1] * own[1])
    norm_incoming = jnp.sum(incoming[0] * incoming[0]) + jnp.sum(incoming[1] * incoming[1])
    is_upper = upper_flag == 1
    norm_low = jnp.where(is_upper, norm_incoming, norm_own)
    norm_high = jnp.where(is_upper, norm_own, norm_incoming)
    totals = group_total(jnp.stack([product, norm_low, norm_high]), section, levels)
    coef_low = 1.0 - totals[0] / (2.0 * (totals[1] + epsilon))
    coef_high = 1.0 - totals[0] / (2.0 * (totals[2] + epsilon))
    coef_own = jnp.where(is_upper, coef_high, coef_low)
    coef_incoming = jnp.where(is_upper, coef_low, coef_high)
    return (
        coef_own * own[0] + coef_incoming * incoming[0],
        coef_own * own[1] + coef_incoming * incoming[1],
    )


def pair_list(count):
    return [(i, j) for i in range(count) for j in range(i, count)]


def gram_kernel(count, first_ref, second_ref, out_ref, totals):
    pairs = pair_list(count)
    step = pl.program_id(0)

    @pl.when(step == 0)
    def _():
        totals[...] = jnp.zeros_like(totals)

    columns = first_ref.shape[2] // 128
    groups = first_ref.shape[1] // 8

    for ref in (first_ref, second_ref):

        def body(index, sums, ref=ref):
            row = pl.multiple_of((index // columns) * 8, 8)
            column = pl.multiple_of((index % columns) * 128, 128)
            members = [ref[i, pl.ds(row, 8), pl.ds(column, 128)] for i in range(count)]
            return tuple(s + members[i] * members[j] for s, (i, j) in zip(sums, pairs))

        zero = jnp.zeros((8, 128), jnp.float32)
        sums = lax.fori_loop(0, groups * columns, body, (zero,) * len(pairs))
        for n, s in enumerate(sums):
            totals[n] += s

    @pl.when(step == pl.num_programs(0) - 1)
    def _():
        out_ref[...] = jnp.sum(totals[...], axis=1)


def gram(first, second):
    count, rows, width = first.shape
    block = max(b for b in range(8, min(rows, 40) + 1, 8) if rows % b == 0)
    pairs = len(pair_list(count))
    spec = pl.BlockSpec((count, block, width), lambda i: (0, i, 0))
    return pl.pallas_call(
        functools.partial(gram_kernel, count),
        grid=(rows // block,),
        in_specs=[spec, spec],
        out_specs=pl.BlockSpec((pairs, 128), lambda i: (0, 0)),
        out_shape=jax.ShapeDtypeStruct((pairs, 128), jnp.float32),
        scratch_shapes=[pltpu.VMEM((pairs, 8, 128), jnp.float32)],
        compiler_params=pltpu.CompilerParams(vmem_limit_bytes=40 * 2**20),
        name="gram",
    )(first, second)


def tree_weights(count, entry):
    def inner(a, b):
        total = 0.0
        for i, u in a.items():
            for j, v in b.items():
                total = total + u * v * entry(i, j)
        return total

    items = [{i: 1.0} for i in range(count)]
    while len(items) > 1:
        half = len(items) // 2
        merged = []
        for low, high in zip(items[:half], items[half:]):
            product = inner(low, high)
            scale_low = 1.0 - product / (2.0 * (jnp.maximum(inner(low, low), 0.0) + epsilon))
            scale_high = 1.0 - product / (2.0 * (jnp.maximum(inner(high, high), 0.0) + epsilon))
            joined = {i: u * scale_low for i, u in low.items()}
            joined.update({i: u * scale_high for i, u in high.items()})
            merged.append(joined)
        items = merged
    return [items[0][i] for i in range(count)]


def merge_kernel(count, totals_ref, first_ref, second_ref, first_out, second_out):
    place = {pair: n for n, pair in enumerate(pair_list(count))}

    def entry(i, j):
        return totals_ref[place[(min(i, j), max(i, j))]]

    weights = tree_weights(count, entry)
    for source, target in ((first_ref, first_out), (second_ref, second_out)):
        total = weights[0] * source[0]
        for i in range(1, count):
            total = total + weights[i] * source[i]
        target[...] = total


def merge(totals, first, second):
    count, rows, width = first.shape
    block = max(b for b in range(8, min(rows, 32) + 1, 8) if rows % b == 0)
    spec = pl.BlockSpec((count, block, width), lambda i: (0, i, 0))
    out_spec = pl.BlockSpec((block, width), lambda i: (i, 0))
    shape = jax.ShapeDtypeStruct((rows, width), jnp.float32)
    return pl.pallas_call(
        functools.partial(merge_kernel, count),
        grid=(rows // block,),
        in_specs=[pl.BlockSpec(memory_space=pltpu.SMEM), spec, spec],
        out_specs=[out_spec, out_spec],
        out_shape=[shape, shape],
        compiler_params=pltpu.CompilerParams(vmem_limit_bytes=40 * 2**20),
        name="merge",
    )(totals, first, second)


def on_device(inputs, targets, w_in, w_out):
    row_count = inputs.shape[0]
    workers = lax.axis_size("dp")
    shards = lax.axis_size("tensor")
    levels = workers.bit_length() - 1
    shard_levels = shards.bit_length() - 1
    gathered = min(levels, gather_levels_limit)
    members = 2**gathered
    others = workers // members
    position = lax.axis_index("dp")
    shard = lax.axis_index("tensor")

    if others == 1:
        groups = None
    else:
        groups = [
            [(m * others + r) * shards + t for m in range(members) for t in range(shards)]
            for r in range(others)
        ]

    def gather_rows(part):
        return lax.all_gather(part, ("dp", "tensor"), axis_index_groups=groups, tiled=True)

    part_rows = row_count // shards
    part = 0
    for bit in range(shard_levels):
        part = part * 2 + (shard >> bit & 1)
    inputs_part = lax.dynamic_slice_in_dim(inputs, part * part_rows, part_rows, 0)
    targets_part = lax.dynamic_slice_in_dim(targets, part * part_rows, part_rows, 0)
    all_inputs = gather_rows(inputs_part)

    hidden = activate(jnp.dot(inputs, w_in, preferred_element_type=jnp.float32)).astype(jnp.bfloat16)
    summed = jnp.dot(hidden, w_out, preferred_element_type=jnp.float32)
    for bit in range(shard_levels):
        keep, send = split_piece(summed, shard >> bit & 1)
        summed = keep + from_partner(send, "tensor", bit)
    error = ((summed - targets_part.astype(jnp.float32)) / row_count).astype(jnp.bfloat16)
    all_errors = gather_rows(error)

    all_preact = jnp.dot(all_inputs, w_in, preferred_element_type=jnp.float32)
    all_hidden, pullback = jax.vjp(activate, all_preact)
    all_hidden = all_hidden.astype(jnp.bfloat16)
    back = jnp.dot(all_errors, w_out.T, preferred_element_type=jnp.float32)
    all_dpre = pullback(back)[0].astype(jnp.bfloat16)

    member = position // others
    width = inputs.shape[1] // members
    by_member = (members, row_count, -1)

    def gradient_rows(left, right):
        own = lax.dynamic_slice_in_dim(left, member * width, width, 1)
        return lax.dot_general(
            own.reshape(by_member),
            right.reshape(by_member),
            (((1,), (1,)), ((0,), (0,))),
            preferred_element_type=jnp.float32,
        )

    first = gradient_rows(all_inputs, all_dpre)
    second = gradient_rows(all_errors, all_hidden)
    totals = group_total(jnp.sum(gram(first, second), axis=1), gathered - 1, levels)
    pieces = merge(totals, first, second)

    for section in range(gathered, levels):
        upper_flag = position >> levels - 1 - section & 1
        keep_first, send_first = split_piece(pieces[0], upper_flag)
        keep_second, send_second = split_piece(pieces[1], upper_flag)
        got_first, got_second = from_partner((send_first, send_second), "dp", levels - 1 - section)
        pieces = combine(
            (keep_first, keep_second), (got_first, got_second), upper_flag, section, levels
        )
    return (pieces[0], pieces[1])


def solution(mesh):
    placed = (P("dp", None), P("dp", None), P(None, "tensor"), P("tensor", None))
    return jax.shard_map(
        on_device,
        mesh=mesh,
        in_specs=placed,
        out_specs=(P("dp", "tensor"), P("dp", "tensor")),
        check_vma=False,
    )
```

```python
import functools
import math

import jax
import jax.numpy as jnp
from jax import lax
from jax.experimental import pallas as pl
from jax.experimental.pallas import tpu as pltpu
from jax.sharding import PartitionSpec as P

epsilon = 1e-06
gather_levels_limit = 3
vmem_bytes = 40 * 2**20


def from_partner(value, axis, distance):
    mask = 2**distance
    pairs = [(source, source ^ mask) for source in range(lax.axis_size(axis))]
    return lax.ppermute(value, axis, pairs)


def from_mask(value, dp_mask, tensor_mask):
    shards = lax.axis_size("tensor")
    mask = dp_mask * shards + tensor_mask
    pairs = [(source, source ^ mask) for source in range(lax.axis_size("dp") * shards)]
    return lax.ppermute(value, ("dp", "tensor"), pairs)


def split_piece(piece, upper_flag):
    half = piece.shape[0] // 2
    keep = lax.dynamic_slice_in_dim(piece, upper_flag * half, half, 0)
    send = lax.dynamic_slice_in_dim(piece, (1 - upper_flag) * half, half, 0)
    return (keep, send)


def group_total(values, section, levels):
    summed = lax.psum(values, "tensor")
    for offset in range(section + 1):
        summed = summed + from_partner(summed, "dp", levels - 1 - offset)
    return summed


def combine(own, incoming, upper_flag, section, levels):
    product = jnp.sum(own[0] * incoming[0]) + jnp.sum(own[1] * incoming[1])
    norm_own = jnp.sum(own[0] * own[0]) + jnp.sum(own[1] * own[1])
    norm_incoming = jnp.sum(incoming[0] * incoming[0]) + jnp.sum(incoming[1] * incoming[1])
    is_upper = upper_flag == 1
    norm_low = jnp.where(is_upper, norm_incoming, norm_own)
    norm_high = jnp.where(is_upper, norm_own, norm_incoming)
    totals = group_total(jnp.stack([product, norm_low, norm_high]), section, levels)
    coef_low = 1.0 - totals[0] / (2.0 * (totals[1] + epsilon))
    coef_high = 1.0 - totals[0] / (2.0 * (totals[2] + epsilon))
    coef_own = jnp.where(is_upper, coef_high, coef_low)
    coef_incoming = jnp.where(is_upper, coef_low, coef_high)
    return (
        coef_own * own[0] + coef_incoming * incoming[0],
        coef_own * own[1] + coef_incoming * incoming[1],
    )


def tile_of(size, limit):
    return max(b for b in range(128, limit + 1, 128) if size % b == 0)


def contract(left, right, left_dim, right_dim):
    dims = (((left_dim,), (right_dim,)), ((), ()))
    return lax.dot_general(left, right, dims, preferred_element_type=jnp.float32)


def call(kernel, name, flops, operands, shapes, **spec):
    moved = sum(math.prod(a.shape) * a.dtype.itemsize for a in (*operands, *shapes))
    return pl.pallas_call(
        kernel,
        grid_spec=pltpu.PrefetchScalarGridSpec(num_scalar_prefetch=1, **spec),
        out_shape=shapes,
        compiler_params=pltpu.CompilerParams(vmem_limit_bytes=vmem_bytes),
        cost_estimate=pl.CostEstimate(flops=flops, bytes_accessed=moved, transcendentals=0),
        name=name,
    )(*operands)


def forward_kernel(place_ref, *refs):
    halves, (w_ref, hidden_ref, slope_ref) = refs[:-3], refs[-3:]
    for n, half in enumerate(halves):
        rows = half.shape[0]
        start = pl.multiple_of(jnp.bitwise_xor(place_ref[0], n) * rows, 16)
        if len(halves) == 1:
            start = 0
        v = jnp.dot(half[...], w_ref[...], preferred_element_type=jnp.float32)
        scale = math.sqrt(2.0 / math.pi)
        square = v * v
        t = jnp.tanh(v * (scale + (scale * 0.044715) * square))
        upper = 0.5 + 0.5 * t
        slope = upper + (0.5 * v) * (1.0 - t * t) * (scale + (3.0 * scale * 0.044715) * square)
        hidden_ref[pl.ds(start, rows), :] = (v * upper).astype(jnp.bfloat16)
        slope_ref[pl.ds(start, rows), :] = slope


def forward(place, halves, w_in):
    rows = sum(h.shape[0] for h in halves)
    depth, width = w_in.shape
    tile = tile_of(width, 256)
    out_spec = pl.BlockSpec((rows, tile), lambda n, s: (0, n))
    return call(
        forward_kernel,
        "forward",
        2 * rows * depth * width,
        (place, *halves, w_in),
        [
            jax.ShapeDtypeStruct((rows, width), jnp.bfloat16),
            jax.ShapeDtypeStruct((rows, width), jnp.float32),
        ],
        grid=(width // tile,),
        in_specs=[pl.BlockSpec(h.shape, lambda n, s: (0, 0)) for h in halves]
        + [pl.BlockSpec((depth, tile), lambda n, s: (0, n))],
        out_specs=[out_spec, out_spec],
    )


def output_kernel(place_ref, hidden_ref, w_ref, out_ref):
    out_ref[...] = jnp.dot(hidden_ref[...], w_ref[...], preferred_element_type=jnp.float32)


def output_half(index, hidden, w_out):
    rows = hidden.shape[0] // 2
    depth, width = w_out.shape
    tile = tile_of(width, 256)
    return call(
        output_kernel,
        "output_half",
        2 * rows * depth * width,
        (index, hidden, w_out),
        [jax.ShapeDtypeStruct((rows, width), jnp.float32)],
        grid=(width // tile,),
        in_specs=[
            pl.BlockSpec((rows, depth), lambda n, s: (s[0], 0)),
            pl.BlockSpec((depth, tile), lambda n, s: (0, n)),
        ],
        out_specs=[pl.BlockSpec((rows, tile), lambda n, s: (0, n))],
    )[0]


def gradient_kernel(shape, place_ref, *refs):
    blocks, halves, window, earlier, width, step_rows = shape
    refs = list(refs)

    def take(n):
        taken = refs[:n]
        del refs[:n]
        return taken

    error_refs = take(blocks)
    input_refs = [take(window) for _ in range(halves)]
    hidden_ref, slope_ref, w_ref = take(3)
    old_first, old_second = take(earlier), take(earlier)
    first_ref, second_ref, products_ref = take(3)
    errors, own_inputs, own_errors, spread, totals = refs
    step = pl.program_id(0)

    @pl.when(step == 0)
    def _():
        totals[...] = jnp.zeros_like(totals)
        part = place_ref[1]
        for n, block in enumerate(error_refs):
            rows = block.shape[0]
            start = pl.multiple_of(place_ref[4 + n] * rows, 16)
            errors[pl.ds(start, rows), :] = block[...]
        for n, pieces in enumerate(input_refs):
            rows = pieces[0].shape[0]
            start = pl.multiple_of(jnp.bitwise_xor(place_ref[0], n) * rows, 16)
            if halves == 1:
                start = 0
            for m, piece in enumerate(pieces):
                own_inputs[pl.ds(start, rows), m * 128 : (m + 1) * 128] = piece[...]
        lane = pl.multiple_of(place_ref[2] * 128, 128)
        own_errors[...] = errors[:, pl.ds(lane, window * 128)]

    shift = pl.multiple_of(place_ref[3], step_rows)
    back = contract(errors[...], w_ref[...], 1, 1)
    dpre = (back * slope_ref[...]).astype(jnp.bfloat16)
    spread[...] = contract(own_inputs[...], dpre, 0, 0)
    first_ref[...] = spread[pl.ds(shift, width), :]
    spread[...] = contract(own_errors[...], hidden_ref[...], 0, 0)
    second_ref[...] = spread[pl.ds(shift, width), :]

    first, second = first_ref[...], second_ref[...]
    for n in range(earlier + 1):
        f = first if n == earlier else old_first[n][...]
        s = second if n == earlier else old_second[n][...]
        both = first * f + second * s
        totals[n] += jnp.sum(both.reshape(width // 8, 8, -1), axis=0)

    @pl.when(step == pl.num_programs(0) - 1)
    def _():
        products_ref[...] = jnp.zeros_like(products_ref)
        for n in range(earlier + 1):
            lanes = jnp.sum(totals[n], axis=0, keepdims=True)
            products_ref[n : n + 1, :] = sum(
                lanes[:, i : i + 128] for i in range(0, lanes.shape[1], 128)
            )


def gradient(place, members, blocks, inputs, hidden, slope, w_out, first, second):
    rows, width = hidden.shape
    depth = w_out.shape[1]
    own = depth // members
    step_rows = math.gcd(own, 128)
    reach = max(m * own % 128 + own for m in range(members))
    window = -(-reach // 128)
    tile = tile_of(width, 256)
    earlier = len(first)
    shape = (len(blocks), len(inputs), window, earlier, own, step_rows)

    def lanes(offset):
        return lambda n, s: (0, s[2] + offset)

    whole = lambda n, s: (0, 0)
    column = lambda n, s: (0, n)
    old_spec = [pl.BlockSpec((own, tile), column)] * earlier
    return call(
        functools.partial(gradient_kernel, shape),
        "gradient",
        2 * rows * depth * width + 4 * rows * own * width,
        (
            place,
            *blocks,
            *[half for half in inputs for _ in range(window)],
            hidden,
            slope,
            w_out,
            *first,
            *second,
        ),
        [
            jax.ShapeDtypeStruct((own, width), jnp.float32),
            jax.ShapeDtypeStruct((own, width), jnp.float32),
            jax.ShapeDtypeStruct((members, 128), jnp.float32),
        ],
        grid=(width // tile,),
        in_specs=[pl.BlockSpec(b.shape, whole) for b in blocks]
        + [pl.BlockSpec((h.shape[0], 128), lanes(m)) for h in inputs for m in range(window)]
        + [
            pl.BlockSpec((rows, tile), column),
            pl.BlockSpec((rows, tile), column),
            pl.BlockSpec((tile, depth), lambda n, s: (n, 0)),
        ]
        + old_spec
        + old_spec,
        out_specs=[
            pl.BlockSpec((own, tile), column),
            pl.BlockSpec((own, tile), column),
            pl.BlockSpec((members, 128), whole),
        ],
        scratch_shapes=[
            pltpu.VMEM((rows, depth), jnp.bfloat16),
            pltpu.VMEM((rows, window * 128), jnp.bfloat16),
            pltpu.VMEM((rows, window * 128), jnp.bfloat16),
            pltpu.VMEM((window * 128, tile), jnp.float32),
            pltpu.VMEM((earlier + 1, 8, tile), jnp.float32),
        ],
    )


def tree_weights(count, entry):
    def inner(a, b):
        total = 0.0
        for i, u in a.items():
            for j, v in b.items():
                total = total + u * v * entry(i, j)
        return total

    items = [{i: 1.0} for i in range(count)]
    while len(items) > 1:
        half = len(items) // 2
        merged = []
        for low, high in zip(items[:half], items[half:]):
            product = inner(low, high)
            scale_low = 1.0 - product / (2.0 * (jnp.maximum(inner(low, low), 0.0) + epsilon))
            scale_high = 1.0 - product / (2.0 * (jnp.maximum(inner(high, high), 0.0) + epsilon))
            joined = {i: u * scale_low for i, u in low.items()}
            joined.update({i: u * scale_high for i, u in high.items()})
            merged.append(joined)
        items = merged
    return [items[0][i] for i in range(count)]


def merge_kernel(count, totals_ref, *refs):
    weights = tree_weights(count, lambda i, j: totals_ref[max(i, j), min(i, j)])
    for n in range(2):
        sources = refs[n * count : (n + 1) * count]
        total = weights[0] * sources[0][...]
        for i in range(1, count):
            total = total + weights[i] * sources[i][...]
        refs[2 * count + n][...] = total


def merge(totals, first, second):
    count = len(first)
    rows, width = first[0].shape
    block = max(b for b in range(8, min(rows, 32) + 1, 8) if rows % b == 0)
    spec = pl.BlockSpec((block, width), lambda i: (i, 0))
    shape = jax.ShapeDtypeStruct((rows, width), jnp.float32)
    return pl.pallas_call(
        functools.partial(merge_kernel, count),
        grid=(rows // block,),
        in_specs=[pl.BlockSpec(memory_space=pltpu.SMEM)] + [spec] * (2 * count),
        out_specs=[spec, spec],
        out_shape=[shape, shape],
        compiler_params=pltpu.CompilerParams(vmem_limit_bytes=vmem_bytes),
        name="merge",
    )(totals, *first, *second)


def relabel(matrix, mask):
    bits = matrix.shape[0].bit_length() - 1
    axes = [bits - 1 - b for b in range(bits) if mask >> b & 1]
    cube = matrix.reshape((2,) * (2 * bits))
    return lax.rev(cube, axes + [bits + a for a in axes]).reshape(matrix.shape)


def on_device(inputs, targets, w_in, w_out):
    row_count = inputs.shape[0]
    workers = lax.axis_size("dp")
    shards = lax.axis_size("tensor")
    levels = workers.bit_length() - 1
    shard_levels = shards.bit_length() - 1
    gathered = min(levels, gather_levels_limit)
    members = 2**gathered
    others = workers // members
    position = lax.axis_index("dp")
    shard = lax.axis_index("tensor")
    member = position // others

    def part_of(index):
        part = 0
        for bit in range(shard_levels):
            part = part * 2 + (index >> bit & 1)
        return part

    near = shard & 1
    part_rows = row_count // shards
    half_rows = row_count // 2
    own = inputs.shape[1] // members
    place = jnp.stack(
        [near, part_of(shard), member * own // 128, member * own % 128]
        + [part_of(shard ^ mask) for mask in range(shards)]
    ).astype(jnp.int32)

    own_half = lax.dynamic_slice_in_dim(inputs, near * half_rows, half_rows, 0)
    near_half = {0: own_half}
    for mask in range(1, members):
        if mask == 1 or mask % 2 == 0:
            near_half[mask] = from_mask(own_half, mask * others, 0)
        else:
            near_half[mask] = from_mask(near_half[mask - 1], others, 0)
    far_half = {m: from_mask(near_half[m], 0, 1) for m in range(1, members)}

    hidden, slope = {}, {}
    hidden[0], slope[0] = forward(place, [inputs], w_in)

    got = from_mask(output_half((1 - near).reshape(1), hidden[0], w_out), 0, 1)
    summed = output_half(near.reshape(1), hidden[0], w_out) + got
    for bit in range(1, shard_levels):
        keep, send = split_piece(summed, shard >> bit & 1)
        summed = keep + from_mask(send, 0, 2**bit)
    targets_part = lax.dynamic_slice_in_dim(targets, part_of(shard) * part_rows, part_rows, 0)
    error = ((summed - targets_part.astype(jnp.float32)) / row_count).astype(jnp.bfloat16)

    for m in range(1, members):
        hidden[m], slope[m] = forward(place, [near_half[m], far_half[m]], w_in)

    errors = {(0, 0): error}
    for m in range(1, members):
        if m == 1 or m % 2 == 0:
            errors[m, 0] = from_mask(error, m * others, 0)
        else:
            errors[m, 0] = from_mask(errors[m - 1, 0], others, 0)
    for m in range(members):
        for bit in reversed(range(shard_levels)):
            for mask in [k for s, k in errors if s == m]:
                errors[m, mask | 2**bit] = from_mask(errors[m, mask], 0, 2**bit)

    first, second, products = [], [], []
    for m in range(members):
        results = gradient(
            place,
            members,
            [errors[m, k] for k in range(shards)],
            [inputs] if m == 0 else [near_half[m], far_half[m]],
            hidden[m],
            slope[m],
            w_out,
            first,
            second,
        )
        first.append(results[0])
        second.append(results[1])
        products.append(results[2])

    lower = jnp.sum(jnp.stack(products), axis=2)
    totals = lax.psum(lower + jnp.tril(lower, -1).T, "tensor")
    gathered_totals = [from_mask(totals, m * others, 0) for m in range(1, members)]
    for m, got in enumerate(gathered_totals, 1):
        totals = totals + relabel(got, m)
    pieces = merge(totals, first, second)

    for section in range(gathered, levels):
        upper_flag = position >> levels - 1 - section & 1
        keep_first, send_first = split_piece(pieces[0], upper_flag)
        keep_second, send_second = split_piece(pieces[1], upper_flag)
        got_first, got_second = from_partner((send_first, send_second), "dp", levels - 1 - section)
        pieces = combine(
            (keep_first, keep_second), (got_first, got_second), upper_flag, section, levels
        )
    return (pieces[0], pieces[1])


def solution(mesh):
    placed = (P("dp", None), P("dp", None), P(None, "tensor"), P("tensor", None))
    return jax.shard_map(
        on_device,
        mesh=mesh,
        in_specs=placed,
        out_specs=(P("dp", "tensor"), P("dp", "tensor")),
        check_vma=False,
    )
```

```python
import functools
import math

import jax
import jax.numpy as jnp
from jax import lax
from jax.experimental import pallas as pl
from jax.experimental.pallas import tpu as pltpu
from jax.sharding import PartitionSpec as P

epsilon = 1e-06
gather_levels_limit = 3
vmem_bytes = 60 * 2**20


def from_partner(value, axis, distance):
    mask = 2**distance
    pairs = [(source, source ^ mask) for source in range(lax.axis_size(axis))]
    return lax.ppermute(value, axis, pairs)


def from_mask(value, dp_mask, tensor_mask):
    shards = lax.axis_size("tensor")
    mask = dp_mask * shards + tensor_mask
    pairs = [(source, source ^ mask) for source in range(lax.axis_size("dp") * shards)]
    return lax.ppermute(value, ("dp", "tensor"), pairs)


def split_piece(piece, upper_flag):
    half = piece.shape[0] // 2
    keep = lax.dynamic_slice_in_dim(piece, upper_flag * half, half, 0)
    send = lax.dynamic_slice_in_dim(piece, (1 - upper_flag) * half, half, 0)
    return (keep, send)


def group_total(values, section, levels):
    summed = lax.psum(values, "tensor")
    for offset in range(section + 1):
        summed = summed + from_partner(summed, "dp", levels - 1 - offset)
    return summed


def combine(own, incoming, upper_flag, section, levels):
    product = jnp.sum(own[0] * incoming[0]) + jnp.sum(own[1] * incoming[1])
    norm_own = jnp.sum(own[0] * own[0]) + jnp.sum(own[1] * own[1])
    norm_incoming = jnp.sum(incoming[0] * incoming[0]) + jnp.sum(incoming[1] * incoming[1])
    is_upper = upper_flag == 1
    norm_low = jnp.where(is_upper, norm_incoming, norm_own)
    norm_high = jnp.where(is_upper, norm_own, norm_incoming)
    totals = group_total(jnp.stack([product, norm_low, norm_high]), section, levels)
    coef_low = 1.0 - totals[0] / (2.0 * (totals[1] + epsilon))
    coef_high = 1.0 - totals[0] / (2.0 * (totals[2] + epsilon))
    coef_own = jnp.where(is_upper, coef_high, coef_low)
    coef_incoming = jnp.where(is_upper, coef_low, coef_high)
    return (
        coef_own * own[0] + coef_incoming * incoming[0],
        coef_own * own[1] + coef_incoming * incoming[1],
    )


def tile_of(size, limit):
    return max(b for b in range(128, limit + 1, 128) if size % b == 0)


def contract(left, right, left_dim, right_dim):
    dims = (((left_dim,), (right_dim,)), ((), ()))
    return lax.dot_general(left, right, dims, preferred_element_type=jnp.float32)


def call(kernel, name, flops, operands, shapes, after=(), **spec):
    moved = sum(math.prod(a.shape) * a.dtype.itemsize for a in (*operands, *shapes))
    spec["in_specs"] = [pl.BlockSpec(memory_space=pl.ANY)] * len(after) + spec["in_specs"]

    def body(place_ref, *refs):
        kernel(place_ref, *refs[len(after) :])

    return pl.pallas_call(
        body,
        grid_spec=pltpu.PrefetchScalarGridSpec(num_scalar_prefetch=1, **spec),
        out_shape=shapes,
        compiler_params=pltpu.CompilerParams(vmem_limit_bytes=vmem_bytes),
        cost_estimate=pl.CostEstimate(flops=flops, bytes_accessed=moved, transcendentals=0),
        name=name,
    )(operands[0], *after, *operands[1:])


WINDOW, SHIFT, OTHER_SHIFT, MEMBER, NEAR, FAR, PARTS = range(7)


def row_start(place_ref, block, where):
    return 0 if where is None else pl.multiple_of(place_ref[where] * block.shape[0], 16)


def forward_kernel(wheres, place_ref, *refs):
    blocks, (w_ref, hidden_ref, slope_ref) = refs[:-3], refs[-3:]
    chunks = []
    for block, where in zip(blocks, wheres):
        rows = block.shape[0]
        pieces = 2 if where is None else 1
        for n in range(pieces):
            begin = n * rows // pieces
            chunks.append((block, begin, rows // pieces, row_start(place_ref, block, where) + begin))
    for block, begin, rows, start in chunks:
        left = block[begin : begin + rows, :]
        v = jnp.dot(left, w_ref[...], preferred_element_type=jnp.float32)
        scale = math.sqrt(2.0 / math.pi)
        square = v * v
        t = jnp.tanh(v * (scale + (scale * 0.044715) * square))
        upper = 0.5 + 0.5 * t
        slope = upper + (0.5 * v) * (1.0 - t * t) * (scale + (3.0 * scale * 0.044715) * square)
        hidden_ref[pl.ds(start, rows), :] = (v * upper).astype(jnp.bfloat16)
        slope_ref[pl.ds(start, rows), :] = slope


def forward(place, blocks, w_in, after=()):
    arrays, wheres = zip(*blocks)
    rows = sum(a.shape[0] for a in arrays)
    depth, width = w_in.shape
    tile = tile_of(width, 256)
    out_spec = pl.BlockSpec((rows, tile), lambda n, s: (0, n))
    return call(
        functools.partial(forward_kernel, wheres),
        "forward",
        2 * rows * depth * width,
        (place, *arrays, w_in),
        [
            jax.ShapeDtypeStruct((rows, width), jnp.bfloat16),
            jax.ShapeDtypeStruct((rows, width), jnp.float32),
        ],
        after,
        grid=(width // tile,),
        in_specs=[pl.BlockSpec(a.shape, lambda n, s: (0, 0)) for a in arrays]
        + [pl.BlockSpec((depth, tile), lambda n, s: (0, n))],
        out_specs=[out_spec, out_spec],
    )


def output_kernel(place_ref, hidden_ref, w_ref, out_ref):
    out_ref[...] = jnp.dot(hidden_ref[...], w_ref[...], preferred_element_type=jnp.float32)


def output_half(index, hidden, w_out, after=()):
    rows = hidden.shape[0] // 2
    depth, width = w_out.shape
    tile = tile_of(width, 256)
    return call(
        output_kernel,
        "output_half",
        2 * rows * depth * width,
        (index, hidden, w_out),
        [jax.ShapeDtypeStruct((rows, width), jnp.float32)],
        after,
        grid=(width // tile,),
        in_specs=[
            pl.BlockSpec((rows, depth), lambda n, s: (s[0], 0)),
            pl.BlockSpec((depth, tile), lambda n, s: (0, n)),
        ],
        out_specs=[pl.BlockSpec((rows, tile), lambda n, s: (0, n))],
    )[0]


def gradient_kernel(wheres, window, own, step_rows, place_ref, *refs):
    error_wheres, input_wheres = wheres
    refs = list(refs)

    def take(n):
        taken = refs[:n]
        del refs[:n]
        return taken

    error_refs = take(len(error_wheres))
    input_refs = [take(window) for _ in input_wheres]
    hidden_ref, slope_ref, w_ref, first_ref, second_ref, send_ref = take(6)
    errors, inputs, inputs_turned, errors_turned, spread_first, spread_second = refs

    @pl.when(pl.program_id(0) == 0)
    def _():
        for block, where in zip(error_refs, error_wheres):
            errors[pl.ds(row_start(place_ref, block, where), block.shape[0]), :] = block[...]
        for pieces, where in zip(input_refs, input_wheres):
            start = row_start(place_ref, pieces[0], where)
            for m, piece in enumerate(pieces):
                inputs[pl.ds(start, piece.shape[0]), m * 128 : (m + 1) * 128] = piece[...]
        lane = pl.multiple_of(place_ref[WINDOW] * 128, 128)
        inputs_turned[...] = inputs[...].T
        errors_turned[...] = errors[:, pl.ds(lane, window * 128)].T

    shift = pl.multiple_of(place_ref[SHIFT], step_rows)
    other_shift = pl.multiple_of(place_ref[OTHER_SHIFT], step_rows)
    back = jnp.dot(errors[...], w_ref[...], preferred_element_type=jnp.float32)
    dpre = (back * slope_ref[...]).astype(jnp.bfloat16)
    spread_second[...] = jnp.dot(
        errors_turned[...], hidden_ref[...], preferred_element_type=jnp.float32
    )
    spread_first[...] = jnp.dot(inputs_turned[...], dpre, preferred_element_type=jnp.float32)
    second_ref[...] = spread_second[pl.ds(shift, own), :]
    send_ref[own:, :] = spread_second[pl.ds(other_shift, own), :].astype(jnp.bfloat16)
    first_ref[...] = spread_first[pl.ds(shift, own), :]
    send_ref[:own, :] = spread_first[pl.ds(other_shift, own), :].astype(jnp.bfloat16)


def gradient(place, members, errors, inputs, hidden, slope, turned_w_out, after=()):
    error_arrays, error_wheres = zip(*errors)
    input_arrays, input_wheres = zip(*inputs)
    rows, width = hidden.shape
    depth = turned_w_out.shape[0]
    own = depth // members
    reach = max(m * own % 128 + 2 * own for m in range(0, members, 2))
    window = -(-reach // 128)
    tile = tile_of(width, 256)

    def lanes(offset):
        return lambda n, s: (0, s[WINDOW] + offset)

    whole = lambda n, s: (0, 0)
    column = lambda n, s: (0, n)
    return call(
        functools.partial(
            gradient_kernel, (error_wheres, input_wheres), window, own, math.gcd(own, 128)
        ),
        "gradient",
        2 * rows * depth * width + 4 * rows * window * 128 * width,
        (
            place,
            *error_arrays,
            *[a for a in input_arrays for _ in range(window)],
            hidden,
            slope,
            turned_w_out,
        ),
        [
            jax.ShapeDtypeStruct((own, width), jnp.float32),
            jax.ShapeDtypeStruct((own, width), jnp.float32),
            jax.ShapeDtypeStruct((2 * own, width), jnp.bfloat16),
        ],
        after,
        grid=(width // tile,),
        in_specs=[pl.BlockSpec(a.shape, whole) for a in error_arrays]
        + [pl.BlockSpec((a.shape[0], 128), lanes(m)) for a in input_arrays for m in range(window)]
        + [
            pl.BlockSpec((rows, tile), column),
            pl.BlockSpec((rows, tile), column),
            pl.BlockSpec((depth, tile), column),
        ],
        out_specs=[
            pl.BlockSpec((own, tile), column),
            pl.BlockSpec((own, tile), column),
            pl.BlockSpec((2 * own, tile), column),
        ],
        scratch_shapes=[
            pltpu.VMEM((rows, depth), jnp.bfloat16),
            pltpu.VMEM((rows, window * 128), jnp.bfloat16),
            pltpu.VMEM((window * 128, rows), jnp.bfloat16),
            pltpu.VMEM((window * 128, rows), jnp.bfloat16),
            pltpu.VMEM((window * 128, tile), jnp.float32),
            pltpu.VMEM((window * 128, tile), jnp.float32),
        ],
    )


def products_kernel(counts, fresh, place_ref, *refs):
    own = refs[0].shape[0]
    slots, at = [], 0
    for count in counts:
        slots.append(refs[at : at + count])
        at += count
    known_ref, out_ref, totals = refs[at:]
    pairs = [(i, j) for i in range(len(slots) - fresh, len(slots)) for j in range(i + 1)]

    @pl.when(pl.program_id(0) == 0)
    def _():
        totals[...] = jnp.zeros_like(totals)

    def values(slot):
        if len(slot) == 2:
            return slot[0][...], slot[1][...]
        return slot[0][:own, :].astype(jnp.float32), slot[0][own:, :].astype(jnp.float32)

    for n, (i, j) in enumerate(pairs):
        a, b = values(slots[i]), values(slots[j])
        both = a[0] * b[0] + a[1] * b[1]
        totals[n] += jnp.sum(both.reshape(own // 8, 8, -1), axis=0)

    @pl.when(pl.program_id(0) == pl.num_programs(0) - 1)
    def _():
        result = known_ref[...]
        row = lax.broadcasted_iota(jnp.int32, result.shape, 0)
        column = lax.broadcasted_iota(jnp.int32, result.shape, 1)
        for n, (i, j) in enumerate(pairs):
            i, j = (jnp.bitwise_xor(place_ref[MEMBER], k) for k in (i, j))
            here = ((row == i) & (column == j)) | ((row == j) & (column == i))
            result = result + jnp.where(here, jnp.sum(totals[n]), 0.0)
        out_ref[...] = result


def products(place, slots, fresh, known, after=()):
    arrays = [a for slot in slots for a in slot]
    own, width = slots[0][0].shape
    tile = tile_of(width, 256)
    pairs = sum(len(slots) - n for n in range(fresh))
    whole = lambda n, s: (0, 0)
    return call(
        functools.partial(products_kernel, [len(slot) for slot in slots], fresh),
        "products",
        4 * pairs * own * width,
        (place, *arrays, known),
        [jax.ShapeDtypeStruct(known.shape, jnp.float32)],
        after,
        grid=(width // tile,),
        in_specs=[pl.BlockSpec((a.shape[0], tile), lambda n, s: (0, n)) for a in arrays]
        + [pl.BlockSpec(known.shape, whole)],
        out_specs=[pl.BlockSpec(known.shape, whole)],
        scratch_shapes=[pltpu.VMEM((pairs, 8, tile), jnp.float32)],
    )[0]


def tree_weights(count, entry):
    def inner(a, b):
        total = 0.0
        for i, u in a.items():
            for j, v in b.items():
                total = total + u * v * entry(i, j)
        return total

    items = [{i: 1.0} for i in range(count)]
    while len(items) > 1:
        half = len(items) // 2
        merged = []
        for low, high in zip(items[:half], items[half:]):
            product = inner(low, high)
            scale_low = 1.0 - product / (2.0 * (jnp.maximum(inner(low, low), 0.0) + epsilon))
            scale_high = 1.0 - product / (2.0 * (jnp.maximum(inner(high, high), 0.0) + epsilon))
            joined = {i: u * scale_low for i, u in low.items()}
            joined.update({i: u * scale_high for i, u in high.items()})
            merged.append(joined)
        items = merged
    return [items[0][i] for i in range(count)]


def merge_kernel(counts, place_ref, totals_ref, *refs):
    refs, (first_ref, second_ref, weights_ref) = refs[:-3], refs[-3:]

    @pl.when(pl.program_id(0) == 0)
    def _():
        def entry(i, j):
            i, j = (jnp.bitwise_xor(place_ref[MEMBER], k) for k in (i, j))
            return totals_ref[i, j]

        for n, weight in enumerate(tree_weights(len(counts), entry)):
            weights_ref[n] = weight

    first = second = 0.0
    for n in range(len(counts)):
        weight = weights_ref[n]
        first = first + weight * refs[2 * n][...].astype(jnp.float32)
        second = second + weight * refs[2 * n + 1][...].astype(jnp.float32)
    first_ref[...] = first
    second_ref[...] = second


def merge(place, totals, slots):
    own, width = slots[0][0].shape
    block = max(b for b in range(16, min(own, 32) + 1, 16) if own % b == 0)
    steps = own // block
    upper = pl.BlockSpec((block, width), lambda n, s: (n, 0))
    lower = pl.BlockSpec((block, width), lambda n, s: (n + steps, 0))
    arrays, specs = [], []
    for slot in slots:
        arrays += [slot[0], slot[-1]]
        specs += [upper, upper if len(slot) == 2 else lower]
    shape = jax.ShapeDtypeStruct((own, width), jnp.float32)
    return call(
        functools.partial(merge_kernel, [len(slot) for slot in slots]),
        "merge",
        4 * len(slots) * own * width,
        (place, totals, *arrays),
        [shape, shape],
        grid=(steps,),
        in_specs=[pl.BlockSpec(memory_space=pltpu.SMEM)] + specs,
        out_specs=[upper, upper],
        scratch_shapes=[pltpu.SMEM((len(slots),), jnp.float32)],
    )


def on_device(inputs, targets, w_in, w_out):
    row_count = inputs.shape[0]
    workers = lax.axis_size("dp")
    shards = lax.axis_size("tensor")
    levels = workers.bit_length() - 1
    shard_levels = shards.bit_length() - 1
    gathered = min(levels, gather_levels_limit)
    members = 2**gathered
    others = workers // members
    position = lax.axis_index("dp")
    shard = lax.axis_index("tensor")
    member = position // others

    def part_of(index):
        part = 0
        for bit in range(shard_levels):
            part = part * 2 + (index >> bit & 1)
        return part

    near = shard & 1
    part_rows = row_count // shards
    half_rows = row_count // 2
    own = inputs.shape[1] // members
    pair_start = member // 2 * 2 * own
    place = jnp.stack(
        [
            pair_start // 128,
            pair_start % 128 + member % 2 * own,
            pair_start % 128 + (1 - member % 2) * own,
            member,
            near,
            1 - near,
        ]
        + [part_of(shard ^ mask) for mask in range(shards)]
    ).astype(jnp.int32)
    turned_w_out = w_out.T

    own_half = lax.dynamic_slice_in_dim(inputs, near * half_rows, half_rows, 0)
    own_part = lax.dynamic_slice_in_dim(inputs, part_of(shard) * part_rows, part_rows, 0)
    blocks = {0: [(inputs, None)]}
    for m in range(1, members // 2):
        if m == 1:
            got = from_mask(own_half, 2 * m * others, 0)
            blocks[m] = [(got, NEAR), (from_mask(got, 0, 1), FAR)]
        else:
            found = {0: from_mask(own_part, 2 * m * others, 0)}
            for bit in reversed(range(shard_levels)):
                for mask in list(found):
                    found[mask | 2**bit] = from_mask(found[mask], 0, 2**bit)
            blocks[m] = [(found[k], PARTS + k) for k in range(shards)]

    hidden, slope = {}, {}
    hidden[0], slope[0] = forward(place, blocks[0], w_in)

    got = from_mask(output_half((1 - near).reshape(1), hidden[0], w_out), 0, 1)
    summed = output_half(near.reshape(1), hidden[0], w_out) + got
    for bit in range(1, shard_levels):
        keep, send = split_piece(summed, shard >> bit & 1)
        summed = keep + from_mask(send, 0, 2**bit)
    targets_part = lax.dynamic_slice_in_dim(targets, part_of(shard) * part_rows, part_rows, 0)
    error = ((summed - targets_part.astype(jnp.float32)) / row_count).astype(jnp.bfloat16)

    errors = {}
    for m in range(members // 2):
        found = {0: from_mask(error, 2 * m * others, 0) if m else error}
        for bit in reversed(range(shard_levels)):
            for mask in list(found):
                found[mask | 2**bit] = from_mask(found[mask], 0, 2**bit)
        errors[m] = [(found[k], PARTS + k) for k in range(shards)]

    for m in range(1, members // 2):
        hidden[m], slope[m] = forward(place, blocks[m], w_in)

    slots = []
    totals = jnp.zeros((8, 128), jnp.float32)
    for m in range(members // 2):
        first, second, send = gradient(
            place, members, errors[m], blocks[m], hidden[m], slope[m], turned_w_out
        )
        slots.append((first, second))
        if m == members // 2 - 1:
            totals = products(place, slots, 1, totals)
        slots.append((from_mask(send, others, 0),))
        totals = products(place, slots, 1 if m == members // 2 - 1 else 2, totals)

    totals = group_total(totals, gathered - 1, levels)
    pieces = merge(place, totals, slots)

    for section in range(gathered, levels):
        upper_flag = position >> levels - 1 - section & 1
        keep_first, send_first = split_piece(pieces[0], upper_flag)
        keep_second, send_second = split_piece(pieces[1], upper_flag)
        got_first, got_second = from_partner((send_first, send_second), "dp", levels - 1 - section)
        pieces = combine(
            (keep_first, keep_second), (got_first, got_second), upper_flag, section, levels
        )
    return (pieces[0], pieces[1])


def solution(mesh):
    placed = (P("dp", None), P("dp", None), P(None, "tensor"), P("tensor", None))
    return jax.shard_map(
        on_device,
        mesh=mesh,
        in_specs=placed,
        out_specs=(P("dp", "tensor"), P("dp", "tensor")),
        check_vma=False,
    )
```

```python
import functools
import math

import jax
import jax.numpy as jnp
from jax import lax
from jax.experimental import pallas as pl
from jax.experimental.pallas import tpu as pltpu
from jax.sharding import PartitionSpec as P

epsilon = 1e-06
gather_levels_limit = 3
vmem_bytes = 24 * 2**20


def from_partner(value, axis, distance):
    mask = 2**distance
    pairs = [(source, source ^ mask) for source in range(lax.axis_size(axis))]
    return lax.ppermute(value, axis, pairs)


def from_mask(value, dp_mask, tensor_mask):
    shards = lax.axis_size("tensor")
    mask = dp_mask * shards + tensor_mask
    pairs = [(source, source ^ mask) for source in range(lax.axis_size("dp") * shards)]
    return lax.ppermute(value, ("dp", "tensor"), pairs)


def ordered(value, *before):
    return lax.optimization_barrier((value, *before))[0]


def split_piece(piece, upper_flag):
    half = piece.shape[0] // 2
    keep = lax.dynamic_slice_in_dim(piece, upper_flag * half, half, 0)
    send = lax.dynamic_slice_in_dim(piece, (1 - upper_flag) * half, half, 0)
    return (keep, send)


def group_total(values, section, levels):
    summed = lax.psum(values, "tensor")
    for offset in range(section + 1):
        summed = summed + from_partner(summed, "dp", levels - 1 - offset)
    return summed


def combine(own, incoming, upper_flag, section, levels):
    product = jnp.sum(own[0] * incoming[0]) + jnp.sum(own[1] * incoming[1])
    norm_own = jnp.sum(own[0] * own[0]) + jnp.sum(own[1] * own[1])
    norm_incoming = jnp.sum(incoming[0] * incoming[0]) + jnp.sum(incoming[1] * incoming[1])
    is_upper = upper_flag == 1
    norm_low = jnp.where(is_upper, norm_incoming, norm_own)
    norm_high = jnp.where(is_upper, norm_own, norm_incoming)
    totals = group_total(jnp.stack([product, norm_low, norm_high]), section, levels)
    coef_low = 1.0 - totals[0] / (2.0 * (totals[1] + epsilon))
    coef_high = 1.0 - totals[0] / (2.0 * (totals[2] + epsilon))
    coef_own = jnp.where(is_upper, coef_high, coef_low)
    coef_incoming = jnp.where(is_upper, coef_low, coef_high)
    return (
        coef_own * own[0] + coef_incoming * incoming[0],
        coef_own * own[1] + coef_incoming * incoming[1],
    )


def tile_of(size, limit):
    return max(b for b in range(128, limit + 1, 128) if size % b == 0)


def contract(left, right, left_dim, right_dim):
    dims = (((left_dim,), (right_dim,)), ((), ()))
    return lax.dot_general(left, right, dims, preferred_element_type=jnp.float32)


def call(kernel, name, flops, operands, shapes, after=(), **spec):
    moved = sum(math.prod(a.shape) * a.dtype.itemsize for a in (*operands, *shapes))
    spec["in_specs"] = [pl.BlockSpec(memory_space=pl.ANY)] * len(after) + spec["in_specs"]

    def body(place_ref, *refs):
        kernel(place_ref, *refs[len(after) :])

    return pl.pallas_call(
        body,
        grid_spec=pltpu.PrefetchScalarGridSpec(num_scalar_prefetch=1, **spec),
        out_shape=shapes,
        compiler_params=pltpu.CompilerParams(vmem_limit_bytes=vmem_bytes),
        cost_estimate=pl.CostEstimate(flops=flops, bytes_accessed=moved, transcendentals=0),
        name=name,
    )(operands[0], *after, *operands[1:])


WINDOW, SHIFT, OTHER_SHIFT, MEMBER, NEAR, FAR, PARTS = range(7)


def row_start(place_ref, block, where):
    return 0 if where is None else pl.multiple_of(place_ref[where] * block.shape[0], 16)


def whole(n, s):
    return (0, 0)


def column(n, s):
    return (0, n)


SCALE = math.sqrt(2.0 / math.pi)
CUBE = 0.044715


def output_kernel(place_ref, rows_ref, w_in_ref, w_out_ref, out_ref, total):
    step = pl.program_id(0)
    v = jnp.dot(rows_ref[...], w_in_ref[...], preferred_element_type=jnp.float32)
    t = jnp.tanh(v * (SCALE + (SCALE * CUBE) * (v * v)))
    hidden = (v * (0.5 + 0.5 * t)).astype(jnp.bfloat16)
    part = jnp.dot(hidden, w_out_ref[...], preferred_element_type=jnp.float32)

    @pl.when(step == 0)
    def _():
        total[...] = part

    @pl.when(step > 0)
    def _():
        total[...] += part

    @pl.when(step == pl.num_programs(0) - 1)
    def _():
        out_ref[...] = total[...]


def output_half(place, which, inputs, w_in, w_out, after=()):
    rows = inputs.shape[0] // 2
    depth, width = w_in.shape
    tile = tile_of(width, 256)
    return call(
        output_kernel,
        "output_half",
        4 * rows * depth * width,
        (place, inputs, w_in, w_out),
        [jax.ShapeDtypeStruct((rows, depth), jnp.float32)],
        after,
        grid=(width // tile,),
        in_specs=[
            pl.BlockSpec((rows, depth), lambda n, s: (s[which], 0)),
            pl.BlockSpec((depth, tile), column),
            pl.BlockSpec((tile, depth), lambda n, s: (n, 0)),
        ],
        out_specs=[pl.BlockSpec((rows, depth), whole)],
        scratch_shapes=[pltpu.VMEM((rows, depth), jnp.float32)],
    )[0]


def add_kernel(place_ref, own_send, got_send, own_keep, got_keep, send_ref, keep_ref):
    send_ref[...] = own_send[...] + got_send[...]
    keep_ref[...] = own_keep[...] + got_keep[...]


def add_and_split(flag, own, got):
    rows, depth = own.shape[0] // 2, own.shape[1]
    sent = pl.BlockSpec((rows, depth), lambda n, s: (1 - s[0], 0))
    kept = pl.BlockSpec((rows, depth), lambda n, s: (s[0], 0))
    shape = jax.ShapeDtypeStruct((rows, depth), jnp.float32)
    return call(
        add_kernel,
        "add_and_split",
        2 * rows * depth,
        (flag.reshape(1), own, got, own, got),
        [shape, shape],
        grid=(1,),
        in_specs=[sent, sent, kept, kept],
        out_specs=[pl.BlockSpec((rows, depth), whole)] * 2,
    )


def error_kernel(row_count, place_ref, own_ref, got_ref, targets_ref, error_ref):
    out = own_ref[...] + got_ref[...]
    error = (out - targets_ref[...].astype(jnp.float32)) / row_count
    error_ref[...] = error.astype(jnp.bfloat16)


def error_part(place, own, got, targets):
    rows, depth = own.shape
    return call(
        functools.partial(error_kernel, targets.shape[0]),
        "error_part",
        3 * rows * depth,
        (place, own, got, targets),
        [jax.ShapeDtypeStruct((rows, depth), jnp.bfloat16)],
        grid=(1,),
        in_specs=[
            pl.BlockSpec((rows, depth), whole),
            pl.BlockSpec((rows, depth), whole),
            pl.BlockSpec((rows, depth), lambda n, s: (s[PARTS], 0)),
        ],
        out_specs=[pl.BlockSpec((rows, depth), whole)],
    )[0]


def gradient_kernel(wheres, window, own, step_rows, place_ref, *refs):
    error_wheres, input_wheres = wheres
    refs = list(refs)

    def take(n):
        taken = refs[:n]
        del refs[:n]
        return taken

    error_refs, input_refs = take(len(error_wheres)), take(len(input_wheres))
    w_in_ref, w_out_ref, first_ref, second_ref, send_ref = take(5)
    errors, inputs, inputs_turned, errors_turned, spread_first, spread_second = refs

    @pl.when(pl.program_id(0) == 0)
    def _():
        for block, where in zip(error_refs, error_wheres):
            errors[pl.ds(row_start(place_ref, block, where), block.shape[0]), :] = block[...]
        for block, where in zip(input_refs, input_wheres):
            inputs[pl.ds(row_start(place_ref, block, where), block.shape[0]), :] = block[...]
        lane = pl.multiple_of(place_ref[WINDOW] * 128, 128)
        inputs_turned[...] = inputs[:, pl.ds(lane, window * 128)].T
        errors_turned[...] = errors[:, pl.ds(lane, window * 128)].T

    shift = pl.multiple_of(place_ref[SHIFT], step_rows)
    other_shift = pl.multiple_of(place_ref[OTHER_SHIFT], step_rows)
    v = jnp.dot(inputs[...], w_in_ref[...], preferred_element_type=jnp.float32)
    back = jnp.dot(errors[...], w_out_ref[...], preferred_element_type=jnp.float32)
    square = v * v
    t = jnp.tanh(v * (SCALE + (SCALE * CUBE) * square))
    upper = 0.5 + 0.5 * t
    hidden = (v * upper).astype(jnp.bfloat16)
    spread_second[...] = jnp.dot(errors_turned[...], hidden, preferred_element_type=jnp.float32)
    slope = upper + (0.5 * v) * (1.0 - t * t) * (SCALE + (3.0 * SCALE * CUBE) * square)
    dpre = (back * slope).astype(jnp.bfloat16)
    spread_first[...] = jnp.dot(inputs_turned[...], dpre, preferred_element_type=jnp.float32)
    second_ref[...] = spread_second[pl.ds(shift, own), :]
    send_ref[own:, :] = spread_second[pl.ds(other_shift, own), :].astype(jnp.bfloat16)
    first_ref[...] = spread_first[pl.ds(shift, own), :]
    send_ref[:own, :] = spread_first[pl.ds(other_shift, own), :].astype(jnp.bfloat16)


def gradient(place, members, errors, inputs, w_in, turned_w_out, after=()):
    error_arrays, error_wheres = zip(*errors)
    input_arrays, input_wheres = zip(*inputs)
    depth, width = w_in.shape
    rows = sum(a.shape[0] for a in input_arrays)
    own = depth // members
    reach = max(m * own % 128 + 2 * own for m in range(0, members, 2))
    window = -(-reach // 128)
    tile = tile_of(width, 256)
    return call(
        functools.partial(
            gradient_kernel, (error_wheres, input_wheres), window, own, math.gcd(own, 128)
        ),
        "gradient",
        4 * rows * depth * width + 4 * rows * window * 128 * width,
        (place, *error_arrays, *input_arrays, w_in, turned_w_out),
        [
            jax.ShapeDtypeStruct((own, width), jnp.float32),
            jax.ShapeDtypeStruct((own, width), jnp.float32),
            jax.ShapeDtypeStruct((2 * own, width), jnp.bfloat16),
        ],
        after,
        grid=(width // tile,),
        in_specs=[pl.BlockSpec(a.shape, whole) for a in (*error_arrays, *input_arrays)]
        + [pl.BlockSpec((depth, tile), column)] * 2,
        out_specs=[
            pl.BlockSpec((own, tile), column),
            pl.BlockSpec((own, tile), column),
            pl.BlockSpec((2 * own, tile), column),
        ],
        scratch_shapes=[
            pltpu.VMEM((rows, depth), jnp.bfloat16),
            pltpu.VMEM((rows, depth), jnp.bfloat16),
            pltpu.VMEM((window * 128, rows), jnp.bfloat16),
            pltpu.VMEM((window * 128, rows), jnp.bfloat16),
            pltpu.VMEM((window * 128, tile), jnp.float32),
            pltpu.VMEM((window * 128, tile), jnp.float32),
        ],
    )


def products_kernel(counts, fresh, place_ref, *refs):
    own = refs[0].shape[0]
    slots, at = [], 0
    for count in counts:
        slots.append(refs[at : at + count])
        at += count
    known_ref, out_ref, totals = refs[at:]
    pairs = [(i, j) for i in range(len(slots) - fresh, len(slots)) for j in range(i + 1)]

    @pl.when(pl.program_id(0) == 0)
    def _():
        totals[...] = jnp.zeros_like(totals)

    def values(slot):
        if len(slot) == 2:
            return slot[0][...], slot[1][...]
        return slot[0][:own, :].astype(jnp.float32), slot[0][own:, :].astype(jnp.float32)

    for n, (i, j) in enumerate(pairs):
        a, b = values(slots[i]), values(slots[j])
        both = a[0] * b[0] + a[1] * b[1]
        totals[n] += jnp.sum(both.reshape(own // 8, 8, -1), axis=0)

    @pl.when(pl.program_id(0) == pl.num_programs(0) - 1)
    def _():
        result = known_ref[...]
        row = lax.broadcasted_iota(jnp.int32, result.shape, 0)
        column = lax.broadcasted_iota(jnp.int32, result.shape, 1)
        for n, (i, j) in enumerate(pairs):
            i, j = (jnp.bitwise_xor(place_ref[MEMBER], k) for k in (i, j))
            here = ((row == i) & (column == j)) | ((row == j) & (column == i))
            result = result + jnp.where(here, jnp.sum(totals[n]), 0.0)
        out_ref[...] = result


def products(place, slots, fresh, known, after=()):
    arrays = [a for slot in slots for a in slot]
    own, width = slots[0][0].shape
    tile = tile_of(width, 256)
    pairs = sum(len(slots) - n for n in range(fresh))
    return call(
        functools.partial(products_kernel, [len(slot) for slot in slots], fresh),
        "products",
        4 * pairs * own * width,
        (place, *arrays, known),
        [jax.ShapeDtypeStruct(known.shape, jnp.float32)],
        after,
        grid=(width // tile,),
        in_specs=[pl.BlockSpec((a.shape[0], tile), lambda n, s: (0, n)) for a in arrays]
        + [pl.BlockSpec(known.shape, whole)],
        out_specs=[pl.BlockSpec(known.shape, whole)],
        scratch_shapes=[pltpu.VMEM((pairs, 8, tile), jnp.float32)],
    )[0]


def tree_weights(count, entry):
    def inner(a, b):
        total = 0.0
        for i, u in a.items():
            for j, v in b.items():
                total = total + u * v * entry(i, j)
        return total

    items = [{i: 1.0} for i in range(count)]
    while len(items) > 1:
        half = len(items) // 2
        merged = []
        for low, high in zip(items[:half], items[half:]):
            product = inner(low, high)
            scale_low = 1.0 - product / (2.0 * (jnp.maximum(inner(low, low), 0.0) + epsilon))
            scale_high = 1.0 - product / (2.0 * (jnp.maximum(inner(high, high), 0.0) + epsilon))
            joined = {i: u * scale_low for i, u in low.items()}
            joined.update({i: u * scale_high for i, u in high.items()})
            merged.append(joined)
        items = merged
    return [items[0][i] for i in range(count)]


def merge_kernel(counts, place_ref, totals_ref, *refs):
    refs, (first_ref, second_ref, weights_ref) = refs[:-3], refs[-3:]

    @pl.when(pl.program_id(0) == 0)
    def _():
        def entry(i, j):
            i, j = (jnp.bitwise_xor(place_ref[MEMBER], k) for k in (i, j))
            return totals_ref[i, j]

        for n, weight in enumerate(tree_weights(len(counts), entry)):
            weights_ref[n] = weight

    first = second = 0.0
    for n in range(len(counts)):
        weight = weights_ref[n]
        first = first + weight * refs[2 * n][...].astype(jnp.float32)
        second = second + weight * refs[2 * n + 1][...].astype(jnp.float32)
    first_ref[...] = first
    second_ref[...] = second


def merge(place, totals, slots):
    own, width = slots[0][0].shape
    block = max(b for b in range(16, min(own, 32) + 1, 16) if own % b == 0)
    steps = own // block
    upper = pl.BlockSpec((block, width), lambda n, s: (n, 0))
    lower = pl.BlockSpec((block, width), lambda n, s: (n + steps, 0))
    arrays, specs = [], []
    for slot in slots:
        arrays += [slot[0], slot[-1]]
        specs += [upper, upper if len(slot) == 2 else lower]
    shape = jax.ShapeDtypeStruct((own, width), jnp.float32)
    return call(
        functools.partial(merge_kernel, [len(slot) for slot in slots]),
        "merge",
        4 * len(slots) * own * width,
        (place, totals, *arrays),
        [shape, shape],
        grid=(steps,),
        in_specs=[pl.BlockSpec(memory_space=pltpu.SMEM)] + specs,
        out_specs=[upper, upper],
        scratch_shapes=[pltpu.SMEM((len(slots),), jnp.float32)],
    )


def on_device(inputs, targets, w_in, w_out):
    row_count = inputs.shape[0]
    workers = lax.axis_size("dp")
    shards = lax.axis_size("tensor")
    levels = workers.bit_length() - 1
    shard_levels = shards.bit_length() - 1
    gathered = min(levels, gather_levels_limit)
    members = 2**gathered
    others = workers // members
    position = lax.axis_index("dp")
    shard = lax.axis_index("tensor")
    member = position // others

    def part_of(index):
        part = 0
        for bit in range(shard_levels):
            part = part * 2 + (index >> bit & 1)
        return part

    near = shard & 1
    part_rows = row_count // shards
    half_rows = row_count // 2
    own = inputs.shape[1] // members
    pair_start = member // 2 * 2 * own
    place = jnp.stack(
        [
            pair_start // 128,
            pair_start % 128 + member % 2 * own,
            pair_start % 128 + (1 - member % 2) * own,
            member,
            near,
            1 - near,
        ]
        + [part_of(shard ^ mask) for mask in range(shards)]
    ).astype(jnp.int32)

    own_half = lax.dynamic_slice_in_dim(inputs, near * half_rows, half_rows, 0)
    own_part = lax.dynamic_slice_in_dim(inputs, part_of(shard) * part_rows, part_rows, 0)
    arrived = {
        m: from_mask(own_half if m == 1 else own_part, 2 * m * others, 0)
        for m in range(1, members // 2)
    }

    got = from_mask(output_half(place, FAR, inputs, w_in, w_out), 0, 1)
    summed = output_half(place, NEAR, inputs, w_in, w_out)
    for bit in range(1, shard_levels):
        send, summed = add_and_split(shard >> bit & 1, summed, got)
        got = from_mask(send, 0, 2**bit)
    turned_w_out = ordered(w_out, send).T
    error = error_part(place, summed, got, targets)

    def spread_over_tensor(found):
        for bit in reversed(range(shard_levels)):
            for mask in list(found):
                found[mask | 2**bit] = from_mask(found[mask], 0, 2**bit)
        return [(found[k], PARTS + k) for k in range(shards)]

    errors, blocks = {}, {0: [(inputs, None)]}
    for m in range(members // 2):
        errors[m] = spread_over_tensor({0: from_mask(error, 2 * m * others, 0) if m else error})
    for m in range(1, members // 2):
        block = ordered(arrived[m], error)
        if m == 1:
            blocks[m] = [(block, NEAR), (from_mask(block, 0, 1), FAR)]
        else:
            blocks[m] = spread_over_tensor({0: block})

    slots = []
    totals = jnp.zeros((8, 128), jnp.float32)
    for m in range(members // 2):
        first, second, send = gradient(
            place, members, errors[m], blocks[m], w_in, turned_w_out
        )
        slots.append((first, second))
        if m == members // 2 - 1:
            totals = products(place, slots, 1, totals)
        slots.append((from_mask(send, others, 0),))
        totals = products(place, slots, 1 if m == members // 2 - 1 else 2, totals)

    totals = group_total(totals, gathered - 1, levels)
    pieces = merge(place, totals, slots)

    for section in range(gathered, levels):
        upper_flag = position >> levels - 1 - section & 1
        keep_first, send_first = split_piece(pieces[0], upper_flag)
        keep_second, send_second = split_piece(pieces[1], upper_flag)
        got_first, got_second = from_partner((send_first, send_second), "dp", levels - 1 - section)
        pieces = combine(
            (keep_first, keep_second), (got_first, got_second), upper_flag, section, levels
        )
    return (pieces[0], pieces[1])


def solution(mesh):
    placed = (P("dp", None), P("dp", None), P(None, "tensor"), P("tensor", None))
    return jax.shard_map(
        on_device,
        mesh=mesh,
        in_specs=placed,
        out_specs=(P("dp", "tensor"), P("dp", "tensor")),
        check_vma=False,
    )
```

```python
import functools
import math

import jax
import jax.numpy as jnp
from jax import lax
from jax.experimental import pallas as pl
from jax.experimental.pallas import tpu as pltpu
from jax.sharding import PartitionSpec as P

epsilon = 1e-06
gather_levels_limit = 3
vmem_bytes = 36 * 2**20
vmem_most = 60 * 2**20


def from_partner(value, axis, distance):
    mask = 2**distance
    pairs = [(source, source ^ mask) for source in range(lax.axis_size(axis))]
    return lax.ppermute(value, axis, pairs)


def from_mask(value, dp_mask, tensor_mask):
    shards = lax.axis_size("tensor")
    mask = dp_mask * shards + tensor_mask
    pairs = [(source, source ^ mask) for source in range(lax.axis_size("dp") * shards)]
    return lax.ppermute(value, ("dp", "tensor"), pairs)


def ordered(value, *before):
    return lax.optimization_barrier((value, *before))[0]


def split_piece(piece, upper_flag):
    half = piece.shape[0] // 2
    keep = lax.dynamic_slice_in_dim(piece, upper_flag * half, half, 0)
    send = lax.dynamic_slice_in_dim(piece, (1 - upper_flag) * half, half, 0)
    return (keep, send)


def group_total(values, section, levels):
    summed = lax.psum(values, "tensor")
    for offset in range(section + 1):
        summed = summed + from_partner(summed, "dp", levels - 1 - offset)
    return summed


def combine(own, incoming, upper_flag, section, levels):
    product = jnp.sum(own[0] * incoming[0]) + jnp.sum(own[1] * incoming[1])
    norm_own = jnp.sum(own[0] * own[0]) + jnp.sum(own[1] * own[1])
    norm_incoming = jnp.sum(incoming[0] * incoming[0]) + jnp.sum(incoming[1] * incoming[1])
    is_upper = upper_flag == 1
    norm_low = jnp.where(is_upper, norm_incoming, norm_own)
    norm_high = jnp.where(is_upper, norm_own, norm_incoming)
    totals = group_total(jnp.stack([product, norm_low, norm_high]), section, levels)
    coef_low = 1.0 - totals[0] / (2.0 * (totals[1] + epsilon))
    coef_high = 1.0 - totals[0] / (2.0 * (totals[2] + epsilon))
    coef_own = jnp.where(is_upper, coef_high, coef_low)
    coef_incoming = jnp.where(is_upper, coef_low, coef_high)
    return (
        coef_own * own[0] + coef_incoming * incoming[0],
        coef_own * own[1] + coef_incoming * incoming[1],
    )


def tile_of(size, limit):
    return max(b for b in range(128, limit + 1, 128) if size % b == 0)


def contract(left, right, left_dim, right_dim):
    dims = (((left_dim,), (right_dim,)), ((), ()))
    return lax.dot_general(left, right, dims, preferred_element_type=jnp.float32)


def call(kernel, name, operands, shapes, after=(), vmem=vmem_bytes, **spec):
    spec["in_specs"] = [pl.BlockSpec(memory_space=pl.ANY)] * len(after) + spec["in_specs"]

    def body(place_ref, *refs):
        kernel(place_ref, *refs[len(after) :])

    return pl.pallas_call(
        body,
        grid_spec=pltpu.PrefetchScalarGridSpec(num_scalar_prefetch=1, **spec),
        out_shape=shapes,
        compiler_params=pltpu.CompilerParams(vmem_limit_bytes=vmem),
        cost_estimate=pl.CostEstimate(flops=1, bytes_accessed=1, transcendentals=0),
        name=name,
    )(operands[0], *after, *operands[1:])


WINDOW, SHIFT, OTHER_SHIFT, MEMBER, NEAR, FAR, PARTS = range(7)


def row_start(place_ref, block, where):
    return 0 if where is None else pl.multiple_of(place_ref[where] * block.shape[0], 16)


def whole(n, s):
    return (0, 0)


def column(n, s):
    return (0, n)


SCALE = math.sqrt(2.0 / math.pi)
CUBE = 0.044715


def output_kernel(place_ref, rows_ref, w_in_ref, w_out_ref, far_ref, near_ref, total):
    step = pl.program_id(0)
    v = jnp.dot(rows_ref[...], w_in_ref[...], preferred_element_type=jnp.float32)
    t = jnp.tanh(v * (SCALE + (SCALE * CUBE) * (v * v)))
    hidden = (v * (0.5 + 0.5 * t)).astype(jnp.bfloat16)
    part = jnp.dot(hidden, w_out_ref[...], preferred_element_type=jnp.float32)

    @pl.when(step == 0)
    def _():
        total[...] = part

    @pl.when(step > 0)
    def _():
        total[...] += part

    @pl.when(step == pl.num_programs(0) - 1)
    def _():
        far_ref[...] = total[pl.ds(row_start(place_ref, far_ref, FAR), far_ref.shape[0]), :]
        near_ref[...] = total[pl.ds(row_start(place_ref, near_ref, NEAR), near_ref.shape[0]), :]


def output_halves(place, inputs, w_in, w_out):
    rows = inputs.shape[0]
    depth, width = w_in.shape
    tile = tile_of(width, 256)
    shape = jax.ShapeDtypeStruct((rows // 2, depth), jnp.float32)
    return call(
        output_kernel,
        "output_halves",
        (place, inputs, w_in, w_out),
        [shape, shape],
        vmem=vmem_most,
        grid=(width // tile,),
        in_specs=[
            pl.BlockSpec((rows, depth), whole),
            pl.BlockSpec((depth, tile), column),
            pl.BlockSpec((tile, depth), lambda n, s: (n, 0)),
        ],
        out_specs=[pl.BlockSpec((rows // 2, depth), whole)] * 2,
        scratch_shapes=[pltpu.VMEM((rows, depth), jnp.float32)],
    )


def add_kernel(place_ref, own_send, got_send, own_keep, got_keep, send_ref, keep_ref):
    send_ref[...] = own_send[...] + got_send[...]
    keep_ref[...] = own_keep[...] + got_keep[...]


def add_and_split(flag, own, got):
    rows, depth = own.shape[0] // 2, own.shape[1]
    sent = pl.BlockSpec((rows, depth), lambda n, s: (1 - s[0], 0))
    kept = pl.BlockSpec((rows, depth), lambda n, s: (s[0], 0))
    shape = jax.ShapeDtypeStruct((rows, depth), jnp.float32)
    return call(
        add_kernel,
        "add_and_split",
        (flag.reshape(1), own, got, own, got),
        [shape, shape],
        grid=(1,),
        in_specs=[sent, sent, kept, kept],
        out_specs=[pl.BlockSpec((rows, depth), whole)] * 2,
    )


def error_kernel(row_count, place_ref, own_ref, got_ref, targets_ref, error_ref):
    out = own_ref[...] + got_ref[...]
    error = (out - targets_ref[...].astype(jnp.float32)) / row_count
    error_ref[...] = error.astype(jnp.bfloat16)


def error_part(place, own, got, targets):
    rows, depth = own.shape
    return call(
        functools.partial(error_kernel, targets.shape[0]),
        "error_part",
        (place, own, got, targets),
        [jax.ShapeDtypeStruct((rows, depth), jnp.bfloat16)],
        grid=(1,),
        in_specs=[
            pl.BlockSpec((rows, depth), whole),
            pl.BlockSpec((rows, depth), whole),
            pl.BlockSpec((rows, depth), lambda n, s: (s[PARTS], 0)),
        ],
        out_specs=[pl.BlockSpec((rows, depth), whole)],
    )[0]


def gradient_kernel(wheres, window, own, step_rows, place_ref, *refs):
    error_wheres, input_wheres = wheres
    refs = list(refs)

    def take(n):
        taken = refs[:n]
        del refs[:n]
        return taken

    error_refs, input_refs = take(len(error_wheres)), take(len(input_wheres))
    w_in_ref, w_out_ref, first_ref, second_ref, send_ref = take(5)
    errors, inputs, inputs_turned, errors_turned, spread_first, spread_second = refs

    @pl.when(pl.program_id(0) == 0)
    def _():
        for block, where in zip(error_refs, error_wheres):
            errors[pl.ds(row_start(place_ref, block, where), block.shape[0]), :] = block[...]
        for block, where in zip(input_refs, input_wheres):
            inputs[pl.ds(row_start(place_ref, block, where), block.shape[0]), :] = block[...]
        lane = pl.multiple_of(place_ref[WINDOW] * 128, 128)
        inputs_turned[...] = inputs[:, pl.ds(lane, window * 128)].T
        errors_turned[...] = errors[:, pl.ds(lane, window * 128)].T

    shift = pl.multiple_of(place_ref[SHIFT], step_rows)
    other_shift = pl.multiple_of(place_ref[OTHER_SHIFT], step_rows)
    v = jnp.dot(inputs[...], w_in_ref[...], preferred_element_type=jnp.float32)
    back = lax.dot_general(
        errors[...], w_out_ref[...], (((1,), (1,)), ((), ())), preferred_element_type=jnp.float32
    )
    square = v * v
    t = jnp.tanh(v * (SCALE + (SCALE * CUBE) * square))
    upper = 0.5 + 0.5 * t
    hidden = (v * upper).astype(jnp.bfloat16)
    spread_second[...] = jnp.dot(errors_turned[...], hidden, preferred_element_type=jnp.float32)
    slope = upper + (0.5 * v) * (1.0 - t * t) * (SCALE + (3.0 * SCALE * CUBE) * square)
    dpre = (back * slope).astype(jnp.bfloat16)
    spread_first[...] = jnp.dot(inputs_turned[...], dpre, preferred_element_type=jnp.float32)
    second_ref[...] = spread_second[pl.ds(shift, own), :]
    send_ref[own:, :] = spread_second[pl.ds(other_shift, own), :].astype(jnp.bfloat16)
    first_ref[...] = spread_first[pl.ds(shift, own), :]
    send_ref[:own, :] = spread_first[pl.ds(other_shift, own), :].astype(jnp.bfloat16)


def gradient(place, members, errors, inputs, w_in, w_out, after=()):
    error_arrays, error_wheres = zip(*errors)
    input_arrays, input_wheres = zip(*inputs)
    depth, width = w_in.shape
    rows = sum(a.shape[0] for a in input_arrays)
    own = depth // members
    reach = max(m * own % 128 + 2 * own for m in range(0, members, 2))
    window = -(-reach // 128)
    tile = tile_of(width, 640)
    once = pl.Buffered(1)
    return call(
        functools.partial(
            gradient_kernel, (error_wheres, input_wheres), window, own, math.gcd(own, 128)
        ),
        "gradient",
        (place, *error_arrays, *input_arrays, w_in, w_out),
        [
            jax.ShapeDtypeStruct((own, width), jnp.float32),
            jax.ShapeDtypeStruct((own, width), jnp.float32),
            jax.ShapeDtypeStruct((2 * own, width), jnp.bfloat16),
        ],
        after,
        grid=(width // tile,),
        in_specs=[
            pl.BlockSpec(a.shape, whole, pipeline_mode=once)
            for a in (*error_arrays, *input_arrays)
        ]
        + [pl.BlockSpec((depth, tile), column), pl.BlockSpec((tile, depth), lambda n, s: (n, 0))],
        out_specs=[
            pl.BlockSpec((own, tile), column),
            pl.BlockSpec((own, tile), column),
            pl.BlockSpec((2 * own, tile), column),
        ],
        scratch_shapes=[
            pltpu.VMEM((rows, depth), jnp.bfloat16),
            pltpu.VMEM((rows, depth), jnp.bfloat16),
            pltpu.VMEM((window * 128, rows), jnp.bfloat16),
            pltpu.VMEM((window * 128, rows), jnp.bfloat16),
            pltpu.VMEM((window * 128, tile), jnp.float32),
            pltpu.VMEM((window * 128, tile), jnp.float32),
        ],
    )


def products_kernel(counts, fresh, place_ref, *refs):
    own = refs[0].shape[0]
    slots, at = [], 0
    for count in counts:
        slots.append(refs[at : at + count])
        at += count
    known_ref, out_ref, totals = refs[at:]
    pairs = [(i, j) for i in range(len(slots) - fresh, len(slots)) for j in range(i + 1)]

    @pl.when(pl.program_id(0) == 0)
    def _():
        totals[...] = jnp.zeros_like(totals)

    def values(slot):
        if len(slot) == 2:
            return slot[0][...], slot[1][...]
        return slot[0][:own, :].astype(jnp.float32), slot[0][own:, :].astype(jnp.float32)

    for n, (i, j) in enumerate(pairs):
        a, b = values(slots[i]), values(slots[j])
        both = a[0] * b[0] + a[1] * b[1]
        totals[n] += jnp.sum(both.reshape(own // 8, 8, -1), axis=0)

    @pl.when(pl.program_id(0) == pl.num_programs(0) - 1)
    def _():
        result = known_ref[...]
        row = lax.broadcasted_iota(jnp.int32, result.shape, 0)
        column = lax.broadcasted_iota(jnp.int32, result.shape, 1)
        for n, (i, j) in enumerate(pairs):
            i, j = (jnp.bitwise_xor(place_ref[MEMBER], k) for k in (i, j))
            here = ((row == i) & (column == j)) | ((row == j) & (column == i))
            result = result + jnp.where(here, jnp.sum(totals[n]), 0.0)
        out_ref[...] = result


def products(place, slots, fresh, known, after=()):
    arrays = [a for slot in slots for a in slot]
    own, width = slots[0][0].shape
    tile = tile_of(width, 256)
    pairs = sum(len(slots) - n for n in range(fresh))
    return call(
        functools.partial(products_kernel, [len(slot) for slot in slots], fresh),
        "products",
        (place, *arrays, known),
        [jax.ShapeDtypeStruct(known.shape, jnp.float32)],
        after,
        grid=(width // tile,),
        in_specs=[pl.BlockSpec((a.shape[0], tile), lambda n, s: (0, n)) for a in arrays]
        + [pl.BlockSpec(known.shape, whole)],
        out_specs=[pl.BlockSpec(known.shape, whole)],
        scratch_shapes=[pltpu.VMEM((pairs, 8, tile), jnp.float32)],
    )[0]


def tree_weights(count, entry):
    def inner(a, b):
        total = 0.0
        for i, u in a.items():
            for j, v in b.items():
                total = total + u * v * entry(i, j)
        return total

    items = [{i: 1.0} for i in range(count)]
    while len(items) > 1:
        half = len(items) // 2
        merged = []
        for low, high in zip(items[:half], items[half:]):
            product = inner(low, high)
            scale_low = 1.0 - product / (2.0 * (jnp.maximum(inner(low, low), 0.0) + epsilon))
            scale_high = 1.0 - product / (2.0 * (jnp.maximum(inner(high, high), 0.0) + epsilon))
            joined = {i: u * scale_low for i, u in low.items()}
            joined.update({i: u * scale_high for i, u in high.items()})
            merged.append(joined)
        items = merged
    return [items[0][i] for i in range(count)]


def merge_kernel(counts, place_ref, totals_ref, *refs):
    refs, (first_ref, second_ref, weights_ref) = refs[:-3], refs[-3:]

    @pl.when(pl.program_id(0) == 0)
    def _():
        def entry(i, j):
            i, j = (jnp.bitwise_xor(place_ref[MEMBER], k) for k in (i, j))
            return totals_ref[i, j]

        for n, weight in enumerate(tree_weights(len(counts), entry)):
            weights_ref[n] = weight

    first = second = 0.0
    for n in range(len(counts)):
        weight = weights_ref[n]
        first = first + weight * refs[2 * n][...].astype(jnp.float32)
        second = second + weight * refs[2 * n + 1][...].astype(jnp.float32)
    first_ref[...] = first
    second_ref[...] = second


def merge(place, totals, slots):
    own, width = slots[0][0].shape
    block = max(b for b in range(16, min(own, 32) + 1, 16) if own % b == 0)
    steps = own // block
    upper = pl.BlockSpec((block, width), lambda n, s: (n, 0))
    lower = pl.BlockSpec((block, width), lambda n, s: (n + steps, 0))
    arrays, specs = [], []
    for slot in slots:
        arrays += [slot[0], slot[-1]]
        specs += [upper, upper if len(slot) == 2 else lower]
    shape = jax.ShapeDtypeStruct((own, width), jnp.float32)
    return call(
        functools.partial(merge_kernel, [len(slot) for slot in slots]),
        "merge",
        (place, totals, *arrays),
        [shape, shape],
        vmem=vmem_most,
        grid=(steps,),
        in_specs=[pl.BlockSpec(memory_space=pltpu.SMEM)] + specs,
        out_specs=[upper, upper],
        scratch_shapes=[pltpu.SMEM((len(slots),), jnp.float32)],
    )


def on_device(inputs, targets, w_in, w_out):
    row_count = inputs.shape[0]
    workers = lax.axis_size("dp")
    shards = lax.axis_size("tensor")
    levels = workers.bit_length() - 1
    shard_levels = shards.bit_length() - 1
    gathered = min(levels, gather_levels_limit)
    members = 2**gathered
    others = workers // members
    position = lax.axis_index("dp")
    shard = lax.axis_index("tensor")
    member = position // others

    def part_of(index):
        part = 0
        for bit in range(shard_levels):
            part = part * 2 + (index >> bit & 1)
        return part

    near = shard & 1
    part_rows = row_count // shards
    half_rows = row_count // 2
    own = inputs.shape[1] // members
    pair_start = member // 2 * 2 * own
    place = jnp.stack(
        [
            pair_start // 128,
            pair_start % 128 + member % 2 * own,
            pair_start % 128 + (1 - member % 2) * own,
            member,
            near,
            1 - near,
        ]
        + [part_of(shard ^ mask) for mask in range(shards)]
    ).astype(jnp.int32)

    own_half = lax.dynamic_slice_in_dim(inputs, near * half_rows, half_rows, 0)
    own_part = lax.dynamic_slice_in_dim(inputs, part_of(shard) * part_rows, part_rows, 0)
    arrived = {
        m: from_mask(own_half if m == 1 else own_part, 2 * m * others, 0)
        for m in range(1, members // 2)
    }

    send, summed = output_halves(place, inputs, w_in, w_out)
    got = from_mask(send, 0, 1)
    for bit in range(1, shard_levels):
        send, summed = add_and_split(shard >> bit & 1, summed, got)
        got = from_mask(send, 0, 2**bit)
    error = error_part(place, summed, got, targets)

    def spread_over_tensor(found):
        for bit in reversed(range(shard_levels)):
            for mask in list(found):
                found[mask | 2**bit] = from_mask(found[mask], 0, 2**bit)
        return [(found[k], PARTS + k) for k in range(shards)]

    errors, blocks = {}, {0: [(inputs, None)]}
    for m in range(members // 2):
        errors[m] = spread_over_tensor({0: from_mask(error, 2 * m * others, 0) if m else error})
    for m in range(1, members // 2):
        block = ordered(arrived[m], error)
        if m == 1:
            blocks[m] = [(block, NEAR), (from_mask(block, 0, 1), FAR)]
        else:
            blocks[m] = spread_over_tensor({0: block})

    slots, known = [], []
    totals = jnp.zeros((8, 128), jnp.float32)
    for m in range(members // 2):
        first, second, send = gradient(
            place, members, errors[m], blocks[m], w_in, w_out, known[-2:-1]
        )
        slots.append((first, second))
        if m == members // 2 - 1:
            totals = products(place, slots, 1, totals)
        slots.append((from_mask(send, others, 0),))
        totals = products(place, slots, 1 if m == members // 2 - 1 else 2, totals)
        known.append(totals)

    totals = group_total(totals, gathered - 1, levels)
    pieces = merge(place, totals, slots)

    for section in range(gathered, levels):
        upper_flag = position >> levels - 1 - section & 1
        keep_first, send_first = split_piece(pieces[0], upper_flag)
        keep_second, send_second = split_piece(pieces[1], upper_flag)
        got_first, got_second = from_partner((send_first, send_second), "dp", levels - 1 - section)
        pieces = combine(
            (keep_first, keep_second), (got_first, got_second), upper_flag, section, levels
        )
    return (pieces[0], pieces[1])


def solution(mesh):
    placed = (P("dp", None), P("dp", None), P(None, "tensor"), P("tensor", None))
    return jax.shard_map(
        on_device,
        mesh=mesh,
        in_specs=placed,
        out_specs=(P("dp", "tensor"), P("dp", "tensor")),
        check_vma=False,
    )
```

```python
import functools
import math

import jax
import jax.numpy as jnp
from jax import lax
from jax.experimental import pallas as pl
from jax.experimental.pallas import tpu as pltpu
from jax.sharding import PartitionSpec as P

epsilon = 1e-06
gather_levels_limit = 3
vmem_bytes = 36 * 2**20
vmem_large = 46 * 2**20
vmem_most = 60 * 2**20


def from_partner(value, axis, distance):
    mask = 2**distance
    pairs = [(source, source ^ mask) for source in range(lax.axis_size(axis))]
    return lax.ppermute(value, axis, pairs)


def from_mask(value, dp_mask, tensor_mask):
    shards = lax.axis_size("tensor")
    mask = dp_mask * shards + tensor_mask
    pairs = [(source, source ^ mask) for source in range(lax.axis_size("dp") * shards)]
    return lax.ppermute(value, ("dp", "tensor"), pairs)


def ordered(value, *before):
    return lax.optimization_barrier((value, *before))[0]


def split_piece(piece, upper_flag):
    half = piece.shape[0] // 2
    keep = lax.dynamic_slice_in_dim(piece, upper_flag * half, half, 0)
    send = lax.dynamic_slice_in_dim(piece, (1 - upper_flag) * half, half, 0)
    return (keep, send)


def group_total(values, section, levels):
    summed = lax.psum(values, "tensor")
    for offset in range(section + 1):
        summed = summed + from_partner(summed, "dp", levels - 1 - offset)
    return summed


def combine(own, incoming, upper_flag, section, levels):
    product = jnp.sum(own[0] * incoming[0]) + jnp.sum(own[1] * incoming[1])
    norm_own = jnp.sum(own[0] * own[0]) + jnp.sum(own[1] * own[1])
    norm_incoming = jnp.sum(incoming[0] * incoming[0]) + jnp.sum(incoming[1] * incoming[1])
    is_upper = upper_flag == 1
    norm_low = jnp.where(is_upper, norm_incoming, norm_own)
    norm_high = jnp.where(is_upper, norm_own, norm_incoming)
    totals = group_total(jnp.stack([product, norm_low, norm_high]), section, levels)
    coef_low = 1.0 - totals[0] / (2.0 * (totals[1] + epsilon))
    coef_high = 1.0 - totals[0] / (2.0 * (totals[2] + epsilon))
    coef_own = jnp.where(is_upper, coef_high, coef_low)
    coef_incoming = jnp.where(is_upper, coef_low, coef_high)
    return (
        coef_own * own[0] + coef_incoming * incoming[0],
        coef_own * own[1] + coef_incoming * incoming[1],
    )


def tile_of(size, limit):
    return max(b for b in range(128, limit + 1, 128) if size % b == 0)


def contract(left, right, left_dim, right_dim):
    dims = (((left_dim,), (right_dim,)), ((), ()))
    return lax.dot_general(left, right, dims, preferred_element_type=jnp.float32)


def call(kernel, name, operands, shapes, after=(), vmem=vmem_bytes, **spec):
    spec["in_specs"] = [pl.BlockSpec(memory_space=pl.ANY)] * len(after) + spec["in_specs"]

    def body(place_ref, *refs):
        kernel(place_ref, *refs[len(after) :])

    return pl.pallas_call(
        body,
        grid_spec=pltpu.PrefetchScalarGridSpec(num_scalar_prefetch=1, **spec),
        out_shape=shapes,
        compiler_params=pltpu.CompilerParams(vmem_limit_bytes=vmem),
        cost_estimate=pl.CostEstimate(flops=1, bytes_accessed=1, transcendentals=0),
        name=name,
    )(operands[0], *after, *operands[1:])


WINDOW, SHIFT, OTHER_SHIFT, MEMBER, NEAR, FAR, ZERO, PARTS = range(8)


def row_start(place_ref, block, where):
    return 0 if where is None else pl.multiple_of(place_ref[where] * block.shape[0], 16)


def whole(n, s):
    return (0, 0)


def column(n, s):
    return (0, n)


SCALE = math.sqrt(2.0 / math.pi)
CUBE = 0.044715


def forward_kernel(steps, place_ref, rows_ref, w_in_ref, w_out_ref, out_ref, near_ref, hidden):
    step = pl.program_id(0)
    half = out_ref.shape[0]
    far = pl.ds(row_start(place_ref, out_ref, FAR), half)
    tile = w_in_ref.shape[1]

    for n in range(steps):

        @pl.when(step == n)
        def _():
            v = jnp.dot(rows_ref[...], w_in_ref[...], preferred_element_type=jnp.float32)
            t = jnp.tanh(v * (SCALE + (SCALE * CUBE) * (v * v)))
            hidden[:, n * tile : (n + 1) * tile] = (v * (0.5 + 0.5 * t)).astype(jnp.bfloat16)

    @pl.when(step == steps)
    def _():
        near_ref[...] = hidden[pl.ds(row_start(place_ref, out_ref, NEAR), half), :]

    @pl.when(step >= steps)
    def _():
        out_ref[...] = jnp.dot(hidden[far, :], w_out_ref[...], preferred_element_type=jnp.float32)


def forward(place, inputs, w_in, w_out):
    rows = inputs.shape[0]
    depth, width = w_in.shape
    tile, out_tile = tile_of(width, 640), tile_of(depth, 640)
    steps = width // tile
    last = lambda n: jnp.maximum(n - steps, 0)
    return call(
        functools.partial(forward_kernel, steps),
        "forward",
        (place, inputs, w_in, w_out),
        [
            jax.ShapeDtypeStruct((rows // 2, depth), jnp.float32),
            jax.ShapeDtypeStruct((rows // 2, width), jnp.bfloat16),
        ],
        vmem=vmem_most,
        grid=(steps + depth // out_tile,),
        in_specs=[
            pl.BlockSpec((rows, depth), whole),
            pl.BlockSpec((depth, tile), lambda n, s: (0, jnp.minimum(n, steps - 1))),
            pl.BlockSpec((width, out_tile), lambda n, s: (0, last(n))),
        ],
        out_specs=[
            pl.BlockSpec((rows // 2, out_tile), lambda n, s: (0, last(n))),
            pl.BlockSpec((rows // 2, width), whole),
        ],
        scratch_shapes=[pltpu.VMEM((rows, width), jnp.bfloat16)],
    )


def product_kernel(place_ref, left_ref, right_ref, out_ref):
    out_ref[...] = jnp.dot(left_ref[...], right_ref[...], preferred_element_type=jnp.float32)


def product(place, left, right):
    rows, depth = left.shape
    width = right.shape[1]
    tile = tile_of(width, 640)
    return call(
        product_kernel,
        "product",
        (place, left, right),
        [jax.ShapeDtypeStruct((rows, width), jnp.float32)],
        grid=(width // tile,),
        in_specs=[pl.BlockSpec((rows, depth), whole), pl.BlockSpec((depth, tile), column)],
        out_specs=[pl.BlockSpec((rows, tile), column)],
    )[0]


def add_kernel(place_ref, own_send, got_send, own_keep, got_keep, send_ref, keep_ref):
    send_ref[...] = own_send[...] + got_send[...]
    keep_ref[...] = own_keep[...] + got_keep[...]


def add_and_split(flag, own, got):
    rows, depth = own.shape[0] // 2, own.shape[1]
    sent = pl.BlockSpec((rows, depth), lambda n, s: (1 - s[0], 0))
    kept = pl.BlockSpec((rows, depth), lambda n, s: (s[0], 0))
    shape = jax.ShapeDtypeStruct((rows, depth), jnp.float32)
    return call(
        add_kernel,
        "add_and_split",
        (flag.reshape(1), own, got, own, got),
        [shape, shape],
        grid=(1,),
        in_specs=[sent, sent, kept, kept],
        out_specs=[pl.BlockSpec((rows, depth), whole)] * 2,
    )


def error_kernel(row_count, place_ref, own_ref, got_ref, targets_ref, error_ref):
    out = own_ref[...] + got_ref[...]
    error = (out - targets_ref[...].astype(jnp.float32)) / row_count
    error_ref[...] = error.astype(jnp.bfloat16)


def error_part(place, own, got, targets):
    rows, depth = own.shape
    return call(
        functools.partial(error_kernel, targets.shape[0]),
        "error_part",
        (place, own, got, targets),
        [jax.ShapeDtypeStruct((rows, depth), jnp.bfloat16)],
        grid=(1,),
        in_specs=[
            pl.BlockSpec((rows, depth), whole),
            pl.BlockSpec((rows, depth), whole),
            pl.BlockSpec((rows, depth), lambda n, s: (s[PARTS], 0)),
        ],
        out_specs=[pl.BlockSpec((rows, depth), whole)],
    )[0]


def gradient_kernel(wheres, worker, window, own, step_rows, place_ref, *refs):
    error_refs, refs = refs[: len(wheres)], refs[len(wheres) :]
    all_inputs, w_in_ref, w_out_ref, first_ref, second_ref, send_ref = refs[:6]
    errors, inputs, inputs_turned, errors_turned, spread_first, spread_second, done = refs[6:]

    @pl.when(pl.program_id(0) == 0)
    def _():
        rows = inputs.shape[0]
        start = pl.multiple_of(place_ref[worker] * rows, 16)
        fetch = pltpu.make_async_copy(all_inputs.at[pl.ds(start, rows), :], inputs, done)
        fetch.start()
        for block, where in zip(error_refs, wheres):
            errors[pl.ds(row_start(place_ref, block, where), block.shape[0]), :] = block[...]
        lane = pl.multiple_of(place_ref[WINDOW] * 128, 128)
        errors_turned[...] = errors[:, pl.ds(lane, window * 128)].T
        fetch.wait()
        inputs_turned[...] = inputs[:, pl.ds(lane, window * 128)].T

    shift = pl.multiple_of(place_ref[SHIFT], step_rows)
    other_shift = pl.multiple_of(place_ref[OTHER_SHIFT], step_rows)
    v = jnp.dot(inputs[...], w_in_ref[...], preferred_element_type=jnp.float32)
    back = lax.dot_general(
        errors[...], w_out_ref[...], (((1,), (1,)), ((), ())), preferred_element_type=jnp.float32
    )
    square = v * v
    t = jnp.tanh(v * (SCALE + (SCALE * CUBE) * square))
    upper = 0.5 + 0.5 * t
    hidden = (v * upper).astype(jnp.bfloat16)
    spread_second[...] = jnp.dot(errors_turned[...], hidden, preferred_element_type=jnp.float32)
    slope = upper + (0.5 * v) * (1.0 - t * t) * (SCALE + (3.0 * SCALE * CUBE) * square)
    dpre = (back * slope).astype(jnp.bfloat16)
    spread_first[...] = jnp.dot(inputs_turned[...], dpre, preferred_element_type=jnp.float32)
    second_ref[...] = spread_second[pl.ds(shift, own), :]
    send_ref[own:, :] = spread_second[pl.ds(other_shift, own), :].astype(jnp.bfloat16)
    first_ref[...] = spread_first[pl.ds(shift, own), :]
    send_ref[:own, :] = spread_first[pl.ds(other_shift, own), :].astype(jnp.bfloat16)


def gradient(place, members, rows, errors, inputs, worker, w_in, w_out, after=()):
    arrays, wheres = zip(*errors)
    depth, width = w_in.shape
    own = depth // members
    reach = max(m * own % 128 + 2 * own for m in range(0, members, 2))
    window = -(-reach // 128)
    tile = tile_of(width, 640)
    once = pl.Buffered(1)
    return call(
        functools.partial(gradient_kernel, wheres, worker, window, own, math.gcd(own, 128)),
        "gradient",
        (place, *arrays, inputs, w_in, w_out),
        [
            jax.ShapeDtypeStruct((own, width), jnp.float32),
            jax.ShapeDtypeStruct((own, width), jnp.float32),
            jax.ShapeDtypeStruct((2 * own, width), jnp.bfloat16),
        ],
        after,
        vmem=vmem_large,
        grid=(width // tile,),
        in_specs=[pl.BlockSpec(a.shape, whole, pipeline_mode=once) for a in arrays]
        + [
            pl.BlockSpec(memory_space=pltpu.HBM),
            pl.BlockSpec((depth, tile), column),
            pl.BlockSpec((tile, depth), lambda n, s: (n, 0)),
        ],
        out_specs=[
            pl.BlockSpec((own, tile), column),
            pl.BlockSpec((own, tile), column),
            pl.BlockSpec((2 * own, tile), column),
        ],
        scratch_shapes=[
            pltpu.VMEM((rows, depth), jnp.bfloat16),
            pltpu.VMEM((rows, depth), jnp.bfloat16),
            pltpu.VMEM((window * 128, rows), jnp.bfloat16),
            pltpu.VMEM((window * 128, rows), jnp.bfloat16),
            pltpu.VMEM((window * 128, tile), jnp.float32),
            pltpu.VMEM((window * 128, tile), jnp.float32),
            pltpu.SemaphoreType.DMA,
        ],
    )


def products_kernel(counts, fresh, place_ref, *refs):
    own = refs[0].shape[0]
    slots, at = [], 0
    for count in counts:
        slots.append(refs[at : at + count])
        at += count
    known_ref, out_ref, totals = refs[at:]
    pairs = [(i, j) for i in range(len(slots) - fresh, len(slots)) for j in range(i + 1)]

    @pl.when(pl.program_id(0) == 0)
    def _():
        totals[...] = jnp.zeros_like(totals)

    def values(slot):
        if len(slot) == 2:
            return slot[0][...], slot[1][...]
        return slot[0][:own, :].astype(jnp.float32), slot[0][own:, :].astype(jnp.float32)

    for n, (i, j) in enumerate(pairs):
        a, b = values(slots[i]), values(slots[j])
        both = a[0] * b[0] + a[1] * b[1]
        totals[n] += jnp.sum(both.reshape(own // 8, 8, -1), axis=0)

    @pl.when(pl.program_id(0) == pl.num_programs(0) - 1)
    def _():
        result = known_ref[...]
        row = lax.broadcasted_iota(jnp.int32, result.shape, 0)
        column = lax.broadcasted_iota(jnp.int32, result.shape, 1)
        for n, (i, j) in enumerate(pairs):
            i, j = (jnp.bitwise_xor(place_ref[MEMBER], k) for k in (i, j))
            here = ((row == i) & (column == j)) | ((row == j) & (column == i))
            result = result + jnp.where(here, jnp.sum(totals[n]), 0.0)
        out_ref[...] = result


def products(place, slots, fresh, known, after=()):
    arrays = [a for slot in slots for a in slot]
    own, width = slots[0][0].shape
    tile = tile_of(width, 256)
    pairs = sum(len(slots) - n for n in range(fresh))
    return call(
        functools.partial(products_kernel, [len(slot) for slot in slots], fresh),
        "products",
        (place, *arrays, known),
        [jax.ShapeDtypeStruct(known.shape, jnp.float32)],
        after,
        grid=(width // tile,),
        in_specs=[pl.BlockSpec((a.shape[0], tile), lambda n, s: (0, n)) for a in arrays]
        + [pl.BlockSpec(known.shape, whole)],
        out_specs=[pl.BlockSpec(known.shape, whole)],
        scratch_shapes=[pltpu.VMEM((pairs, 8, tile), jnp.float32)],
    )[0]


def tree_weights(count, entry):
    def inner(a, b):
        total = 0.0
        for i, u in a.items():
            for j, v in b.items():
                total = total + u * v * entry(i, j)
        return total

    items = [{i: 1.0} for i in range(count)]
    while len(items) > 1:
        half = len(items) // 2
        merged = []
        for low, high in zip(items[:half], items[half:]):
            product = inner(low, high)
            scale_low = 1.0 - product / (2.0 * (jnp.maximum(inner(low, low), 0.0) + epsilon))
            scale_high = 1.0 - product / (2.0 * (jnp.maximum(inner(high, high), 0.0) + epsilon))
            joined = {i: u * scale_low for i, u in low.items()}
            joined.update({i: u * scale_high for i, u in high.items()})
            merged.append(joined)
        items = merged
    return [items[0][i] for i in range(count)]


def merge_kernel(counts, place_ref, totals_ref, *refs):
    refs, (first_ref, second_ref, weights_ref) = refs[:-3], refs[-3:]

    @pl.when(pl.program_id(0) == 0)
    def _():
        def entry(i, j):
            i, j = (jnp.bitwise_xor(place_ref[MEMBER], k) for k in (i, j))
            return totals_ref[i, j]

        for n, weight in enumerate(tree_weights(len(counts), entry)):
            weights_ref[n] = weight

    first = second = 0.0
    for n in range(len(counts)):
        weight = weights_ref[n]
        first = first + weight * refs[2 * n][...].astype(jnp.float32)
        second = second + weight * refs[2 * n + 1][...].astype(jnp.float32)
    first_ref[...] = first
    second_ref[...] = second


def merge(place, totals, slots):
    own, width = slots[0][0].shape
    block = max(b for b in range(16, min(own, 32) + 1, 16) if own % b == 0)
    steps = own // block
    upper = pl.BlockSpec((block, width), lambda n, s: (n, 0))
    lower = pl.BlockSpec((block, width), lambda n, s: (n + steps, 0))
    arrays, specs = [], []
    for slot in slots:
        arrays += [slot[0], slot[-1]]
        specs += [upper, upper if len(slot) == 2 else lower]
    shape = jax.ShapeDtypeStruct((own, width), jnp.float32)
    return call(
        functools.partial(merge_kernel, [len(slot) for slot in slots]),
        "merge",
        (place, totals, *arrays),
        [shape, shape],
        vmem=vmem_most,
        grid=(steps,),
        in_specs=[pl.BlockSpec(memory_space=pltpu.SMEM)] + specs,
        out_specs=[upper, upper],
        scratch_shapes=[pltpu.SMEM((len(slots),), jnp.float32)],
    )


def on_device(inputs, targets, w_in, w_out):
    row_count = inputs.shape[0]
    workers = lax.axis_size("dp")
    shards = lax.axis_size("tensor")
    levels = workers.bit_length() - 1
    shard_levels = shards.bit_length() - 1
    gathered = min(levels, gather_levels_limit)
    members = 2**gathered
    others = workers // members
    position = lax.axis_index("dp")
    shard = lax.axis_index("tensor")
    member = position // others

    def part_of(index):
        part = 0
        for bit in range(shard_levels):
            part = part * 2 + (index >> bit & 1)
        return part

    near = shard & 1
    part_rows = row_count // shards
    own = inputs.shape[1] // members
    pair_start = member // 2 * 2 * own
    place = jnp.stack(
        [
            pair_start // 128,
            pair_start % 128 + member % 2 * own,
            pair_start % 128 + (1 - member % 2) * own,
            member,
            near,
            1 - near,
            jnp.zeros_like(near),
        ]
        + [part_of(shard ^ mask) for mask in range(shards)]
        + [member // 2 ^ mask for mask in range(1, members // 2)]
    ).astype(jnp.int32)

    groups = [
        [
            ((2 * m + lowest) * others + r) * shards + t
            for m in range(members // 2)
            for t in range(shards)
        ]
        for lowest in range(2)
        for r in range(others)
    ]
    inputs_part = lax.dynamic_slice_in_dim(inputs, shard * part_rows, part_rows, 0)
    all_inputs = lax.all_gather(
        inputs_part, ("dp", "tensor"), axis_index_groups=groups, tiled=True
    )

    send, hidden_near = forward(place, inputs, w_in, w_out)
    got = from_mask(send, 0, 1)
    summed = product(place, hidden_near, w_out)
    for bit in range(1, shard_levels):
        send, summed = add_and_split(shard >> bit & 1, summed, got)
        got = from_mask(send, 0, 2**bit)
    error = error_part(place, summed, got, targets)

    def spread_over_tensor(found):
        for bit in reversed(range(shard_levels)):
            for mask in list(found):
                found[mask | 2**bit] = from_mask(found[mask], 0, 2**bit)
        return [(found[k], PARTS + k) for k in range(shards)]

    arrived = {m: from_mask(error, 2 * m * others, 0) for m in range(1, members // 2)}
    arrived[0] = error
    slots, known = [], []
    totals = jnp.zeros((8, 128), jnp.float32)
    for m in range(members // 2):
        found = ordered(arrived[m], sent, arrived[min(2, members // 2 - 1)]) if m else error
        first, second, send = gradient(
            place,
            members,
            row_count,
            spread_over_tensor({0: found}),
            all_inputs if m else inputs,
            PARTS + shards + m - 1 if m else ZERO,
            w_in,
            w_out,
            known[-2:-1],
        )
        if m == 0:
            sent = send
        slots.append((first, second))
        if m == members // 2 - 1:
            totals = products(place, slots, 1, totals)
        slots.append((from_mask(send, others, 0),))
        totals = products(place, slots, 1 if m == members // 2 - 1 else 2, totals)
        known.append(totals)

    totals = group_total(totals, gathered - 1, levels)
    pieces = merge(place, totals, slots)

    for section in range(gathered, levels):
        upper_flag = position >> levels - 1 - section & 1
        keep_first, send_first = split_piece(pieces[0], upper_flag)
        keep_second, send_second = split_piece(pieces[1], upper_flag)
        got_first, got_second = from_partner((send_first, send_second), "dp", levels - 1 - section)
        pieces = combine(
            (keep_first, keep_second), (got_first, got_second), upper_flag, section, levels
        )
    return (pieces[0], pieces[1])


def solution(mesh):
    placed = (P("dp", None), P("dp", None), P(None, "tensor"), P("tensor", None))
    return jax.shard_map(
        on_device,
        mesh=mesh,
        in_specs=placed,
        out_specs=(P("dp", "tensor"), P("dp", "tensor")),
        check_vma=False,
    )
```

```python
import functools
import math

import jax
import jax.numpy as jnp
from jax import lax
from jax.experimental import pallas as pl
from jax.experimental.pallas import tpu as pltpu
from jax.sharding import PartitionSpec as P

epsilon = 1e-06
gather_levels_limit = 3
vmem_bytes = 36 * 2**20
vmem_most = 60 * 2**20


def from_partner(value, axis, distance):
    mask = 2**distance
    pairs = [(source, source ^ mask) for source in range(lax.axis_size(axis))]
    return lax.ppermute(value, axis, pairs)


def from_mask(value, dp_mask, tensor_mask):
    shards = lax.axis_size("tensor")
    mask = dp_mask * shards + tensor_mask
    pairs = [(source, source ^ mask) for source in range(lax.axis_size("dp") * shards)]
    return lax.ppermute(value, ("dp", "tensor"), pairs)


def ordered(value, *before):
    return lax.optimization_barrier((value, *before))[0]


def split_piece(piece, upper_flag):
    half = piece.shape[0] // 2
    keep = lax.dynamic_slice_in_dim(piece, upper_flag * half, half, 0)
    send = lax.dynamic_slice_in_dim(piece, (1 - upper_flag) * half, half, 0)
    return (keep, send)


def group_total(values, section, levels):
    summed = lax.psum(values, "tensor")
    for offset in range(section + 1):
        summed = summed + from_partner(summed, "dp", levels - 1 - offset)
    return summed


def combine(own, incoming, upper_flag, section, levels):
    product = jnp.sum(own[0] * incoming[0]) + jnp.sum(own[1] * incoming[1])
    norm_own = jnp.sum(own[0] * own[0]) + jnp.sum(own[1] * own[1])
    norm_incoming = jnp.sum(incoming[0] * incoming[0]) + jnp.sum(incoming[1] * incoming[1])
    is_upper = upper_flag == 1
    norm_low = jnp.where(is_upper, norm_incoming, norm_own)
    norm_high = jnp.where(is_upper, norm_own, norm_incoming)
    totals = group_total(jnp.stack([product, norm_low, norm_high]), section, levels)
    coef_low = 1.0 - totals[0] / (2.0 * (totals[1] + epsilon))
    coef_high = 1.0 - totals[0] / (2.0 * (totals[2] + epsilon))
    coef_own = jnp.where(is_upper, coef_high, coef_low)
    coef_incoming = jnp.where(is_upper, coef_low, coef_high)
    return (
        coef_own * own[0] + coef_incoming * incoming[0],
        coef_own * own[1] + coef_incoming * incoming[1],
    )


def tile_of(size, limit):
    return max(b for b in range(128, limit + 1, 128) if size % b == 0)


def contract(left, right, left_dim, right_dim):
    dims = (((left_dim,), (right_dim,)), ((), ()))
    return lax.dot_general(left, right, dims, preferred_element_type=jnp.float32)


def call(kernel, name, operands, shapes, after=(), vmem=vmem_bytes, **spec):
    spec["in_specs"] = [pl.BlockSpec(memory_space=pl.ANY)] * len(after) + spec["in_specs"]

    def body(place_ref, *refs):
        kernel(place_ref, *refs[len(after) :])

    return pl.pallas_call(
        body,
        grid_spec=pltpu.PrefetchScalarGridSpec(num_scalar_prefetch=1, **spec),
        out_shape=shapes,
        compiler_params=pltpu.CompilerParams(vmem_limit_bytes=vmem),
        cost_estimate=pl.CostEstimate(flops=1, bytes_accessed=1, transcendentals=0),
        name=name,
    )(operands[0], *after, *operands[1:])


WINDOW, SHIFT, OTHER_SHIFT, MEMBER, NEAR, FAR, PART = range(7)


def row_start(place_ref, block, where):
    return 0 if where is None else pl.multiple_of(place_ref[where] * block.shape[0], 16)


def whole(n, s):
    return (0, 0)


def column(n, s):
    return (0, n)


SCALE = math.sqrt(2.0 / math.pi)
CUBE = 0.044715


def forward_kernel(steps, place_ref, rows_ref, w_in_ref, w_out_ref, out_ref, near_ref, hidden):
    step = pl.program_id(0)
    half = out_ref.shape[0]
    far = pl.ds(row_start(place_ref, out_ref, FAR), half)
    tile = w_in_ref.shape[1]

    for n in range(steps):

        @pl.when(step == n)
        def _():
            v = jnp.dot(rows_ref[...], w_in_ref[...], preferred_element_type=jnp.float32)
            t = jnp.tanh(v * (SCALE + (SCALE * CUBE) * (v * v)))
            hidden[:, n * tile : (n + 1) * tile] = (v * (0.5 + 0.5 * t)).astype(jnp.bfloat16)

    @pl.when(step == steps)
    def _():
        near_ref[...] = hidden[pl.ds(row_start(place_ref, out_ref, NEAR), half), :]

    @pl.when(step >= steps)
    def _():
        out_ref[...] = jnp.dot(hidden[far, :], w_out_ref[...], preferred_element_type=jnp.float32)


def forward(place, inputs, w_in, w_out):
    rows = inputs.shape[0]
    depth, width = w_in.shape
    tile, out_tile = tile_of(width, 640), tile_of(depth, 640)
    steps = width // tile
    last = lambda n: jnp.maximum(n - steps, 0)
    return call(
        functools.partial(forward_kernel, steps),
        "forward",
        (place, inputs, w_in, w_out),
        [
            jax.ShapeDtypeStruct((rows // 2, depth), jnp.float32),
            jax.ShapeDtypeStruct((rows // 2, width), jnp.bfloat16),
        ],
        vmem=vmem_most,
        grid=(steps + depth // out_tile,),
        in_specs=[
            pl.BlockSpec((rows, depth), whole),
            pl.BlockSpec((depth, tile), lambda n, s: (0, jnp.minimum(n, steps - 1))),
            pl.BlockSpec((width, out_tile), lambda n, s: (0, last(n))),
        ],
        out_specs=[
            pl.BlockSpec((rows // 2, out_tile), lambda n, s: (0, last(n))),
            pl.BlockSpec((rows // 2, width), whole),
        ],
        scratch_shapes=[pltpu.VMEM((rows, width), jnp.bfloat16)],
    )


def product_kernel(place_ref, left_ref, right_ref, out_ref):
    out_ref[...] = jnp.dot(left_ref[...], right_ref[...], preferred_element_type=jnp.float32)


def product(place, left, right):
    rows, depth = left.shape
    width = right.shape[1]
    tile = tile_of(width, 640)
    return call(
        product_kernel,
        "product",
        (place, left, right),
        [jax.ShapeDtypeStruct((rows, width), jnp.float32)],
        grid=(width // tile,),
        in_specs=[pl.BlockSpec((rows, depth), whole), pl.BlockSpec((depth, tile), column)],
        out_specs=[pl.BlockSpec((rows, tile), column)],
    )[0]


def add_kernel(place_ref, own_send, got_send, own_keep, got_keep, send_ref, keep_ref):
    send_ref[...] = own_send[...] + got_send[...]
    keep_ref[...] = own_keep[...] + got_keep[...]


def add_and_split(flag, own, got):
    rows, depth = own.shape[0] // 2, own.shape[1]
    sent = pl.BlockSpec((rows, depth), lambda n, s: (1 - s[0], 0))
    kept = pl.BlockSpec((rows, depth), lambda n, s: (s[0], 0))
    shape = jax.ShapeDtypeStruct((rows, depth), jnp.float32)
    return call(
        add_kernel,
        "add_and_split",
        (flag.reshape(1), own, got, own, got),
        [shape, shape],
        grid=(1,),
        in_specs=[sent, sent, kept, kept],
        out_specs=[pl.BlockSpec((rows, depth), whole)] * 2,
    )


def join_kernel(place_ref, own_ref, got_ref, out_ref):
    rows = own_ref.shape[0]
    out_ref[pl.ds(pl.multiple_of(place_ref[0] * rows, 16), rows), :] = own_ref[...]
    out_ref[pl.ds(pl.multiple_of((1 - place_ref[0]) * rows, 16), rows), :] = got_ref[...]


def join(flag, own, got):
    rows, depth = own.shape
    return call(
        join_kernel,
        "join",
        (flag.reshape(1), own, got),
        [jax.ShapeDtypeStruct((2 * rows, depth), own.dtype)],
        grid=(1,),
        in_specs=[pl.BlockSpec((rows, depth), whole)] * 2,
        out_specs=[pl.BlockSpec((2 * rows, depth), whole)],
    )[0]


def error_kernel(row_count, place_ref, own_ref, got_ref, targets_ref, error_ref):
    out = own_ref[...] + got_ref[...]
    error = (out - targets_ref[...].astype(jnp.float32)) / row_count
    error_ref[...] = error.astype(jnp.bfloat16)


def error_part(place, own, got, targets, after):
    rows, depth = own.shape
    return call(
        functools.partial(error_kernel, targets.shape[0]),
        "error_part",
        (place, own, got, targets),
        [jax.ShapeDtypeStruct((rows, depth), jnp.bfloat16)],
        after,
        grid=(1,),
        in_specs=[
            pl.BlockSpec((rows, depth), whole),
            pl.BlockSpec((rows, depth), whole),
            pl.BlockSpec((rows, depth), lambda n, s: (s[PART], 0)),
        ],
        out_specs=[pl.BlockSpec((rows, depth), whole)],
    )[0]


def gradient_kernel(wheres, window, own, step_rows, place_ref, *refs):
    error_wheres, input_wheres = wheres
    refs = list(refs)

    def take(n):
        taken = refs[:n]
        del refs[:n]
        return taken

    error_refs, input_refs = take(len(error_wheres)), take(len(input_wheres))
    w_in_ref, w_out_ref, first_ref, second_ref, send_ref = take(5)
    errors, inputs, inputs_turned, errors_turned, spread_first, spread_second = refs
    if len(input_refs) == 1:
        inputs = input_refs[0]

    @pl.when(pl.program_id(0) == 0)
    def _():
        for block, where in zip(error_refs, error_wheres):
            errors[pl.ds(row_start(place_ref, block, where), block.shape[0]), :] = block[...]
        if len(input_refs) > 1:
            for block, where in zip(input_refs, input_wheres):
                inputs[pl.ds(row_start(place_ref, block, where), block.shape[0]), :] = block[...]
        lane = pl.multiple_of(place_ref[WINDOW] * 128, 128)
        inputs_turned[...] = inputs[:, pl.ds(lane, window * 128)].T
        errors_turned[...] = errors[:, pl.ds(lane, window * 128)].T

    shift = pl.multiple_of(place_ref[SHIFT], step_rows)
    other_shift = pl.multiple_of(place_ref[OTHER_SHIFT], step_rows)
    v = jnp.dot(inputs[...], w_in_ref[...], preferred_element_type=jnp.float32)
    back = lax.dot_general(
        errors[...], w_out_ref[...], (((1,), (1,)), ((), ())), preferred_element_type=jnp.float32
    )
    square = v * v
    t = jnp.tanh(v * (SCALE + (SCALE * CUBE) * square))
    upper = 0.5 + 0.5 * t
    hidden = (v * upper).astype(jnp.bfloat16)
    spread_second[...] = jnp.dot(errors_turned[...], hidden, preferred_element_type=jnp.float32)
    slope = upper + (0.5 * v) * (1.0 - t * t) * (SCALE + (3.0 * SCALE * CUBE) * square)
    dpre = (back * slope).astype(jnp.bfloat16)
    spread_first[...] = jnp.dot(inputs_turned[...], dpre, preferred_element_type=jnp.float32)
    second_ref[...] = spread_second[pl.ds(shift, own), :]
    send_ref[own:, :] = spread_second[pl.ds(other_shift, own), :].astype(jnp.bfloat16)
    first_ref[...] = spread_first[pl.ds(shift, own), :]
    send_ref[:own, :] = spread_first[pl.ds(other_shift, own), :].astype(jnp.bfloat16)


def gradient(place, members, swap, errors, inputs, w_in, w_out, after=()):
    error_arrays, error_wheres = zip(*errors)
    input_arrays, input_wheres = zip(*inputs)
    depth, width = w_in.shape
    rows = sum(a.shape[0] for a in input_arrays)
    own = depth // members
    reach = max(m * own % 128 for m in range(members) if not m & swap) + (swap + 1) * own
    window = -(-reach // 128)
    tile = tile_of(width, 640)
    once = pl.Buffered(1)
    return call(
        functools.partial(
            gradient_kernel, (error_wheres, input_wheres), window, own, math.gcd(own, 128)
        ),
        "gradient",
        (place, *error_arrays, *input_arrays, w_in, w_out),
        [
            jax.ShapeDtypeStruct((own, width), jnp.float32),
            jax.ShapeDtypeStruct((own, width), jnp.float32),
            jax.ShapeDtypeStruct((2 * own, width), jnp.bfloat16),
        ],
        after,
        grid=(width // tile,),
        in_specs=[
            pl.BlockSpec(a.shape, whole, pipeline_mode=once)
            for a in (*error_arrays, *input_arrays)
        ]
        + [pl.BlockSpec((depth, tile), column), pl.BlockSpec((tile, depth), lambda n, s: (n, 0))],
        out_specs=[
            pl.BlockSpec((own, tile), column),
            pl.BlockSpec((own, tile), column),
            pl.BlockSpec((2 * own, tile), column),
        ],
        scratch_shapes=[
            pltpu.VMEM((rows, depth), jnp.bfloat16),
            pltpu.VMEM((rows, depth), jnp.bfloat16),
            pltpu.VMEM((window * 128, rows), jnp.bfloat16),
            pltpu.VMEM((window * 128, rows), jnp.bfloat16),
            pltpu.VMEM((window * 128, tile), jnp.float32),
            pltpu.VMEM((window * 128, tile), jnp.float32),
        ],
    )


def products_kernel(counts, labels, fresh, place_ref, *refs):
    own = refs[0].shape[0]
    slots, at = [], 0
    for count in counts:
        slots.append(refs[at : at + count])
        at += count
    known_ref, out_ref, totals = refs[at:]
    pairs = [(i, j) for i in range(len(slots) - fresh, len(slots)) for j in range(i + 1)]

    @pl.when(pl.program_id(0) == 0)
    def _():
        totals[...] = jnp.zeros_like(totals)

    def values(slot):
        if len(slot) == 2:
            return slot[0][...], slot[1][...]
        return slot[0][:own, :].astype(jnp.float32), slot[0][own:, :].astype(jnp.float32)

    for n, (i, j) in enumerate(pairs):
        a, b = values(slots[i]), values(slots[j])
        both = a[0] * b[0] + a[1] * b[1]
        totals[n] += jnp.sum(both.reshape(own // 8, 8, -1), axis=0)

    @pl.when(pl.program_id(0) == pl.num_programs(0) - 1)
    def _():
        result = known_ref[...]
        row = lax.broadcasted_iota(jnp.int32, result.shape, 0)
        column = lax.broadcasted_iota(jnp.int32, result.shape, 1)
        for n, (i, j) in enumerate(pairs):
            i, j = (jnp.bitwise_xor(place_ref[MEMBER], labels[k]) for k in (i, j))
            here = ((row == i) & (column == j)) | ((row == j) & (column == i))
            result = result + jnp.where(here, jnp.sum(totals[n]), 0.0)
        out_ref[...] = result


def products(place, slots, labels, fresh, known, after=()):
    arrays = [a for slot in slots for a in slot]
    own, width = slots[0][0].shape
    tile = tile_of(width, 256)
    pairs = sum(len(slots) - n for n in range(fresh))
    return call(
        functools.partial(products_kernel, [len(slot) for slot in slots], tuple(labels), fresh),
        "products",
        (place, *arrays, known),
        [jax.ShapeDtypeStruct(known.shape, jnp.float32)],
        after,
        grid=(width // tile,),
        in_specs=[pl.BlockSpec((a.shape[0], tile), lambda n, s: (0, n)) for a in arrays]
        + [pl.BlockSpec(known.shape, whole)],
        out_specs=[pl.BlockSpec(known.shape, whole)],
        scratch_shapes=[pltpu.VMEM((pairs, 8, tile), jnp.float32)],
    )[0]


def tree_weights(count, entry):
    def inner(a, b):
        total = 0.0
        for i, u in a.items():
            for j, v in b.items():
                total = total + u * v * entry(i, j)
        return total

    items = [{i: 1.0} for i in range(count)]
    while len(items) > 1:
        half = len(items) // 2
        merged = []
        for low, high in zip(items[:half], items[half:]):
            product = inner(low, high)
            scale_low = 1.0 - product / (2.0 * (jnp.maximum(inner(low, low), 0.0) + epsilon))
            scale_high = 1.0 - product / (2.0 * (jnp.maximum(inner(high, high), 0.0) + epsilon))
            joined = {i: u * scale_low for i, u in low.items()}
            joined.update({i: u * scale_high for i, u in high.items()})
            merged.append(joined)
        items = merged
    return [items[0][i] for i in range(count)]


def merge_kernel(labels, place_ref, totals_ref, *refs):
    refs, (first_ref, second_ref, weights_ref) = refs[:-3], refs[-3:]

    @pl.when(pl.program_id(0) == 0)
    def _():
        def entry(i, j):
            i, j = (jnp.bitwise_xor(place_ref[MEMBER], k) for k in (i, j))
            return totals_ref[i, j]

        for n, weight in enumerate(tree_weights(len(labels), entry)):
            weights_ref[n] = weight

    first = second = 0.0
    for n, label in enumerate(labels):
        weight = weights_ref[label]
        first = first + weight * refs[2 * n][...].astype(jnp.float32)
        second = second + weight * refs[2 * n + 1][...].astype(jnp.float32)
    first_ref[...] = first
    second_ref[...] = second


def merge(place, totals, slots, labels):
    own, width = slots[0][0].shape
    block = max(b for b in range(16, min(own, 32) + 1, 16) if own % b == 0)
    steps = own // block
    upper = pl.BlockSpec((block, width), lambda n, s: (n, 0))
    lower = pl.BlockSpec((block, width), lambda n, s: (n + steps, 0))
    arrays, specs = [], []
    for slot in slots:
        arrays += [slot[0], slot[-1]]
        specs += [upper, upper if len(slot) == 2 else lower]
    shape = jax.ShapeDtypeStruct((own, width), jnp.float32)
    return call(
        functools.partial(merge_kernel, tuple(labels)),
        "merge",
        (place, totals, *arrays),
        [shape, shape],
        vmem=vmem_most,
        grid=(steps,),
        in_specs=[pl.BlockSpec(memory_space=pltpu.SMEM)] + specs,
        out_specs=[upper, upper],
        scratch_shapes=[pltpu.SMEM((len(slots),), jnp.float32)],
    )


def on_device(inputs, targets, w_in, w_out):
    row_count = inputs.shape[0]
    workers = lax.axis_size("dp")
    shards = lax.axis_size("tensor")
    levels = workers.bit_length() - 1
    shard_levels = shards.bit_length() - 1
    gathered = min(levels, gather_levels_limit)
    members = 2**gathered
    others = workers // members
    position = lax.axis_index("dp")
    shard = lax.axis_index("tensor")
    member = position // others

    def part_of(index):
        part = 0
        for bit in range(shard_levels):
            part = part * 2 + (index >> bit & 1)
        return part

    near = shard & 1
    part_rows = row_count // shards
    half_rows = row_count // 2
    own = inputs.shape[1] // members
    swap = min(2, members // 2)
    bits = [2**b for b in reversed(range(gathered)) if 2**b != swap]
    upper = member // swap % 2
    first_row = (member - upper * swap) * own
    place = jnp.stack(
        [
            first_row // 128,
            first_row % 128 + upper * swap * own,
            first_row % 128 + (1 - upper) * swap * own,
            member,
            near,
            1 - near,
            part_of(shard),
        ]
    ).astype(jnp.int32)

    def to_half(piece, *before):
        for bit in reversed(range(1, shard_levels)):
            got = ordered(from_mask(piece, 0, 2**bit), *before)
            piece = join(shard >> bit & 1, piece, got)
        return piece

    own_half = lax.dynamic_slice_in_dim(inputs, near * half_rows, half_rows, 0)
    own_part = lax.dynamic_slice_in_dim(inputs, part_of(shard) * part_rows, part_rows, 0)
    inputs_near = {
        bit: from_mask(own_part if bit == bits[0] else own_half, bit * others, 0) for bit in bits
    }

    send, hidden_near = forward(place, inputs, w_in, w_out)
    got = from_mask(send, 0, 1)
    summed = product(place, hidden_near, w_out)
    for bit in range(1, shard_levels):
        send, summed = add_and_split(shard >> bit & 1, summed, got)
        got = from_mask(send, 0, 2**bit)
    error = error_part(place, summed, got, targets, tuple(inputs_near.values()))

    errors_near = {bit: from_mask(error, bit * others, 0) for bit in bits[:1]}
    error = to_half(error)
    errors_near.update({bit: from_mask(error, bit * others, 0) for bit in bits[1:]})
    masks = [m for m in range(members) if not m & swap]
    lowest = {m: m & -m for m in masks}

    def both_halves(half):
        return [(half, NEAR), (from_mask(half, 0, 1), FAR)]

    slots, labels, known, sent = [], [], [], []
    totals = jnp.zeros((8, 128), jnp.float32)
    for n, m in enumerate(masks):
        if n == 0:
            half = error
        elif m not in errors_near:
            half = from_mask(errors_near[m - lowest[m]], lowest[m] * others, 0)
            ready = ordered(inputs_near[m - lowest[m]], errors_near[lowest[m]])
            inputs_near[m] = from_mask(ready, lowest[m] * others, 0)
            half, inputs_near[m] = (ordered(a, sent[-1]) for a in (half, inputs_near[m]))
        elif m == bits[0]:
            half = ordered(errors_near[m], sent[0])
            half = errors_near[m] = to_half(half, *sent[1:2], *(s for slot in slots[1:2] for s in slot))
        else:
            half = errors_near[m] = ordered(errors_near[m], sent[0], inputs_near[bits[0]])
        if n > 1:
            half = ordered(half, slots[2 * n - 3][0])
        first, second, send = gradient(
            place,
            members,
            swap,
            both_halves(half),
            both_halves(inputs_near[m]) if n else [(inputs, None)],
            w_in,
            w_out,
            known[-2:-1],
        )
        if n == 0 and len(masks) > 1:
            inputs_near[bits[0]] = to_half(inputs_near[bits[0]], send)
        sent.append(send)
        slots.append((first, second))
        labels.append(m)
        last = n == len(masks) - 1
        if last:
            totals = products(place, slots, labels, 1, totals)
        slots.append((from_mask(send, swap * others, 0),))
        labels.append(m ^ swap)
        totals = products(place, slots, labels, 1 if last else 2, totals)
        known.append(totals)

    totals = group_total(totals, gathered - 1, levels)
    pieces = merge(place, totals, slots, labels)

    for section in range(gathered, levels):
        upper_flag = position >> levels - 1 - section & 1
        keep_first, send_first = split_piece(pieces[0], upper_flag)
        keep_second, send_second = split_piece(pieces[1], upper_flag)
        got_first, got_second = from_partner((send_first, send_second), "dp", levels - 1 - section)
        pieces = combine(
            (keep_first, keep_second), (got_first, got_second), upper_flag, section, levels
        )
    return (pieces[0], pieces[1])


def solution(mesh):
    placed = (P("dp", None), P("dp", None), P(None, "tensor"), P("tensor", None))
    return jax.shard_map(
        on_device,
        mesh=mesh,
        in_specs=placed,
        out_specs=(P("dp", "tensor"), P("dp", "tensor")),
        check_vma=False,
    )
```

```python
import functools
import math

import jax
import jax.numpy as jnp
from jax import lax
from jax.experimental import pallas as pl
from jax.experimental.pallas import tpu as pltpu
from jax.sharding import PartitionSpec as P

epsilon = 1e-06
gather_levels_limit = 3
vmem_bytes = 36 * 2**20
vmem_most = 60 * 2**20


def from_partner(value, axis, distance):
    mask = 2**distance
    pairs = [(source, source ^ mask) for source in range(lax.axis_size(axis))]
    return lax.ppermute(value, axis, pairs)


def from_mask(value, dp_mask, tensor_mask):
    shards = lax.axis_size("tensor")
    mask = dp_mask * shards + tensor_mask
    pairs = [(source, source ^ mask) for source in range(lax.axis_size("dp") * shards)]
    return lax.ppermute(value, ("dp", "tensor"), pairs)


def ordered(value, *before):
    return lax.optimization_barrier((value, *before))[0]


def split_piece(piece, upper_flag):
    half = piece.shape[0] // 2
    keep = lax.dynamic_slice_in_dim(piece, upper_flag * half, half, 0)
    send = lax.dynamic_slice_in_dim(piece, (1 - upper_flag) * half, half, 0)
    return (keep, send)


def group_total(values, section, levels):
    summed = lax.psum(values, "tensor")
    for offset in range(section + 1):
        summed = summed + from_partner(summed, "dp", levels - 1 - offset)
    return summed


def combine(own, incoming, upper_flag, section, levels):
    product = jnp.sum(own[0] * incoming[0]) + jnp.sum(own[1] * incoming[1])
    norm_own = jnp.sum(own[0] * own[0]) + jnp.sum(own[1] * own[1])
    norm_incoming = jnp.sum(incoming[0] * incoming[0]) + jnp.sum(incoming[1] * incoming[1])
    is_upper = upper_flag == 1
    norm_low = jnp.where(is_upper, norm_incoming, norm_own)
    norm_high = jnp.where(is_upper, norm_own, norm_incoming)
    totals = group_total(jnp.stack([product, norm_low, norm_high]), section, levels)
    coef_low = 1.0 - totals[0] / (2.0 * (totals[1] + epsilon))
    coef_high = 1.0 - totals[0] / (2.0 * (totals[2] + epsilon))
    coef_own = jnp.where(is_upper, coef_high, coef_low)
    coef_incoming = jnp.where(is_upper, coef_low, coef_high)
    return (
        coef_own * own[0] + coef_incoming * incoming[0],
        coef_own * own[1] + coef_incoming * incoming[1],
    )


def tile_of(size, limit):
    return max(b for b in range(128, limit + 1, 128) if size % b == 0)


def contract(left, right, left_dim, right_dim):
    dims = (((left_dim,), (right_dim,)), ((), ()))
    return lax.dot_general(left, right, dims, preferred_element_type=jnp.float32)


def call(kernel, name, operands, shapes, after=(), vmem=vmem_bytes, **spec):
    spec["in_specs"] = [pl.BlockSpec(memory_space=pl.ANY)] * len(after) + spec["in_specs"]

    def body(place_ref, *refs):
        kernel(place_ref, *refs[len(after) :])

    return pl.pallas_call(
        body,
        grid_spec=pltpu.PrefetchScalarGridSpec(num_scalar_prefetch=1, **spec),
        out_shape=shapes,
        compiler_params=pltpu.CompilerParams(vmem_limit_bytes=vmem),
        cost_estimate=pl.CostEstimate(flops=1, bytes_accessed=1, transcendentals=0),
        name=name,
    )(operands[0], *after, *operands[1:])


WINDOW, SHIFT, OTHER_SHIFT, MEMBER, NEAR, FAR, PART = range(7)


def row_start(place_ref, block, where):
    return 0 if where is None else pl.multiple_of(place_ref[where] * block.shape[0], 16)


def whole(n, s):
    return (0, 0)


def column(n, s):
    return (0, n)


SCALE = math.sqrt(2.0 / math.pi)
CUBE = 0.044715


def forward_kernel(
    steps, place_ref, rows_ref, w_in_ref, w_out_ref, out_ref, near_ref, half_ref, part_ref, hidden
):
    step = pl.program_id(0)
    half = out_ref.shape[0]
    far = pl.ds(row_start(place_ref, out_ref, FAR), half)
    tile = w_in_ref.shape[1]

    for n in range(steps):

        @pl.when(step == n)
        def _():
            v = jnp.dot(rows_ref[...], w_in_ref[...], preferred_element_type=jnp.float32)
            t = jnp.tanh(v * (SCALE + (SCALE * CUBE) * (v * v)))
            hidden[:, n * tile : (n + 1) * tile] = (v * (0.5 + 0.5 * t)).astype(jnp.bfloat16)

    @pl.when(step == 0)
    def _():
        half_ref[...] = rows_ref[pl.ds(row_start(place_ref, half_ref, NEAR), half), :]
        part_ref[...] = rows_ref[pl.ds(row_start(place_ref, part_ref, PART), part_ref.shape[0]), :]

    @pl.when(step == steps)
    def _():
        near_ref[...] = hidden[pl.ds(row_start(place_ref, out_ref, NEAR), half), :]

    @pl.when(step >= steps)
    def _():
        out_ref[...] = jnp.dot(hidden[far, :], w_out_ref[...], preferred_element_type=jnp.float32)


def forward(place, part_rows, inputs, w_in, w_out):
    rows = inputs.shape[0]
    depth, width = w_in.shape
    tile, out_tile = tile_of(width, 640), tile_of(depth, 640)
    steps = width // tile
    last = lambda n: jnp.maximum(n - steps, 0)
    return call(
        functools.partial(forward_kernel, steps),
        "forward",
        (place, inputs, w_in, w_out),
        [
            jax.ShapeDtypeStruct((rows // 2, depth), jnp.float32),
            jax.ShapeDtypeStruct((rows // 2, width), jnp.bfloat16),
            jax.ShapeDtypeStruct((rows // 2, depth), jnp.bfloat16),
            jax.ShapeDtypeStruct((part_rows, depth), jnp.bfloat16),
        ],
        vmem=vmem_most,
        grid=(steps + depth // out_tile,),
        in_specs=[
            pl.BlockSpec((rows, depth), whole),
            pl.BlockSpec((depth, tile), lambda n, s: (0, jnp.minimum(n, steps - 1))),
            pl.BlockSpec((width, out_tile), lambda n, s: (0, last(n))),
        ],
        out_specs=[
            pl.BlockSpec((rows // 2, out_tile), lambda n, s: (0, last(n))),
            pl.BlockSpec((rows // 2, width), whole),
            pl.BlockSpec((rows // 2, depth), whole),
            pl.BlockSpec((part_rows, depth), whole),
        ],
        scratch_shapes=[pltpu.VMEM((rows, width), jnp.bfloat16)],
    )


def product_kernel(place_ref, left_ref, right_ref, out_ref):
    out_ref[...] = jnp.dot(left_ref[...], right_ref[...], preferred_element_type=jnp.float32)


def product(place, left, right):
    rows, depth = left.shape
    width = right.shape[1]
    tile = tile_of(width, 640)
    return call(
        product_kernel,
        "product",
        (place, left, right),
        [jax.ShapeDtypeStruct((rows, width), jnp.float32)],
        grid=(width // tile,),
        in_specs=[pl.BlockSpec((rows, depth), whole), pl.BlockSpec((depth, tile), column)],
        out_specs=[pl.BlockSpec((rows, tile), column)],
    )[0]


def add_kernel(place_ref, own_send, got_send, own_keep, got_keep, send_ref, keep_ref):
    send_ref[...] = own_send[...] + got_send[...]
    keep_ref[...] = own_keep[...] + got_keep[...]


def add_and_split(flag, own, got):
    rows, depth = own.shape[0] // 2, own.shape[1]
    sent = pl.BlockSpec((rows, depth), lambda n, s: (1 - s[0], 0))
    kept = pl.BlockSpec((rows, depth), lambda n, s: (s[0], 0))
    shape = jax.ShapeDtypeStruct((rows, depth), jnp.float32)
    return call(
        add_kernel,
        "add_and_split",
        (flag.reshape(1), own, got, own, got),
        [shape, shape],
        grid=(1,),
        in_specs=[sent, sent, kept, kept],
        out_specs=[pl.BlockSpec((rows, depth), whole)] * 2,
    )


def join_kernel(place_ref, own_ref, got_ref, out_ref):
    rows = own_ref.shape[0]
    out_ref[pl.ds(pl.multiple_of(place_ref[0] * rows, 16), rows), :] = own_ref[...]
    out_ref[pl.ds(pl.multiple_of((1 - place_ref[0]) * rows, 16), rows), :] = got_ref[...]


def join(flag, own, got):
    rows, depth = own.shape
    return call(
        join_kernel,
        "join",
        (flag.reshape(1), own, got),
        [jax.ShapeDtypeStruct((2 * rows, depth), own.dtype)],
        grid=(1,),
        in_specs=[pl.BlockSpec((rows, depth), whole)] * 2,
        out_specs=[pl.BlockSpec((2 * rows, depth), whole)],
    )[0]


def error_kernel(row_count, place_ref, own_ref, got_ref, targets_ref, error_ref):
    out = own_ref[...] + got_ref[...]
    error = (out - targets_ref[...].astype(jnp.float32)) / row_count
    error_ref[...] = error.astype(jnp.bfloat16)


def error_part(place, own, got, targets, after):
    rows, depth = own.shape
    return call(
        functools.partial(error_kernel, targets.shape[0]),
        "error_part",
        (place, own, got, targets),
        [jax.ShapeDtypeStruct((rows, depth), jnp.bfloat16)],
        after,
        grid=(1,),
        in_specs=[
            pl.BlockSpec((rows, depth), whole),
            pl.BlockSpec((rows, depth), whole),
            pl.BlockSpec((rows, depth), lambda n, s: (s[PART], 0)),
        ],
        out_specs=[pl.BlockSpec((rows, depth), whole)],
    )[0]


def gradient_kernel(wheres, window, own, step_rows, place_ref, *refs):
    error_wheres, input_wheres = wheres
    refs = list(refs)

    def take(n):
        taken = refs[:n]
        del refs[:n]
        return taken

    error_refs, input_refs = take(len(error_wheres)), take(len(input_wheres))
    w_in_ref, w_out_ref, first_ref, second_ref, send_first_ref, send_second_ref = take(6)
    errors, inputs, inputs_turned, errors_turned, spread_first, spread_second = refs
    if len(input_refs) == 1:
        inputs = input_refs[0]

    @pl.when(pl.program_id(0) == 0)
    def _():
        for block, where in zip(error_refs, error_wheres):
            errors[pl.ds(row_start(place_ref, block, where), block.shape[0]), :] = block[...]
        if len(input_refs) > 1:
            for block, where in zip(input_refs, input_wheres):
                inputs[pl.ds(row_start(place_ref, block, where), block.shape[0]), :] = block[...]
        lane = pl.multiple_of(place_ref[WINDOW] * 128, 128)
        inputs_turned[...] = inputs[:, pl.ds(lane, window * 128)].T
        errors_turned[...] = errors[:, pl.ds(lane, window * 128)].T

    shift = pl.multiple_of(place_ref[SHIFT], step_rows)
    other_shift = pl.multiple_of(place_ref[OTHER_SHIFT], step_rows)
    v = jnp.dot(inputs[...], w_in_ref[...], preferred_element_type=jnp.float32)
    back = lax.dot_general(
        errors[...], w_out_ref[...], (((1,), (1,)), ((), ())), preferred_element_type=jnp.float32
    )
    square = v * v
    t = jnp.tanh(v * (SCALE + (SCALE * CUBE) * square))
    upper = 0.5 + 0.5 * t
    hidden = (v * upper).astype(jnp.bfloat16)
    spread_second[...] = jnp.dot(errors_turned[...], hidden, preferred_element_type=jnp.float32)
    slope = upper + (0.5 * v) * (1.0 - t * t) * (SCALE + (3.0 * SCALE * CUBE) * square)
    dpre = (back * slope).astype(jnp.bfloat16)
    spread_first[...] = jnp.dot(inputs_turned[...], dpre, preferred_element_type=jnp.float32)
    second_ref[...] = spread_second[pl.ds(shift, own), :]
    send_second_ref[...] = spread_second[pl.ds(other_shift, own), :].astype(jnp.bfloat16)
    first_ref[...] = spread_first[pl.ds(shift, own), :]
    send_first_ref[...] = spread_first[pl.ds(other_shift, own), :].astype(jnp.bfloat16)


def gradient(place, members, swap, errors, inputs, w_in, w_out, after=()):
    error_arrays, error_wheres = zip(*errors)
    input_arrays, input_wheres = zip(*inputs)
    depth, width = w_in.shape
    rows = sum(a.shape[0] for a in input_arrays)
    own = depth // members
    reach = max(m * own % 128 for m in range(members) if not m & swap) + (swap + 1) * own
    window = -(-reach // 128)
    tile = tile_of(width, 640)
    once = pl.Buffered(1)
    return call(
        functools.partial(
            gradient_kernel, (error_wheres, input_wheres), window, own, math.gcd(own, 128)
        ),
        "gradient",
        (place, *error_arrays, *input_arrays, w_in, w_out),
        [
            jax.ShapeDtypeStruct((own, width), jnp.float32),
            jax.ShapeDtypeStruct((own, width), jnp.float32),
            jax.ShapeDtypeStruct((own, width), jnp.bfloat16),
            jax.ShapeDtypeStruct((own, width), jnp.bfloat16),
        ],
        after,
        grid=(width // tile,),
        in_specs=[
            pl.BlockSpec(a.shape, whole, pipeline_mode=once)
            for a in (*error_arrays, *input_arrays)
        ]
        + [pl.BlockSpec((depth, tile), column), pl.BlockSpec((tile, depth), lambda n, s: (n, 0))],
        out_specs=[pl.BlockSpec((own, tile), column)] * 4,
        scratch_shapes=[
            pltpu.VMEM((rows, depth), jnp.bfloat16),
            pltpu.VMEM((rows, depth), jnp.bfloat16),
            pltpu.VMEM((window * 128, rows), jnp.bfloat16),
            pltpu.VMEM((window * 128, rows), jnp.bfloat16),
            pltpu.VMEM((window * 128, tile), jnp.float32),
            pltpu.VMEM((window * 128, tile), jnp.float32),
        ],
    )


def products_kernel(labels, fresh, place_ref, *refs):
    own = refs[0].shape[0]
    slots = [refs[2 * n : 2 * n + 2] for n in range(len(labels))]
    known_ref, out_ref, totals = refs[2 * len(labels) :]
    pairs = [(i, j) for i in range(len(slots) - fresh, len(slots)) for j in range(i + 1)]

    @pl.when(pl.program_id(0) == 0)
    def _():
        totals[...] = jnp.zeros_like(totals)

    def values(slot):
        return [ref[...].astype(jnp.float32) for ref in slot]

    for n, (i, j) in enumerate(pairs):
        a, b = values(slots[i]), values(slots[j])
        both = a[0] * b[0] + a[1] * b[1]
        totals[n] += jnp.sum(both.reshape(own // 8, 8, -1), axis=0)

    @pl.when(pl.program_id(0) == pl.num_programs(0) - 1)
    def _():
        result = known_ref[...]
        row = lax.broadcasted_iota(jnp.int32, result.shape, 0)
        column = lax.broadcasted_iota(jnp.int32, result.shape, 1)
        for n, (i, j) in enumerate(pairs):
            i, j = (jnp.bitwise_xor(place_ref[MEMBER], labels[k]) for k in (i, j))
            here = ((row == i) & (column == j)) | ((row == j) & (column == i))
            result = result + jnp.where(here, jnp.sum(totals[n]), 0.0)
        out_ref[...] = result


def products(place, slots, labels, fresh, known, after=()):
    arrays = [a for slot in slots for a in slot]
    own, width = slots[0][0].shape
    tile = tile_of(width, 256)
    pairs = sum(len(slots) - n for n in range(fresh))
    return call(
        functools.partial(products_kernel, tuple(labels), fresh),
        "products",
        (place, *arrays, known),
        [jax.ShapeDtypeStruct(known.shape, jnp.float32)],
        after,
        grid=(width // tile,),
        in_specs=[pl.BlockSpec((a.shape[0], tile), lambda n, s: (0, n)) for a in arrays]
        + [pl.BlockSpec(known.shape, whole)],
        out_specs=[pl.BlockSpec(known.shape, whole)],
        scratch_shapes=[pltpu.VMEM((pairs, 8, tile), jnp.float32)],
    )[0]


def tree_weights(count, entry):
    def inner(a, b):
        total = 0.0
        for i, u in a.items():
            for j, v in b.items():
                total = total + u * v * entry(i, j)
        return total

    items = [{i: 1.0} for i in range(count)]
    while len(items) > 1:
        half = len(items) // 2
        merged = []
        for low, high in zip(items[:half], items[half:]):
            product = inner(low, high)
            scale_low = 1.0 - product / (2.0 * (jnp.maximum(inner(low, low), 0.0) + epsilon))
            scale_high = 1.0 - product / (2.0 * (jnp.maximum(inner(high, high), 0.0) + epsilon))
            joined = {i: u * scale_low for i, u in low.items()}
            joined.update({i: u * scale_high for i, u in high.items()})
            merged.append(joined)
        items = merged
    return [items[0][i] for i in range(count)]


def merge_kernel(labels, place_ref, totals_ref, *refs):
    refs, (first_ref, second_ref, weights_ref) = refs[:-3], refs[-3:]

    @pl.when(pl.program_id(0) == 0)
    def _():
        def entry(i, j):
            i, j = (jnp.bitwise_xor(place_ref[MEMBER], k) for k in (i, j))
            return totals_ref[i, j]

        for n, weight in enumerate(tree_weights(len(labels), entry)):
            weights_ref[n] = weight

    first = second = 0.0
    for n, label in enumerate(labels):
        weight = weights_ref[label]
        first = first + weight * refs[2 * n][...].astype(jnp.float32)
        second = second + weight * refs[2 * n + 1][...].astype(jnp.float32)
    first_ref[...] = first
    second_ref[...] = second


def merge(place, totals, slots, labels):
    own, width = slots[0][0].shape
    block = max(b for b in range(16, min(own, 32) + 1, 16) if own % b == 0)
    spec = pl.BlockSpec((block, width), lambda n, s: (n, 0))
    arrays = [a for slot in slots for a in slot]
    shape = jax.ShapeDtypeStruct((own, width), jnp.float32)
    return call(
        functools.partial(merge_kernel, tuple(labels)),
        "merge",
        (place, totals, *arrays),
        [shape, shape],
        vmem=vmem_most,
        grid=(own // block,),
        in_specs=[pl.BlockSpec(memory_space=pltpu.SMEM)] + [spec] * len(arrays),
        out_specs=[spec, spec],
        scratch_shapes=[pltpu.SMEM((len(slots),), jnp.float32)],
    )


def on_device(inputs, targets, w_in, w_out):
    row_count = inputs.shape[0]
    workers = lax.axis_size("dp")
    shards = lax.axis_size("tensor")
    levels = workers.bit_length() - 1
    shard_levels = shards.bit_length() - 1
    gathered = min(levels, gather_levels_limit)
    members = 2**gathered
    others = workers // members
    position = lax.axis_index("dp")
    shard = lax.axis_index("tensor")
    member = position // others

    def part_of(index):
        part = 0
        for bit in range(shard_levels):
            part = part * 2 + (index >> bit & 1)
        return part

    near = shard & 1
    part_rows = row_count // shards
    own = inputs.shape[1] // members
    swap = min(2, members // 2)
    bits = [2**b for b in reversed(range(gathered)) if 2**b != swap]
    upper = member // swap % 2
    first_row = (member - upper * swap) * own
    place = jnp.stack(
        [
            first_row // 128,
            first_row % 128 + upper * swap * own,
            first_row % 128 + (1 - upper) * swap * own,
            member,
            near,
            1 - near,
            part_of(shard),
        ]
    ).astype(jnp.int32)

    def to_half(piece, *before):
        for bit in reversed(range(1, shard_levels)):
            got = ordered(from_mask(piece, 0, 2**bit), *before)
            piece = join(shard >> bit & 1, piece, got)
        return piece

    send, hidden_near, own_half, own_part = forward(place, part_rows, inputs, w_in, w_out)
    got = from_mask(send, 0, 1)
    inputs_near = {
        bit: from_mask(own_part if bit == bits[0] else own_half, bit * others, 0) for bit in bits
    }
    summed = product(place, hidden_near, w_out)
    for bit in range(1, shard_levels):
        send, summed = add_and_split(shard >> bit & 1, summed, got)
        got = from_mask(send, 0, 2**bit)
    error = error_part(place, summed, got, targets, tuple(inputs_near.values()))

    errors_near = {bit: from_mask(error, bit * others, 0) for bit in bits[:1]}
    error = to_half(error)
    errors_near.update({bit: from_mask(error, bit * others, 0) for bit in bits[1:]})
    masks = [m for m in range(members) if not m & swap]
    lowest = {m: m & -m for m in masks}

    def both_halves(half):
        return [(half, NEAR), (from_mask(half, 0, 1), FAR)]

    slots, labels, known, sent = [], [], [], []
    totals = jnp.zeros((8, 128), jnp.float32)
    for n, m in enumerate(masks):
        if n == 0:
            half = error
        elif m not in errors_near:
            half = from_mask(errors_near[m - lowest[m]], lowest[m] * others, 0)
            half, inputs_near[m] = (ordered(a, sent[-1]) for a in (half, inputs_near[m]))
            half = ordered(half, *slots[2 * n - 3])
        elif m == bits[0]:
            before = [sent[-1], *slots[1]]
            for bit in bits[1:]:
                ready = ordered(inputs_near[m], errors_near[bit])
                inputs_near[m | bit] = from_mask(ready, bit * others, 0)
                before.append(inputs_near[m | bit])
            half = to_half(ordered(errors_near[m], sent[0]), *before)
            errors_near[m] = half
        else:
            first_bit = bits[0]
            half = ordered(errors_near[m], sent[0], inputs_near[first_bit], errors_near[first_bit])
            errors_near[m] = half
            half = ordered(half, slots[2 * n - 1][0])
        first, second, *send = gradient(
            place,
            members,
            swap,
            both_halves(half),
            both_halves(inputs_near[m]) if n else [(inputs, None)],
            w_in,
            w_out,
            known[-2:-1],
        )
        if n == 0 and len(masks) > 1:
            inputs_near[bits[0]] = to_half(inputs_near[bits[0]], send[0])
        sent.append(send[0])
        slots.append((first, second))
        labels.append(m)
        last = n == len(masks) - 1
        if last:
            totals = products(place, slots, labels, 1, totals)
        slots.append(tuple(from_mask(a, swap * others, 0) for a in send))
        labels.append(m ^ swap)
        totals = products(place, slots, labels, 1 if last else 2, totals)
        known.append(totals)

    totals = group_total(totals, gathered - 1, levels)
    pieces = merge(place, totals, slots, labels)

    for section in range(gathered, levels):
        upper_flag = position >> levels - 1 - section & 1
        keep_first, send_first = split_piece(pieces[0], upper_flag)
        keep_second, send_second = split_piece(pieces[1], upper_flag)
        got_first, got_second = from_partner((send_first, send_second), "dp", levels - 1 - section)
        pieces = combine(
            (keep_first, keep_second), (got_first, got_second), upper_flag, section, levels
        )
    return (pieces[0], pieces[1])


def solution(mesh):
    placed = (P("dp", None), P("dp", None), P(None, "tensor"), P("tensor", None))
    return jax.shard_map(
        on_device,
        mesh=mesh,
        in_specs=placed,
        out_specs=(P("dp", "tensor"), P("dp", "tensor")),
        check_vma=False,
    )
```

```python
import functools
import math

import jax
import jax.numpy as jnp
from jax import lax
from jax.experimental import pallas as pl
from jax.experimental.pallas import tpu as pltpu
from jax.sharding import PartitionSpec as P

epsilon = 1e-06
gather_levels_limit = 3
vmem_bytes = 36 * 2**20
vmem_most = 60 * 2**20


def from_partner(value, axis, distance):
    mask = 2**distance
    pairs = [(source, source ^ mask) for source in range(lax.axis_size(axis))]
    return lax.ppermute(value, axis, pairs)


def from_mask(value, dp_mask, tensor_mask):
    shards = lax.axis_size("tensor")
    mask = dp_mask * shards + tensor_mask
    pairs = [(source, source ^ mask) for source in range(lax.axis_size("dp") * shards)]
    return lax.ppermute(value, ("dp", "tensor"), pairs)


def ordered(value, *before):
    return lax.optimization_barrier((value, *before))[0]


def split_piece(piece, upper_flag):
    half = piece.shape[0] // 2
    keep = lax.dynamic_slice_in_dim(piece, upper_flag * half, half, 0)
    send = lax.dynamic_slice_in_dim(piece, (1 - upper_flag) * half, half, 0)
    return (keep, send)


def group_total(values, section, levels):
    summed = lax.psum(values, "tensor")
    for offset in range(section + 1):
        summed = summed + from_partner(summed, "dp", levels - 1 - offset)
    return summed


def combine(own, incoming, upper_flag, section, levels):
    product = jnp.sum(own[0] * incoming[0]) + jnp.sum(own[1] * incoming[1])
    norm_own = jnp.sum(own[0] * own[0]) + jnp.sum(own[1] * own[1])
    norm_incoming = jnp.sum(incoming[0] * incoming[0]) + jnp.sum(incoming[1] * incoming[1])
    is_upper = upper_flag == 1
    norm_low = jnp.where(is_upper, norm_incoming, norm_own)
    norm_high = jnp.where(is_upper, norm_own, norm_incoming)
    totals = group_total(jnp.stack([product, norm_low, norm_high]), section, levels)
    coef_low = 1.0 - totals[0] / (2.0 * (totals[1] + epsilon))
    coef_high = 1.0 - totals[0] / (2.0 * (totals[2] + epsilon))
    coef_own = jnp.where(is_upper, coef_high, coef_low)
    coef_incoming = jnp.where(is_upper, coef_low, coef_high)
    return (
        coef_own * own[0] + coef_incoming * incoming[0],
        coef_own * own[1] + coef_incoming * incoming[1],
    )


def tile_of(size, limit):
    return max(b for b in range(128, limit + 1, 128) if size % b == 0)


def contract(left, right, left_dim, right_dim):
    dims = (((left_dim,), (right_dim,)), ((), ()))
    return lax.dot_general(left, right, dims, preferred_element_type=jnp.float32)


def call(kernel, name, operands, shapes, after=(), vmem=vmem_bytes, **spec):
    spec["in_specs"] = [pl.BlockSpec(memory_space=pl.ANY)] * len(after) + spec["in_specs"]

    def body(place_ref, *refs):
        kernel(place_ref, *refs[len(after) :])

    return pl.pallas_call(
        body,
        grid_spec=pltpu.PrefetchScalarGridSpec(num_scalar_prefetch=1, **spec),
        out_shape=shapes,
        compiler_params=pltpu.CompilerParams(vmem_limit_bytes=vmem),
        cost_estimate=pl.CostEstimate(flops=1, bytes_accessed=1, transcendentals=0),
        name=name,
    )(operands[0], *after, *operands[1:])


WINDOW, SHIFT, OTHER_SHIFT, MEMBER, NEAR, FAR, PART, PIECE = range(8)


def row_start(place_ref, block, where):
    return 0 if where is None else pl.multiple_of(place_ref[where] * block.shape[0], 16)


def whole(n, s):
    return (0, 0)


def column(n, s):
    return (0, n)


SCALE = math.sqrt(2.0 / math.pi)
CUBE = 0.044715


def forward_kernel(
    steps, place_ref, rows_ref, w_in_ref, w_out_ref, out_ref, near_ref, half_ref, part_ref, hidden
):
    step = pl.program_id(0)
    half = out_ref.shape[0]
    far = pl.ds(row_start(place_ref, out_ref, FAR), half)
    tile = w_in_ref.shape[1]

    for n in range(steps):

        @pl.when(step == n)
        def _():
            v = jnp.dot(rows_ref[...], w_in_ref[...], preferred_element_type=jnp.float32)
            t = jnp.tanh(v * (SCALE + (SCALE * CUBE) * (v * v)))
            hidden[:, n * tile : (n + 1) * tile] = (v * (0.5 + 0.5 * t)).astype(jnp.bfloat16)

    @pl.when(step == 0)
    def _():
        half_ref[...] = rows_ref[pl.ds(row_start(place_ref, half_ref, NEAR), half), :]
        part_ref[...] = rows_ref[pl.ds(row_start(place_ref, part_ref, PART), part_ref.shape[0]), :]

    @pl.when(step == steps)
    def _():
        near_ref[...] = hidden[pl.ds(row_start(place_ref, out_ref, NEAR), half), :]

    @pl.when(step >= steps)
    def _():
        out_ref[...] = jnp.dot(hidden[far, :], w_out_ref[...], preferred_element_type=jnp.float32)


def forward(place, part_rows, inputs, w_in, w_out):
    rows = inputs.shape[0]
    depth, width = w_in.shape
    tile, out_tile = tile_of(width, 640), tile_of(depth, 640)
    steps = width // tile
    last = lambda n: jnp.maximum(n - steps, 0)
    return call(
        functools.partial(forward_kernel, steps),
        "forward",
        (place, inputs, w_in, w_out),
        [
            jax.ShapeDtypeStruct((rows // 2, depth), jnp.float32),
            jax.ShapeDtypeStruct((rows // 2, width), jnp.bfloat16),
            jax.ShapeDtypeStruct((rows // 2, depth), jnp.bfloat16),
            jax.ShapeDtypeStruct((part_rows, depth), jnp.bfloat16),
        ],
        vmem=vmem_most,
        grid=(steps + depth // out_tile,),
        in_specs=[
            pl.BlockSpec((rows, depth), whole),
            pl.BlockSpec((depth, tile), lambda n, s: (0, jnp.minimum(n, steps - 1))),
            pl.BlockSpec((width, out_tile), lambda n, s: (0, last(n))),
        ],
        out_specs=[
            pl.BlockSpec((rows // 2, out_tile), lambda n, s: (0, last(n))),
            pl.BlockSpec((rows // 2, width), whole),
            pl.BlockSpec((rows // 2, depth), whole),
            pl.BlockSpec((part_rows, depth), whole),
        ],
        scratch_shapes=[pltpu.VMEM((rows, width), jnp.bfloat16)],
    )


def product_kernel(place_ref, left_ref, right_ref, out_ref):
    out_ref[...] = jnp.dot(left_ref[...], right_ref[...], preferred_element_type=jnp.float32)


def product(place, left, right):
    rows, depth = left.shape
    width = right.shape[1]
    tile = tile_of(width, 640)
    return call(
        product_kernel,
        "product",
        (place, left, right),
        [jax.ShapeDtypeStruct((rows, width), jnp.float32)],
        grid=(width // tile,),
        in_specs=[pl.BlockSpec((rows, depth), whole), pl.BlockSpec((depth, tile), column)],
        out_specs=[pl.BlockSpec((rows, tile), column)],
    )[0]


def add_kernel(place_ref, own_ref, got_ref, sum_ref, rounded_ref):
    total = own_ref[...] + got_ref[...].astype(jnp.float32)
    sum_ref[...] = total
    rounded_ref[...] = total.astype(jnp.bfloat16)


def add_and_round(place, own, got):
    shape = own.shape
    spec = pl.BlockSpec((shape[0] // 2, shape[1]), lambda n, s: (n, 0))
    return call(
        add_kernel,
        "add_and_round",
        (place, own, got),
        [jax.ShapeDtypeStruct(shape, jnp.float32), jax.ShapeDtypeStruct(shape, jnp.bfloat16)],
        grid=(2,),
        in_specs=[spec, spec],
        out_specs=[spec, spec],
    )


def join_kernel(place_ref, own_ref, got_ref, out_ref):
    rows = own_ref.shape[0]
    out_ref[pl.ds(pl.multiple_of(place_ref[0] * rows, 16), rows), :] = own_ref[...]
    out_ref[pl.ds(pl.multiple_of((1 - place_ref[0]) * rows, 16), rows), :] = got_ref[...]


def join(flag, own, got):
    rows, depth = own.shape
    return call(
        join_kernel,
        "join",
        (flag.reshape(1), own, got),
        [jax.ShapeDtypeStruct((2 * rows, depth), own.dtype)],
        grid=(1,),
        in_specs=[pl.BlockSpec((rows, depth), whole)] * 2,
        out_specs=[pl.BlockSpec((2 * rows, depth), whole)],
    )[0]


def error_kernel(row_count, place_ref, own_ref, got_ref, targets_ref, half_ref, part_ref):
    out = own_ref[...] + got_ref[...].astype(jnp.float32)
    error = (out - targets_ref[...].astype(jnp.float32)) / row_count
    half_ref[...] = error.astype(jnp.bfloat16)
    rows = part_ref.shape[0]
    part_ref[...] = half_ref[pl.ds(pl.multiple_of(place_ref[PIECE] * rows, 16), rows), :]


def error_half(place, part_rows, own, got, targets, after):
    rows, depth = own.shape
    return call(
        functools.partial(error_kernel, targets.shape[0]),
        "error_half",
        (place, own, got, targets),
        [
            jax.ShapeDtypeStruct((rows, depth), jnp.bfloat16),
            jax.ShapeDtypeStruct((part_rows, depth), jnp.bfloat16),
        ],
        after,
        grid=(1,),
        in_specs=[
            pl.BlockSpec((rows, depth), whole),
            pl.BlockSpec((rows, depth), whole),
            pl.BlockSpec((rows, depth), lambda n, s: (s[NEAR], 0)),
        ],
        out_specs=[pl.BlockSpec((rows, depth), whole), pl.BlockSpec((part_rows, depth), whole)],
    )


def gradient_kernel(wheres, window, own, step_rows, place_ref, *refs):
    error_wheres, input_wheres = wheres
    refs = list(refs)

    def take(n):
        taken = refs[:n]
        del refs[:n]
        return taken

    error_refs, input_refs = take(len(error_wheres)), take(len(input_wheres))
    w_in_ref, w_out_ref, first_ref, second_ref, send_first_ref, send_second_ref = take(6)
    errors, inputs, inputs_turned, errors_turned, spread_first, spread_second = refs
    if len(input_refs) == 1:
        inputs = input_refs[0]

    @pl.when(pl.program_id(0) == 0)
    def _():
        for block, where in zip(error_refs, error_wheres):
            errors[pl.ds(row_start(place_ref, block, where), block.shape[0]), :] = block[...]
        if len(input_refs) > 1:
            for block, where in zip(input_refs, input_wheres):
                inputs[pl.ds(row_start(place_ref, block, where), block.shape[0]), :] = block[...]
        lane = pl.multiple_of(place_ref[WINDOW] * 128, 128)
        inputs_turned[...] = inputs[:, pl.ds(lane, window * 128)].T
        errors_turned[...] = errors[:, pl.ds(lane, window * 128)].T

    shift = pl.multiple_of(place_ref[SHIFT], step_rows)
    other_shift = pl.multiple_of(place_ref[OTHER_SHIFT], step_rows)
    v = jnp.dot(inputs[...], w_in_ref[...], preferred_element_type=jnp.float32)
    back = lax.dot_general(
        errors[...], w_out_ref[...], (((1,), (1,)), ((), ())), preferred_element_type=jnp.float32
    )
    square = v * v
    t = jnp.tanh(v * (SCALE + (SCALE * CUBE) * square))
    upper = 0.5 + 0.5 * t
    hidden = (v * upper).astype(jnp.bfloat16)
    spread_second[...] = jnp.dot(errors_turned[...], hidden, preferred_element_type=jnp.float32)
    slope = upper + (0.5 * v) * (1.0 - t * t) * (SCALE + (3.0 * SCALE * CUBE) * square)
    dpre = (back * slope).astype(jnp.bfloat16)
    spread_first[...] = jnp.dot(inputs_turned[...], dpre, preferred_element_type=jnp.float32)
    second_ref[...] = spread_second[pl.ds(shift, own), :]
    send_second_ref[...] = spread_second[pl.ds(other_shift, own), :].astype(jnp.bfloat16)
    first_ref[...] = spread_first[pl.ds(shift, own), :]
    send_first_ref[...] = spread_first[pl.ds(other_shift, own), :].astype(jnp.bfloat16)


def gradient(place, members, swap, errors, inputs, w_in, w_out, after=()):
    error_arrays, error_wheres = zip(*errors)
    input_arrays, input_wheres = zip(*inputs)
    depth, width = w_in.shape
    rows = sum(a.shape[0] for a in input_arrays)
    own = depth // members
    reach = max(m * own % 128 for m in range(members) if not m & swap) + (swap + 1) * own
    window = -(-reach // 128)
    tile = tile_of(width, 640)
    once = pl.Buffered(1)
    return call(
        functools.partial(
            gradient_kernel, (error_wheres, input_wheres), window, own, math.gcd(own, 128)
        ),
        "gradient",
        (place, *error_arrays, *input_arrays, w_in, w_out),
        [
            jax.ShapeDtypeStruct((own, width), jnp.float32),
            jax.ShapeDtypeStruct((own, width), jnp.float32),
            jax.ShapeDtypeStruct((own, width), jnp.bfloat16),
            jax.ShapeDtypeStruct((own, width), jnp.bfloat16),
        ],
        after,
        grid=(width // tile,),
        in_specs=[
            pl.BlockSpec(a.shape, whole, pipeline_mode=once)
            for a in (*error_arrays, *input_arrays)
        ]
        + [pl.BlockSpec((depth, tile), column), pl.BlockSpec((tile, depth), lambda n, s: (n, 0))],
        out_specs=[pl.BlockSpec((own, tile), column)] * 4,
        scratch_shapes=[
            pltpu.VMEM((rows, depth), jnp.bfloat16),
            pltpu.VMEM((rows, depth), jnp.bfloat16),
            pltpu.VMEM((window * 128, rows), jnp.bfloat16),
            pltpu.VMEM((window * 128, rows), jnp.bfloat16),
            pltpu.VMEM((window * 128, tile), jnp.float32),
            pltpu.VMEM((window * 128, tile), jnp.float32),
        ],
    )


def products_kernel(labels, fresh, place_ref, *refs):
    own = refs[0].shape[0]
    slots = [refs[2 * n : 2 * n + 2] for n in range(len(labels))]
    known_ref, out_ref, totals = refs[2 * len(labels) :]
    pairs = [(i, j) for i in range(len(slots) - fresh, len(slots)) for j in range(i + 1)]

    @pl.when(pl.program_id(0) == 0)
    def _():
        totals[...] = jnp.zeros_like(totals)

    def values(slot):
        return [ref[...].astype(jnp.float32) for ref in slot]

    for n, (i, j) in enumerate(pairs):
        a, b = values(slots[i]), values(slots[j])
        both = a[0] * b[0] + a[1] * b[1]
        totals[n] += jnp.sum(both.reshape(own // 8, 8, -1), axis=0)

    @pl.when(pl.program_id(0) == pl.num_programs(0) - 1)
    def _():
        result = known_ref[...]
        row = lax.broadcasted_iota(jnp.int32, result.shape, 0)
        column = lax.broadcasted_iota(jnp.int32, result.shape, 1)
        for n, (i, j) in enumerate(pairs):
            i, j = (jnp.bitwise_xor(place_ref[MEMBER], labels[k]) for k in (i, j))
            here = ((row == i) & (column == j)) | ((row == j) & (column == i))
            result = result + jnp.where(here, jnp.sum(totals[n]), 0.0)
        out_ref[...] = result


def products(place, slots, labels, fresh, known, after=()):
    arrays = [a for slot in slots for a in slot]
    own, width = slots[0][0].shape
    tile = tile_of(width, 256)
    pairs = sum(len(slots) - n for n in range(fresh))
    return call(
        functools.partial(products_kernel, tuple(labels), fresh),
        "products",
        (place, *arrays, known),
        [jax.ShapeDtypeStruct(known.shape, jnp.float32)],
        after,
        grid=(width // tile,),
        in_specs=[pl.BlockSpec((a.shape[0], tile), lambda n, s: (0, n)) for a in arrays]
        + [pl.BlockSpec(known.shape, whole)],
        out_specs=[pl.BlockSpec(known.shape, whole)],
        scratch_shapes=[pltpu.VMEM((pairs, 8, tile), jnp.float32)],
    )[0]


def tree_weights(count, entry):
    def inner(a, b):
        total = 0.0
        for i, u in a.items():
            for j, v in b.items():
                total = total + u * v * entry(i, j)
        return total

    items = [{i: 1.0} for i in range(count)]
    while len(items) > 1:
        half = len(items) // 2
        merged = []
        for low, high in zip(items[:half], items[half:]):
            product = inner(low, high)
            scale_low = 1.0 - product / (2.0 * (jnp.maximum(inner(low, low), 0.0) + epsilon))
            scale_high = 1.0 - product / (2.0 * (jnp.maximum(inner(high, high), 0.0) + epsilon))
            joined = {i: u * scale_low for i, u in low.items()}
            joined.update({i: u * scale_high for i, u in high.items()})
            merged.append(joined)
        items = merged
    return [items[0][i] for i in range(count)]


def merge_kernel(labels, place_ref, totals_ref, *refs):
    refs, (first_ref, second_ref, weights_ref) = refs[:-3], refs[-3:]

    @pl.when(pl.program_id(0) == 0)
    def _():
        def entry(i, j):
            i, j = (jnp.bitwise_xor(place_ref[MEMBER], k) for k in (i, j))
            return totals_ref[i, j]

        for n, weight in enumerate(tree_weights(len(labels), entry)):
            weights_ref[n] = weight

    first = second = 0.0
    for n, label in enumerate(labels):
        weight = weights_ref[label]
        first = first + weight * refs[2 * n][...].astype(jnp.float32)
        second = second + weight * refs[2 * n + 1][...].astype(jnp.float32)
    first_ref[...] = first
    second_ref[...] = second


def merge(place, totals, slots, labels):
    own, width = slots[0][0].shape
    block = max(b for b in range(16, min(own, 32) + 1, 16) if own % b == 0)
    spec = pl.BlockSpec((block, width), lambda n, s: (n, 0))
    arrays = [a for slot in slots for a in slot]
    shape = jax.ShapeDtypeStruct((own, width), jnp.float32)
    return call(
        functools.partial(merge_kernel, tuple(labels)),
        "merge",
        (place, totals, *arrays),
        [shape, shape],
        vmem=vmem_most,
        grid=(own // block,),
        in_specs=[pl.BlockSpec(memory_space=pltpu.SMEM)] + [spec] * len(arrays),
        out_specs=[spec, spec],
        scratch_shapes=[pltpu.SMEM((len(slots),), jnp.float32)],
    )


def on_device(inputs, targets, w_in, w_out):
    row_count = inputs.shape[0]
    workers = lax.axis_size("dp")
    shards = lax.axis_size("tensor")
    levels = workers.bit_length() - 1
    shard_levels = shards.bit_length() - 1
    gathered = min(levels, gather_levels_limit)
    members = 2**gathered
    others = workers // members
    position = lax.axis_index("dp")
    shard = lax.axis_index("tensor")
    member = position // others

    def part_of(index):
        part = 0
        for bit in range(shard_levels):
            part = part * 2 + (index >> bit & 1)
        return part

    near = shard & 1
    part_rows = row_count // shards
    own = inputs.shape[1] // members
    swap = min(2, members // 2)
    bits = [2**b for b in reversed(range(gathered)) if 2**b != swap]
    upper = member // swap % 2
    first_row = (member - upper * swap) * own
    place = jnp.stack(
        [
            first_row // 128,
            first_row % 128 + upper * swap * own,
            first_row % 128 + (1 - upper) * swap * own,
            member,
            near,
            1 - near,
            part_of(shard),
            part_of(shard) - near * (shards // 2),
        ]
    ).astype(jnp.int32)

    first_bit = bits[0]
    send, hidden_near, own_half, own_part = forward(place, part_rows, inputs, w_in, w_out)
    got = from_mask(send, 0, 1)
    inputs_of = {
        bit: from_mask(own_part if bit == first_bit else own_half, bit * others, 0) for bit in bits
    }

    summed = product(place, hidden_near, w_out)
    for bit in range(1, shard_levels):
        summed, rounded = add_and_round(place, summed, got)
        got = from_mask(rounded, 0, 2**bit)
    error, error_piece = error_half(
        place, part_rows, summed, got, targets, tuple(inputs_of.values())
    )
    errors_of = {
        bit: from_mask(error_piece if bit == first_bit else error, bit * others, 0) for bit in bits
    }

    def to_half(piece, *before):
        for bit in reversed(range(1, shard_levels)):
            got = ordered(from_mask(piece, 0, 2**bit), *before)
            piece = join(shard >> bit & 1, piece, got)
        return piece

    def both_halves(half):
        return [(half, NEAR), (from_mask(half, 0, 1), FAR)]

    slots, labels, known, sent = [], [], [], []
    totals = jnp.zeros((8, 128), jnp.float32)
    masks = [m for m in range(members) if not m & swap]
    for n, m in enumerate(masks):
        if n == 0:
            half = error
        elif not m & first_bit:
            half = errors_of[m] = ordered(errors_of[m], sent[0], inputs_half, errors_of[first_bit])
            half = ordered(half, slots[2 * n - 1][0])
            other_inputs = inputs_of[m]
        elif m == first_bit:
            for bit in bits[1:]:
                ready = ordered(inputs_of[first_bit], errors_of[bit])
                inputs_of[first_bit | bit] = from_mask(ready, bit * others, 0)
                ready = ordered(errors_of[first_bit], errors_of[bit])
                errors_of[first_bit | bit] = from_mask(ready, bit * others, 0)
            before = [errors_of[first_bit | bit] for bit in bits[1:]]
            half = to_half(ordered(errors_of[m], sent[0]), sent[-1], *slots[1], *before)
            other_inputs = inputs_half
        else:
            other_inputs = to_half(ordered(inputs_of[m], sent[-1]))
            half = to_half(ordered(errors_of[m], sent[-2]), sent[-1], *slots[2 * n - 3])
        first, second, *send = gradient(
            place,
            members,
            swap,
            both_halves(half),
            both_halves(other_inputs) if n else [(inputs, None)],
            w_in,
            w_out,
            known[-2:-1],
        )
        if n == 0:
            inputs_half = to_half(inputs_of[first_bit], send[0])
        sent.append(send[0])
        slots.append((first, second))
        labels.append(m)
        last = n == len(masks) - 1
        if last:
            totals = products(place, slots, labels, 1, totals)
        slots.append(tuple(from_mask(a, swap * others, 0) for a in send))
        labels.append(m ^ swap)
        totals = products(place, slots, labels, 1 if last else 2, totals)
        known.append(totals)

    totals = group_total(totals, gathered - 1, levels)
    pieces = merge(place, totals, slots, labels)

    for section in range(gathered, levels):
        upper_flag = position >> levels - 1 - section & 1
        keep_first, send_first = split_piece(pieces[0], upper_flag)
        keep_second, send_second = split_piece(pieces[1], upper_flag)
        got_first, got_second = from_partner((send_first, send_second), "dp", levels - 1 - section)
        pieces = combine(
            (keep_first, keep_second), (got_first, got_second), upper_flag, section, levels
        )
    return (pieces[0], pieces[1])


def solution(mesh):
    placed = (P("dp", None), P("dp", None), P(None, "tensor"), P("tensor", None))
    return jax.shard_map(
        on_device,
        mesh=mesh,
        in_specs=placed,
        out_specs=(P("dp", "tensor"), P("dp", "tensor")),
        check_vma=False,
    )
```

```python
import functools
import math

import jax
import jax.numpy as jnp
from jax import lax
from jax.experimental import pallas as pl
from jax.experimental.pallas import tpu as pltpu
from jax.sharding import PartitionSpec as P

epsilon = 1e-06
gather_levels_limit = 3
vmem_bytes = 36 * 2**20
vmem_most = 60 * 2**20


def from_partner(value, axis, distance):
    mask = 2**distance
    pairs = [(source, source ^ mask) for source in range(lax.axis_size(axis))]
    return lax.ppermute(value, axis, pairs)


def from_mask(value, dp_mask, tensor_mask):
    shards = lax.axis_size("tensor")
    mask = dp_mask * shards + tensor_mask
    pairs = [(source, source ^ mask) for source in range(lax.axis_size("dp") * shards)]
    return lax.ppermute(value, ("dp", "tensor"), pairs)


def ordered(value, *before):
    return lax.optimization_barrier((value, *before))[0]


def split_piece(piece, upper_flag):
    half = piece.shape[0] // 2
    keep = lax.dynamic_slice_in_dim(piece, upper_flag * half, half, 0)
    send = lax.dynamic_slice_in_dim(piece, (1 - upper_flag) * half, half, 0)
    return (keep, send)


def group_total(values, section, levels):
    summed = lax.psum(values, "tensor")
    for offset in range(section + 1):
        summed = summed + from_partner(summed, "dp", levels - 1 - offset)
    return summed


def combine(own, incoming, upper_flag, section, levels):
    product = jnp.sum(own[0] * incoming[0]) + jnp.sum(own[1] * incoming[1])
    norm_own = jnp.sum(own[0] * own[0]) + jnp.sum(own[1] * own[1])
    norm_incoming = jnp.sum(incoming[0] * incoming[0]) + jnp.sum(incoming[1] * incoming[1])
    is_upper = upper_flag == 1
    norm_low = jnp.where(is_upper, norm_incoming, norm_own)
    norm_high = jnp.where(is_upper, norm_own, norm_incoming)
    totals = group_total(jnp.stack([product, norm_low, norm_high]), section, levels)
    coef_low = 1.0 - totals[0] / (2.0 * (totals[1] + epsilon))
    coef_high = 1.0 - totals[0] / (2.0 * (totals[2] + epsilon))
    coef_own = jnp.where(is_upper, coef_high, coef_low)
    coef_incoming = jnp.where(is_upper, coef_low, coef_high)
    return (
        coef_own * own[0] + coef_incoming * incoming[0],
        coef_own * own[1] + coef_incoming * incoming[1],
    )


def tile_of(size, limit):
    return max(b for b in range(128, limit + 1, 128) if size % b == 0)


def contract(left, right, left_dim, right_dim):
    dims = (((left_dim,), (right_dim,)), ((), ()))
    return lax.dot_general(left, right, dims, preferred_element_type=jnp.float32)


def call(kernel, name, operands, shapes, after=(), vmem=vmem_bytes, **spec):
    spec["in_specs"] = [pl.BlockSpec(memory_space=pl.ANY)] * len(after) + spec["in_specs"]

    def body(place_ref, *refs):
        kernel(place_ref, *refs[len(after) :])

    return pl.pallas_call(
        body,
        grid_spec=pltpu.PrefetchScalarGridSpec(num_scalar_prefetch=1, **spec),
        out_shape=shapes,
        compiler_params=pltpu.CompilerParams(vmem_limit_bytes=vmem),
        cost_estimate=pl.CostEstimate(flops=1, bytes_accessed=1, transcendentals=0),
        name=name,
    )(operands[0], *after, *operands[1:])


WINDOW, SHIFT, OTHER_SHIFT, MEMBER, NEAR, FAR, PART, PIECE = range(8)


def row_start(place_ref, block, where):
    return 0 if where is None else pl.multiple_of(place_ref[where] * block.shape[0], 16)


def whole(n, s):
    return (0, 0)


def column(n, s):
    return (0, n)


SCALE = math.sqrt(2.0 / math.pi)
CUBE = 0.044715


def forward_kernel(
    steps, place_ref, rows_ref, w_in_ref, w_out_ref, out_ref, near_ref, half_ref, part_ref, hidden
):
    step = pl.program_id(0)
    half = out_ref.shape[0]
    far = pl.ds(row_start(place_ref, out_ref, FAR), half)
    tile = w_in_ref.shape[1]

    for n in range(steps):

        @pl.when(step == n)
        def _():
            v = jnp.dot(rows_ref[...], w_in_ref[...], preferred_element_type=jnp.float32)
            t = jnp.tanh(v * (SCALE + (SCALE * CUBE) * (v * v)))
            hidden[:, n * tile : (n + 1) * tile] = (v * (0.5 + 0.5 * t)).astype(jnp.bfloat16)

    @pl.when(step == 0)
    def _():
        half_ref[...] = rows_ref[pl.ds(row_start(place_ref, half_ref, NEAR), half), :]
        part_ref[...] = rows_ref[pl.ds(row_start(place_ref, part_ref, PART), part_ref.shape[0]), :]

    @pl.when(step == steps)
    def _():
        near_ref[...] = hidden[pl.ds(row_start(place_ref, out_ref, NEAR), half), :]

    @pl.when(step >= steps)
    def _():
        out_ref[...] = jnp.dot(hidden[far, :], w_out_ref[...], preferred_element_type=jnp.float32)


def forward(place, part_rows, inputs, w_in, w_out):
    rows = inputs.shape[0]
    depth, width = w_in.shape
    tile, out_tile = tile_of(width, 640), tile_of(depth, 640)
    steps = width // tile
    last = lambda n: jnp.maximum(n - steps, 0)
    return call(
        functools.partial(forward_kernel, steps),
        "forward",
        (place, inputs, w_in, w_out),
        [
            jax.ShapeDtypeStruct((rows // 2, depth), jnp.float32),
            jax.ShapeDtypeStruct((rows // 2, width), jnp.bfloat16),
            jax.ShapeDtypeStruct((rows // 2, depth), jnp.bfloat16),
            jax.ShapeDtypeStruct((part_rows, depth), jnp.bfloat16),
        ],
        vmem=vmem_most,
        grid=(steps + depth // out_tile,),
        in_specs=[
            pl.BlockSpec((rows, depth), whole),
            pl.BlockSpec((depth, tile), lambda n, s: (0, jnp.minimum(n, steps - 1))),
            pl.BlockSpec((width, out_tile), lambda n, s: (0, last(n))),
        ],
        out_specs=[
            pl.BlockSpec((rows // 2, out_tile), lambda n, s: (0, last(n))),
            pl.BlockSpec((rows // 2, width), whole),
            pl.BlockSpec((rows // 2, depth), whole),
            pl.BlockSpec((part_rows, depth), whole),
        ],
        scratch_shapes=[pltpu.VMEM((rows, width), jnp.bfloat16)],
    )


def product_kernel(place_ref, left_ref, right_ref, out_ref):
    out_ref[...] = jnp.dot(left_ref[...], right_ref[...], preferred_element_type=jnp.float32)


def product(place, left, right):
    rows, depth = left.shape
    width = right.shape[1]
    tile = tile_of(width, 640)
    return call(
        product_kernel,
        "product",
        (place, left, right),
        [jax.ShapeDtypeStruct((rows, width), jnp.float32)],
        grid=(width // tile,),
        in_specs=[pl.BlockSpec((rows, depth), whole), pl.BlockSpec((depth, tile), column)],
        out_specs=[pl.BlockSpec((rows, tile), column)],
    )[0]


def join_kernel(place_ref, own_ref, got_ref, out_ref):
    rows = own_ref.shape[0]
    out_ref[pl.ds(pl.multiple_of(place_ref[0] * rows, 16), rows), :] = own_ref[...]
    out_ref[pl.ds(pl.multiple_of((1 - place_ref[0]) * rows, 16), rows), :] = got_ref[...]


def join(flag, own, got):
    rows, depth = own.shape
    return call(
        join_kernel,
        "join",
        (flag.reshape(1), own, got),
        [jax.ShapeDtypeStruct((2 * rows, depth), own.dtype)],
        grid=(1,),
        in_specs=[pl.BlockSpec((rows, depth), whole)] * 2,
        out_specs=[pl.BlockSpec((2 * rows, depth), whole)],
    )[0]


def error_kernel(row_count, place_ref, own_ref, got_ref, targets_ref, half_ref, part_ref):
    out = own_ref[...] + got_ref[...]
    error = (out - targets_ref[...].astype(jnp.float32)) / row_count
    half_ref[...] = error.astype(jnp.bfloat16)
    rows = part_ref.shape[0]
    part_ref[...] = half_ref[pl.ds(pl.multiple_of(place_ref[PIECE] * rows, 16), rows), :]


def error_half(place, part_rows, own, got, targets, after):
    rows, depth = own.shape
    return call(
        functools.partial(error_kernel, targets.shape[0]),
        "error_half",
        (place, own, got, targets),
        [
            jax.ShapeDtypeStruct((rows, depth), jnp.bfloat16),
            jax.ShapeDtypeStruct((part_rows, depth), jnp.bfloat16),
        ],
        after,
        grid=(1,),
        in_specs=[
            pl.BlockSpec((rows, depth), whole),
            pl.BlockSpec((rows, depth), whole),
            pl.BlockSpec((rows, depth), lambda n, s: (s[NEAR], 0)),
        ],
        out_specs=[pl.BlockSpec((rows, depth), whole), pl.BlockSpec((part_rows, depth), whole)],
    )


def gradient_kernel(wheres, window, own, step_rows, place_ref, *refs):
    error_wheres, input_wheres = wheres
    refs = list(refs)

    def take(n):
        taken = refs[:n]
        del refs[:n]
        return taken

    error_refs, input_refs = take(len(error_wheres)), take(len(input_wheres))
    w_in_ref, w_out_ref, first_ref, second_ref, send_first_ref, send_second_ref = take(6)
    errors, inputs, inputs_turned, errors_turned, spread_first, spread_second = refs
    if len(input_refs) == 1:
        inputs = input_refs[0]

    @pl.when(pl.program_id(0) == 0)
    def _():
        for block, where in zip(error_refs, error_wheres):
            errors[pl.ds(row_start(place_ref, block, where), block.shape[0]), :] = block[...]
        if len(input_refs) > 1:
            for block, where in zip(input_refs, input_wheres):
                inputs[pl.ds(row_start(place_ref, block, where), block.shape[0]), :] = block[...]
        lane = pl.multiple_of(place_ref[WINDOW] * 128, 128)
        inputs_turned[...] = inputs[:, pl.ds(lane, window * 128)].T
        errors_turned[...] = errors[:, pl.ds(lane, window * 128)].T

    shift = pl.multiple_of(place_ref[SHIFT], step_rows)
    other_shift = pl.multiple_of(place_ref[OTHER_SHIFT], step_rows)
    v = jnp.dot(inputs[...], w_in_ref[...], preferred_element_type=jnp.float32)
    back = lax.dot_general(
        errors[...], w_out_ref[...], (((1,), (1,)), ((), ())), preferred_element_type=jnp.float32
    )
    square = v * v
    t = jnp.tanh(v * (SCALE + (SCALE * CUBE) * square))
    upper = 0.5 + 0.5 * t
    hidden = (v * upper).astype(jnp.bfloat16)
    spread_second[...] = jnp.dot(errors_turned[...], hidden, preferred_element_type=jnp.float32)
    slope = upper + (0.5 * v) * (1.0 - t * t) * (SCALE + (3.0 * SCALE * CUBE) * square)
    dpre = (back * slope).astype(jnp.bfloat16)
    spread_first[...] = jnp.dot(inputs_turned[...], dpre, preferred_element_type=jnp.float32)
    second_ref[...] = spread_second[pl.ds(shift, own), :]
    send_second_ref[...] = spread_second[pl.ds(other_shift, own), :].astype(jnp.bfloat16)
    first_ref[...] = spread_first[pl.ds(shift, own), :]
    send_first_ref[...] = spread_first[pl.ds(other_shift, own), :].astype(jnp.bfloat16)


def gradient(place, members, swap, errors, inputs, w_in, w_out, after=()):
    error_arrays, error_wheres = zip(*errors)
    input_arrays, input_wheres = zip(*inputs)
    depth, width = w_in.shape
    rows = sum(a.shape[0] for a in input_arrays)
    own = depth // members
    reach = max(m * own % 128 for m in range(members) if not m & swap) + (swap + 1) * own
    window = -(-reach // 128)
    tile = tile_of(width, 640)
    once = pl.Buffered(1)
    return call(
        functools.partial(
            gradient_kernel, (error_wheres, input_wheres), window, own, math.gcd(own, 128)
        ),
        "gradient",
        (place, *error_arrays, *input_arrays, w_in, w_out),
        [
            jax.ShapeDtypeStruct((own, width), jnp.float32),
            jax.ShapeDtypeStruct((own, width), jnp.float32),
            jax.ShapeDtypeStruct((own, width), jnp.bfloat16),
            jax.ShapeDtypeStruct((own, width), jnp.bfloat16),
        ],
        after,
        grid=(width // tile,),
        in_specs=[
            pl.BlockSpec(a.shape, whole, pipeline_mode=once)
            for a in (*error_arrays, *input_arrays)
        ]
        + [pl.BlockSpec((depth, tile), column), pl.BlockSpec((tile, depth), lambda n, s: (n, 0))],
        out_specs=[pl.BlockSpec((own, tile), column)] * 4,
        scratch_shapes=[
            pltpu.VMEM((rows, depth), jnp.bfloat16),
            pltpu.VMEM((rows, depth), jnp.bfloat16),
            pltpu.VMEM((window * 128, rows), jnp.bfloat16),
            pltpu.VMEM((window * 128, rows), jnp.bfloat16),
            pltpu.VMEM((window * 128, tile), jnp.float32),
            pltpu.VMEM((window * 128, tile), jnp.float32),
        ],
    )


def products_kernel(labels, fresh, place_ref, *refs):
    own = refs[0].shape[0]
    slots = [refs[2 * n : 2 * n + 2] for n in range(len(labels))]
    known_ref, out_ref, totals = refs[2 * len(labels) :]
    pairs = [(i, j) for i in range(len(slots) - fresh, len(slots)) for j in range(i + 1)]

    @pl.when(pl.program_id(0) == 0)
    def _():
        totals[...] = jnp.zeros_like(totals)

    def values(slot):
        return [ref[...].astype(jnp.float32) for ref in slot]

    for n, (i, j) in enumerate(pairs):
        a, b = values(slots[i]), values(slots[j])
        both = a[0] * b[0] + a[1] * b[1]
        totals[n] += jnp.sum(both.reshape(own // 8, 8, -1), axis=0)

    @pl.when(pl.program_id(0) == pl.num_programs(0) - 1)
    def _():
        result = known_ref[...]
        row = lax.broadcasted_iota(jnp.int32, result.shape, 0)
        column = lax.broadcasted_iota(jnp.int32, result.shape, 1)
        for n, (i, j) in enumerate(pairs):
            i, j = (jnp.bitwise_xor(place_ref[MEMBER], labels[k]) for k in (i, j))
            here = ((row == i) & (column == j)) | ((row == j) & (column == i))
            result = result + jnp.where(here, jnp.sum(totals[n]), 0.0)
        out_ref[...] = result


def products(place, slots, labels, fresh, known, after=()):
    arrays = [a for slot in slots for a in slot]
    own, width = slots[0][0].shape
    tile = tile_of(width, 256)
    pairs = sum(len(slots) - n for n in range(fresh))
    return call(
        functools.partial(products_kernel, tuple(labels), fresh),
        "products",
        (place, *arrays, known),
        [jax.ShapeDtypeStruct(known.shape, jnp.float32)],
        after,
        grid=(width // tile,),
        in_specs=[pl.BlockSpec((a.shape[0], tile), lambda n, s: (0, n)) for a in arrays]
        + [pl.BlockSpec(known.shape, whole)],
        out_specs=[pl.BlockSpec(known.shape, whole)],
        scratch_shapes=[pltpu.VMEM((pairs, 8, tile), jnp.float32)],
    )[0]


def tree_weights(count, entry):
    def inner(a, b):
        total = 0.0
        for i, u in a.items():
            for j, v in b.items():
                total = total + u * v * entry(i, j)
        return total

    items = [{i: 1.0} for i in range(count)]
    while len(items) > 1:
        half = len(items) // 2
        merged = []
        for low, high in zip(items[:half], items[half:]):
            product = inner(low, high)
            scale_low = 1.0 - product / (2.0 * (jnp.maximum(inner(low, low), 0.0) + epsilon))
            scale_high = 1.0 - product / (2.0 * (jnp.maximum(inner(high, high), 0.0) + epsilon))
            joined = {i: u * scale_low for i, u in low.items()}
            joined.update({i: u * scale_high for i, u in high.items()})
            merged.append(joined)
        items = merged
    return [items[0][i] for i in range(count)]


def sum_kernel(place_ref, *refs):
    refs[-1][...] = sum(ref[...] for ref in refs[:-1])


def sum_of(place, parts):
    shape = parts[0].shape
    return call(
        sum_kernel,
        "sum_of",
        (place, *parts),
        [jax.ShapeDtypeStruct(shape, jnp.float32)],
        vmem=4 * 2**20,
        grid=(1,),
        in_specs=[pl.BlockSpec(shape, whole)] * len(parts),
        out_specs=[pl.BlockSpec(shape, whole)],
    )[0]


def merge_kernel(labels, place_ref, totals_ref, *refs):
    refs, (first_ref, second_ref, weights_ref) = refs[:-3], refs[-3:]

    @pl.when(pl.program_id(0) == 0)
    def _():
        def entry(i, j):
            i, j = (jnp.bitwise_xor(place_ref[MEMBER], k) for k in (i, j))
            return totals_ref[i, j]

        for n, weight in enumerate(tree_weights(len(labels), entry)):
            weights_ref[n] = weight

    first = second = 0.0
    for n, label in enumerate(labels):
        weight = weights_ref[label]
        first = first + weight * refs[2 * n][...].astype(jnp.float32)
        second = second + weight * refs[2 * n + 1][...].astype(jnp.float32)
    first_ref[...] = first
    second_ref[...] = second


def merge(place, totals, slots, labels):
    own, width = slots[0][0].shape
    block = max(b for b in range(16, min(own, 32) + 1, 16) if own % b == 0)
    spec = pl.BlockSpec((block, width), lambda n, s: (n, 0))
    arrays = [a for slot in slots for a in slot]
    shape = jax.ShapeDtypeStruct((own, width), jnp.float32)
    return call(
        functools.partial(merge_kernel, tuple(labels)),
        "merge",
        (place, totals, *arrays),
        [shape, shape],
        vmem=16 * 2**20,
        grid=(own // block,),
        in_specs=[pl.BlockSpec(memory_space=pltpu.SMEM)] + [spec] * len(arrays),
        out_specs=[spec, spec],
        scratch_shapes=[pltpu.SMEM((len(slots),), jnp.float32)],
    )


def on_device(inputs, targets, w_in, w_out):
    row_count = inputs.shape[0]
    workers = lax.axis_size("dp")
    shards = lax.axis_size("tensor")
    levels = workers.bit_length() - 1
    shard_levels = shards.bit_length() - 1
    gathered = min(levels, gather_levels_limit)
    members = 2**gathered
    others = workers // members
    position = lax.axis_index("dp")
    shard = lax.axis_index("tensor")
    member = position // others

    def part_of(index):
        part = 0
        for bit in range(shard_levels):
            part = part * 2 + (index >> bit & 1)
        return part

    near = shard & 1
    part_rows = row_count // shards
    own = inputs.shape[1] // members
    swap = min(2, members // 2)
    bits = [2**b for b in reversed(range(gathered)) if 2**b != swap]
    upper = member // swap % 2
    first_row = (member - upper * swap) * own
    place = jnp.stack(
        [
            first_row // 128,
            first_row % 128 + upper * swap * own,
            first_row % 128 + (1 - upper) * swap * own,
            member,
            near,
            1 - near,
            part_of(shard),
            part_of(shard) - near * (shards // 2),
        ]
    ).astype(jnp.int32)

    first_bit = bits[0]
    send, hidden_near, own_half, own_part = forward(place, part_rows, inputs, w_in, w_out)
    got = from_mask(send, 0, 1)

    inputs_of = {
        bit: from_mask(own_part if bit == first_bit else own_half, bit * others, 0) for bit in bits
    }

    summed = product(place, hidden_near, w_out) + got
    most = 24.0 * 0.15625 * 0.078125 * inputs.shape[1] * w_in.shape[1] * shards
    scale = 2.0 ** math.ceil(math.log2(most / 65504.0))
    sums = [summed]
    for bit in range(1, shard_levels):
        rounded = (sum(sums) * (1.0 / scale)).astype(jnp.float16)
        sums.append(from_mask(rounded, 0, 2**bit).astype(jnp.float32) * scale)
    error, error_piece = error_half(
        place,
        part_rows,
        sum(sums[:-1]),
        sums[-1],
        targets,
        tuple(inputs_of.values()),
    )
    errors_of = {
        bit: from_mask(error_piece if bit == first_bit else error, bit * others, 0) for bit in bits
    }

    def to_half(piece, *before):
        for bit in reversed(range(1, shard_levels)):
            got = ordered(from_mask(piece, 0, 2**bit), *before)
            piece = join(shard >> bit & 1, piece, got)
        return piece

    def both_halves(half):
        return [(half, NEAR), (from_mask(half, 0, 1), FAR)]

    slots, labels, known, sent = [], [], [], []
    totals = jnp.zeros((8, 128), jnp.float32)
    masks = [m for m in range(members) if not m & swap]
    for n, m in enumerate(masks):
        if n == 0:
            half = error
        elif not m & first_bit:
            half = errors_of[m] = ordered(errors_of[m], sent[0], inputs_half, errors_of[first_bit])
            other_inputs = inputs_of[m]
        elif m == first_bit:
            for bit in bits[1:]:
                ready = ordered(inputs_of[first_bit], errors_of[bit])
                inputs_of[first_bit | bit] = from_mask(ready, bit * others, 0)
                ready = ordered(errors_of[first_bit], errors_of[bit])
                errors_of[first_bit | bit] = from_mask(ready, bit * others, 0)
            before = [errors_of[first_bit | bit] for bit in bits[1:]]
            half = to_half(ordered(errors_of[m], sent[0]), sent[-1], *slots[1], *before)
            other_inputs = inputs_half
        else:
            other_inputs = to_half(ordered(inputs_of[m], sent[-1], slots[2 * n - 3][0]))
            half = to_half(ordered(errors_of[m], sent[-2]), sent[-1], *slots[2 * n - 3])
        first, second, *send = gradient(
            place,
            members,
            swap,
            both_halves(half),
            both_halves(other_inputs) if n else [(inputs, None)],
            w_in,
            w_out,
            known[-2:-1],
        )
        if n == 0:
            inputs_half = to_half(inputs_of[first_bit], send[0])
        sent.append(send[0])
        slots.append((first, second))
        labels.append(m)
        last = n == len(masks) - 1
        if last:
            totals = products(place, slots, labels, 1, totals)
        slots.append(tuple(from_mask(a, swap * others, 0) for a in send))
        labels.append(m ^ swap)
        totals = products(place, slots, labels, 1 if last else 2, totals)
        known.append(totals)

    rounds = [[(0, mask) for mask in range(1, shards)]]
    rounds.append([(m * others, 0) for m in range(2, members, 2)])
    rounds.append([(others, 0)])
    for partners in rounds:
        totals = sum_of(place, [totals] + [from_mask(totals, *mask) for mask in partners])
    pieces = merge(place, totals, slots, labels)

    for section in range(gathered, levels):
        upper_flag = position >> levels - 1 - section & 1
        keep_first, send_first = split_piece(pieces[0], upper_flag)
        keep_second, send_second = split_piece(pieces[1], upper_flag)
        got_first, got_second = from_partner((send_first, send_second), "dp", levels - 1 - section)
        pieces = combine(
            (keep_first, keep_second), (got_first, got_second), upper_flag, section, levels
        )
    return (pieces[0], pieces[1])


def solution(mesh):
    placed = (P("dp", None), P("dp", None), P(None, "tensor"), P("tensor", None))
    return jax.shard_map(
        on_device,
        mesh=mesh,
        in_specs=placed,
        out_specs=(P("dp", "tensor"), P("dp", "tensor")),
        check_vma=False,
    )
```

```python
import functools
import math

import jax
import jax.numpy as jnp
from jax import lax
from jax.experimental import pallas as pl
from jax.experimental.pallas import tpu as pltpu
from jax.sharding import PartitionSpec as P

epsilon = 1e-06
gather_levels_limit = 3
vmem_bytes = 36 * 2**20
vmem_most = 60 * 2**20


def from_partner(value, axis, distance):
    mask = 2**distance
    pairs = [(source, source ^ mask) for source in range(lax.axis_size(axis))]
    return lax.ppermute(value, axis, pairs)


def from_mask(value, dp_mask, tensor_mask):
    shards = lax.axis_size("tensor")
    mask = dp_mask * shards + tensor_mask
    pairs = [(source, source ^ mask) for source in range(lax.axis_size("dp") * shards)]
    return lax.ppermute(value, ("dp", "tensor"), pairs)


def ordered(value, *before):
    return lax.optimization_barrier((value, *before))[0]


def split_piece(piece, upper_flag):
    half = piece.shape[0] // 2
    keep = lax.dynamic_slice_in_dim(piece, upper_flag * half, half, 0)
    send = lax.dynamic_slice_in_dim(piece, (1 - upper_flag) * half, half, 0)
    return (keep, send)


def group_total(values, section, levels):
    summed = lax.psum(values, "tensor")
    for offset in range(section + 1):
        summed = summed + from_partner(summed, "dp", levels - 1 - offset)
    return summed


def combine(own, incoming, upper_flag, section, levels):
    product = jnp.sum(own[0] * incoming[0]) + jnp.sum(own[1] * incoming[1])
    norm_own = jnp.sum(own[0] * own[0]) + jnp.sum(own[1] * own[1])
    norm_incoming = jnp.sum(incoming[0] * incoming[0]) + jnp.sum(incoming[1] * incoming[1])
    is_upper = upper_flag == 1
    norm_low = jnp.where(is_upper, norm_incoming, norm_own)
    norm_high = jnp.where(is_upper, norm_own, norm_incoming)
    totals = group_total(jnp.stack([product, norm_low, norm_high]), section, levels)
    coef_low = 1.0 - totals[0] / (2.0 * (totals[1] + epsilon))
    coef_high = 1.0 - totals[0] / (2.0 * (totals[2] + epsilon))
    coef_own = jnp.where(is_upper, coef_high, coef_low)
    coef_incoming = jnp.where(is_upper, coef_low, coef_high)
    return (
        coef_own * own[0] + coef_incoming * incoming[0],
        coef_own * own[1] + coef_incoming * incoming[1],
    )


def tile_of(size, limit):
    return max(b for b in range(128, limit + 1, 128) if size % b == 0)


def contract(left, right, left_dim, right_dim):
    dims = (((left_dim,), (right_dim,)), ((), ()))
    return lax.dot_general(left, right, dims, preferred_element_type=jnp.float32)


def call(kernel, name, operands, shapes, after=(), vmem=vmem_bytes, **spec):
    spec["in_specs"] = [pl.BlockSpec(memory_space=pl.ANY)] * len(after) + spec["in_specs"]

    def body(place_ref, *refs):
        kernel(place_ref, *refs[len(after) :])

    return pl.pallas_call(
        body,
        grid_spec=pltpu.PrefetchScalarGridSpec(num_scalar_prefetch=1, **spec),
        out_shape=shapes,
        compiler_params=pltpu.CompilerParams(vmem_limit_bytes=vmem),
        cost_estimate=pl.CostEstimate(flops=1, bytes_accessed=1, transcendentals=0),
        name=name,
    )(operands[0], *after, *operands[1:])


WINDOW, SHIFT, OTHER_SHIFT, MEMBER, NEAR, FAR, PART, PIECE = range(8)


def row_start(place_ref, block, where):
    return 0 if where is None else pl.multiple_of(place_ref[where] * block.shape[0], 16)


def whole(n, s):
    return (0, 0)


def column(n, s):
    return (0, n)


SCALE = math.sqrt(2.0 / math.pi)
CUBE = 0.044715


def forward_kernel(
    steps, place_ref, rows_ref, w_in_ref, w_out_ref, out_ref, near_ref, half_ref, part_ref, hidden
):
    step = pl.program_id(0)
    half = out_ref.shape[0]
    far = pl.ds(row_start(place_ref, out_ref, FAR), half)
    tile = w_in_ref.shape[1]

    for n in range(steps):

        @pl.when(step == n)
        def _():
            v = jnp.dot(rows_ref[...], w_in_ref[...], preferred_element_type=jnp.float32)
            t = jnp.tanh(v * (SCALE + (SCALE * CUBE) * (v * v)))
            hidden[:, n * tile : (n + 1) * tile] = (v * (0.5 + 0.5 * t)).astype(jnp.bfloat16)

    @pl.when(step == 0)
    def _():
        half_ref[...] = rows_ref[pl.ds(row_start(place_ref, half_ref, NEAR), half), :]
        part_ref[...] = rows_ref[pl.ds(row_start(place_ref, part_ref, PART), part_ref.shape[0]), :]

    @pl.when(step == steps)
    def _():
        near_ref[...] = hidden[pl.ds(row_start(place_ref, out_ref, NEAR), half), :]

    @pl.when(step >= steps)
    def _():
        out_ref[...] = jnp.dot(hidden[far, :], w_out_ref[...], preferred_element_type=jnp.float32)


def forward(place, part_rows, inputs, w_in, w_out):
    rows = inputs.shape[0]
    depth, width = w_in.shape
    tile, out_tile = tile_of(width, 640), tile_of(depth, 640)
    steps = width // tile
    last = lambda n: jnp.maximum(n - steps, 0)
    return call(
        functools.partial(forward_kernel, steps),
        "forward",
        (place, inputs, w_in, w_out),
        [
            jax.ShapeDtypeStruct((rows // 2, depth), jnp.float32),
            jax.ShapeDtypeStruct((rows // 2, width), jnp.bfloat16),
            jax.ShapeDtypeStruct((rows // 2, depth), jnp.bfloat16),
            jax.ShapeDtypeStruct((part_rows, depth), jnp.bfloat16),
        ],
        vmem=vmem_most,
        grid=(steps + depth // out_tile,),
        in_specs=[
            pl.BlockSpec((rows, depth), whole),
            pl.BlockSpec((depth, tile), lambda n, s: (0, jnp.minimum(n, steps - 1))),
            pl.BlockSpec((width, out_tile), lambda n, s: (0, last(n))),
        ],
        out_specs=[
            pl.BlockSpec((rows // 2, out_tile), lambda n, s: (0, last(n))),
            pl.BlockSpec((rows // 2, width), whole),
            pl.BlockSpec((rows // 2, depth), whole),
            pl.BlockSpec((part_rows, depth), whole),
        ],
        scratch_shapes=[pltpu.VMEM((rows, width), jnp.bfloat16)],
    )


def product_kernel(place_ref, left_ref, right_ref, out_ref):
    out_ref[...] = jnp.dot(left_ref[...], right_ref[...], preferred_element_type=jnp.float32)


def product(place, left, right):
    rows, depth = left.shape
    width = right.shape[1]
    tile = tile_of(width, 640)
    return call(
        product_kernel,
        "product",
        (place, left, right),
        [jax.ShapeDtypeStruct((rows, width), jnp.float32)],
        grid=(width // tile,),
        in_specs=[pl.BlockSpec((rows, depth), whole), pl.BlockSpec((depth, tile), column)],
        out_specs=[pl.BlockSpec((rows, tile), column)],
    )[0]


def join_kernel(place_ref, own_ref, got_ref, out_ref):
    rows = own_ref.shape[0]
    out_ref[pl.ds(pl.multiple_of(place_ref[0] * rows, 16), rows), :] = own_ref[...]
    out_ref[pl.ds(pl.multiple_of((1 - place_ref[0]) * rows, 16), rows), :] = got_ref[...]


def join(flag, own, got):
    rows, depth = own.shape
    return call(
        join_kernel,
        "join",
        (flag.reshape(1), own, got),
        [jax.ShapeDtypeStruct((2 * rows, depth), own.dtype)],
        grid=(1,),
        in_specs=[pl.BlockSpec((rows, depth), whole)] * 2,
        out_specs=[pl.BlockSpec((2 * rows, depth), whole)],
    )[0]


def error_kernel(row_count, place_ref, own_ref, got_ref, targets_ref, half_ref, part_ref):
    out = own_ref[...] + got_ref[...]
    error = (out - targets_ref[...].astype(jnp.float32)) / row_count
    half_ref[...] = error.astype(jnp.bfloat16)
    rows = part_ref.shape[0]
    part_ref[...] = half_ref[pl.ds(pl.multiple_of(place_ref[PIECE] * rows, 16), rows), :]


def error_half(place, part_rows, own, got, targets, after):
    rows, depth = own.shape
    return call(
        functools.partial(error_kernel, targets.shape[0]),
        "error_half",
        (place, own, got, targets),
        [
            jax.ShapeDtypeStruct((rows, depth), jnp.bfloat16),
            jax.ShapeDtypeStruct((part_rows, depth), jnp.bfloat16),
        ],
        after,
        grid=(1,),
        in_specs=[
            pl.BlockSpec((rows, depth), whole),
            pl.BlockSpec((rows, depth), whole),
            pl.BlockSpec((rows, depth), lambda n, s: (s[NEAR], 0)),
        ],
        out_specs=[pl.BlockSpec((rows, depth), whole), pl.BlockSpec((part_rows, depth), whole)],
    )


def gradient_kernel(wheres, window, own, step_rows, place_ref, *refs):
    error_wheres, input_wheres = wheres
    refs = list(refs)

    def take(n):
        taken = refs[:n]
        del refs[:n]
        return taken

    error_refs, input_refs = take(len(error_wheres)), take(len(input_wheres))
    w_in_ref, w_out_ref, first_ref, second_ref, send_first_ref, send_second_ref = take(6)
    errors, inputs, inputs_turned, errors_turned, spread_first, spread_second = refs
    if len(input_refs) == 1:
        inputs = input_refs[0]

    @pl.when(pl.program_id(0) == 0)
    def _():
        for block, where in zip(error_refs, error_wheres):
            errors[pl.ds(row_start(place_ref, block, where), block.shape[0]), :] = block[...]
        if len(input_refs) > 1:
            for block, where in zip(input_refs, input_wheres):
                inputs[pl.ds(row_start(place_ref, block, where), block.shape[0]), :] = block[...]
        lane = pl.multiple_of(place_ref[WINDOW] * 128, 128)
        inputs_turned[...] = inputs[:, pl.ds(lane, window * 128)].T
        errors_turned[...] = errors[:, pl.ds(lane, window * 128)].T

    shift = pl.multiple_of(place_ref[SHIFT], step_rows)
    other_shift = pl.multiple_of(place_ref[OTHER_SHIFT], step_rows)
    v = jnp.dot(inputs[...], w_in_ref[...], preferred_element_type=jnp.float32)
    back = lax.dot_general(
        errors[...], w_out_ref[...], (((1,), (1,)), ((), ())), preferred_element_type=jnp.float32
    )
    square = v * v
    t = jnp.tanh(v * (SCALE + (SCALE * CUBE) * square))
    upper = 0.5 + 0.5 * t
    hidden = (v * upper).astype(jnp.bfloat16)
    spread_second[...] = jnp.dot(errors_turned[...], hidden, preferred_element_type=jnp.float32)
    slope = upper + (0.5 * v) * (1.0 - t * t) * (SCALE + (3.0 * SCALE * CUBE) * square)
    dpre = (back * slope).astype(jnp.bfloat16)
    spread_first[...] = jnp.dot(inputs_turned[...], dpre, preferred_element_type=jnp.float32)
    second_ref[...] = spread_second[pl.ds(shift, own), :]
    send_second_ref[...] = spread_second[pl.ds(other_shift, own), :].astype(jnp.bfloat16)
    first_ref[...] = spread_first[pl.ds(shift, own), :]
    send_first_ref[...] = spread_first[pl.ds(other_shift, own), :].astype(jnp.bfloat16)


def gradient(place, members, swap, errors, inputs, w_in, w_out, after=()):
    error_arrays, error_wheres = zip(*errors)
    input_arrays, input_wheres = zip(*inputs)
    depth, width = w_in.shape
    rows = sum(a.shape[0] for a in input_arrays)
    own = depth // members
    reach = max(m * own % 128 for m in range(members) if not m & swap) + (swap + 1) * own
    window = -(-reach // 128)
    tile = tile_of(width, 640)
    once = pl.Buffered(1)
    return call(
        functools.partial(
            gradient_kernel, (error_wheres, input_wheres), window, own, math.gcd(own, 128)
        ),
        "gradient",
        (place, *error_arrays, *input_arrays, w_in, w_out),
        [
            jax.ShapeDtypeStruct((own, width), jnp.float32),
            jax.ShapeDtypeStruct((own, width), jnp.float32),
            jax.ShapeDtypeStruct((own, width), jnp.bfloat16),
            jax.ShapeDtypeStruct((own, width), jnp.bfloat16),
        ],
        after,
        grid=(width // tile,),
        in_specs=[
            pl.BlockSpec(a.shape, whole, pipeline_mode=once)
            for a in (*error_arrays, *input_arrays)
        ]
        + [pl.BlockSpec((depth, tile), column), pl.BlockSpec((tile, depth), lambda n, s: (n, 0))],
        out_specs=[pl.BlockSpec((own, tile), column)] * 4,
        scratch_shapes=[
            pltpu.VMEM((rows, depth), jnp.bfloat16),
            pltpu.VMEM((rows, depth), jnp.bfloat16),
            pltpu.VMEM((window * 128, rows), jnp.bfloat16),
            pltpu.VMEM((window * 128, rows), jnp.bfloat16),
            pltpu.VMEM((window * 128, tile), jnp.float32),
            pltpu.VMEM((window * 128, tile), jnp.float32),
        ],
    )


def products_kernel(labels, fresh, place_ref, *refs):
    own = refs[0].shape[0]
    refs, (known_ref, out_ref, totals) = refs[:-3], refs[-3:]
    each = len(refs) // len(labels)
    slots = [refs[each * n : each * (n + 1)] for n in range(len(labels))]
    pairs = [(i, j) for i in range(len(slots) - fresh, len(slots)) for j in range(i + 1)]

    @pl.when(pl.program_id(0) == 0)
    def _():
        totals[...] = jnp.zeros_like(totals)

    def values(slot):
        return [ref[...].astype(jnp.float32) for ref in slot]

    for n, (i, j) in enumerate(pairs):
        a, b = values(slots[i]), values(slots[j])
        both = sum(u * v for u, v in zip(a, b))
        totals[n] += jnp.sum(both.reshape(own // 8, 8, -1), axis=0)

    @pl.when(pl.program_id(0) == pl.num_programs(0) - 1)
    def _():
        result = known_ref[...]
        row = lax.broadcasted_iota(jnp.int32, result.shape, 0)
        column = lax.broadcasted_iota(jnp.int32, result.shape, 1)
        for n, (i, j) in enumerate(pairs):
            i, j = (jnp.bitwise_xor(place_ref[MEMBER], labels[k]) for k in (i, j))
            here = ((row == i) & (column == j)) | ((row == j) & (column == i))
            result = result + jnp.where(here, jnp.sum(totals[n]), 0.0)
        out_ref[...] = result


def products(place, slots, labels, fresh, known, after=()):
    arrays = [a for slot in slots for a in slot]
    own, width = slots[0][0].shape
    tile = tile_of(width, 256)
    pairs = sum(len(slots) - n for n in range(fresh))
    return call(
        functools.partial(products_kernel, tuple(labels), fresh),
        "products",
        (place, *arrays, known),
        [jax.ShapeDtypeStruct(known.shape, jnp.float32)],
        after,
        grid=(width // tile,),
        in_specs=[pl.BlockSpec((a.shape[0], tile), lambda n, s: (0, n)) for a in arrays]
        + [pl.BlockSpec(known.shape, whole)],
        out_specs=[pl.BlockSpec(known.shape, whole)],
        scratch_shapes=[pltpu.VMEM((pairs, 8, tile), jnp.float32)],
    )[0]


def tree_weights(count, entry):
    def inner(a, b):
        total = 0.0
        for i, u in a.items():
            for j, v in b.items():
                total = total + u * v * entry(i, j)
        return total

    items = [{i: 1.0} for i in range(count)]
    while len(items) > 1:
        half = len(items) // 2
        merged = []
        for low, high in zip(items[:half], items[half:]):
            product = inner(low, high)
            scale_low = 1.0 - product / (2.0 * (jnp.maximum(inner(low, low), 0.0) + epsilon))
            scale_high = 1.0 - product / (2.0 * (jnp.maximum(inner(high, high), 0.0) + epsilon))
            joined = {i: u * scale_low for i, u in low.items()}
            joined.update({i: u * scale_high for i, u in high.items()})
            merged.append(joined)
        items = merged
    return [items[0][i] for i in range(count)]


def sum_kernel(place_ref, *refs):
    refs[-1][...] = sum(ref[...] for ref in refs[:-1])


def sum_of(place, parts):
    shape = parts[0].shape
    return call(
        sum_kernel,
        "sum_of",
        (place, *parts),
        [jax.ShapeDtypeStruct(shape, jnp.float32)],
        vmem=4 * 2**20,
        grid=(1,),
        in_specs=[pl.BlockSpec(shape, whole)] * len(parts),
        out_specs=[pl.BlockSpec(shape, whole)],
    )[0]


def merge_kernel(labels, place_ref, totals_ref, *refs):
    refs, (first_ref, second_ref, weights_ref) = refs[:-3], refs[-3:]

    @pl.when(pl.program_id(0) == 0)
    def _():
        def entry(i, j):
            i, j = (jnp.bitwise_xor(place_ref[MEMBER], k) for k in (i, j))
            return totals_ref[i, j]

        for n, weight in enumerate(tree_weights(len(labels), entry)):
            weights_ref[n] = weight

    first = second = 0.0
    for n, label in enumerate(labels):
        weight = weights_ref[label]
        first = first + weight * refs[2 * n][...].astype(jnp.float32)
        second = second + weight * refs[2 * n + 1][...].astype(jnp.float32)
    first_ref[...] = first
    second_ref[...] = second


def merge(place, totals, slots, labels):
    own, width = slots[0][0].shape
    block = max(b for b in range(16, min(own, 32) + 1, 16) if own % b == 0)
    spec = pl.BlockSpec((block, width), lambda n, s: (n, 0))
    arrays = [a for slot in slots for a in slot]
    shape = jax.ShapeDtypeStruct((own, width), jnp.float32)
    return call(
        functools.partial(merge_kernel, tuple(labels)),
        "merge",
        (place, totals, *arrays),
        [shape, shape],
        vmem=16 * 2**20,
        grid=(own // block,),
        in_specs=[pl.BlockSpec(memory_space=pltpu.SMEM)] + [spec] * len(arrays),
        out_specs=[spec, spec],
        scratch_shapes=[pltpu.SMEM((len(slots),), jnp.float32)],
    )


def on_device(inputs, targets, w_in, w_out):
    row_count = inputs.shape[0]
    workers = lax.axis_size("dp")
    shards = lax.axis_size("tensor")
    levels = workers.bit_length() - 1
    shard_levels = shards.bit_length() - 1
    gathered = min(levels, gather_levels_limit)
    members = 2**gathered
    others = workers // members
    position = lax.axis_index("dp")
    shard = lax.axis_index("tensor")
    member = position // others

    def part_of(index):
        part = 0
        for bit in range(shard_levels):
            part = part * 2 + (index >> bit & 1)
        return part

    near = shard & 1
    part_rows = row_count // shards
    own = inputs.shape[1] // members
    swap = 1
    bits = [2**b for b in reversed(range(gathered)) if 2**b != swap]
    upper = member // swap % 2
    first_row = (member - upper * swap) * own
    place = jnp.stack(
        [
            first_row // 128,
            first_row % 128 + upper * swap * own,
            first_row % 128 + (1 - upper) * swap * own,
            member,
            near,
            1 - near,
            part_of(shard),
            part_of(shard) - near * (shards // 2),
        ]
    ).astype(jnp.int32)

    first_bit = bits[0]
    send, hidden_near, own_half, own_part = forward(place, part_rows, inputs, w_in, w_out)
    got = from_mask(send, 0, 1)

    inputs_of = {
        bit: from_mask(own_part if bit == first_bit else own_half, bit * others, 0) for bit in bits
    }

    summed = product(place, hidden_near, w_out) + got
    most = 24.0 * 0.15625 * 0.078125 * inputs.shape[1] * w_in.shape[1] * shards
    scale = 2.0 ** math.ceil(math.log2(most / 65504.0))
    sums = [summed]
    for bit in range(1, shard_levels):
        rounded = (sum(sums) * (1.0 / scale)).astype(jnp.float16)
        sums.append(from_mask(rounded, 0, 2**bit).astype(jnp.float32) * scale)
    error, error_piece = error_half(
        place,
        part_rows,
        sum(sums[:-1]),
        sums[-1],
        targets,
        (inputs_of[first_bit],),
    )
    errors_of = {first_bit: from_mask(error_piece, first_bit * others, 0)}
    for bit in bits[1:]:
        errors_of[bit] = from_mask(ordered(error, inputs_of[bit]), bit * others, 0)

    def to_half(piece, *before):
        for bit in reversed(range(1, shard_levels)):
            got = ordered(from_mask(piece, 0, 2**bit), *before)
            piece = join(shard >> bit & 1, piece, got)
        return piece

    def both_halves(half):
        return [(half, NEAR), (from_mask(half, 0, 1), FAR)]

    slots, labels, known, sent = [], [], [], []
    totals = jnp.zeros((8, 128), jnp.float32)
    masks = [m for m in range(members) if not m & swap]
    for n, m in enumerate(masks):
        if n == 0:
            half = error
        elif not m & first_bit:
            half = errors_of[m] = ordered(
                errors_of[m], sent[0], inputs_half, errors_of[first_bit], slots[1][0]
            )
            other_inputs = inputs_of[m]
        elif m == first_bit:
            for bit in bits[1:]:
                ready = ordered(inputs_of[first_bit], errors_of[bit])
                inputs_of[first_bit | bit] = from_mask(ready, bit * others, 0)
                ready = ordered(errors_of[first_bit], errors_of[bit])
                errors_of[first_bit | bit] = from_mask(ready, bit * others, 0)
            before = [of[first_bit | bit] for bit in bits[1:] for of in (errors_of, inputs_of)]
            half = to_half(ordered(errors_of[m], sent[0]), sent[-1], *slots[1], *before)
            other_inputs = inputs_half
        else:
            other_inputs, half = (
                to_half(ordered(of[m], sent[-2]), sent[-1], *slots[2 * n - 3])
                for of in (inputs_of, errors_of)
            )
        first, second, *send = gradient(
            place,
            members,
            swap,
            both_halves(half),
            both_halves(other_inputs) if n else [(inputs, None)],
            w_in,
            w_out,
            known[-2:-1],
        )
        if n == 0:
            inputs_half = to_half(inputs_of[first_bit], send[0])
        sent.append(send[0])
        slots.append((first, second))
        labels.append(m)
        last = n == len(masks) - 1
        if last:
            totals = products(place, slots, labels, 1, totals)
        slots.append(tuple(from_mask(a, swap * others, 0) for a in send))
        labels.append(m ^ swap)
        if last:
            for k in range(2):
                totals = products(place, [slot[k : k + 1] for slot in slots], labels, 1, totals)
        else:
            totals = products(place, slots, labels, 2, totals)
        known.append(totals)

    rounds = [[(0, mask) for mask in range(1, shards)]]
    rounds.append([(m * others, 0) for m in range(2, members, 2)])
    rounds.append([(others, 0)])
    for partners in rounds:
        totals = sum_of(place, [totals] + [from_mask(totals, *mask) for mask in partners])
    pieces = merge(place, totals, slots, labels)

    for section in range(gathered, levels):
        upper_flag = position >> levels - 1 - section & 1
        keep_first, send_first = split_piece(pieces[0], upper_flag)
        keep_second, send_second = split_piece(pieces[1], upper_flag)
        got_first, got_second = from_partner((send_first, send_second), "dp", levels - 1 - section)
        pieces = combine(
            (keep_first, keep_second), (got_first, got_second), upper_flag, section, levels
        )
    return (pieces[0], pieces[1])


def solution(mesh):
    placed = (P("dp", None), P("dp", None), P(None, "tensor"), P("tensor", None))
    return jax.shard_map(
        on_device,
        mesh=mesh,
        in_specs=placed,
        out_specs=(P("dp", "tensor"), P("dp", "tensor")),
        check_vma=False,
    )
```

```python
import functools
import math

import jax
import jax.numpy as jnp
from jax import lax
from jax.experimental import pallas as pl
from jax.experimental.pallas import tpu as pltpu
from jax.sharding import PartitionSpec as P

epsilon = 1e-06
gather_levels_limit = 3
vmem_bytes = 36 * 2**20
vmem_most = 60 * 2**20


def from_partner(value, axis, distance):
    mask = 2**distance
    pairs = [(source, source ^ mask) for source in range(lax.axis_size(axis))]
    return lax.ppermute(value, axis, pairs)


def from_mask(value, dp_mask, tensor_mask):
    shards = lax.axis_size("tensor")
    mask = dp_mask * shards + tensor_mask
    pairs = [(source, source ^ mask) for source in range(lax.axis_size("dp") * shards)]
    return lax.ppermute(value, ("dp", "tensor"), pairs)


def ordered(value, *before):
    return lax.optimization_barrier((value, *before))[0]


def split_piece(piece, upper_flag):
    half = piece.shape[0] // 2
    keep = lax.dynamic_slice_in_dim(piece, upper_flag * half, half, 0)
    send = lax.dynamic_slice_in_dim(piece, (1 - upper_flag) * half, half, 0)
    return (keep, send)


def group_total(values, section, levels):
    summed = lax.psum(values, "tensor")
    for offset in range(section + 1):
        summed = summed + from_partner(summed, "dp", levels - 1 - offset)
    return summed


def combine(own, incoming, upper_flag, section, levels):
    product = jnp.sum(own[0] * incoming[0]) + jnp.sum(own[1] * incoming[1])
    norm_own = jnp.sum(own[0] * own[0]) + jnp.sum(own[1] * own[1])
    norm_incoming = jnp.sum(incoming[0] * incoming[0]) + jnp.sum(incoming[1] * incoming[1])
    is_upper = upper_flag == 1
    norm_low = jnp.where(is_upper, norm_incoming, norm_own)
    norm_high = jnp.where(is_upper, norm_own, norm_incoming)
    totals = group_total(jnp.stack([product, norm_low, norm_high]), section, levels)
    coef_low = 1.0 - totals[0] / (2.0 * (totals[1] + epsilon))
    coef_high = 1.0 - totals[0] / (2.0 * (totals[2] + epsilon))
    coef_own = jnp.where(is_upper, coef_high, coef_low)
    coef_incoming = jnp.where(is_upper, coef_low, coef_high)
    return (
        coef_own * own[0] + coef_incoming * incoming[0],
        coef_own * own[1] + coef_incoming * incoming[1],
    )


def tile_of(size, limit):
    return max(b for b in range(128, limit + 1, 128) if size % b == 0)


def contract(left, right, left_dim, right_dim):
    dims = (((left_dim,), (right_dim,)), ((), ()))
    return lax.dot_general(left, right, dims, preferred_element_type=jnp.float32)


def call(kernel, name, operands, shapes, after=(), vmem=vmem_bytes, **spec):
    spec["in_specs"] = [pl.BlockSpec(memory_space=pl.ANY)] * len(after) + spec["in_specs"]

    def body(place_ref, *refs):
        kernel(place_ref, *refs[len(after) :])

    return pl.pallas_call(
        body,
        grid_spec=pltpu.PrefetchScalarGridSpec(num_scalar_prefetch=1, **spec),
        out_shape=shapes,
        compiler_params=pltpu.CompilerParams(vmem_limit_bytes=vmem),
        cost_estimate=pl.CostEstimate(flops=1, bytes_accessed=1, transcendentals=0),
        name=name,
    )(operands[0], *after, *operands[1:])


WINDOW, SHIFT, OTHER_SHIFT, MEMBER, NEAR, FAR, PART, PIECE = range(8)


def row_start(place_ref, block, where):
    return 0 if where is None else pl.multiple_of(place_ref[where] * block.shape[0], 16)


def whole(n, s):
    return (0, 0)


def column(n, s):
    return (0, n)


SCALE = math.sqrt(2.0 / math.pi)
CUBE = 0.044715


def forward_kernel(
    steps, place_ref, rows_ref, w_in_ref, w_out_ref, out_ref, near_ref, part_ref, hidden
):
    step = pl.program_id(0)
    half = out_ref.shape[0]
    far = pl.ds(row_start(place_ref, out_ref, FAR), half)
    tile = w_in_ref.shape[1]

    for n in range(steps):

        @pl.when(step == n)
        def _():
            v = jnp.dot(rows_ref[...], w_in_ref[...], preferred_element_type=jnp.float32)
            t = jnp.tanh(v * (SCALE + (SCALE * CUBE) * (v * v)))
            hidden[:, n * tile : (n + 1) * tile] = (v * (0.5 + 0.5 * t)).astype(jnp.bfloat16)

    @pl.when(step == 0)
    def _():
        part_ref[...] = rows_ref[pl.ds(row_start(place_ref, part_ref, PART), part_ref.shape[0]), :]

    @pl.when(step == steps)
    def _():
        near_ref[...] = hidden[pl.ds(row_start(place_ref, out_ref, NEAR), half), :]

    @pl.when(step >= steps)
    def _():
        out_ref[...] = jnp.dot(hidden[far, :], w_out_ref[...], preferred_element_type=jnp.float32)


def forward(place, part_rows, inputs, w_in, w_out):
    rows = inputs.shape[0]
    depth, width = w_in.shape
    tile, out_tile = tile_of(width, 640), tile_of(depth, 640)
    steps = width // tile
    last = lambda n: jnp.maximum(n - steps, 0)
    return call(
        functools.partial(forward_kernel, steps),
        "forward",
        (place, inputs, w_in, w_out),
        [
            jax.ShapeDtypeStruct((rows // 2, depth), jnp.float32),
            jax.ShapeDtypeStruct((rows // 2, width), jnp.bfloat16),
            jax.ShapeDtypeStruct((part_rows, depth), jnp.bfloat16),
        ],
        vmem=vmem_most,
        grid=(steps + depth // out_tile,),
        in_specs=[
            pl.BlockSpec((rows, depth), whole),
            pl.BlockSpec((depth, tile), lambda n, s: (0, jnp.minimum(n, steps - 1))),
            pl.BlockSpec((width, out_tile), lambda n, s: (0, last(n))),
        ],
        out_specs=[
            pl.BlockSpec((rows // 2, out_tile), lambda n, s: (0, last(n))),
            pl.BlockSpec((rows // 2, width), whole),
            pl.BlockSpec((part_rows, depth), whole),
        ],
        scratch_shapes=[pltpu.VMEM((rows, width), jnp.bfloat16)],
    )


def product_kernel(place_ref, left_ref, right_ref, out_ref):
    out_ref[...] = jnp.dot(left_ref[...], right_ref[...], preferred_element_type=jnp.float32)


def product(place, left, right):
    rows, depth = left.shape
    width = right.shape[1]
    tile = tile_of(width, 640)
    return call(
        product_kernel,
        "product",
        (place, left, right),
        [jax.ShapeDtypeStruct((rows, width), jnp.float32)],
        grid=(width // tile,),
        in_specs=[pl.BlockSpec((rows, depth), whole), pl.BlockSpec((depth, tile), column)],
        out_specs=[pl.BlockSpec((rows, tile), column)],
    )[0]


def join_kernel(place_ref, own_ref, got_ref, out_ref):
    rows = own_ref.shape[0]
    out_ref[pl.ds(pl.multiple_of(place_ref[0] * rows, 16), rows), :] = own_ref[...]
    out_ref[pl.ds(pl.multiple_of((1 - place_ref[0]) * rows, 16), rows), :] = got_ref[...]


def join(flag, own, got):
    rows, depth = own.shape
    return call(
        join_kernel,
        "join",
        (flag.reshape(1), own, got),
        [jax.ShapeDtypeStruct((2 * rows, depth), own.dtype)],
        grid=(1,),
        in_specs=[pl.BlockSpec((rows, depth), whole)] * 2,
        out_specs=[pl.BlockSpec((2 * rows, depth), whole)],
    )[0]


def error_kernel(row_count, place_ref, own_ref, got_ref, targets_ref, half_ref, part_ref):
    out = own_ref[...] + got_ref[...]
    error = (out - targets_ref[...].astype(jnp.float32)) / row_count
    half_ref[...] = error.astype(jnp.bfloat16)
    rows = part_ref.shape[0]
    part_ref[...] = half_ref[pl.ds(pl.multiple_of(place_ref[PIECE] * rows, 16), rows), :]


def error_half(place, part_rows, own, got, targets, after):
    rows, depth = own.shape
    return call(
        functools.partial(error_kernel, targets.shape[0]),
        "error_half",
        (place, own, got, targets),
        [
            jax.ShapeDtypeStruct((rows, depth), jnp.bfloat16),
            jax.ShapeDtypeStruct((part_rows, depth), jnp.bfloat16),
        ],
        after,
        grid=(1,),
        in_specs=[
            pl.BlockSpec((rows, depth), whole),
            pl.BlockSpec((rows, depth), whole),
            pl.BlockSpec((rows, depth), lambda n, s: (s[NEAR], 0)),
        ],
        out_specs=[pl.BlockSpec((rows, depth), whole), pl.BlockSpec((part_rows, depth), whole)],
    )


def gradient_kernel(wheres, window, own, step_rows, place_ref, *refs):
    error_wheres, input_wheres = wheres
    refs = list(refs)

    def take(n):
        taken = refs[:n]
        del refs[:n]
        return taken

    error_refs, input_refs = take(len(error_wheres)), take(len(input_wheres))
    w_in_ref, w_out_ref, first_ref, second_ref, send_first_ref, send_second_ref = take(6)
    errors, inputs, inputs_turned, errors_turned, spread_first, spread_second = refs
    if len(input_refs) == 1:
        inputs = input_refs[0]

    @pl.when(pl.program_id(0) == 0)
    def _():
        for block, where in zip(error_refs, error_wheres):
            errors[pl.ds(row_start(place_ref, block, where), block.shape[0]), :] = block[...]
        if len(input_refs) > 1:
            for block, where in zip(input_refs, input_wheres):
                inputs[pl.ds(row_start(place_ref, block, where), block.shape[0]), :] = block[...]
        lane = pl.multiple_of(place_ref[WINDOW] * 128, 128)
        inputs_turned[...] = inputs[:, pl.ds(lane, window * 128)].T
        errors_turned[...] = errors[:, pl.ds(lane, window * 128)].T

    shift = pl.multiple_of(place_ref[SHIFT], step_rows)
    other_shift = pl.multiple_of(place_ref[OTHER_SHIFT], step_rows)
    v = jnp.dot(inputs[...], w_in_ref[...], preferred_element_type=jnp.float32)
    back = lax.dot_general(
        errors[...], w_out_ref[...], (((1,), (1,)), ((), ())), preferred_element_type=jnp.float32
    )
    square = v * v
    t = jnp.tanh(v * (SCALE + (SCALE * CUBE) * square))
    upper = 0.5 + 0.5 * t
    hidden = (v * upper).astype(jnp.bfloat16)
    spread_second[...] = jnp.dot(errors_turned[...], hidden, preferred_element_type=jnp.float32)
    slope = upper + (0.5 * v) * (1.0 - t * t) * (SCALE + (3.0 * SCALE * CUBE) * square)
    dpre = (back * slope).astype(jnp.bfloat16)
    spread_first[...] = jnp.dot(inputs_turned[...], dpre, preferred_element_type=jnp.float32)
    second_ref[...] = spread_second[pl.ds(shift, own), :]
    send_second_ref[...] = spread_second[pl.ds(other_shift, own), :].astype(jnp.bfloat16)
    first_ref[...] = spread_first[pl.ds(shift, own), :]
    send_first_ref[...] = spread_first[pl.ds(other_shift, own), :].astype(jnp.bfloat16)


def gradient(place, members, swap, errors, inputs, w_in, w_out, after=()):
    error_arrays, error_wheres = zip(*errors)
    input_arrays, input_wheres = zip(*inputs)
    depth, width = w_in.shape
    rows = sum(a.shape[0] for a in input_arrays)
    own = depth // members
    reach = max(m * own % 128 for m in range(members) if not m & swap) + (swap + 1) * own
    window = -(-reach // 128)
    tile = tile_of(width, 640)
    once = pl.Buffered(1)
    return call(
        functools.partial(
            gradient_kernel, (error_wheres, input_wheres), window, own, math.gcd(own, 128)
        ),
        "gradient",
        (place, *error_arrays, *input_arrays, w_in, w_out),
        [
            jax.ShapeDtypeStruct((own, width), jnp.float32),
            jax.ShapeDtypeStruct((own, width), jnp.float32),
            jax.ShapeDtypeStruct((own, width), jnp.bfloat16),
            jax.ShapeDtypeStruct((own, width), jnp.bfloat16),
        ],
        after,
        grid=(width // tile,),
        in_specs=[
            pl.BlockSpec(a.shape, whole, pipeline_mode=once)
            for a in (*error_arrays, *input_arrays)
        ]
        + [pl.BlockSpec((depth, tile), column), pl.BlockSpec((tile, depth), lambda n, s: (n, 0))],
        out_specs=[pl.BlockSpec((own, tile), column)] * 4,
        scratch_shapes=[
            pltpu.VMEM((rows, depth), jnp.bfloat16),
            pltpu.VMEM((rows, depth), jnp.bfloat16),
            pltpu.VMEM((window * 128, rows), jnp.bfloat16),
            pltpu.VMEM((window * 128, rows), jnp.bfloat16),
            pltpu.VMEM((window * 128, tile), jnp.float32),
            pltpu.VMEM((window * 128, tile), jnp.float32),
        ],
    )


def products_kernel(labels, fresh, place_ref, *refs):
    own = refs[0].shape[0]
    refs, (known_ref, out_ref, totals) = refs[:-3], refs[-3:]
    each = len(refs) // len(labels)
    slots = [refs[each * n : each * (n + 1)] for n in range(len(labels))]
    pairs = [(i, j) for i in range(len(slots) - fresh, len(slots)) for j in range(i + 1)]

    @pl.when(pl.program_id(0) == 0)
    def _():
        totals[...] = jnp.zeros_like(totals)

    def values(slot):
        return [ref[...].astype(jnp.float32) for ref in slot]

    for n, (i, j) in enumerate(pairs):
        a, b = values(slots[i]), values(slots[j])
        both = sum(u * v for u, v in zip(a, b))
        totals[n] += jnp.sum(both.reshape(own // 8, 8, -1), axis=0)

    @pl.when(pl.program_id(0) == pl.num_programs(0) - 1)
    def _():
        result = known_ref[...]
        row = lax.broadcasted_iota(jnp.int32, result.shape, 0)
        column = lax.broadcasted_iota(jnp.int32, result.shape, 1)
        for n, (i, j) in enumerate(pairs):
            i, j = (jnp.bitwise_xor(place_ref[MEMBER], labels[k]) for k in (i, j))
            here = ((row == i) & (column == j)) | ((row == j) & (column == i))
            result = result + jnp.where(here, jnp.sum(totals[n]), 0.0)
        out_ref[...] = result


def products(place, slots, labels, fresh, known, after=()):
    arrays = [a for slot in slots for a in slot]
    own, width = slots[0][0].shape
    tile = tile_of(width, 256)
    pairs = sum(len(slots) - n for n in range(fresh))
    return call(
        functools.partial(products_kernel, tuple(labels), fresh),
        "products",
        (place, *arrays, known),
        [jax.ShapeDtypeStruct(known.shape, jnp.float32)],
        after,
        grid=(width // tile,),
        in_specs=[pl.BlockSpec((a.shape[0], tile), lambda n, s: (0, n)) for a in arrays]
        + [pl.BlockSpec(known.shape, whole)],
        out_specs=[pl.BlockSpec(known.shape, whole)],
        scratch_shapes=[pltpu.VMEM((pairs, 8, tile), jnp.float32)],
    )[0]


def tree_weights(count, entry):
    def inner(a, b):
        total = 0.0
        for i, u in a.items():
            for j, v in b.items():
                total = total + u * v * entry(i, j)
        return total

    items = [{i: 1.0} for i in range(count)]
    while len(items) > 1:
        half = len(items) // 2
        merged = []
        for low, high in zip(items[:half], items[half:]):
            product = inner(low, high)
            scale_low = 1.0 - product / (2.0 * (jnp.maximum(inner(low, low), 0.0) + epsilon))
            scale_high = 1.0 - product / (2.0 * (jnp.maximum(inner(high, high), 0.0) + epsilon))
            joined = {i: u * scale_low for i, u in low.items()}
            joined.update({i: u * scale_high for i, u in high.items()})
            merged.append(joined)
        items = merged
    return [items[0][i] for i in range(count)]


def sum_kernel(place_ref, *refs):
    refs[-1][...] = sum(ref[...] for ref in refs[:-1])


def sum_of(place, parts):
    shape = parts[0].shape
    return call(
        sum_kernel,
        "sum_of",
        (place, *parts),
        [jax.ShapeDtypeStruct(shape, jnp.float32)],
        vmem=4 * 2**20,
        grid=(1,),
        in_specs=[pl.BlockSpec(shape, whole)] * len(parts),
        out_specs=[pl.BlockSpec(shape, whole)],
    )[0]


def merge_kernel(labels, place_ref, totals_ref, *refs):
    refs, (first_ref, second_ref, weights_ref) = refs[:-3], refs[-3:]

    @pl.when(pl.program_id(0) == 0)
    def _():
        def entry(i, j):
            i, j = (jnp.bitwise_xor(place_ref[MEMBER], k) for k in (i, j))
            return totals_ref[i, j]

        for n, weight in enumerate(tree_weights(len(labels), entry)):
            weights_ref[n] = weight

    first = second = 0.0
    for n, label in enumerate(labels):
        weight = weights_ref[label]
        first = first + weight * refs[2 * n][...].astype(jnp.float32)
        second = second + weight * refs[2 * n + 1][...].astype(jnp.float32)
    first_ref[...] = first
    second_ref[...] = second


def merge(place, totals, slots, labels):
    own, width = slots[0][0].shape
    block = max(b for b in range(16, min(own, 32) + 1, 16) if own % b == 0)
    spec = pl.BlockSpec((block, width), lambda n, s: (n, 0))
    arrays = [a for slot in slots for a in slot]
    shape = jax.ShapeDtypeStruct((own, width), jnp.float32)
    return call(
        functools.partial(merge_kernel, tuple(labels)),
        "merge",
        (place, totals, *arrays),
        [shape, shape],
        vmem=16 * 2**20,
        grid=(own // block,),
        in_specs=[pl.BlockSpec(memory_space=pltpu.SMEM)] + [spec] * len(arrays),
        out_specs=[spec, spec],
        scratch_shapes=[pltpu.SMEM((len(slots),), jnp.float32)],
    )


def on_device(inputs, targets, w_in, w_out):
    row_count = inputs.shape[0]
    workers = lax.axis_size("dp")
    shards = lax.axis_size("tensor")
    levels = workers.bit_length() - 1
    shard_levels = shards.bit_length() - 1
    gathered = min(levels, gather_levels_limit)
    members = 2**gathered
    others = workers // members
    position = lax.axis_index("dp")
    shard = lax.axis_index("tensor")
    member = position // others

    def part_of(index):
        part = 0
        for bit in range(shard_levels):
            part = part * 2 + (index >> bit & 1)
        return part

    near = shard & 1
    part_rows = row_count // shards
    own = inputs.shape[1] // members
    swap = 1
    bits = [2**b for b in reversed(range(gathered)) if 2**b != swap]
    upper = member // swap % 2
    first_row = (member - upper * swap) * own
    place = jnp.stack(
        [
            first_row // 128,
            first_row % 128 + upper * swap * own,
            first_row % 128 + (1 - upper) * swap * own,
            member,
            near,
            1 - near,
            part_of(shard),
            part_of(shard) - near * (shards // 2),
        ]
    ).astype(jnp.int32)

    send, hidden_near, own_part = forward(place, part_rows, inputs, w_in, w_out)
    got = from_mask(send, 0, 1)
    inputs_of = {bit: from_mask(own_part, bit * others, 0) for bit in bits}

    summed = product(place, hidden_near, w_out) + got
    most = 24.0 * 0.15625 * 0.078125 * inputs.shape[1] * w_in.shape[1] * shards
    scale = 2.0 ** math.ceil(math.log2(most / 65504.0))
    sums = [summed]
    for bit in range(1, shard_levels):
        rounded = (sum(sums) * (1.0 / scale)).astype(jnp.float16)
        sums.append(from_mask(rounded, 0, 2**bit).astype(jnp.float32) * scale)
    error, error_piece = error_half(
        place,
        part_rows,
        sum(sums[:-1]),
        sums[-1],
        targets,
        tuple(inputs_of.values()),
    )
    errors_of = {bit: from_mask(error_piece, bit * others, 0) for bit in bits}

    def to_half(piece, *before):
        for bit in reversed(range(1, shard_levels)):
            got = ordered(from_mask(piece, 0, 2**bit), *before)
            piece = join(shard >> bit & 1, piece, got)
        return piece

    def both_halves(half):
        return [(half, NEAR), (from_mask(half, 0, 1), FAR)]

    slots, labels, known, sent, halves = [], [], [], [], {}
    totals = jnp.zeros((8, 128), jnp.float32)
    masks = [m for m in range(members) if not m & swap]
    for n, m in enumerate(masks):
        if n == 0:
            half = error
        elif m in bits:
            errors_of[m] = ordered(errors_of[m], sent[0])
            top, of = (bits[0], inputs_of) if n == 1 else (m, errors_of)
            both = [top | bit for bit in bits[1:]]
            for to in both:
                of[to] = from_mask(ordered(of[top], errors_of[m]), (to ^ top) * others, 0)
            before = [of[to] for to in both] + list(slots[1][: 2 * n - 1]) + sent[1:]
            half = to_half(errors_of[m], *before)
            other_inputs = halves[m]
        else:
            other_inputs, half = (
                to_half(ordered(of[m], sent[-2]), sent[-1], *slots[2 * n - 3])
                for of in (inputs_of, errors_of)
            )
        first, second, *send = gradient(
            place,
            members,
            swap,
            both_halves(half),
            both_halves(other_inputs) if n else [(inputs, None)],
            w_in,
            w_out,
            known[-2:-1],
        )
        if n == 0:
            for bit in bits:
                halves[bit] = to_half(inputs_of[bit], send[0], errors_of[bits[0]], *halves.values())
        sent.append(send[0])
        slots.append((first, second))
        labels.append(m)
        last = n == len(masks) - 1
        if last:
            totals = products(place, slots, labels, 1, totals)
        slots.append(tuple(from_mask(a, swap * others, 0) for a in send))
        labels.append(m ^ swap)
        if last:
            for k in range(2):
                totals = products(place, [slot[k : k + 1] for slot in slots], labels, 1, totals)
        else:
            totals = products(place, slots, labels, 2, totals)
        known.append(totals)

    rounds = [[(0, mask) for mask in range(1, shards)]]
    rounds.append([(m * others, 0) for m in range(2, members, 2)])
    rounds.append([(others, 0)])
    for partners in rounds:
        totals = sum_of(place, [totals] + [from_mask(totals, *mask) for mask in partners])
    pieces = merge(place, totals, slots, labels)

    for section in range(gathered, levels):
        upper_flag = position >> levels - 1 - section & 1
        keep_first, send_first = split_piece(pieces[0], upper_flag)
        keep_second, send_second = split_piece(pieces[1], upper_flag)
        got_first, got_second = from_partner((send_first, send_second), "dp", levels - 1 - section)
        pieces = combine(
            (keep_first, keep_second), (got_first, got_second), upper_flag, section, levels
        )
    return (pieces[0], pieces[1])


def solution(mesh):
    placed = (P("dp", None), P("dp", None), P(None, "tensor"), P("tensor", None))
    return jax.shard_map(
        on_device,
        mesh=mesh,
        in_specs=placed,
        out_specs=(P("dp", "tensor"), P("dp", "tensor")),
        check_vma=False,
    )
```

```python
import functools
import math

import jax
import jax.numpy as jnp
from jax import lax
from jax.experimental import pallas as pl
from jax.experimental.pallas import tpu as pltpu
from jax.sharding import PartitionSpec as P

epsilon = 1e-06
gather_levels_limit = 3
vmem_bytes = 36 * 2**20
vmem_most = 60 * 2**20


def from_partner(value, axis, distance):
    mask = 2**distance
    pairs = [(source, source ^ mask) for source in range(lax.axis_size(axis))]
    return lax.ppermute(value, axis, pairs)


def from_mask(value, dp_mask, tensor_mask):
    shards = lax.axis_size("tensor")
    mask = dp_mask * shards + tensor_mask
    pairs = [(source, source ^ mask) for source in range(lax.axis_size("dp") * shards)]
    return lax.ppermute(value, ("dp", "tensor"), pairs)


def ordered(value, *before):
    return lax.optimization_barrier((value, *before))[0]


def split_piece(piece, upper_flag):
    half = piece.shape[0] // 2
    keep = lax.dynamic_slice_in_dim(piece, upper_flag * half, half, 0)
    send = lax.dynamic_slice_in_dim(piece, (1 - upper_flag) * half, half, 0)
    return (keep, send)


def group_total(values, section, levels):
    summed = lax.psum(values, "tensor")
    for offset in range(section + 1):
        summed = summed + from_partner(summed, "dp", levels - 1 - offset)
    return summed


def combine(own, incoming, upper_flag, section, levels):
    product = jnp.sum(own[0] * incoming[0]) + jnp.sum(own[1] * incoming[1])
    norm_own = jnp.sum(own[0] * own[0]) + jnp.sum(own[1] * own[1])
    norm_incoming = jnp.sum(incoming[0] * incoming[0]) + jnp.sum(incoming[1] * incoming[1])
    is_upper = upper_flag == 1
    norm_low = jnp.where(is_upper, norm_incoming, norm_own)
    norm_high = jnp.where(is_upper, norm_own, norm_incoming)
    totals = group_total(jnp.stack([product, norm_low, norm_high]), section, levels)
    coef_low = 1.0 - totals[0] / (2.0 * (totals[1] + epsilon))
    coef_high = 1.0 - totals[0] / (2.0 * (totals[2] + epsilon))
    coef_own = jnp.where(is_upper, coef_high, coef_low)
    coef_incoming = jnp.where(is_upper, coef_low, coef_high)
    return (
        coef_own * own[0] + coef_incoming * incoming[0],
        coef_own * own[1] + coef_incoming * incoming[1],
    )


def tile_of(size, limit):
    return max(b for b in range(128, limit + 1, 128) if size % b == 0)


def contract(left, right, left_dim, right_dim):
    dims = (((left_dim,), (right_dim,)), ((), ()))
    return lax.dot_general(left, right, dims, preferred_element_type=jnp.float32)


def call(kernel, name, operands, shapes, after=(), vmem=vmem_bytes, **spec):
    spec["in_specs"] = [pl.BlockSpec(memory_space=pl.ANY)] * len(after) + spec["in_specs"]

    def body(place_ref, *refs):
        kernel(place_ref, *refs[len(after) :])

    return pl.pallas_call(
        body,
        grid_spec=pltpu.PrefetchScalarGridSpec(num_scalar_prefetch=1, **spec),
        out_shape=shapes,
        compiler_params=pltpu.CompilerParams(vmem_limit_bytes=vmem),
        cost_estimate=pl.CostEstimate(flops=1, bytes_accessed=1, transcendentals=0),
        name=name,
    )(operands[0], *after, *operands[1:])


WINDOW, SHIFT, OTHER_SHIFT, MEMBER, NEAR, FAR, PART, PIECE = range(8)


def row_start(place_ref, block, where):
    return 0 if where is None else pl.multiple_of(place_ref[where] * block.shape[0], 16)


def whole(n, s):
    return (0, 0)


def column(n, s):
    return (0, n)


SCALE = math.sqrt(2.0 / math.pi)
CUBE = 0.044715


def forward_kernel(
    steps, place_ref, rows_ref, w_in_ref, w_out_ref, out_ref, near_ref, part_ref, hidden
):
    step = pl.program_id(0)
    half = out_ref.shape[0]
    far = pl.ds(row_start(place_ref, out_ref, FAR), half)
    tile = w_in_ref.shape[1]

    for n in range(steps):

        @pl.when(step == n)
        def _():
            v = jnp.dot(rows_ref[...], w_in_ref[...], preferred_element_type=jnp.float32)
            t = jnp.tanh(v * (SCALE + (SCALE * CUBE) * (v * v)))
            hidden[:, n * tile : (n + 1) * tile] = (v * (0.5 + 0.5 * t)).astype(jnp.bfloat16)

    @pl.when(step == 0)
    def _():
        part_ref[...] = rows_ref[pl.ds(row_start(place_ref, part_ref, PART), part_ref.shape[0]), :]

    @pl.when(step == steps)
    def _():
        near_ref[...] = hidden[pl.ds(row_start(place_ref, out_ref, NEAR), half), :]

    @pl.when(step >= steps)
    def _():
        out_ref[...] = jnp.dot(hidden[far, :], w_out_ref[...], preferred_element_type=jnp.float32)


def forward(place, part_rows, inputs, w_in, w_out):
    rows = inputs.shape[0]
    depth, width = w_in.shape
    tile, out_tile = tile_of(width, 640), tile_of(depth, 640)
    steps = width // tile
    last = lambda n: jnp.maximum(n - steps, 0)
    return call(
        functools.partial(forward_kernel, steps),
        "forward",
        (place, inputs, w_in, w_out),
        [
            jax.ShapeDtypeStruct((rows // 2, depth), jnp.float32),
            jax.ShapeDtypeStruct((rows // 2, width), jnp.bfloat16),
            jax.ShapeDtypeStruct((part_rows, depth), jnp.bfloat16),
        ],
        vmem=vmem_most,
        grid=(steps + depth // out_tile,),
        in_specs=[
            pl.BlockSpec((rows, depth), whole),
            pl.BlockSpec((depth, tile), lambda n, s: (0, jnp.minimum(n, steps - 1))),
            pl.BlockSpec((width, out_tile), lambda n, s: (0, last(n))),
        ],
        out_specs=[
            pl.BlockSpec((rows // 2, out_tile), lambda n, s: (0, last(n))),
            pl.BlockSpec((rows // 2, width), whole),
            pl.BlockSpec((part_rows, depth), whole),
        ],
        scratch_shapes=[pltpu.VMEM((rows, width), jnp.bfloat16)],
    )


def product_kernel(place_ref, left_ref, right_ref, out_ref):
    out_ref[...] = jnp.dot(left_ref[...], right_ref[...], preferred_element_type=jnp.float32)


def product(place, left, right):
    rows, depth = left.shape
    width = right.shape[1]
    tile = tile_of(width, 640)
    return call(
        product_kernel,
        "product",
        (place, left, right),
        [jax.ShapeDtypeStruct((rows, width), jnp.float32)],
        grid=(width // tile,),
        in_specs=[pl.BlockSpec((rows, depth), whole), pl.BlockSpec((depth, tile), column)],
        out_specs=[pl.BlockSpec((rows, tile), column)],
    )[0]


def join_kernel(place_ref, own_ref, got_ref, out_ref):
    rows = own_ref.shape[0]
    out_ref[pl.ds(pl.multiple_of(place_ref[0] * rows, 16), rows), :] = own_ref[...]
    out_ref[pl.ds(pl.multiple_of((1 - place_ref[0]) * rows, 16), rows), :] = got_ref[...]


def join(flag, own, got):
    rows, depth = own.shape
    return call(
        join_kernel,
        "join",
        (flag.reshape(1), own, got),
        [jax.ShapeDtypeStruct((2 * rows, depth), own.dtype)],
        grid=(1,),
        in_specs=[pl.BlockSpec((rows, depth), whole)] * 2,
        out_specs=[pl.BlockSpec((2 * rows, depth), whole)],
    )[0]


def error_kernel(row_count, place_ref, own_ref, got_ref, targets_ref, half_ref, part_ref):
    out = own_ref[...] + got_ref[...]
    error = (out - targets_ref[...].astype(jnp.float32)) / row_count
    half_ref[...] = error.astype(jnp.bfloat16)
    rows = part_ref.shape[0]
    part_ref[...] = half_ref[pl.ds(pl.multiple_of(place_ref[PIECE] * rows, 16), rows), :]


def error_half(place, part_rows, own, got, targets, after):
    rows, depth = own.shape
    return call(
        functools.partial(error_kernel, targets.shape[0]),
        "error_half",
        (place, own, got, targets),
        [
            jax.ShapeDtypeStruct((rows, depth), jnp.bfloat16),
            jax.ShapeDtypeStruct((part_rows, depth), jnp.bfloat16),
        ],
        after,
        grid=(1,),
        in_specs=[
            pl.BlockSpec((rows, depth), whole),
            pl.BlockSpec((rows, depth), whole),
            pl.BlockSpec((rows, depth), lambda n, s: (s[NEAR], 0)),
        ],
        out_specs=[pl.BlockSpec((rows, depth), whole), pl.BlockSpec((part_rows, depth), whole)],
    )


def gradient_kernel(wheres, window, own, step_rows, place_ref, *refs):
    error_wheres, input_wheres = wheres
    refs = list(refs)

    def take(n):
        taken = refs[:n]
        del refs[:n]
        return taken

    error_refs, input_refs = take(len(error_wheres)), take(len(input_wheres))
    w_in_ref, w_out_ref, first_ref, second_ref, send_first_ref, send_second_ref = take(6)
    errors, inputs, inputs_turned, errors_turned, spread_first, spread_second = refs
    if len(input_refs) == 1:
        inputs = input_refs[0]

    @pl.when(pl.program_id(0) == 0)
    def _():
        for block, where in zip(error_refs, error_wheres):
            errors[pl.ds(row_start(place_ref, block, where), block.shape[0]), :] = block[...]
        if len(input_refs) > 1:
            for block, where in zip(input_refs, input_wheres):
                inputs[pl.ds(row_start(place_ref, block, where), block.shape[0]), :] = block[...]
        lane = pl.multiple_of(place_ref[WINDOW] * 128, 128)
        inputs_turned[...] = inputs[:, pl.ds(lane, window * 128)].T
        errors_turned[...] = errors[:, pl.ds(lane, window * 128)].T

    shift = pl.multiple_of(place_ref[SHIFT], step_rows)
    other_shift = pl.multiple_of(place_ref[OTHER_SHIFT], step_rows)
    v = jnp.dot(inputs[...], w_in_ref[...], preferred_element_type=jnp.float32)
    back = lax.dot_general(
        errors[...], w_out_ref[...], (((1,), (1,)), ((), ())), preferred_element_type=jnp.float32
    )
    square = v * v
    t = jnp.tanh(v * (SCALE + (SCALE * CUBE) * square))
    upper = 0.5 + 0.5 * t
    hidden = (v * upper).astype(jnp.bfloat16)
    spread_second[...] = jnp.dot(errors_turned[...], hidden, preferred_element_type=jnp.float32)
    slope = upper + (0.5 * v) * (1.0 - t * t) * (SCALE + (3.0 * SCALE * CUBE) * square)
    dpre = (back * slope).astype(jnp.bfloat16)
    spread_first[...] = jnp.dot(inputs_turned[...], dpre, preferred_element_type=jnp.float32)
    second_ref[...] = spread_second[pl.ds(shift, own), :]
    send_second_ref[...] = spread_second[pl.ds(other_shift, own), :].astype(jnp.bfloat16)
    first_ref[...] = spread_first[pl.ds(shift, own), :]
    send_first_ref[...] = spread_first[pl.ds(other_shift, own), :].astype(jnp.bfloat16)


def gradient(place, members, swap, errors, inputs, w_in, w_out, after=()):
    error_arrays, error_wheres = zip(*errors)
    input_arrays, input_wheres = zip(*inputs)
    depth, width = w_in.shape
    rows = sum(a.shape[0] for a in input_arrays)
    own = depth // members
    reach = max(m * own % 128 for m in range(members) if not m & swap) + (swap + 1) * own
    window = -(-reach // 128)
    tile = tile_of(width, 640)
    once = pl.Buffered(1)
    return call(
        functools.partial(
            gradient_kernel, (error_wheres, input_wheres), window, own, math.gcd(own, 128)
        ),
        "gradient",
        (place, *error_arrays, *input_arrays, w_in, w_out),
        [
            jax.ShapeDtypeStruct((own, width), jnp.float32),
            jax.ShapeDtypeStruct((own, width), jnp.float32),
            jax.ShapeDtypeStruct((own, width), jnp.bfloat16),
            jax.ShapeDtypeStruct((own, width), jnp.bfloat16),
        ],
        after,
        grid=(width // tile,),
        in_specs=[
            pl.BlockSpec(a.shape, whole, pipeline_mode=once)
            for a in (*error_arrays, *input_arrays)
        ]
        + [pl.BlockSpec((depth, tile), column), pl.BlockSpec((tile, depth), lambda n, s: (n, 0))],
        out_specs=[pl.BlockSpec((own, tile), column)] * 4,
        scratch_shapes=[
            pltpu.VMEM((rows, depth), jnp.bfloat16),
            pltpu.VMEM((rows, depth), jnp.bfloat16),
            pltpu.VMEM((window * 128, rows), jnp.bfloat16),
            pltpu.VMEM((window * 128, rows), jnp.bfloat16),
            pltpu.VMEM((window * 128, tile), jnp.float32),
            pltpu.VMEM((window * 128, tile), jnp.float32),
        ],
    )


def products_kernel(labels, fresh, place_ref, *refs):
    own = refs[0].shape[0]
    refs, (known_ref, out_ref, totals) = refs[:-3], refs[-3:]
    each = len(refs) // len(labels)
    slots = [refs[each * n : each * (n + 1)] for n in range(len(labels))]
    pairs = [(i, j) for i in range(len(slots) - fresh, len(slots)) for j in range(i + 1)]

    @pl.when(pl.program_id(0) == 0)
    def _():
        totals[...] = jnp.zeros_like(totals)

    def values(slot):
        return [ref[...].astype(jnp.float32) for ref in slot]

    for n, (i, j) in enumerate(pairs):
        a, b = values(slots[i]), values(slots[j])
        both = sum(u * v for u, v in zip(a, b))
        totals[n] += jnp.sum(both.reshape(own // 8, 8, -1), axis=0)

    @pl.when(pl.program_id(0) == pl.num_programs(0) - 1)
    def _():
        result = known_ref[...]
        row = lax.broadcasted_iota(jnp.int32, result.shape, 0)
        column = lax.broadcasted_iota(jnp.int32, result.shape, 1)
        for n, (i, j) in enumerate(pairs):
            i, j = (jnp.bitwise_xor(place_ref[MEMBER], labels[k]) for k in (i, j))
            here = ((row == i) & (column == j)) | ((row == j) & (column == i))
            result = result + jnp.where(here, jnp.sum(totals[n]), 0.0)
        out_ref[...] = result


def products(place, slots, labels, fresh, known, after=()):
    arrays = [a for slot in slots for a in slot]
    own, width = slots[0][0].shape
    tile = tile_of(width, 256)
    pairs = sum(len(slots) - n for n in range(fresh))
    return call(
        functools.partial(products_kernel, tuple(labels), fresh),
        "products",
        (place, *arrays, known),
        [jax.ShapeDtypeStruct(known.shape, jnp.float32)],
        after,
        grid=(width // tile,),
        in_specs=[pl.BlockSpec((a.shape[0], tile), lambda n, s: (0, n)) for a in arrays]
        + [pl.BlockSpec(known.shape, whole)],
        out_specs=[pl.BlockSpec(known.shape, whole)],
        scratch_shapes=[pltpu.VMEM((pairs, 8, tile), jnp.float32)],
    )[0]


def tree_weights(count, entry):
    def inner(a, b):
        total = 0.0
        for i, u in a.items():
            for j, v in b.items():
                total = total + u * v * entry(i, j)
        return total

    items = [{i: 1.0} for i in range(count)]
    while len(items) > 1:
        half = len(items) // 2
        merged = []
        for low, high in zip(items[:half], items[half:]):
            product = inner(low, high)
            scale_low = 1.0 - product / (2.0 * (jnp.maximum(inner(low, low), 0.0) + epsilon))
            scale_high = 1.0 - product / (2.0 * (jnp.maximum(inner(high, high), 0.0) + epsilon))
            joined = {i: u * scale_low for i, u in low.items()}
            joined.update({i: u * scale_high for i, u in high.items()})
            merged.append(joined)
        items = merged
    return [items[0][i] for i in range(count)]


def sum_kernel(place_ref, *refs):
    refs[-1][...] = sum(ref[...] for ref in refs[:-1])


def sum_of(place, parts):
    shape = parts[0].shape
    return call(
        sum_kernel,
        "sum_of",
        (place, *parts),
        [jax.ShapeDtypeStruct(shape, jnp.float32)],
        vmem=4 * 2**20,
        grid=(1,),
        in_specs=[pl.BlockSpec(shape, whole)] * len(parts),
        out_specs=[pl.BlockSpec(shape, whole)],
    )[0]


def merge_kernel(labels, place_ref, totals_ref, *refs):
    refs, (first_ref, second_ref, weights_ref) = refs[:-3], refs[-3:]

    @pl.when(pl.program_id(0) == 0)
    def _():
        def entry(i, j):
            i, j = (jnp.bitwise_xor(place_ref[MEMBER], k) for k in (i, j))
            return totals_ref[i, j]

        for n, weight in enumerate(tree_weights(len(labels), entry)):
            weights_ref[n] = weight

    first = second = 0.0
    for n, label in enumerate(labels):
        weight = weights_ref[label]
        first = first + weight * refs[2 * n][...].astype(jnp.float32)
        second = second + weight * refs[2 * n + 1][...].astype(jnp.float32)
    first_ref[...] = first
    second_ref[...] = second


def merge(place, totals, slots, labels):
    own, width = slots[0][0].shape
    block = max(b for b in range(16, min(own, 32) + 1, 16) if own % b == 0)
    spec = pl.BlockSpec((block, width), lambda n, s: (n, 0))
    arrays = [a for slot in slots for a in slot]
    shape = jax.ShapeDtypeStruct((own, width), jnp.float32)
    return call(
        functools.partial(merge_kernel, tuple(labels)),
        "merge",
        (place, totals, *arrays),
        [shape, shape],
        vmem=16 * 2**20,
        grid=(own // block,),
        in_specs=[pl.BlockSpec(memory_space=pltpu.SMEM)] + [spec] * len(arrays),
        out_specs=[spec, spec],
        scratch_shapes=[pltpu.SMEM((len(slots),), jnp.float32)],
    )


def on_device(inputs, targets, w_in, w_out):
    row_count = inputs.shape[0]
    workers = lax.axis_size("dp")
    shards = lax.axis_size("tensor")
    levels = workers.bit_length() - 1
    shard_levels = shards.bit_length() - 1
    gathered = min(levels, gather_levels_limit)
    members = 2**gathered
    others = workers // members
    position = lax.axis_index("dp")
    shard = lax.axis_index("tensor")
    member = position // others

    def part_of(index):
        part = 0
        for bit in range(shard_levels):
            part = part * 2 + (index >> bit & 1)
        return part

    near = shard & 1
    part_rows = row_count // shards
    own = inputs.shape[1] // members
    swap = 1
    bits = [2**b for b in reversed(range(gathered)) if 2**b != swap]
    upper = member // swap % 2
    first_row = (member - upper * swap) * own
    place = jnp.stack(
        [
            first_row // 128,
            first_row % 128 + upper * swap * own,
            first_row % 128 + (1 - upper) * swap * own,
            member,
            near,
            1 - near,
            part_of(shard),
            part_of(shard) - near * (shards // 2),
        ]
    ).astype(jnp.int32)

    send, hidden_near, own_part = forward(place, part_rows, inputs, w_in, w_out)
    got = from_mask(send, 0, 1)
    inputs_of = {bit: from_mask(own_part, bit * others, 0) for bit in bits}

    summed = product(place, hidden_near, w_out) + got
    most = 24.0 * 0.15625 * 0.078125 * inputs.shape[1] * w_in.shape[1] * shards
    scale = 2.0 ** math.ceil(math.log2(most / 65504.0))
    sums = [summed]
    for bit in range(1, shard_levels):
        rounded = (sum(sums) * (1.0 / scale)).astype(jnp.float16)
        sums.append(from_mask(rounded, 0, 2**bit).astype(jnp.float32) * scale)
    error, error_piece = error_half(
        place,
        part_rows,
        sum(sums[:-1]),
        sums[-1],
        targets,
        tuple(inputs_of.values()),
    )
    errors_of = {
        bit: from_mask(error_piece if bit == bits[0] else error, bit * others, 0) for bit in bits
    }

    def to_half(piece, *before):
        for bit in reversed(range(1, shard_levels)):
            got = ordered(from_mask(piece, 0, 2**bit), *before)
            piece = join(shard >> bit & 1, piece, got)
        return piece

    def both_halves(half):
        return [(half, NEAR), (from_mask(half, 0, 1), FAR)]

    slots, labels, known, sent, halves = [], [], [], [], {}
    totals = jnp.zeros((8, 128), jnp.float32)
    masks = [m for m in range(members) if not m & swap]
    for n, m in enumerate(masks):
        if n == 0:
            half = error
        elif m not in (bits[0], masks[-1]):
            half = errors_of[m] = ordered(errors_of[m], sent[0], *slots[1][:1])
            other_inputs = halves[m]
        elif m == bits[0]:
            before = [sent[-1], *slots[1]]
            errors_of[m] = ordered(errors_of[m], sent[0])
            for bit in bits[1:]:
                ready = ordered(errors_of[m], errors_of[bit])
                errors_of[m | bit] = from_mask(ready, bit * others, 0)
                before.append(errors_of[m | bit])
                ready = ordered(halves[m], errors_of[bit])
                halves[m | bit] = from_mask(ready, bit * others, 0)
            half = to_half(errors_of[m], *before)
            other_inputs = halves[m]
        else:
            half = to_half(ordered(errors_of[m], sent[-2]), sent[-1], *slots[2 * n - 3])
            other_inputs = ordered(halves[m], sent[-1])
        first, second, *send = gradient(
            place,
            members,
            swap,
            both_halves(half),
            both_halves(other_inputs) if n else [(inputs, None)],
            w_in,
            w_out,
            known[-2:-1],
        )
        if n == 0:
            for bit in bits:
                halves[bit] = to_half(inputs_of[bit], send[0], errors_of[bits[0]], *halves.values())
        sent.append(send[0])
        slots.append((first, second))
        labels.append(m)
        last = n == len(masks) - 1
        if last:
            totals = products(place, slots, labels, 1, totals)
        slots.append(tuple(from_mask(a, swap * others, 0) for a in send))
        labels.append(m ^ swap)
        if last:
            for k in range(2):
                totals = products(place, [slot[k : k + 1] for slot in slots], labels, 1, totals)
        else:
            totals = products(place, slots, labels, 2, totals)
        known.append(totals)

    rounds = [[(0, mask) for mask in range(1, shards)]]
    rounds.append([(m * others, 0) for m in range(2, members, 2)])
    rounds.append([(others, 0)])
    for partners in rounds:
        totals = sum_of(place, [totals] + [from_mask(totals, *mask) for mask in partners])
    pieces = merge(place, totals, slots, labels)

    for section in range(gathered, levels):
        upper_flag = position >> levels - 1 - section & 1
        keep_first, send_first = split_piece(pieces[0], upper_flag)
        keep_second, send_second = split_piece(pieces[1], upper_flag)
        got_first, got_second = from_partner((send_first, send_second), "dp", levels - 1 - section)
        pieces = combine(
            (keep_first, keep_second), (got_first, got_second), upper_flag, section, levels
        )
    return (pieces[0], pieces[1])


def solution(mesh):
    placed = (P("dp", None), P("dp", None), P(None, "tensor"), P("tensor", None))
    return jax.shard_map(
        on_device,
        mesh=mesh,
        in_specs=placed,
        out_specs=(P("dp", "tensor"), P("dp", "tensor")),
        check_vma=False,
    )
```

```python
import functools
import math

import jax
import jax.numpy as jnp
from jax import lax
from jax.experimental import pallas as pl
from jax.experimental.pallas import tpu as pltpu
from jax.sharding import PartitionSpec as P

epsilon = 1e-06
gather_levels_limit = 3
vmem_bytes = 36 * 2**20
vmem_most = 60 * 2**20


def from_partner(value, axis, distance):
    mask = 2**distance
    pairs = [(source, source ^ mask) for source in range(lax.axis_size(axis))]
    return lax.ppermute(value, axis, pairs)


def from_mask(value, dp_mask, tensor_mask):
    shards = lax.axis_size("tensor")
    mask = dp_mask * shards + tensor_mask
    pairs = [(source, source ^ mask) for source in range(lax.axis_size("dp") * shards)]
    return lax.ppermute(value, ("dp", "tensor"), pairs)


def ordered(value, *before):
    return lax.optimization_barrier((value, *before))[0]


def split_piece(piece, upper_flag):
    half = piece.shape[0] // 2
    keep = lax.dynamic_slice_in_dim(piece, upper_flag * half, half, 0)
    send = lax.dynamic_slice_in_dim(piece, (1 - upper_flag) * half, half, 0)
    return (keep, send)


def group_total(values, section, levels):
    summed = lax.psum(values, "tensor")
    for offset in range(section + 1):
        summed = summed + from_partner(summed, "dp", levels - 1 - offset)
    return summed


def combine(own, incoming, upper_flag, section, levels):
    product = jnp.sum(own[0] * incoming[0]) + jnp.sum(own[1] * incoming[1])
    norm_own = jnp.sum(own[0] * own[0]) + jnp.sum(own[1] * own[1])
    norm_incoming = jnp.sum(incoming[0] * incoming[0]) + jnp.sum(incoming[1] * incoming[1])
    is_upper = upper_flag == 1
    norm_low = jnp.where(is_upper, norm_incoming, norm_own)
    norm_high = jnp.where(is_upper, norm_own, norm_incoming)
    totals = group_total(jnp.stack([product, norm_low, norm_high]), section, levels)
    coef_low = 1.0 - totals[0] / (2.0 * (totals[1] + epsilon))
    coef_high = 1.0 - totals[0] / (2.0 * (totals[2] + epsilon))
    coef_own = jnp.where(is_upper, coef_high, coef_low)
    coef_incoming = jnp.where(is_upper, coef_low, coef_high)
    return (
        coef_own * own[0] + coef_incoming * incoming[0],
        coef_own * own[1] + coef_incoming * incoming[1],
    )


def tile_of(size, limit):
    return max(b for b in range(128, limit + 1, 128) if size % b == 0)


def contract(left, right, left_dim, right_dim):
    dims = (((left_dim,), (right_dim,)), ((), ()))
    return lax.dot_general(left, right, dims, preferred_element_type=jnp.float32)


def call(kernel, name, operands, shapes, after=(), vmem=vmem_bytes, **spec):
    spec["in_specs"] = [pl.BlockSpec(memory_space=pl.ANY)] * len(after) + spec["in_specs"]

    def body(place_ref, *refs):
        kernel(place_ref, *refs[len(after) :])

    return pl.pallas_call(
        body,
        grid_spec=pltpu.PrefetchScalarGridSpec(num_scalar_prefetch=1, **spec),
        out_shape=shapes,
        compiler_params=pltpu.CompilerParams(vmem_limit_bytes=vmem),
        cost_estimate=pl.CostEstimate(flops=1, bytes_accessed=1, transcendentals=0),
        name=name,
    )(operands[0], *after, *operands[1:])


WINDOW, SHIFT, OTHER_SHIFT, MEMBER, NEAR, FAR, PART, PIECE, OWN_WINDOW, OWN_SHIFT = range(10)


def row_start(place_ref, block, where):
    return 0 if where is None else pl.multiple_of(place_ref[where] * block.shape[0], 16)


def whole(n, s):
    return (0, 0)


def column(n, s):
    return (0, n)


SCALE = math.sqrt(2.0 / math.pi)
CUBE = 0.044715


def forward_kernel(
    steps, place_ref, rows_ref, w_in_ref, w_out_ref, out_ref, near_ref, part_ref, hidden
):
    step = pl.program_id(0)
    half = out_ref.shape[0]
    far = pl.ds(row_start(place_ref, out_ref, FAR), half)
    tile = w_in_ref.shape[1]

    for n in range(steps):

        @pl.when(step == n)
        def _():
            v = jnp.dot(rows_ref[...], w_in_ref[...], preferred_element_type=jnp.float32)
            t = jnp.tanh(v * (SCALE + (SCALE * CUBE) * (v * v)))
            hidden[:, n * tile : (n + 1) * tile] = (v * (0.5 + 0.5 * t)).astype(jnp.bfloat16)

    @pl.when(step == 0)
    def _():
        part_ref[...] = rows_ref[pl.ds(row_start(place_ref, part_ref, PART), part_ref.shape[0]), :]

    @pl.when(step == steps)
    def _():
        near_ref[...] = hidden[pl.ds(row_start(place_ref, out_ref, NEAR), half), :]

    @pl.when(step >= steps)
    def _():
        out_ref[...] = jnp.dot(hidden[far, :], w_out_ref[...], preferred_element_type=jnp.float32)


def forward(place, part_rows, inputs, w_in, w_out):
    rows = inputs.shape[0]
    depth, width = w_in.shape
    tile, out_tile = tile_of(width, 640), tile_of(depth, 640)
    steps = width // tile
    last = lambda n: jnp.maximum(n - steps, 0)
    return call(
        functools.partial(forward_kernel, steps),
        "forward",
        (place, inputs, w_in, w_out),
        [
            jax.ShapeDtypeStruct((rows // 2, depth), jnp.float32),
            jax.ShapeDtypeStruct((rows // 2, width), jnp.bfloat16),
            jax.ShapeDtypeStruct((part_rows, depth), jnp.bfloat16),
        ],
        vmem=vmem_most,
        grid=(steps + depth // out_tile,),
        in_specs=[
            pl.BlockSpec((rows, depth), whole),
            pl.BlockSpec((depth, tile), lambda n, s: (0, jnp.minimum(n, steps - 1))),
            pl.BlockSpec((width, out_tile), lambda n, s: (0, last(n))),
        ],
        out_specs=[
            pl.BlockSpec((rows // 2, out_tile), lambda n, s: (0, last(n))),
            pl.BlockSpec((rows // 2, width), whole),
            pl.BlockSpec((part_rows, depth), whole),
        ],
        scratch_shapes=[pltpu.VMEM((rows, width), jnp.bfloat16)],
    )


def product_kernel(place_ref, left_ref, right_ref, out_ref):
    out_ref[...] = jnp.dot(left_ref[...], right_ref[...], preferred_element_type=jnp.float32)


def product(place, left, right):
    rows, depth = left.shape
    width = right.shape[1]
    tile = tile_of(width, 640)
    return call(
        product_kernel,
        "product",
        (place, left, right),
        [jax.ShapeDtypeStruct((rows, width), jnp.float32)],
        grid=(width // tile,),
        in_specs=[pl.BlockSpec((rows, depth), whole), pl.BlockSpec((depth, tile), column)],
        out_specs=[pl.BlockSpec((rows, tile), column)],
    )[0]


def join_kernel(place_ref, own_ref, got_ref, out_ref):
    rows = own_ref.shape[0]
    out_ref[pl.ds(pl.multiple_of(place_ref[0] * rows, 16), rows), :] = own_ref[...]
    out_ref[pl.ds(pl.multiple_of((1 - place_ref[0]) * rows, 16), rows), :] = got_ref[...]


def join(flag, own, got):
    rows, depth = own.shape
    return call(
        join_kernel,
        "join",
        (flag.reshape(1), own, got),
        [jax.ShapeDtypeStruct((2 * rows, depth), own.dtype)],
        grid=(1,),
        in_specs=[pl.BlockSpec((rows, depth), whole)] * 2,
        out_specs=[pl.BlockSpec((2 * rows, depth), whole)],
    )[0]


def error_kernel(row_count, place_ref, own_ref, got_ref, targets_ref, half_ref, part_ref):
    out = own_ref[...] + got_ref[...]
    error = (out - targets_ref[...].astype(jnp.float32)) / row_count
    half_ref[...] = error.astype(jnp.bfloat16)
    rows = part_ref.shape[0]
    part_ref[...] = half_ref[pl.ds(pl.multiple_of(place_ref[PIECE] * rows, 16), rows), :]


def error_half(place, part_rows, own, got, targets, after):
    rows, depth = own.shape
    return call(
        functools.partial(error_kernel, targets.shape[0]),
        "error_half",
        (place, own, got, targets),
        [
            jax.ShapeDtypeStruct((rows, depth), jnp.bfloat16),
            jax.ShapeDtypeStruct((part_rows, depth), jnp.bfloat16),
        ],
        after,
        grid=(1,),
        in_specs=[
            pl.BlockSpec((rows, depth), whole),
            pl.BlockSpec((rows, depth), whole),
            pl.BlockSpec((rows, depth), lambda n, s: (s[NEAR], 0)),
        ],
        out_specs=[pl.BlockSpec((rows, depth), whole), pl.BlockSpec((part_rows, depth), whole)],
    )


def gradient_kernel(wheres, window, own, step_rows, shared, place_ref, *refs):
    error_wheres, input_wheres = wheres
    refs = list(refs)

    def take(n):
        taken = refs[:n]
        del refs[:n]
        return taken

    error_refs, input_refs = take(len(error_wheres)), take(len(input_wheres))
    w_in_ref, w_out_ref, first_ref, second_ref = take(4)
    send_refs = take(2 if shared else 0)
    errors, inputs, inputs_turned, errors_turned, spread_first, spread_second = refs
    if len(input_refs) == 1:
        inputs = input_refs[0]

    @pl.when(pl.program_id(0) == 0)
    def _():
        for block, where in zip(error_refs, error_wheres):
            errors[pl.ds(row_start(place_ref, block, where), block.shape[0]), :] = block[...]
        if len(input_refs) > 1:
            for block, where in zip(input_refs, input_wheres):
                inputs[pl.ds(row_start(place_ref, block, where), block.shape[0]), :] = block[...]
        lane = pl.multiple_of(place_ref[WINDOW if shared else OWN_WINDOW] * 128, 128)
        inputs_turned[...] = inputs[:, pl.ds(lane, window * 128)].T
        errors_turned[...] = errors[:, pl.ds(lane, window * 128)].T

    shift = pl.multiple_of(place_ref[SHIFT if shared else OWN_SHIFT], step_rows)
    v = jnp.dot(inputs[...], w_in_ref[...], preferred_element_type=jnp.float32)
    back = lax.dot_general(
        errors[...], w_out_ref[...], (((1,), (1,)), ((), ())), preferred_element_type=jnp.float32
    )
    square = v * v
    t = jnp.tanh(v * (SCALE + (SCALE * CUBE) * square))
    upper = 0.5 + 0.5 * t
    hidden = (v * upper).astype(jnp.bfloat16)
    spread_second[...] = jnp.dot(errors_turned[...], hidden, preferred_element_type=jnp.float32)
    slope = upper + (0.5 * v) * (1.0 - t * t) * (SCALE + (3.0 * SCALE * CUBE) * square)
    dpre = (back * slope).astype(jnp.bfloat16)
    spread_first[...] = jnp.dot(inputs_turned[...], dpre, preferred_element_type=jnp.float32)
    second_ref[...] = spread_second[pl.ds(shift, own), :]
    first_ref[...] = spread_first[pl.ds(shift, own), :]
    if shared:
        other = pl.ds(pl.multiple_of(place_ref[OTHER_SHIFT], step_rows), own)
        send_refs[0][...] = spread_first[other, :].astype(jnp.bfloat16)
        send_refs[1][...] = spread_second[other, :].astype(jnp.bfloat16)


def gradient(place, members, swap, shared, errors, inputs, w_in, w_out, after=()):
    error_arrays, error_wheres = zip(*errors)
    input_arrays, input_wheres = zip(*inputs)
    depth, width = w_in.shape
    rows = sum(a.shape[0] for a in input_arrays)
    own = depth // members
    starts = [m * own % 128 for m in range(members) if not (shared and m & swap)]
    reach = max(starts) + (swap + 1 if shared else 1) * own
    window = -(-reach // 128)
    tile = tile_of(width, 640)
    once = pl.Buffered(1)
    return call(
        functools.partial(
            gradient_kernel, (error_wheres, input_wheres), window, own, math.gcd(own, 128), shared
        ),
        "gradient",
        (place, *error_arrays, *input_arrays, w_in, w_out),
        [
            jax.ShapeDtypeStruct((own, width), jnp.float32),
            jax.ShapeDtypeStruct((own, width), jnp.float32),
        ]
        + [jax.ShapeDtypeStruct((own, width), jnp.bfloat16)] * (2 if shared else 0),
        after,
        grid=(width // tile,),
        in_specs=[
            pl.BlockSpec(a.shape, whole, pipeline_mode=once)
            for a in (*error_arrays, *input_arrays)
        ]
        + [pl.BlockSpec((depth, tile), column), pl.BlockSpec((tile, depth), lambda n, s: (n, 0))],
        out_specs=[pl.BlockSpec((own, tile), column)] * (4 if shared else 2),
        scratch_shapes=[
            pltpu.VMEM((rows, depth), jnp.bfloat16),
            pltpu.VMEM((rows, depth), jnp.bfloat16),
            pltpu.VMEM((window * 128, rows), jnp.bfloat16),
            pltpu.VMEM((window * 128, rows), jnp.bfloat16),
            pltpu.VMEM((window * 128, tile), jnp.float32),
            pltpu.VMEM((window * 128, tile), jnp.float32),
        ],
    )


def products_kernel(labels, fresh, place_ref, *refs):
    own = refs[0].shape[0]
    refs, (known_ref, out_ref, totals) = refs[:-3], refs[-3:]
    each = len(refs) // len(labels)
    slots = [refs[each * n : each * (n + 1)] for n in range(len(labels))]
    pairs = [(i, j) for i in range(len(slots) - fresh, len(slots)) for j in range(i + 1)]

    @pl.when(pl.program_id(0) == 0)
    def _():
        totals[...] = jnp.zeros_like(totals)

    def values(slot):
        return [ref[...].astype(jnp.float32) for ref in slot]

    for n, (i, j) in enumerate(pairs):
        a, b = values(slots[i]), values(slots[j])
        both = sum(u * v for u, v in zip(a, b))
        totals[n] += jnp.sum(both.reshape(own // 8, 8, -1), axis=0)

    @pl.when(pl.program_id(0) == pl.num_programs(0) - 1)
    def _():
        result = known_ref[...]
        row = lax.broadcasted_iota(jnp.int32, result.shape, 0)
        column = lax.broadcasted_iota(jnp.int32, result.shape, 1)
        for n, (i, j) in enumerate(pairs):
            i, j = (jnp.bitwise_xor(place_ref[MEMBER], labels[k]) for k in (i, j))
            here = ((row == i) & (column == j)) | ((row == j) & (column == i))
            result = result + jnp.where(here, jnp.sum(totals[n]), 0.0)
        out_ref[...] = result


def products(place, slots, labels, fresh, known, after=()):
    arrays = [a for slot in slots for a in slot]
    own, width = slots[0][0].shape
    tile = tile_of(width, 256)
    pairs = sum(len(slots) - n for n in range(fresh))
    return call(
        functools.partial(products_kernel, tuple(labels), fresh),
        "products",
        (place, *arrays, known),
        [jax.ShapeDtypeStruct(known.shape, jnp.float32)],
        after,
        grid=(width // tile,),
        in_specs=[pl.BlockSpec((a.shape[0], tile), lambda n, s: (0, n)) for a in arrays]
        + [pl.BlockSpec(known.shape, whole)],
        out_specs=[pl.BlockSpec(known.shape, whole)],
        scratch_shapes=[pltpu.VMEM((pairs, 8, tile), jnp.float32)],
    )[0]


def tree_weights(count, entry):
    def inner(a, b):
        total = 0.0
        for i, u in a.items():
            for j, v in b.items():
                total = total + u * v * entry(i, j)
        return total

    items = [{i: 1.0} for i in range(count)]
    while len(items) > 1:
        half = len(items) // 2
        merged = []
        for low, high in zip(items[:half], items[half:]):
            product = inner(low, high)
            scale_low = 1.0 - product / (2.0 * (jnp.maximum(inner(low, low), 0.0) + epsilon))
            scale_high = 1.0 - product / (2.0 * (jnp.maximum(inner(high, high), 0.0) + epsilon))
            joined = {i: u * scale_low for i, u in low.items()}
            joined.update({i: u * scale_high for i, u in high.items()})
            merged.append(joined)
        items = merged
    return [items[0][i] for i in range(count)]


def sum_kernel(place_ref, *refs):
    refs[-1][...] = sum(ref[...] for ref in refs[:-1])


def sum_of(place, parts):
    shape = parts[0].shape
    return call(
        sum_kernel,
        "sum_of",
        (place, *parts),
        [jax.ShapeDtypeStruct(shape, jnp.float32)],
        vmem=4 * 2**20,
        grid=(1,),
        in_specs=[pl.BlockSpec(shape, whole)] * len(parts),
        out_specs=[pl.BlockSpec(shape, whole)],
    )[0]


def merge_kernel(labels, place_ref, totals_ref, *refs):
    refs, (first_ref, second_ref, weights_ref) = refs[:-3], refs[-3:]

    @pl.when(pl.program_id(0) == 0)
    def _():
        def entry(i, j):
            i, j = (jnp.bitwise_xor(place_ref[MEMBER], k) for k in (i, j))
            return totals_ref[i, j]

        for n, weight in enumerate(tree_weights(len(labels), entry)):
            weights_ref[n] = weight

    first = second = 0.0
    for n, label in enumerate(labels):
        weight = weights_ref[label]
        first = first + weight * refs[2 * n][...].astype(jnp.float32)
        second = second + weight * refs[2 * n + 1][...].astype(jnp.float32)
    first_ref[...] = first
    second_ref[...] = second


def merge(place, totals, slots, labels):
    own, width = slots[0][0].shape
    block = max(b for b in range(16, min(own, 32) + 1, 16) if own % b == 0)
    spec = pl.BlockSpec((block, width), lambda n, s: (n, 0))
    arrays = [a for slot in slots for a in slot]
    shape = jax.ShapeDtypeStruct((own, width), jnp.float32)
    return call(
        functools.partial(merge_kernel, tuple(labels)),
        "merge",
        (place, totals, *arrays),
        [shape, shape],
        vmem=16 * 2**20,
        grid=(own // block,),
        in_specs=[pl.BlockSpec(memory_space=pltpu.SMEM)] + [spec] * len(arrays),
        out_specs=[spec, spec],
        scratch_shapes=[pltpu.SMEM((len(slots),), jnp.float32)],
    )


def on_device(inputs, targets, w_in, w_out):
    row_count = inputs.shape[0]
    workers = lax.axis_size("dp")
    shards = lax.axis_size("tensor")
    levels = workers.bit_length() - 1
    shard_levels = shards.bit_length() - 1
    gathered = min(levels, gather_levels_limit)
    members = 2**gathered
    others = workers // members
    position = lax.axis_index("dp")
    shard = lax.axis_index("tensor")
    member = position // others

    def part_of(index):
        part = 0
        for bit in range(shard_levels):
            part = part * 2 + (index >> bit & 1)
        return part

    near = shard & 1
    part_rows = row_count // shards
    columns = inputs.shape[1] // members
    swap = 1
    bits = [2**b for b in reversed(range(gathered)) if 2**b != swap]
    upper = member // swap % 2
    first_row = (member - upper * swap) * columns
    place = jnp.stack(
        [
            first_row // 128,
            first_row % 128 + upper * swap * columns,
            first_row % 128 + (1 - upper) * swap * columns,
            member,
            near,
            1 - near,
            part_of(shard),
            part_of(shard) - near * (shards // 2),
            member * columns // 128,
            member * columns % 128,
        ]
    ).astype(jnp.int32)

    send, hidden_near, own_part = forward(place, part_rows, inputs, w_in, w_out)
    got = from_mask(send, 0, 1)
    inputs_of = {bit: from_mask(own_part, bit * others, 0) for bit in bits}

    summed = product(place, hidden_near, w_out) + got
    most = 24.0 * 0.15625 * 0.078125 * inputs.shape[1] * w_in.shape[1] * shards
    scale = 2.0 ** math.ceil(math.log2(most / 65504.0))
    sums = [summed]
    for bit in range(1, shard_levels):
        rounded = (sum(sums) * (1.0 / scale)).astype(jnp.float16)
        sums.append(from_mask(rounded, 0, 2**bit).astype(jnp.float32) * scale)
    error, error_piece = error_half(
        place,
        part_rows,
        sum(sums[:-1]),
        sums[-1],
        targets,
        tuple(inputs_of.values()),
    )
    high, low = bits
    errors_of = {
        high: from_mask(error_piece, high * others, 0),
        low: from_mask(error, low * others, 0),
    }
    inputs_of[high | swap] = from_mask(ordered(inputs_of[high], error), swap * others, 0)

    def to_half(piece, *before):
        for bit in reversed(range(1, shard_levels)):
            got = ordered(from_mask(piece, 0, 2**bit), *before)
            piece = join(shard >> bit & 1, piece, got)
        return piece

    def both_halves(half):
        return [(half, NEAR), (from_mask(half, 0, 1), FAR)]

    slots = {}

    def gradient_of(m, half, other_inputs, *after):
        shared = not m & high or bool(m & low)
        results = gradient(
            place, members, swap, shared, both_halves(half), other_inputs, w_in, w_out, after
        )
        slots[m] = tuple(results[:2])
        if shared:
            slots[m | swap] = tuple(from_mask(a, swap * others, 0) for a in results[2:])

    gradient_of(0, error, [(inputs, None)])
    own = slots[0][0]
    halves = {}
    for bit in bits:
        halves[bit] = to_half(inputs_of[bit], own, errors_of[high], *halves.values())

    half = errors_of[low] = ordered(
        errors_of[low], own, slots[swap][0], inputs_of[high | swap]
    )
    gradient_of(low, half, both_halves(halves[low]))
    token = slots[low][0]

    errors_of[high] = ordered(errors_of[high], own)
    ready = ordered(errors_of[high], half)
    errors_of[high | low] = from_mask(ready, low * others, 0)
    errors_of[high | swap] = from_mask(ready, swap * others, 0)
    halves[high | low] = from_mask(ordered(halves[high], half), low * others, 0)
    half = to_half(
        errors_of[high], token, errors_of[high | low], errors_of[high | swap], *slots[swap]
    )
    gradient_of(high, half, both_halves(halves[high]))
    token = slots[high][0]

    totals = jnp.zeros((8, 128), jnp.float32)
    labels = [0, swap, low, high]
    totals = products(place, [slots[m] for m in labels], labels, 4, totals)

    half = to_half(errors_of[high | low], token)
    ready = ordered(halves[high | low], token, *slots[low | swap])
    gradient_of(high | low, half, both_halves(ready), totals)
    token = slots[high | low][0]

    half = to_half(errors_of[high | swap], token)
    halves[high | swap] = to_half(inputs_of[high | swap], token)
    gradient_of(high | swap, half, both_halves(halves[high | swap]))
    labels += [low | swap, high | low, high | swap]
    totals = products(place, [slots[m] for m in labels], labels, 3, totals)
    labels.append(high | low | swap)
    for k in range(2):
        totals = products(place, [slots[m][k : k + 1] for m in labels], labels, 1, totals)
    slots = [slots[m] for m in labels]

    rounds = [[(0, mask) for mask in range(1, shards)]]
    rounds.append([(m * others, 0) for m in range(2, members, 2)])
    rounds.append([(others, 0)])
    for partners in rounds:
        totals = sum_of(place, [totals] + [from_mask(totals, *mask) for mask in partners])
    pieces = merge(place, totals, slots, labels)

    for section in range(gathered, levels):
        upper_flag = position >> levels - 1 - section & 1
        keep_first, send_first = split_piece(pieces[0], upper_flag)
        keep_second, send_second = split_piece(pieces[1], upper_flag)
        got_first, got_second = from_partner((send_first, send_second), "dp", levels - 1 - section)
        pieces = combine(
            (keep_first, keep_second), (got_first, got_second), upper_flag, section, levels
        )
    return (pieces[0], pieces[1])


def solution(mesh):
    placed = (P("dp", None), P("dp", None), P(None, "tensor"), P("tensor", None))
    return jax.shard_map(
        on_device,
        mesh=mesh,
        in_specs=placed,
        out_specs=(P("dp", "tensor"), P("dp", "tensor")),
        check_vma=False,
    )
```

```python
import functools
import math

import jax
import jax.numpy as jnp
from jax import lax
from jax.experimental import pallas as pl
from jax.experimental.pallas import tpu as pltpu
from jax.sharding import PartitionSpec as P

epsilon = 1e-06
gather_levels_limit = 3
vmem_bytes = 36 * 2**20
vmem_most = 60 * 2**20


def from_partner(value, axis, distance):
    mask = 2**distance
    pairs = [(source, source ^ mask) for source in range(lax.axis_size(axis))]
    return lax.ppermute(value, axis, pairs)


def from_mask(value, dp_mask, tensor_mask):
    shards = lax.axis_size("tensor")
    mask = dp_mask * shards + tensor_mask
    pairs = [(source, source ^ mask) for source in range(lax.axis_size("dp") * shards)]
    return lax.ppermute(value, ("dp", "tensor"), pairs)


def ordered(value, *before):
    return lax.optimization_barrier((value, *before))[0]


def split_piece(piece, upper_flag):
    half = piece.shape[0] // 2
    keep = lax.dynamic_slice_in_dim(piece, upper_flag * half, half, 0)
    send = lax.dynamic_slice_in_dim(piece, (1 - upper_flag) * half, half, 0)
    return (keep, send)


def group_total(values, section, levels):
    summed = lax.psum(values, "tensor")
    for offset in range(section + 1):
        summed = summed + from_partner(summed, "dp", levels - 1 - offset)
    return summed


def combine(own, incoming, upper_flag, section, levels):
    product = jnp.sum(own[0] * incoming[0]) + jnp.sum(own[1] * incoming[1])
    norm_own = jnp.sum(own[0] * own[0]) + jnp.sum(own[1] * own[1])
    norm_incoming = jnp.sum(incoming[0] * incoming[0]) + jnp.sum(incoming[1] * incoming[1])
    is_upper = upper_flag == 1
    norm_low = jnp.where(is_upper, norm_incoming, norm_own)
    norm_high = jnp.where(is_upper, norm_own, norm_incoming)
    totals = group_total(jnp.stack([product, norm_low, norm_high]), section, levels)
    coef_low = 1.0 - totals[0] / (2.0 * (totals[1] + epsilon))
    coef_high = 1.0 - totals[0] / (2.0 * (totals[2] + epsilon))
    coef_own = jnp.where(is_upper, coef_high, coef_low)
    coef_incoming = jnp.where(is_upper, coef_low, coef_high)
    return (
        coef_own * own[0] + coef_incoming * incoming[0],
        coef_own * own[1] + coef_incoming * incoming[1],
    )


def tile_of(size, limit):
    return max(b for b in range(128, limit + 1, 128) if size % b == 0)


def contract(left, right, left_dim, right_dim):
    dims = (((left_dim,), (right_dim,)), ((), ()))
    return lax.dot_general(left, right, dims, preferred_element_type=jnp.float32)


def call(kernel, name, operands, shapes, after=(), vmem=vmem_bytes, **spec):
    spec["in_specs"] = [pl.BlockSpec(memory_space=pl.ANY)] * len(after) + spec["in_specs"]

    def body(place_ref, *refs):
        kernel(place_ref, *refs[len(after) :])

    return pl.pallas_call(
        body,
        grid_spec=pltpu.PrefetchScalarGridSpec(num_scalar_prefetch=1, **spec),
        out_shape=shapes,
        compiler_params=pltpu.CompilerParams(vmem_limit_bytes=vmem),
        cost_estimate=pl.CostEstimate(flops=1, bytes_accessed=1, transcendentals=0),
        name=name,
    )(operands[0], *after, *operands[1:])


WINDOW, SHIFT, OTHER_SHIFT, MEMBER, NEAR, FAR, PART, PIECE, OWN_WINDOW, OWN_SHIFT = range(10)


def row_start(place_ref, block, where):
    return 0 if where is None else pl.multiple_of(place_ref[where] * block.shape[0], 16)


def whole(n, s):
    return (0, 0)


def column(n, s):
    return (0, n)


SCALE = math.sqrt(2.0 / math.pi)
CUBE = 0.044715


def forward_kernel(
    steps, place_ref, rows_ref, w_in_ref, w_out_ref, out_ref, near_ref, part_ref, hidden
):
    step = pl.program_id(0)
    half = out_ref.shape[0]
    far = pl.ds(row_start(place_ref, out_ref, FAR), half)
    tile = w_in_ref.shape[1]

    for n in range(steps):

        @pl.when(step == n)
        def _():
            v = jnp.dot(rows_ref[...], w_in_ref[...], preferred_element_type=jnp.float32)
            t = jnp.tanh(v * (SCALE + (SCALE * CUBE) * (v * v)))
            hidden[:, n * tile : (n + 1) * tile] = (v * (0.5 + 0.5 * t)).astype(jnp.bfloat16)

    @pl.when(step == 0)
    def _():
        part_ref[...] = rows_ref[pl.ds(row_start(place_ref, part_ref, PART), part_ref.shape[0]), :]

    @pl.when(step == steps)
    def _():
        near_ref[...] = hidden[pl.ds(row_start(place_ref, out_ref, NEAR), half), :]

    @pl.when(step >= steps)
    def _():
        out_ref[...] = jnp.dot(hidden[far, :], w_out_ref[...], preferred_element_type=jnp.float32)


def forward(place, part_rows, inputs, w_in, w_out):
    rows = inputs.shape[0]
    depth, width = w_in.shape
    tile, out_tile = tile_of(width, 640), tile_of(depth, 640)
    steps = width // tile
    last = lambda n: jnp.maximum(n - steps, 0)
    return call(
        functools.partial(forward_kernel, steps),
        "forward",
        (place, inputs, w_in, w_out),
        [
            jax.ShapeDtypeStruct((rows // 2, depth), jnp.float32),
            jax.ShapeDtypeStruct((rows // 2, width), jnp.bfloat16),
            jax.ShapeDtypeStruct((part_rows, depth), jnp.bfloat16),
        ],
        vmem=vmem_most,
        grid=(steps + depth // out_tile,),
        in_specs=[
            pl.BlockSpec((rows, depth), whole),
            pl.BlockSpec((depth, tile), lambda n, s: (0, jnp.minimum(n, steps - 1))),
            pl.BlockSpec((width, out_tile), lambda n, s: (0, last(n))),
        ],
        out_specs=[
            pl.BlockSpec((rows // 2, out_tile), lambda n, s: (0, last(n))),
            pl.BlockSpec((rows // 2, width), whole),
            pl.BlockSpec((part_rows, depth), whole),
        ],
        scratch_shapes=[pltpu.VMEM((rows, width), jnp.bfloat16)],
    )


def product_kernel(place_ref, left_ref, right_ref, out_ref):
    out_ref[...] = jnp.dot(left_ref[...], right_ref[...], preferred_element_type=jnp.float32)


def product(place, left, right):
    rows, depth = left.shape
    width = right.shape[1]
    tile = tile_of(width, 640)
    return call(
        product_kernel,
        "product",
        (place, left, right),
        [jax.ShapeDtypeStruct((rows, width), jnp.float32)],
        grid=(width // tile,),
        in_specs=[pl.BlockSpec((rows, depth), whole), pl.BlockSpec((depth, tile), column)],
        out_specs=[pl.BlockSpec((rows, tile), column)],
    )[0]


def join_kernel(place_ref, own_ref, got_ref, out_ref):
    rows = own_ref.shape[0]
    out_ref[pl.ds(pl.multiple_of(place_ref[0] * rows, 16), rows), :] = own_ref[...]
    out_ref[pl.ds(pl.multiple_of((1 - place_ref[0]) * rows, 16), rows), :] = got_ref[...]


def join(flag, own, got):
    rows, depth = own.shape
    return call(
        join_kernel,
        "join",
        (flag.reshape(1), own, got),
        [jax.ShapeDtypeStruct((2 * rows, depth), own.dtype)],
        grid=(1,),
        in_specs=[pl.BlockSpec((rows, depth), whole)] * 2,
        out_specs=[pl.BlockSpec((2 * rows, depth), whole)],
    )[0]


def error_kernel(row_count, place_ref, own_ref, got_ref, targets_ref, half_ref, part_ref):
    out = own_ref[...] + got_ref[...]
    error = (out - targets_ref[...].astype(jnp.float32)) / row_count
    half_ref[...] = error.astype(jnp.bfloat16)
    rows = part_ref.shape[0]
    part_ref[...] = half_ref[pl.ds(pl.multiple_of(place_ref[PIECE] * rows, 16), rows), :]


def error_half(place, part_rows, own, got, targets, after):
    rows, depth = own.shape
    return call(
        functools.partial(error_kernel, targets.shape[0]),
        "error_half",
        (place, own, got, targets),
        [
            jax.ShapeDtypeStruct((rows, depth), jnp.bfloat16),
            jax.ShapeDtypeStruct((part_rows, depth), jnp.bfloat16),
        ],
        after,
        grid=(1,),
        in_specs=[
            pl.BlockSpec((rows, depth), whole),
            pl.BlockSpec((rows, depth), whole),
            pl.BlockSpec((rows, depth), lambda n, s: (s[NEAR], 0)),
        ],
        out_specs=[pl.BlockSpec((rows, depth), whole), pl.BlockSpec((part_rows, depth), whole)],
    )


def gradient_kernel(wheres, window, own, step_rows, shared, place_ref, *refs):
    error_wheres, input_wheres = wheres
    refs = list(refs)

    def take(n):
        taken = refs[:n]
        del refs[:n]
        return taken

    error_refs, input_refs = take(len(error_wheres)), take(len(input_wheres))
    w_in_ref, w_out_ref, first_ref, second_ref = take(4)
    send_refs = take(shared)
    errors, inputs, inputs_turned, errors_turned, spread_first, spread_second = refs
    if len(input_refs) == 1:
        inputs = input_refs[0]

    @pl.when(pl.program_id(0) == 0)
    def _():
        for block, where in zip(error_refs, error_wheres):
            errors[pl.ds(row_start(place_ref, block, where), block.shape[0]), :] = block[...]
        if len(input_refs) > 1:
            for block, where in zip(input_refs, input_wheres):
                inputs[pl.ds(row_start(place_ref, block, where), block.shape[0]), :] = block[...]
        lane = pl.multiple_of(place_ref[WINDOW if shared else OWN_WINDOW] * 128, 128)
        inputs_turned[...] = inputs[:, pl.ds(lane, window * 128)].T
        errors_turned[...] = errors[:, pl.ds(lane, window * 128)].T

    shift = pl.multiple_of(place_ref[SHIFT if shared else OWN_SHIFT], step_rows)
    v = jnp.dot(inputs[...], w_in_ref[...], preferred_element_type=jnp.float32)
    back = lax.dot_general(
        errors[...], w_out_ref[...], (((1,), (1,)), ((), ())), preferred_element_type=jnp.float32
    )
    square = v * v
    t = jnp.tanh(v * (SCALE + (SCALE * CUBE) * square))
    upper = 0.5 + 0.5 * t
    hidden = (v * upper).astype(jnp.bfloat16)
    spread_second[...] = jnp.dot(errors_turned[...], hidden, preferred_element_type=jnp.float32)
    slope = upper + (0.5 * v) * (1.0 - t * t) * (SCALE + (3.0 * SCALE * CUBE) * square)
    dpre = (back * slope).astype(jnp.bfloat16)
    spread_first[...] = jnp.dot(inputs_turned[...], dpre, preferred_element_type=jnp.float32)
    second_ref[...] = spread_second[pl.ds(shift, own), :]
    first_ref[...] = spread_first[pl.ds(shift, own), :]
    if shared:
        other = pl.ds(pl.multiple_of(place_ref[OTHER_SHIFT], step_rows), own)
        send_refs[0][:own, :] = spread_first[other, :].astype(jnp.bfloat16)
        last = send_refs[-1].shape[0]
        send_refs[-1][last - own :, :] = spread_second[other, :].astype(jnp.bfloat16)


def gradient(place, members, swap, shared, errors, inputs, w_in, w_out, after=()):
    error_arrays, error_wheres = zip(*errors)
    input_arrays, input_wheres = zip(*inputs)
    depth, width = w_in.shape
    rows = sum(a.shape[0] for a in input_arrays)
    own = depth // members
    starts = [m * own % 128 for m in range(members) if not (shared and m & swap)]
    reach = max(starts) + (swap + 1 if shared else 1) * own
    window = -(-reach // 128)
    tile = tile_of(width, 640)
    once = pl.Buffered(1)
    return call(
        functools.partial(
            gradient_kernel, (error_wheres, input_wheres), window, own, math.gcd(own, 128), shared
        ),
        "gradient",
        (place, *error_arrays, *input_arrays, w_in, w_out),
        [
            jax.ShapeDtypeStruct((own, width), jnp.float32),
            jax.ShapeDtypeStruct((own, width), jnp.float32),
        ]
        + [jax.ShapeDtypeStruct((2 * own // max(shared, 1), width), jnp.bfloat16)] * shared,
        after,
        grid=(width // tile,),
        in_specs=[
            pl.BlockSpec(a.shape, whole, pipeline_mode=once)
            for a in (*error_arrays, *input_arrays)
        ]
        + [pl.BlockSpec((depth, tile), column), pl.BlockSpec((tile, depth), lambda n, s: (n, 0))],
        out_specs=[pl.BlockSpec((own, tile), column)] * 2
        + [pl.BlockSpec((2 * own // max(shared, 1), tile), column)] * shared,
        scratch_shapes=[
            pltpu.VMEM((rows, depth), jnp.bfloat16),
            pltpu.VMEM((rows, depth), jnp.bfloat16),
            pltpu.VMEM((window * 128, rows), jnp.bfloat16),
            pltpu.VMEM((window * 128, rows), jnp.bfloat16),
            pltpu.VMEM((window * 128, tile), jnp.float32),
            pltpu.VMEM((window * 128, tile), jnp.float32),
        ],
    )


def products_kernel(labels, fresh, place_ref, *refs):
    own = refs[0].shape[0]
    refs, (known_ref, out_ref, totals) = refs[:-3], refs[-3:]
    each = len(refs) // len(labels)
    slots = [refs[each * n : each * (n + 1)] for n in range(len(labels))]
    pairs = [(i, j) for i in range(len(slots) - fresh, len(slots)) for j in range(i + 1)]

    @pl.when(pl.program_id(0) == 0)
    def _():
        totals[...] = jnp.zeros_like(totals)

    def values(slot):
        return [ref[...].astype(jnp.float32) for ref in slot]

    for n, (i, j) in enumerate(pairs):
        a, b = values(slots[i]), values(slots[j])
        both = sum(u * v for u, v in zip(a, b))
        totals[n] += jnp.sum(both.reshape(own // 8, 8, -1), axis=0)

    @pl.when(pl.program_id(0) == pl.num_programs(0) - 1)
    def _():
        result = known_ref[...]
        row = lax.broadcasted_iota(jnp.int32, result.shape, 0)
        column = lax.broadcasted_iota(jnp.int32, result.shape, 1)
        for n, (i, j) in enumerate(pairs):
            i, j = (jnp.bitwise_xor(place_ref[MEMBER], labels[k]) for k in (i, j))
            here = ((row == i) & (column == j)) | ((row == j) & (column == i))
            result = result + jnp.where(here, jnp.sum(totals[n]), 0.0)
        out_ref[...] = result


def products(place, slots, labels, fresh, known, after=()):
    arrays = [a for slot in slots for a, _ in slot]
    blocks = [k for slot in slots for _, k in slot]
    own, width = arrays[0].shape
    tile = tile_of(width, 256)
    pairs = sum(len(slots) - n for n in range(fresh))
    return call(
        functools.partial(products_kernel, tuple(labels), fresh),
        "products",
        (place, *arrays, known),
        [jax.ShapeDtypeStruct(known.shape, jnp.float32)],
        after,
        grid=(width // tile,),
        in_specs=[pl.BlockSpec((own, tile), lambda n, s, k=k: (k, n)) for k in blocks]
        + [pl.BlockSpec(known.shape, whole)],
        out_specs=[pl.BlockSpec(known.shape, whole)],
        scratch_shapes=[pltpu.VMEM((pairs, 8, tile), jnp.float32)],
    )[0]


def tree_weights(count, entry):
    def inner(a, b):
        total = 0.0
        for i, u in a.items():
            for j, v in b.items():
                total = total + u * v * entry(i, j)
        return total

    items = [{i: 1.0} for i in range(count)]
    while len(items) > 1:
        half = len(items) // 2
        merged = []
        for low, high in zip(items[:half], items[half:]):
            product = inner(low, high)
            scale_low = 1.0 - product / (2.0 * (jnp.maximum(inner(low, low), 0.0) + epsilon))
            scale_high = 1.0 - product / (2.0 * (jnp.maximum(inner(high, high), 0.0) + epsilon))
            joined = {i: u * scale_low for i, u in low.items()}
            joined.update({i: u * scale_high for i, u in high.items()})
            merged.append(joined)
        items = merged
    return [items[0][i] for i in range(count)]


def sum_kernel(place_ref, *refs):
    refs[-1][...] = sum(ref[...] for ref in refs[:-1])


def sum_of(place, parts):
    shape = parts[0].shape
    return call(
        sum_kernel,
        "sum_of",
        (place, *parts),
        [jax.ShapeDtypeStruct(shape, jnp.float32)],
        vmem=4 * 2**20,
        grid=(1,),
        in_specs=[pl.BlockSpec(shape, whole)] * len(parts),
        out_specs=[pl.BlockSpec(shape, whole)],
    )[0]


def merge_kernel(labels, place_ref, totals_ref, *refs):
    refs, (first_ref, second_ref, weights_ref) = refs[:-3], refs[-3:]

    @pl.when(pl.program_id(0) == 0)
    def _():
        def entry(i, j):
            i, j = (jnp.bitwise_xor(place_ref[MEMBER], k) for k in (i, j))
            return totals_ref[i, j]

        for n, weight in enumerate(tree_weights(len(labels), entry)):
            weights_ref[n] = weight

    first = second = 0.0
    for n, label in enumerate(labels):
        weight = weights_ref[label]
        first = first + weight * refs[2 * n][...].astype(jnp.float32)
        second = second + weight * refs[2 * n + 1][...].astype(jnp.float32)
    first_ref[...] = first
    second_ref[...] = second


def merge(place, totals, slots, labels):
    arrays = [a for slot in slots for a, _ in slot]
    own, width = arrays[0].shape
    block = max(b for b in range(16, min(own, 32) + 1, 16) if own % b == 0)
    steps = own // block
    spec = pl.BlockSpec((block, width), lambda n, s: (n, 0))
    specs = [
        pl.BlockSpec((block, width), lambda n, s, k=k: (n + k * steps, 0))
        for slot in slots
        for _, k in slot
    ]
    shape = jax.ShapeDtypeStruct((own, width), jnp.float32)
    return call(
        functools.partial(merge_kernel, tuple(labels)),
        "merge",
        (place, totals, *arrays),
        [shape, shape],
        vmem=16 * 2**20,
        grid=(steps,),
        in_specs=[pl.BlockSpec(memory_space=pltpu.SMEM)] + specs,
        out_specs=[spec, spec],
        scratch_shapes=[pltpu.SMEM((len(slots),), jnp.float32)],
    )


def on_device(inputs, targets, w_in, w_out):
    row_count = inputs.shape[0]
    workers = lax.axis_size("dp")
    shards = lax.axis_size("tensor")
    levels = workers.bit_length() - 1
    shard_levels = shards.bit_length() - 1
    gathered = min(levels, gather_levels_limit)
    members = 2**gathered
    others = workers // members
    position = lax.axis_index("dp")
    shard = lax.axis_index("tensor")
    member = position // others

    def part_of(index):
        part = 0
        for bit in range(shard_levels):
            part = part * 2 + (index >> bit & 1)
        return part

    near = shard & 1
    part_rows = row_count // shards
    columns = inputs.shape[1] // members
    swap = 1
    bits = [2**b for b in reversed(range(gathered)) if 2**b != swap]
    upper = member // swap % 2
    first_row = (member - upper * swap) * columns
    place = jnp.stack(
        [
            first_row // 128,
            first_row % 128 + upper * swap * columns,
            first_row % 128 + (1 - upper) * swap * columns,
            member,
            near,
            1 - near,
            part_of(shard),
            part_of(shard) - near * (shards // 2),
            member * columns // 128,
            member * columns % 128,
        ]
    ).astype(jnp.int32)

    send, hidden_near, own_part = forward(place, part_rows, inputs, w_in, w_out)
    got = from_mask(send, 0, 1)
    inputs_of = {bit: from_mask(own_part, bit * others, 0) for bit in bits}

    summed = product(place, hidden_near, w_out) + got
    most = 24.0 * 0.15625 * 0.078125 * inputs.shape[1] * w_in.shape[1] * shards
    scale = 2.0 ** math.ceil(math.log2(most / 65504.0))
    sums = [summed]
    for bit in range(1, shard_levels):
        rounded = (sum(sums) * (1.0 / scale)).astype(jnp.float16)
        sums.append(from_mask(rounded, 0, 2**bit).astype(jnp.float32) * scale)
    error, error_piece = error_half(
        place,
        part_rows,
        sum(sums[:-1]),
        sums[-1],
        targets,
        tuple(inputs_of.values()),
    )
    high, low = bits
    errors_of = {
        high: from_mask(error_piece, high * others, 0),
        low: from_mask(error, low * others, 0),
    }
    inputs_of[high | swap] = from_mask(ordered(inputs_of[high], error), swap * others, 0)

    def to_half(piece, *before):
        for bit in reversed(range(1, shard_levels)):
            got = ordered(from_mask(piece, 0, 2**bit), *before)
            piece = join(shard >> bit & 1, piece, got)
        return piece

    def both_halves(half):
        return [(half, NEAR), (from_mask(half, 0, 1), FAR)]

    slots, got = {}, {}

    def gradient_of(m, half, other_inputs, *after):
        shared = 2 if m == high | low else 0 if m & high else 1
        first, second, *send = gradient(
            place, members, swap, shared, both_halves(half), other_inputs, w_in, w_out, after
        )
        if m == 0:
            send = [ordered(a, inputs_of[high | swap]) for a in send]
        slots[m] = ((first, 0), (second, 0))
        got[m] = [from_mask(a, swap * others, 0) for a in send]
        if shared:
            slots[m | swap] = ((got[m][0], 0), (got[m][-1], 2 - shared))

    gradient_of(0, error, [(inputs, None)])
    own = slots[0][0][0]
    halves = {}
    for bit in bits:
        halves[bit] = to_half(inputs_of[bit], own, errors_of[high], *halves.values())

    errors_of[low] = ordered(errors_of[low], own)
    half = ordered(errors_of[low], *got[0])
    gradient_of(low, half, both_halves(halves[low]))
    token = slots[low][0][0]

    errors_of[high] = ordered(errors_of[high], own)
    ready = ordered(errors_of[high], errors_of[low])
    errors_of[high | low] = from_mask(ready, low * others, 0)
    errors_of[high | swap] = from_mask(ready, swap * others, 0)
    halves[high | low] = from_mask(ordered(halves[high], half), low * others, 0)
    before = (errors_of[high | low], errors_of[high | swap])
    half = to_half(errors_of[high], token, *before)
    gradient_of(high, half, both_halves(halves[high]))
    token = slots[high][0][0]

    totals = jnp.zeros((8, 128), jnp.float32)
    labels = [0, swap, low, high]
    totals = products(place, [slots[m] for m in labels], labels, 4, totals)

    half = to_half(errors_of[high | low], token)
    partner_half = to_half(errors_of[high | swap], token)
    ready = ordered(halves[high | low], token, *got[low], partner_half)
    gradient_of(high | low, half, both_halves(ready), totals)
    token = slots[high | low][0][0]

    half = ordered(partner_half, token)
    halves[high | swap] = to_half(inputs_of[high | swap], token)
    gradient_of(high | swap, half, both_halves(halves[high | swap]))
    labels += [low | swap, high | low, high | swap]
    totals = products(place, [slots[m] for m in labels], labels, 3, totals)
    labels.append(high | low | swap)
    for k in range(2):
        totals = products(place, [slots[m][k : k + 1] for m in labels], labels, 1, totals)
    slots = [slots[m] for m in labels]

    rounds = [[(0, mask) for mask in range(1, shards)]]
    rounds.append([(m * others, 0) for m in range(2, members, 2)])
    rounds.append([(others, 0)])
    for partners in rounds:
        totals = sum_of(place, [totals] + [from_mask(totals, *mask) for mask in partners])
    pieces = merge(place, totals, slots, labels)

    for section in range(gathered, levels):
        upper_flag = position >> levels - 1 - section & 1
        keep_first, send_first = split_piece(pieces[0], upper_flag)
        keep_second, send_second = split_piece(pieces[1], upper_flag)
        got_first, got_second = from_partner((send_first, send_second), "dp", levels - 1 - section)
        pieces = combine(
            (keep_first, keep_second), (got_first, got_second), upper_flag, section, levels
        )
    return (pieces[0], pieces[1])


def solution(mesh):
    placed = (P("dp", None), P("dp", None), P(None, "tensor"), P("tensor", None))
    return jax.shard_map(
        on_device,
        mesh=mesh,
        in_specs=placed,
        out_specs=(P("dp", "tensor"), P("dp", "tensor")),
        check_vma=False,
    )
```

```python
import functools
import math

import jax
import jax.numpy as jnp
from jax import lax
from jax.experimental import pallas as pl
from jax.experimental.pallas import tpu as pltpu
from jax.sharding import PartitionSpec as P

epsilon = 1e-06
gather_levels_limit = 3
vmem_bytes = 36 * 2**20
vmem_most = 60 * 2**20


def from_partner(value, axis, distance):
    mask = 2**distance
    pairs = [(source, source ^ mask) for source in range(lax.axis_size(axis))]
    return lax.ppermute(value, axis, pairs)


def from_mask(value, dp_mask, tensor_mask):
    shards = lax.axis_size("tensor")
    mask = dp_mask * shards + tensor_mask
    pairs = [(source, source ^ mask) for source in range(lax.axis_size("dp") * shards)]
    return lax.ppermute(value, ("dp", "tensor"), pairs)


def ordered(value, *before):
    return lax.optimization_barrier((value, *before))[0]


def split_piece(piece, upper_flag):
    half = piece.shape[0] // 2
    keep = lax.dynamic_slice_in_dim(piece, upper_flag * half, half, 0)
    send = lax.dynamic_slice_in_dim(piece, (1 - upper_flag) * half, half, 0)
    return (keep, send)


def group_total(values, section, levels):
    summed = lax.psum(values, "tensor")
    for offset in range(section + 1):
        summed = summed + from_partner(summed, "dp", levels - 1 - offset)
    return summed


def combine(own, incoming, upper_flag, section, levels):
    product = jnp.sum(own[0] * incoming[0]) + jnp.sum(own[1] * incoming[1])
    norm_own = jnp.sum(own[0] * own[0]) + jnp.sum(own[1] * own[1])
    norm_incoming = jnp.sum(incoming[0] * incoming[0]) + jnp.sum(incoming[1] * incoming[1])
    is_upper = upper_flag == 1
    norm_low = jnp.where(is_upper, norm_incoming, norm_own)
    norm_high = jnp.where(is_upper, norm_own, norm_incoming)
    totals = group_total(jnp.stack([product, norm_low, norm_high]), section, levels)
    coef_low = 1.0 - totals[0] / (2.0 * (totals[1] + epsilon))
    coef_high = 1.0 - totals[0] / (2.0 * (totals[2] + epsilon))
    coef_own = jnp.where(is_upper, coef_high, coef_low)
    coef_incoming = jnp.where(is_upper, coef_low, coef_high)
    return (
        coef_own * own[0] + coef_incoming * incoming[0],
        coef_own * own[1] + coef_incoming * incoming[1],
    )


def tile_of(size, limit):
    return max(b for b in range(128, limit + 1, 128) if size % b == 0)


def contract(left, right, left_dim, right_dim):
    dims = (((left_dim,), (right_dim,)), ((), ()))
    return lax.dot_general(left, right, dims, preferred_element_type=jnp.float32)


def call(kernel, name, operands, shapes, after=(), vmem=vmem_bytes, **spec):
    spec["in_specs"] = [pl.BlockSpec(memory_space=pl.ANY)] * len(after) + spec["in_specs"]

    def body(place_ref, *refs):
        kernel(place_ref, *refs[len(after) :])

    return pl.pallas_call(
        body,
        grid_spec=pltpu.PrefetchScalarGridSpec(num_scalar_prefetch=1, **spec),
        out_shape=shapes,
        compiler_params=pltpu.CompilerParams(vmem_limit_bytes=vmem),
        cost_estimate=pl.CostEstimate(flops=1, bytes_accessed=1, transcendentals=0),
        name=name,
    )(operands[0], *after, *operands[1:])


WINDOW, SHIFT, OTHER_SHIFT, MEMBER, NEAR, FAR, PART, PIECE, OWN_WINDOW, OWN_SHIFT = range(10)


def row_start(place_ref, block, where):
    return 0 if where is None else pl.multiple_of(place_ref[where] * block.shape[0], 16)


def whole(n, s):
    return (0, 0)


def column(n, s):
    return (0, n)


SCALE = math.sqrt(2.0 / math.pi)
CUBE = 0.044715


def forward_kernel(
    steps, place_ref, rows_ref, w_in_ref, w_out_ref, out_ref, near_ref, part_ref, hidden
):
    step = pl.program_id(0)
    half = out_ref.shape[0]
    far = pl.ds(row_start(place_ref, out_ref, FAR), half)
    tile = w_in_ref.shape[1]

    for n in range(steps):

        @pl.when(step == n)
        def _():
            v = jnp.dot(rows_ref[...], w_in_ref[...], preferred_element_type=jnp.float32)
            t = jnp.tanh(v * (SCALE + (SCALE * CUBE) * (v * v)))
            hidden[:, n * tile : (n + 1) * tile] = (v * (0.5 + 0.5 * t)).astype(jnp.bfloat16)

    @pl.when(step == 0)
    def _():
        part_ref[...] = rows_ref[pl.ds(row_start(place_ref, part_ref, PART), part_ref.shape[0]), :]

    @pl.when(step == steps)
    def _():
        near_ref[...] = hidden[pl.ds(row_start(place_ref, out_ref, NEAR), half), :]

    @pl.when(step >= steps)
    def _():
        out_ref[...] = jnp.dot(hidden[far, :], w_out_ref[...], preferred_element_type=jnp.float32)


def forward(place, part_rows, inputs, w_in, w_out):
    rows = inputs.shape[0]
    depth, width = w_in.shape
    tile, out_tile = tile_of(width, 640), tile_of(depth, 640)
    steps = width // tile
    last = lambda n: jnp.maximum(n - steps, 0)
    return call(
        functools.partial(forward_kernel, steps),
        "forward",
        (place, inputs, w_in, w_out),
        [
            jax.ShapeDtypeStruct((rows // 2, depth), jnp.float32),
            jax.ShapeDtypeStruct((rows // 2, width), jnp.bfloat16),
            jax.ShapeDtypeStruct((part_rows, depth), jnp.bfloat16),
        ],
        vmem=vmem_most,
        grid=(steps + depth // out_tile,),
        in_specs=[
            pl.BlockSpec((rows, depth), whole),
            pl.BlockSpec((depth, tile), lambda n, s: (0, jnp.minimum(n, steps - 1))),
            pl.BlockSpec((width, out_tile), lambda n, s: (0, last(n))),
        ],
        out_specs=[
            pl.BlockSpec((rows // 2, out_tile), lambda n, s: (0, last(n))),
            pl.BlockSpec((rows // 2, width), whole),
            pl.BlockSpec((part_rows, depth), whole),
        ],
        scratch_shapes=[pltpu.VMEM((rows, width), jnp.bfloat16)],
    )


def product_kernel(place_ref, left_ref, right_ref, out_ref):
    out_ref[...] = jnp.dot(left_ref[...], right_ref[...], preferred_element_type=jnp.float32)


def product(place, left, right):
    rows, depth = left.shape
    width = right.shape[1]
    tile = tile_of(width, 640)
    return call(
        product_kernel,
        "product",
        (place, left, right),
        [jax.ShapeDtypeStruct((rows, width), jnp.float32)],
        grid=(width // tile,),
        in_specs=[pl.BlockSpec((rows, depth), whole), pl.BlockSpec((depth, tile), column)],
        out_specs=[pl.BlockSpec((rows, tile), column)],
    )[0]


def join_kernel(place_ref, own_ref, got_ref, out_ref):
    rows = own_ref.shape[0]
    out_ref[pl.ds(pl.multiple_of(place_ref[0] * rows, 16), rows), :] = own_ref[...]
    out_ref[pl.ds(pl.multiple_of((1 - place_ref[0]) * rows, 16), rows), :] = got_ref[...]


def join(flag, own, got):
    rows, depth = own.shape
    return call(
        join_kernel,
        "join",
        (flag.reshape(1), own, got),
        [jax.ShapeDtypeStruct((2 * rows, depth), own.dtype)],
        grid=(1,),
        in_specs=[pl.BlockSpec((rows, depth), whole)] * 2,
        out_specs=[pl.BlockSpec((2 * rows, depth), whole)],
    )[0]


def error_kernel(row_count, place_ref, own_ref, got_ref, targets_ref, half_ref, part_ref):
    out = own_ref[...] + got_ref[...]
    error = (out - targets_ref[...].astype(jnp.float32)) / row_count
    half_ref[...] = error.astype(jnp.bfloat16)
    rows = part_ref.shape[0]
    part_ref[...] = half_ref[pl.ds(pl.multiple_of(place_ref[PIECE] * rows, 16), rows), :]


def error_half(place, part_rows, own, got, targets, after):
    rows, depth = own.shape
    return call(
        functools.partial(error_kernel, targets.shape[0]),
        "error_half",
        (place, own, got, targets),
        [
            jax.ShapeDtypeStruct((rows, depth), jnp.bfloat16),
            jax.ShapeDtypeStruct((part_rows, depth), jnp.bfloat16),
        ],
        after,
        grid=(1,),
        in_specs=[
            pl.BlockSpec((rows, depth), whole),
            pl.BlockSpec((rows, depth), whole),
            pl.BlockSpec((rows, depth), lambda n, s: (s[NEAR], 0)),
        ],
        out_specs=[pl.BlockSpec((rows, depth), whole), pl.BlockSpec((part_rows, depth), whole)],
    )


def gradient_kernel(wheres, window, own, step_rows, shared, place_ref, *refs):
    error_wheres, input_wheres = wheres
    refs = list(refs)

    def take(n):
        taken = refs[:n]
        del refs[:n]
        return taken

    error_refs, input_refs = take(len(error_wheres)), take(len(input_wheres))
    w_in_ref, w_out_ref, first_ref, second_ref = take(4)
    send_refs = take(shared)
    errors, inputs, inputs_turned, errors_turned, spread_first, spread_second = refs
    if len(input_refs) == 1:
        inputs = input_refs[0]

    @pl.when(pl.program_id(0) == 0)
    def _():
        for block, where in zip(error_refs, error_wheres):
            errors[pl.ds(row_start(place_ref, block, where), block.shape[0]), :] = block[...]
        if len(input_refs) > 1:
            for block, where in zip(input_refs, input_wheres):
                inputs[pl.ds(row_start(place_ref, block, where), block.shape[0]), :] = block[...]
        lane = pl.multiple_of(place_ref[WINDOW if shared else OWN_WINDOW] * 128, 128)
        inputs_turned[...] = inputs[:, pl.ds(lane, window * 128)].T
        errors_turned[...] = errors[:, pl.ds(lane, window * 128)].T

    shift = pl.multiple_of(place_ref[SHIFT if shared else OWN_SHIFT], step_rows)
    v = jnp.dot(inputs[...], w_in_ref[...], preferred_element_type=jnp.float32)
    back = lax.dot_general(
        errors[...], w_out_ref[...], (((1,), (1,)), ((), ())), preferred_element_type=jnp.float32
    )
    square = v * v
    t = jnp.tanh(v * (SCALE + (SCALE * CUBE) * square))
    upper = 0.5 + 0.5 * t
    hidden = (v * upper).astype(jnp.bfloat16)
    spread_second[...] = jnp.dot(errors_turned[...], hidden, preferred_element_type=jnp.float32)
    slope = upper + (0.5 * v) * (1.0 - t * t) * (SCALE + (3.0 * SCALE * CUBE) * square)
    dpre = (back * slope).astype(jnp.bfloat16)
    spread_first[...] = jnp.dot(inputs_turned[...], dpre, preferred_element_type=jnp.float32)
    second_ref[...] = spread_second[pl.ds(shift, own), :]
    first_ref[...] = spread_first[pl.ds(shift, own), :]
    if shared:
        other = pl.ds(pl.multiple_of(place_ref[OTHER_SHIFT], step_rows), own)
        send_refs[0][:own, :] = spread_first[other, :].astype(jnp.bfloat16)
        last = send_refs[-1].shape[0]
        send_refs[-1][last - own :, :] = spread_second[other, :].astype(jnp.bfloat16)


def gradient(place, members, swap, shared, errors, inputs, w_in, w_out, after=()):
    error_arrays, error_wheres = zip(*errors)
    input_arrays, input_wheres = zip(*inputs)
    depth, width = w_in.shape
    rows = sum(a.shape[0] for a in input_arrays)
    own = depth // members
    starts = [m * own % 128 for m in range(members) if not (shared and m & swap)]
    reach = max(starts) + (swap + 1 if shared else 1) * own
    window = -(-reach // 128)
    tile = tile_of(width, 640)
    once = pl.Buffered(1)
    return call(
        functools.partial(
            gradient_kernel, (error_wheres, input_wheres), window, own, math.gcd(own, 128), shared
        ),
        "gradient",
        (place, *error_arrays, *input_arrays, w_in, w_out),
        [
            jax.ShapeDtypeStruct((own, width), jnp.float32),
            jax.ShapeDtypeStruct((own, width), jnp.float32),
        ]
        + [jax.ShapeDtypeStruct((2 * own // max(shared, 1), width), jnp.bfloat16)] * shared,
        after,
        grid=(width // tile,),
        in_specs=[
            pl.BlockSpec(a.shape, whole, pipeline_mode=once)
            for a in (*error_arrays, *input_arrays)
        ]
        + [pl.BlockSpec((depth, tile), column), pl.BlockSpec((tile, depth), lambda n, s: (n, 0))],
        out_specs=[pl.BlockSpec((own, tile), column)] * 2
        + [pl.BlockSpec((2 * own // max(shared, 1), tile), column)] * shared,
        scratch_shapes=[
            pltpu.VMEM((rows, depth), jnp.bfloat16),
            pltpu.VMEM((rows, depth), jnp.bfloat16),
            pltpu.VMEM((window * 128, rows), jnp.bfloat16),
            pltpu.VMEM((window * 128, rows), jnp.bfloat16),
            pltpu.VMEM((window * 128, tile), jnp.float32),
            pltpu.VMEM((window * 128, tile), jnp.float32),
        ],
    )


def products_kernel(labels, fresh, place_ref, *refs):
    own = refs[0].shape[0]
    refs, (known_ref, out_ref, totals) = refs[:-3], refs[-3:]
    each = len(refs) // len(labels)
    slots = [refs[each * n : each * (n + 1)] for n in range(len(labels))]
    pairs = [(i, j) for i in range(len(slots) - fresh, len(slots)) for j in range(i + 1)]

    @pl.when(pl.program_id(0) == 0)
    def _():
        totals[...] = jnp.zeros_like(totals)

    def values(slot):
        return [ref[...].astype(jnp.float32) for ref in slot]

    for n, (i, j) in enumerate(pairs):
        a, b = values(slots[i]), values(slots[j])
        both = sum(u * v for u, v in zip(a, b))
        totals[n] += jnp.sum(both.reshape(own // 8, 8, -1), axis=0)

    @pl.when(pl.program_id(0) == pl.num_programs(0) - 1)
    def _():
        result = known_ref[...]
        row = lax.broadcasted_iota(jnp.int32, result.shape, 0)
        column = lax.broadcasted_iota(jnp.int32, result.shape, 1)
        for n, (i, j) in enumerate(pairs):
            i, j = (jnp.bitwise_xor(place_ref[MEMBER], labels[k]) for k in (i, j))
            here = ((row == i) & (column == j)) | ((row == j) & (column == i))
            result = result + jnp.where(here, jnp.sum(totals[n]), 0.0)
        out_ref[...] = result


def products(place, slots, labels, fresh, known, after=()):
    arrays = [a for slot in slots for a, _ in slot]
    blocks = [k for slot in slots for _, k in slot]
    own, width = arrays[0].shape
    tile = tile_of(width, 256)
    pairs = sum(len(slots) - n for n in range(fresh))
    return call(
        functools.partial(products_kernel, tuple(labels), fresh),
        "products",
        (place, *arrays, known),
        [jax.ShapeDtypeStruct(known.shape, jnp.float32)],
        after,
        grid=(width // tile,),
        in_specs=[pl.BlockSpec((own, tile), lambda n, s, k=k: (k, n)) for k in blocks]
        + [pl.BlockSpec(known.shape, whole)],
        out_specs=[pl.BlockSpec(known.shape, whole)],
        scratch_shapes=[pltpu.VMEM((pairs, 8, tile), jnp.float32)],
    )[0]


def tree_weights(count, entry):
    def inner(a, b):
        total = 0.0
        for i, u in a.items():
            for j, v in b.items():
                total = total + u * v * entry(i, j)
        return total

    items = [{i: 1.0} for i in range(count)]
    while len(items) > 1:
        half = len(items) // 2
        merged = []
        for low, high in zip(items[:half], items[half:]):
            product = inner(low, high)
            scale_low = 1.0 - product / (2.0 * (jnp.maximum(inner(low, low), 0.0) + epsilon))
            scale_high = 1.0 - product / (2.0 * (jnp.maximum(inner(high, high), 0.0) + epsilon))
            joined = {i: u * scale_low for i, u in low.items()}
            joined.update({i: u * scale_high for i, u in high.items()})
            merged.append(joined)
        items = merged
    return [items[0][i] for i in range(count)]


def sum_kernel(place_ref, *refs):
    refs[-1][...] = sum(ref[...] for ref in refs[:-1])


def sum_of(place, parts):
    shape = parts[0].shape
    return call(
        sum_kernel,
        "sum_of",
        (place, *parts),
        [jax.ShapeDtypeStruct(shape, jnp.float32)],
        vmem=4 * 2**20,
        grid=(1,),
        in_specs=[pl.BlockSpec(shape, whole)] * len(parts),
        out_specs=[pl.BlockSpec(shape, whole)],
    )[0]


def merge_kernel(labels, place_ref, totals_ref, *refs):
    refs, (first_ref, second_ref, weights_ref) = refs[:-3], refs[-3:]

    @pl.when(pl.program_id(0) == 0)
    def _():
        def entry(i, j):
            i, j = (jnp.bitwise_xor(place_ref[MEMBER], k) for k in (i, j))
            return totals_ref[i, j]

        for n, weight in enumerate(tree_weights(len(labels), entry)):
            weights_ref[n] = weight

    first = second = 0.0
    for n, label in enumerate(labels):
        weight = weights_ref[label]
        first = first + weight * refs[2 * n][...].astype(jnp.float32)
        second = second + weight * refs[2 * n + 1][...].astype(jnp.float32)
    first_ref[...] = first
    second_ref[...] = second


def merge(place, totals, slots, labels):
    arrays = [a for slot in slots for a, _ in slot]
    own, width = arrays[0].shape
    block = max(b for b in range(16, min(own, 32) + 1, 16) if own % b == 0)
    steps = own // block
    spec = pl.BlockSpec((block, width), lambda n, s: (n, 0))
    specs = [
        pl.BlockSpec((block, width), lambda n, s, k=k: (n + k * steps, 0))
        for slot in slots
        for _, k in slot
    ]
    shape = jax.ShapeDtypeStruct((own, width), jnp.float32)
    return call(
        functools.partial(merge_kernel, tuple(labels)),
        "merge",
        (place, totals, *arrays),
        [shape, shape],
        vmem=16 * 2**20,
        grid=(steps,),
        in_specs=[pl.BlockSpec(memory_space=pltpu.SMEM)] + specs,
        out_specs=[spec, spec],
        scratch_shapes=[pltpu.SMEM((len(slots),), jnp.float32)],
    )


def on_device(inputs, targets, w_in, w_out):
    row_count = inputs.shape[0]
    workers = lax.axis_size("dp")
    shards = lax.axis_size("tensor")
    levels = workers.bit_length() - 1
    shard_levels = shards.bit_length() - 1
    gathered = min(levels, gather_levels_limit)
    members = 2**gathered
    others = workers // members
    position = lax.axis_index("dp")
    shard = lax.axis_index("tensor")
    member = position // others

    def part_of(index):
        part = 0
        for bit in range(shard_levels):
            part = part * 2 + (index >> bit & 1)
        return part

    near = shard & 1
    part_rows = row_count // shards
    columns = inputs.shape[1] // members
    swap = 1
    bits = [2**b for b in reversed(range(gathered)) if 2**b != swap]
    upper = member // swap % 2
    first_row = (member - upper * swap) * columns
    place = jnp.stack(
        [
            first_row // 128,
            first_row % 128 + upper * swap * columns,
            first_row % 128 + (1 - upper) * swap * columns,
            member,
            near,
            1 - near,
            part_of(shard),
            part_of(shard) - near * (shards // 2),
            member * columns // 128,
            member * columns % 128,
        ]
    ).astype(jnp.int32)

    send, hidden_near, own_part = forward(place, part_rows, inputs, w_in, w_out)
    got = from_mask(send, 0, 1)
    inputs_of = {bit: from_mask(own_part, bit * others, 0) for bit in bits}

    summed = product(place, hidden_near, w_out) + got
    most = 24.0 * 0.15625 * 0.078125 * inputs.shape[1] * w_in.shape[1] * shards
    scale = 2.0 ** math.ceil(math.log2(most / 65504.0))
    sums = [summed]
    for bit in range(1, shard_levels):
        rounded = (sum(sums) * (1.0 / scale)).astype(jnp.float16)
        sums.append(from_mask(rounded, 0, 2**bit).astype(jnp.float32) * scale)
    error, error_piece = error_half(
        place,
        part_rows,
        sum(sums[:-1]),
        sums[-1],
        targets,
        tuple(inputs_of.values()),
    )
    high, low = bits
    errors_of = {
        high: from_mask(error_piece, high * others, 0),
        low: from_mask(error, low * others, 0),
    }
    inputs_of[high | swap] = from_mask(ordered(inputs_of[high], error), swap * others, 0)

    def to_half(piece, *before):
        for bit in reversed(range(1, shard_levels)):
            got = ordered(from_mask(piece, 0, 2**bit), *before)
            piece = join(shard >> bit & 1, piece, got)
        return piece

    def both_halves(half):
        return [(half, NEAR), (from_mask(half, 0, 1), FAR)]

    slots, got = {}, {}

    def gradient_of(m, half, other_inputs, *after):
        shared = 2 if m == high | low else 0 if m & high else 1
        first, second, *send = gradient(
            place, members, swap, shared, both_halves(half), other_inputs, w_in, w_out, after
        )
        if m == 0:
            send = [ordered(a, inputs_of[high | swap]) for a in send]
        slots[m] = ((first, 0), (second, 0))
        got[m] = [from_mask(a, swap * others, 0) for a in send]
        if shared:
            slots[m | swap] = ((got[m][0], 0), (got[m][-1], 2 - shared))

    gradient_of(0, error, [(inputs, None)])
    own = slots[0][0][0]
    halves = {}
    for bit in bits:
        halves[bit] = to_half(inputs_of[bit], own, errors_of[high], *halves.values())

    errors_of[low] = ordered(errors_of[low], own)
    half = ordered(errors_of[low], *got[0])
    gradient_of(low, half, both_halves(halves[low]))
    token = slots[low][0][0]

    ready = errors_of[high] = ordered(errors_of[high], errors_of[low])
    errors_of[high | low] = from_mask(ready, low * others, 0)
    errors_of[high | swap] = from_mask(ready, swap * others, 0)
    halves[high | low] = from_mask(ordered(halves[high], errors_of[low]), low * others, 0)
    partner_half = to_half(ready)
    halves[high | swap] = to_half(ordered(inputs_of[high | swap], errors_of[low]))
    half = ordered(
        errors_of[high | low], token, errors_of[high | swap], partner_half, halves[high | swap]
    )
    half = to_half(half, *got[low])
    totals = jnp.zeros((8, 128), jnp.float32)
    labels = [0, swap, low]
    totals = products(place, [slots[m] for m in labels], labels, 3, totals)
    gradient_of(
        high | low, half, both_halves(ordered(halves[high | low], token)), totals
    )
    token = slots[high | low][0][0]

    half = ordered(partner_half, token)
    gradient_of(high, half, both_halves(halves[high]))
    token = slots[high][0][0]

    half = to_half(errors_of[high | swap], slots[high | low][0][0])
    gradient_of(high | swap, half, both_halves(halves[high | swap]), token)
    labels += [low | swap, high | low, high, high | swap]
    totals = products(place, [slots[m] for m in labels], labels, 4, totals)
    labels.append(high | low | swap)
    for k in range(2):
        totals = products(place, [slots[m][k : k + 1] for m in labels], labels, 1, totals)
    slots = [slots[m] for m in labels]

    rounds = [[(0, mask) for mask in range(1, shards)]]
    rounds.append([(m * others, 0) for m in range(2, members, 2)])
    rounds.append([(others, 0)])
    for partners in rounds:
        totals = sum_of(place, [totals] + [from_mask(totals, *mask) for mask in partners])
    pieces = merge(place, totals, slots, labels)

    for section in range(gathered, levels):
        upper_flag = position >> levels - 1 - section & 1
        keep_first, send_first = split_piece(pieces[0], upper_flag)
        keep_second, send_second = split_piece(pieces[1], upper_flag)
        got_first, got_second = from_partner((send_first, send_second), "dp", levels - 1 - section)
        pieces = combine(
            (keep_first, keep_second), (got_first, got_second), upper_flag, section, levels
        )
    return (pieces[0], pieces[1])


def solution(mesh):
    placed = (P("dp", None), P("dp", None), P(None, "tensor"), P("tensor", None))
    return jax.shard_map(
        on_device,
        mesh=mesh,
        in_specs=placed,
        out_specs=(P("dp", "tensor"), P("dp", "tensor")),
        check_vma=False,
    )
```

```python
import functools
import math

import jax
import jax.numpy as jnp
from jax import lax
from jax.experimental import pallas as pl
from jax.experimental.pallas import tpu as pltpu
from jax.sharding import PartitionSpec as P

epsilon = 1e-06
gather_levels_limit = 3
vmem_bytes = 36 * 2**20
vmem_most = 60 * 2**20


def from_partner(value, axis, distance):
    mask = 2**distance
    pairs = [(source, source ^ mask) for source in range(lax.axis_size(axis))]
    return lax.ppermute(value, axis, pairs)


def from_mask(value, dp_mask, tensor_mask):
    shards = lax.axis_size("tensor")
    mask = dp_mask * shards + tensor_mask
    pairs = [(source, source ^ mask) for source in range(lax.axis_size("dp") * shards)]
    return lax.ppermute(value, ("dp", "tensor"), pairs)


def ordered(value, *before):
    return lax.optimization_barrier((value, *before))[0]


def split_piece(piece, upper_flag):
    half = piece.shape[0] // 2
    keep = lax.dynamic_slice_in_dim(piece, upper_flag * half, half, 0)
    send = lax.dynamic_slice_in_dim(piece, (1 - upper_flag) * half, half, 0)
    return (keep, send)


def group_total(values, section, levels):
    summed = lax.psum(values, "tensor")
    for offset in range(section + 1):
        summed = summed + from_partner(summed, "dp", levels - 1 - offset)
    return summed


def combine(own, incoming, upper_flag, section, levels):
    product = jnp.sum(own[0] * incoming[0]) + jnp.sum(own[1] * incoming[1])
    norm_own = jnp.sum(own[0] * own[0]) + jnp.sum(own[1] * own[1])
    norm_incoming = jnp.sum(incoming[0] * incoming[0]) + jnp.sum(incoming[1] * incoming[1])
    is_upper = upper_flag == 1
    norm_low = jnp.where(is_upper, norm_incoming, norm_own)
    norm_high = jnp.where(is_upper, norm_own, norm_incoming)
    totals = group_total(jnp.stack([product, norm_low, norm_high]), section, levels)
    coef_low = 1.0 - totals[0] / (2.0 * (totals[1] + epsilon))
    coef_high = 1.0 - totals[0] / (2.0 * (totals[2] + epsilon))
    coef_own = jnp.where(is_upper, coef_high, coef_low)
    coef_incoming = jnp.where(is_upper, coef_low, coef_high)
    return (
        coef_own * own[0] + coef_incoming * incoming[0],
        coef_own * own[1] + coef_incoming * incoming[1],
    )


def tile_of(size, limit):
    return max(b for b in range(128, limit + 1, 128) if size % b == 0)


def contract(left, right, left_dim, right_dim):
    dims = (((left_dim,), (right_dim,)), ((), ()))
    return lax.dot_general(left, right, dims, preferred_element_type=jnp.float32)


def call(kernel, name, operands, shapes, after=(), vmem=vmem_bytes, **spec):
    spec["in_specs"] = [pl.BlockSpec(memory_space=pl.ANY)] * len(after) + spec["in_specs"]

    def body(place_ref, *refs):
        kernel(place_ref, *refs[len(after) :])

    return pl.pallas_call(
        body,
        grid_spec=pltpu.PrefetchScalarGridSpec(num_scalar_prefetch=1, **spec),
        out_shape=shapes,
        compiler_params=pltpu.CompilerParams(vmem_limit_bytes=vmem),
        cost_estimate=pl.CostEstimate(flops=1, bytes_accessed=1, transcendentals=0),
        name=name,
    )(operands[0], *after, *operands[1:])


WINDOW, SHIFT, OTHER_SHIFT, MEMBER, NEAR, FAR, PART, PIECE, OWN_WINDOW, OWN_SHIFT = range(10)


def row_start(place_ref, block, where):
    return 0 if where is None else pl.multiple_of(place_ref[where] * block.shape[0], 16)


def whole(n, s):
    return (0, 0)


def column(n, s):
    return (0, n)


SCALE = math.sqrt(2.0 / math.pi)
CUBE = 0.044715


def forward_kernel(
    steps, place_ref, rows_ref, w_in_ref, w_out_ref, out_ref, near_ref, part_ref, hidden
):
    step = pl.program_id(0)
    half = out_ref.shape[0]
    far = pl.ds(row_start(place_ref, out_ref, FAR), half)
    tile = w_in_ref.shape[1]

    for n in range(steps):

        @pl.when(step == n)
        def _():
            v = jnp.dot(rows_ref[...], w_in_ref[...], preferred_element_type=jnp.float32)
            t = jnp.tanh(v * (SCALE + (SCALE * CUBE) * (v * v)))
            hidden[:, n * tile : (n + 1) * tile] = (v * (0.5 + 0.5 * t)).astype(jnp.bfloat16)

    @pl.when(step == 0)
    def _():
        part_ref[...] = rows_ref[pl.ds(row_start(place_ref, part_ref, PART), part_ref.shape[0]), :]

    @pl.when(step == steps)
    def _():
        near_ref[...] = hidden[pl.ds(row_start(place_ref, out_ref, NEAR), half), :]

    @pl.when(step >= steps)
    def _():
        out_ref[...] = jnp.dot(hidden[far, :], w_out_ref[...], preferred_element_type=jnp.float32)


def forward(place, part_rows, inputs, w_in, w_out):
    rows = inputs.shape[0]
    depth, width = w_in.shape
    tile, out_tile = tile_of(width, 640), tile_of(depth, 640)
    steps = width // tile
    last = lambda n: jnp.maximum(n - steps, 0)
    return call(
        functools.partial(forward_kernel, steps),
        "forward",
        (place, inputs, w_in, w_out),
        [
            jax.ShapeDtypeStruct((rows // 2, depth), jnp.float32),
            jax.ShapeDtypeStruct((rows // 2, width), jnp.bfloat16),
            jax.ShapeDtypeStruct((part_rows, depth), jnp.bfloat16),
        ],
        vmem=vmem_most,
        grid=(steps + depth // out_tile,),
        in_specs=[
            pl.BlockSpec((rows, depth), whole),
            pl.BlockSpec((depth, tile), lambda n, s: (0, jnp.minimum(n, steps - 1))),
            pl.BlockSpec((width, out_tile), lambda n, s: (0, last(n))),
        ],
        out_specs=[
            pl.BlockSpec((rows // 2, out_tile), lambda n, s: (0, last(n))),
            pl.BlockSpec((rows // 2, width), whole),
            pl.BlockSpec((part_rows, depth), whole),
        ],
        scratch_shapes=[pltpu.VMEM((rows, width), jnp.bfloat16)],
    )


def product_kernel(place_ref, left_ref, right_ref, out_ref):
    out_ref[...] = jnp.dot(left_ref[...], right_ref[...], preferred_element_type=jnp.float32)


def product(place, left, right):
    rows, depth = left.shape
    width = right.shape[1]
    tile = tile_of(width, 640)
    return call(
        product_kernel,
        "product",
        (place, left, right),
        [jax.ShapeDtypeStruct((rows, width), jnp.float32)],
        grid=(width // tile,),
        in_specs=[pl.BlockSpec((rows, depth), whole), pl.BlockSpec((depth, tile), column)],
        out_specs=[pl.BlockSpec((rows, tile), column)],
    )[0]


def join_kernel(place_ref, own_ref, got_ref, out_ref):
    rows = own_ref.shape[0]
    out_ref[pl.ds(pl.multiple_of(place_ref[0] * rows, 16), rows), :] = own_ref[...]
    out_ref[pl.ds(pl.multiple_of((1 - place_ref[0]) * rows, 16), rows), :] = got_ref[...]


def join(flag, own, got):
    rows, depth = own.shape
    return call(
        join_kernel,
        "join",
        (flag.reshape(1), own, got),
        [jax.ShapeDtypeStruct((2 * rows, depth), own.dtype)],
        grid=(1,),
        in_specs=[pl.BlockSpec((rows, depth), whole)] * 2,
        out_specs=[pl.BlockSpec((2 * rows, depth), whole)],
    )[0]


def error_kernel(row_count, place_ref, own_ref, got_ref, targets_ref, half_ref, part_ref):
    out = own_ref[...] + got_ref[...]
    error = (out - targets_ref[...].astype(jnp.float32)) / row_count
    half_ref[...] = error.astype(jnp.bfloat16)
    rows = part_ref.shape[0]
    part_ref[...] = half_ref[pl.ds(pl.multiple_of(place_ref[PIECE] * rows, 16), rows), :]


def error_half(place, part_rows, own, got, targets, after):
    rows, depth = own.shape
    return call(
        functools.partial(error_kernel, targets.shape[0]),
        "error_half",
        (place, own, got, targets),
        [
            jax.ShapeDtypeStruct((rows, depth), jnp.bfloat16),
            jax.ShapeDtypeStruct((part_rows, depth), jnp.bfloat16),
        ],
        after,
        grid=(1,),
        in_specs=[
            pl.BlockSpec((rows, depth), whole),
            pl.BlockSpec((rows, depth), whole),
            pl.BlockSpec((rows, depth), lambda n, s: (s[NEAR], 0)),
        ],
        out_specs=[pl.BlockSpec((rows, depth), whole), pl.BlockSpec((part_rows, depth), whole)],
    )


def gradient_kernel(wheres, window, own, step_rows, shared, place_ref, *refs):
    error_wheres, input_wheres = wheres
    refs = list(refs)

    def take(n):
        taken = refs[:n]
        del refs[:n]
        return taken

    error_refs, input_refs = take(len(error_wheres)), take(len(input_wheres))
    w_in_ref, w_out_ref, first_ref, second_ref = take(4)
    send_refs = take(shared)
    errors, inputs, inputs_turned, errors_turned, spread_first, spread_second = refs
    if len(input_refs) == 1:
        inputs = input_refs[0]

    @pl.when(pl.program_id(0) == 0)
    def _():
        for block, where in zip(error_refs, error_wheres):
            errors[pl.ds(row_start(place_ref, block, where), block.shape[0]), :] = block[...]
        if len(input_refs) > 1:
            for block, where in zip(input_refs, input_wheres):
                inputs[pl.ds(row_start(place_ref, block, where), block.shape[0]), :] = block[...]
        lane = pl.multiple_of(place_ref[WINDOW if shared else OWN_WINDOW] * 128, 128)
        inputs_turned[...] = inputs[:, pl.ds(lane, window * 128)].T
        errors_turned[...] = errors[:, pl.ds(lane, window * 128)].T

    shift = pl.multiple_of(place_ref[SHIFT if shared else OWN_SHIFT], step_rows)
    v = jnp.dot(inputs[...], w_in_ref[...], preferred_element_type=jnp.float32)
    back = lax.dot_general(
        errors[...], w_out_ref[...], (((1,), (1,)), ((), ())), preferred_element_type=jnp.float32
    )
    square = v * v
    t = jnp.tanh(v * (SCALE + (SCALE * CUBE) * square))
    upper = 0.5 + 0.5 * t
    hidden = (v * upper).astype(jnp.bfloat16)
    spread_second[...] = jnp.dot(errors_turned[...], hidden, preferred_element_type=jnp.float32)
    slope = upper + (0.5 * v) * (1.0 - t * t) * (SCALE + (3.0 * SCALE * CUBE) * square)
    dpre = (back * slope).astype(jnp.bfloat16)
    spread_first[...] = jnp.dot(inputs_turned[...], dpre, preferred_element_type=jnp.float32)
    second_ref[...] = spread_second[pl.ds(shift, own), :]
    first_ref[...] = spread_first[pl.ds(shift, own), :]
    if shared:
        other = pl.ds(pl.multiple_of(place_ref[OTHER_SHIFT], step_rows), own)
        send_refs[0][:own, :] = spread_first[other, :].astype(jnp.bfloat16)
        last = send_refs[-1].shape[0]
        send_refs[-1][last - own :, :] = spread_second[other, :].astype(jnp.bfloat16)


def gradient(place, members, swap, shared, errors, inputs, w_in, w_out, after=()):
    error_arrays, error_wheres = zip(*errors)
    input_arrays, input_wheres = zip(*inputs)
    depth, width = w_in.shape
    rows = sum(a.shape[0] for a in input_arrays)
    own = depth // members
    starts = [m * own % 128 for m in range(members) if not (shared and m & swap)]
    reach = max(starts) + (swap + 1 if shared else 1) * own
    window = -(-reach // 128)
    tile = tile_of(width, 640)
    once = pl.Buffered(1)
    return call(
        functools.partial(
            gradient_kernel, (error_wheres, input_wheres), window, own, math.gcd(own, 128), shared
        ),
        "gradient",
        (place, *error_arrays, *input_arrays, w_in, w_out),
        [
            jax.ShapeDtypeStruct((own, width), jnp.float32),
            jax.ShapeDtypeStruct((own, width), jnp.float32),
        ]
        + [jax.ShapeDtypeStruct((2 * own // max(shared, 1), width), jnp.bfloat16)] * shared,
        after,
        grid=(width // tile,),
        in_specs=[
            pl.BlockSpec(a.shape, whole, pipeline_mode=once)
            for a in (*error_arrays, *input_arrays)
        ]
        + [pl.BlockSpec((depth, tile), column), pl.BlockSpec((tile, depth), lambda n, s: (n, 0))],
        out_specs=[pl.BlockSpec((own, tile), column)] * 2
        + [pl.BlockSpec((2 * own // max(shared, 1), tile), column)] * shared,
        scratch_shapes=[
            pltpu.VMEM((rows, depth), jnp.bfloat16),
            pltpu.VMEM((rows, depth), jnp.bfloat16),
            pltpu.VMEM((window * 128, rows), jnp.bfloat16),
            pltpu.VMEM((window * 128, rows), jnp.bfloat16),
            pltpu.VMEM((window * 128, tile), jnp.float32),
            pltpu.VMEM((window * 128, tile), jnp.float32),
        ],
    )


def products_kernel(labels, fresh, place_ref, *refs):
    own = refs[0].shape[0]
    refs, (known_ref, out_ref, totals) = refs[:-3], refs[-3:]
    each = len(refs) // len(labels)
    slots = [refs[each * n : each * (n + 1)] for n in range(len(labels))]
    pairs = [(i, j) for i in range(len(slots) - fresh, len(slots)) for j in range(i + 1)]

    @pl.when(pl.program_id(0) == 0)
    def _():
        totals[...] = jnp.zeros_like(totals)

    def values(slot):
        return [ref[...].astype(jnp.float32) for ref in slot]

    for n, (i, j) in enumerate(pairs):
        a, b = values(slots[i]), values(slots[j])
        both = sum(u * v for u, v in zip(a, b))
        totals[n] += jnp.sum(both.reshape(own // 8, 8, -1), axis=0)

    @pl.when(pl.program_id(0) == pl.num_programs(0) - 1)
    def _():
        result = known_ref[...]
        row = lax.broadcasted_iota(jnp.int32, result.shape, 0)
        column = lax.broadcasted_iota(jnp.int32, result.shape, 1)
        for n, (i, j) in enumerate(pairs):
            i, j = (jnp.bitwise_xor(place_ref[MEMBER], labels[k]) for k in (i, j))
            here = ((row == i) & (column == j)) | ((row == j) & (column == i))
            result = result + jnp.where(here, jnp.sum(totals[n]), 0.0)
        out_ref[...] = result


def products(place, slots, labels, fresh, known, after=()):
    arrays = [a for slot in slots for a, _ in slot]
    blocks = [k for slot in slots for _, k in slot]
    own, width = arrays[0].shape
    tile = tile_of(width, 256)
    pairs = sum(len(slots) - n for n in range(fresh))
    return call(
        functools.partial(products_kernel, tuple(labels), fresh),
        "products",
        (place, *arrays, known),
        [jax.ShapeDtypeStruct(known.shape, jnp.float32)],
        after,
        grid=(width // tile,),
        in_specs=[pl.BlockSpec((own, tile), lambda n, s, k=k: (k, n)) for k in blocks]
        + [pl.BlockSpec(known.shape, whole)],
        out_specs=[pl.BlockSpec(known.shape, whole)],
        scratch_shapes=[pltpu.VMEM((pairs, 8, tile), jnp.float32)],
    )[0]


def tree_weights(count, entry):
    def inner(a, b):
        total = 0.0
        for i, u in a.items():
            for j, v in b.items():
                total = total + u * v * entry(i, j)
        return total

    items = [{i: 1.0} for i in range(count)]
    while len(items) > 1:
        half = len(items) // 2
        merged = []
        for low, high in zip(items[:half], items[half:]):
            product = inner(low, high)
            scale_low = 1.0 - product / (2.0 * (jnp.maximum(inner(low, low), 0.0) + epsilon))
            scale_high = 1.0 - product / (2.0 * (jnp.maximum(inner(high, high), 0.0) + epsilon))
            joined = {i: u * scale_low for i, u in low.items()}
            joined.update({i: u * scale_high for i, u in high.items()})
            merged.append(joined)
        items = merged
    return [items[0][i] for i in range(count)]


def sum_kernel(place_ref, *refs):
    refs[-1][...] = sum(ref[...] for ref in refs[:-1])


def sum_of(place, parts):
    shape = parts[0].shape
    return call(
        sum_kernel,
        "sum_of",
        (place, *parts),
        [jax.ShapeDtypeStruct(shape, jnp.float32)],
        vmem=4 * 2**20,
        grid=(1,),
        in_specs=[pl.BlockSpec(shape, whole)] * len(parts),
        out_specs=[pl.BlockSpec(shape, whole)],
    )[0]


def merge_kernel(labels, place_ref, totals_ref, *refs):
    refs, (first_ref, second_ref, weights_ref) = refs[:-3], refs[-3:]

    @pl.when(pl.program_id(0) == 0)
    def _():
        def entry(i, j):
            i, j = (jnp.bitwise_xor(place_ref[MEMBER], k) for k in (i, j))
            return totals_ref[i, j]

        for n, weight in enumerate(tree_weights(len(labels), entry)):
            weights_ref[n] = weight

    first = second = 0.0
    for n, label in enumerate(labels):
        weight = weights_ref[label]
        first = first + weight * refs[2 * n][...].astype(jnp.float32)
        second = second + weight * refs[2 * n + 1][...].astype(jnp.float32)
    first_ref[...] = first
    second_ref[...] = second


def merge(place, totals, slots, labels):
    arrays = [a for slot in slots for a, _ in slot]
    own, width = arrays[0].shape
    block = max(b for b in range(16, min(own, 32) + 1, 16) if own % b == 0)
    steps = own // block
    spec = pl.BlockSpec((block, width), lambda n, s: (n, 0))
    specs = [
        pl.BlockSpec((block, width), lambda n, s, k=k: (n + k * steps, 0))
        for slot in slots
        for _, k in slot
    ]
    shape = jax.ShapeDtypeStruct((own, width), jnp.float32)
    return call(
        functools.partial(merge_kernel, tuple(labels)),
        "merge",
        (place, totals, *arrays),
        [shape, shape],
        vmem=16 * 2**20,
        grid=(steps,),
        in_specs=[pl.BlockSpec(memory_space=pltpu.SMEM)] + specs,
        out_specs=[spec, spec],
        scratch_shapes=[pltpu.SMEM((len(slots),), jnp.float32)],
    )


def on_device(inputs, targets, w_in, w_out):
    row_count = inputs.shape[0]
    workers = lax.axis_size("dp")
    shards = lax.axis_size("tensor")
    levels = workers.bit_length() - 1
    shard_levels = shards.bit_length() - 1
    gathered = min(levels, gather_levels_limit)
    members = 2**gathered
    others = workers // members
    position = lax.axis_index("dp")
    shard = lax.axis_index("tensor")
    member = position // others

    def part_of(index):
        part = 0
        for bit in range(shard_levels):
            part = part * 2 + (index >> bit & 1)
        return part

    near = shard & 1
    part_rows = row_count // shards
    own = inputs.shape[1] // members
    swap = 1
    bits = [2**b for b in reversed(range(gathered)) if 2**b != swap]
    upper = member // swap % 2
    first_row = (member - upper * swap) * own
    place = jnp.stack(
        [
            first_row // 128,
            first_row % 128 + upper * swap * own,
            first_row % 128 + (1 - upper) * swap * own,
            member,
            near,
            1 - near,
            part_of(shard),
            part_of(shard) - near * (shards // 2),
            member * own // 128,
            member * own % 128,
        ]
    ).astype(jnp.int32)

    send, hidden_near, own_part = forward(place, part_rows, inputs, w_in, w_out)
    got = from_mask(send, 0, 1)
    inputs_of = {bit: from_mask(own_part, bit * others, 0) for bit in bits}

    summed = product(place, hidden_near, w_out) + got
    most = 24.0 * 0.15625 * 0.078125 * inputs.shape[1] * w_in.shape[1] * shards
    scale = 2.0 ** math.ceil(math.log2(most / 65504.0))
    sums = [summed]
    for bit in range(1, shard_levels):
        rounded = (sum(sums) * (1.0 / scale)).astype(jnp.float16)
        sums.append(from_mask(rounded, 0, 2**bit).astype(jnp.float32) * scale)
    error, error_piece = error_half(
        place,
        part_rows,
        sum(sums[:-1]),
        sums[-1],
        targets,
        tuple(inputs_of.values()),
    )
    errors_of = {
        bit: from_mask(error_piece if bit == bits[0] else error, bit * others, 0) for bit in bits
    }

    def to_half(piece, *before):
        for bit in reversed(range(1, shard_levels)):
            got = ordered(from_mask(piece, 0, 2**bit), *before)
            piece = join(shard >> bit & 1, piece, got)
        return piece

    def both_halves(half):
        return [(half, NEAR), (from_mask(half, 0, 1), FAR)]

    slots, labels, known, sent, got, halves = [], [], [], [], [], {}
    totals = jnp.zeros((8, 128), jnp.float32)
    masks = [m for m in range(members) if not m & swap]
    for n, m in enumerate(masks):
        if n == 0:
            half = error
        elif m not in (bits[0], masks[-1]):
            half = errors_of[m] = ordered(errors_of[m], sent[0], *got[0][:1])
            other_inputs = halves[m]
        elif m == bits[0]:
            before = [sent[-1], *got[0]]
            errors_of[m] = ordered(errors_of[m], sent[0])
            for bit in bits[1:]:
                ready = ordered(errors_of[m], errors_of[bit])
                errors_of[m | bit] = from_mask(ready, bit * others, 0)
                before.append(errors_of[m | bit])
                ready = ordered(halves[m], errors_of[bit])
                halves[m | bit] = from_mask(ready, bit * others, 0)
            half = to_half(errors_of[m], *before)
            other_inputs = halves[m]
        else:
            half = to_half(ordered(errors_of[m], sent[-2]), sent[-1], *got[n - 2])
            other_inputs = ordered(halves[m], sent[-1])
        last = n == len(masks) - 1
        shared = 2 if n == 0 or last else 1
        first, second, *send = gradient(
            place,
            members,
            swap,
            shared,
            both_halves(half),
            both_halves(other_inputs) if n else [(inputs, None)],
            w_in,
            w_out,
            known[-2:-1],
        )
        if n == 0:
            for bit in bits:
                halves[bit] = to_half(inputs_of[bit], send[0], errors_of[bits[0]], *halves.values())
        sent.append(first)
        slots.append(((first, 0), (second, 0)))
        labels.append(m)
        if last:
            totals = products(place, slots, labels, 1, totals)
        got.append([from_mask(a, swap * others, 0) for a in send])
        slots.append(((got[n][0], 0), (got[n][-1], 2 - shared)))
        labels.append(m ^ swap)
        if last:
            for k in range(2):
                totals = products(place, [slot[k : k + 1] for slot in slots], labels, 1, totals)
        else:
            totals = products(place, slots, labels, 2, totals)
        known.append(totals)

    rounds = [[(0, mask) for mask in range(1, shards)]]
    rounds.append([(m * others, 0) for m in range(2, members, 2)])
    rounds.append([(others, 0)])
    for partners in rounds:
        totals = sum_of(place, [totals] + [from_mask(totals, *mask) for mask in partners])
    pieces = merge(place, totals, slots, labels)

    for section in range(gathered, levels):
        upper_flag = position >> levels - 1 - section & 1
        keep_first, send_first = split_piece(pieces[0], upper_flag)
        keep_second, send_second = split_piece(pieces[1], upper_flag)
        got_first, got_second = from_partner((send_first, send_second), "dp", levels - 1 - section)
        pieces = combine(
            (keep_first, keep_second), (got_first, got_second), upper_flag, section, levels
        )
    return (pieces[0], pieces[1])


def solution(mesh):
    placed = (P("dp", None), P("dp", None), P(None, "tensor"), P("tensor", None))
    return jax.shard_map(
        on_device,
        mesh=mesh,
        in_specs=placed,
        out_specs=(P("dp", "tensor"), P("dp", "tensor")),
        check_vma=False,
    )
```

```python
import functools
import math

import jax
import jax.numpy as jnp
from jax import lax
from jax.experimental import pallas as pl
from jax.experimental.pallas import tpu as pltpu
from jax.sharding import PartitionSpec as P

epsilon = 1e-06
gather_levels_limit = 3
vmem_bytes = 36 * 2**20
vmem_most = 60 * 2**20


def from_partner(value, axis, distance):
    mask = 2**distance
    pairs = [(source, source ^ mask) for source in range(lax.axis_size(axis))]
    return lax.ppermute(value, axis, pairs)


def from_mask(value, dp_mask, tensor_mask):
    shards = lax.axis_size("tensor")
    mask = dp_mask * shards + tensor_mask
    pairs = [(source, source ^ mask) for source in range(lax.axis_size("dp") * shards)]
    return lax.ppermute(value, ("dp", "tensor"), pairs)


def ordered(value, *before):
    return lax.optimization_barrier((value, *before))[0]


def split_piece(piece, upper_flag):
    half = piece.shape[0] // 2
    keep = lax.dynamic_slice_in_dim(piece, upper_flag * half, half, 0)
    send = lax.dynamic_slice_in_dim(piece, (1 - upper_flag) * half, half, 0)
    return (keep, send)


def group_total(values, section, levels):
    summed = lax.psum(values, "tensor")
    for offset in range(section + 1):
        summed = summed + from_partner(summed, "dp", levels - 1 - offset)
    return summed


def combine(own, incoming, upper_flag, section, levels):
    product = jnp.sum(own[0] * incoming[0]) + jnp.sum(own[1] * incoming[1])
    norm_own = jnp.sum(own[0] * own[0]) + jnp.sum(own[1] * own[1])
    norm_incoming = jnp.sum(incoming[0] * incoming[0]) + jnp.sum(incoming[1] * incoming[1])
    is_upper = upper_flag == 1
    norm_low = jnp.where(is_upper, norm_incoming, norm_own)
    norm_high = jnp.where(is_upper, norm_own, norm_incoming)
    totals = group_total(jnp.stack([product, norm_low, norm_high]), section, levels)
    coef_low = 1.0 - totals[0] / (2.0 * (totals[1] + epsilon))
    coef_high = 1.0 - totals[0] / (2.0 * (totals[2] + epsilon))
    coef_own = jnp.where(is_upper, coef_high, coef_low)
    coef_incoming = jnp.where(is_upper, coef_low, coef_high)
    return (
        coef_own * own[0] + coef_incoming * incoming[0],
        coef_own * own[1] + coef_incoming * incoming[1],
    )


def tile_of(size, limit):
    return max(b for b in range(128, limit + 1, 128) if size % b == 0)


def contract(left, right, left_dim, right_dim):
    dims = (((left_dim,), (right_dim,)), ((), ()))
    return lax.dot_general(left, right, dims, preferred_element_type=jnp.float32)


def call(kernel, name, operands, shapes, after=(), vmem=vmem_bytes, **spec):
    spec["in_specs"] = [pl.BlockSpec(memory_space=pl.ANY)] * len(after) + spec["in_specs"]

    def body(place_ref, *refs):
        kernel(place_ref, *refs[len(after) :])

    return pl.pallas_call(
        body,
        grid_spec=pltpu.PrefetchScalarGridSpec(num_scalar_prefetch=1, **spec),
        out_shape=shapes,
        compiler_params=pltpu.CompilerParams(vmem_limit_bytes=vmem),
        cost_estimate=pl.CostEstimate(flops=1, bytes_accessed=1, transcendentals=0),
        name=name,
    )(operands[0], *after, *operands[1:])


WINDOW, SHIFT, OTHER_SHIFT, MEMBER, NEAR, FAR, PART, PIECE = range(8)


def row_start(place_ref, block, where):
    return 0 if where is None else pl.multiple_of(place_ref[where] * block.shape[0], 16)


def whole(n, s):
    return (0, 0)


def column(n, s):
    return (0, n)


SCALE = math.sqrt(2.0 / math.pi)
CUBE = 0.044715


def forward_kernel(steps, place_ref, rows_ref, w_in_ref, w_out_ref, out_ref, part_ref, hidden):
    step = pl.program_id(0)
    tile = w_in_ref.shape[1]

    for n in range(steps):

        @pl.when(step == n)
        def _():
            v = jnp.dot(rows_ref[...], w_in_ref[...], preferred_element_type=jnp.float32)
            t = jnp.tanh(v * (SCALE + (SCALE * CUBE) * (v * v)))
            hidden[:, n * tile : (n + 1) * tile] = (v * (0.5 + 0.5 * t)).astype(jnp.bfloat16)

    @pl.when(step == 0)
    def _():
        part_ref[...] = rows_ref[pl.ds(row_start(place_ref, part_ref, PIECE), part_ref.shape[0]), :]

    @pl.when(step >= steps)
    def _():
        out_ref[...] = jnp.dot(hidden[...], w_out_ref[...], preferred_element_type=jnp.float32)


def forward(place, which, part_rows, inputs, w_in, w_out):
    rows = inputs.shape[0] // 2
    depth, width = w_in.shape
    tile, out_tile = tile_of(width, 640), tile_of(depth, 640)
    steps = width // tile
    last = lambda n: jnp.maximum(n - steps, 0)
    return call(
        functools.partial(forward_kernel, steps),
        "forward",
        (place, inputs, w_in, w_out),
        [
            jax.ShapeDtypeStruct((rows, depth), jnp.float32),
            jax.ShapeDtypeStruct((part_rows, depth), jnp.bfloat16),
        ],
        vmem=vmem_most,
        grid=(steps + depth // out_tile,),
        in_specs=[
            pl.BlockSpec((rows, depth), lambda n, s: (s[which], 0)),
            pl.BlockSpec((depth, tile), lambda n, s: (0, jnp.minimum(n, steps - 1))),
            pl.BlockSpec((width, out_tile), lambda n, s: (0, last(n))),
        ],
        out_specs=[
            pl.BlockSpec((rows, out_tile), lambda n, s: (0, last(n))),
            pl.BlockSpec((part_rows, depth), whole),
        ],
        scratch_shapes=[pltpu.VMEM((rows, width), jnp.bfloat16)],
    )


def join_kernel(place_ref, own_ref, got_ref, out_ref):
    rows = own_ref.shape[0]
    out_ref[pl.ds(pl.multiple_of(place_ref[0] * rows, 16), rows), :] = own_ref[...]
    out_ref[pl.ds(pl.multiple_of((1 - place_ref[0]) * rows, 16), rows), :] = got_ref[...]


def join(flag, own, got):
    rows, depth = own.shape
    return call(
        join_kernel,
        "join",
        (flag.reshape(1), own, got),
        [jax.ShapeDtypeStruct((2 * rows, depth), own.dtype)],
        grid=(1,),
        in_specs=[pl.BlockSpec((rows, depth), whole)] * 2,
        out_specs=[pl.BlockSpec((2 * rows, depth), whole)],
    )[0]


def error_kernel(row_count, place_ref, own_ref, got_ref, targets_ref, half_ref, part_ref):
    out = own_ref[...] + got_ref[...]
    error = (out - targets_ref[...].astype(jnp.float32)) / row_count
    half_ref[...] = error.astype(jnp.bfloat16)
    rows = part_ref.shape[0]
    part_ref[...] = half_ref[pl.ds(pl.multiple_of(place_ref[PIECE] * rows, 16), rows), :]


def error_half(place, part_rows, own, got, targets, after):
    rows, depth = own.shape
    return call(
        functools.partial(error_kernel, targets.shape[0]),
        "error_half",
        (place, own, got, targets),
        [
            jax.ShapeDtypeStruct((rows, depth), jnp.bfloat16),
            jax.ShapeDtypeStruct((part_rows, depth), jnp.bfloat16),
        ],
        after,
        grid=(1,),
        in_specs=[
            pl.BlockSpec((rows, depth), whole),
            pl.BlockSpec((rows, depth), whole),
            pl.BlockSpec((rows, depth), lambda n, s: (s[NEAR], 0)),
        ],
        out_specs=[pl.BlockSpec((rows, depth), whole), pl.BlockSpec((part_rows, depth), whole)],
    )


def gradient_kernel(wheres, window, own, step_rows, place_ref, *refs):
    error_wheres, input_wheres = wheres
    refs = list(refs)

    def take(n):
        taken = refs[:n]
        del refs[:n]
        return taken

    error_refs, input_refs = take(len(error_wheres)), take(len(input_wheres))
    w_in_ref, w_out_ref, first_ref, second_ref, send_first_ref, send_second_ref = take(6)
    errors, inputs, inputs_turned, errors_turned, spread_first, spread_second = refs
    if len(input_refs) == 1:
        inputs = input_refs[0]

    @pl.when(pl.program_id(0) == 0)
    def _():
        for block, where in zip(error_refs, error_wheres):
            errors[pl.ds(row_start(place_ref, block, where), block.shape[0]), :] = block[...]
        if len(input_refs) > 1:
            for block, where in zip(input_refs, input_wheres):
                inputs[pl.ds(row_start(place_ref, block, where), block.shape[0]), :] = block[...]
        lane = pl.multiple_of(place_ref[WINDOW] * 128, 128)
        inputs_turned[...] = inputs[:, pl.ds(lane, window * 128)].T
        errors_turned[...] = errors[:, pl.ds(lane, window * 128)].T

    shift = pl.multiple_of(place_ref[SHIFT], step_rows)
    other_shift = pl.multiple_of(place_ref[OTHER_SHIFT], step_rows)
    v = jnp.dot(inputs[...], w_in_ref[...], preferred_element_type=jnp.float32)
    back = lax.dot_general(
        errors[...], w_out_ref[...], (((1,), (1,)), ((), ())), preferred_element_type=jnp.float32
    )
    square = v * v
    t = jnp.tanh(v * (SCALE + (SCALE * CUBE) * square))
    upper = 0.5 + 0.5 * t
    hidden = (v * upper).astype(jnp.bfloat16)
    spread_second[...] = jnp.dot(errors_turned[...], hidden, preferred_element_type=jnp.float32)
    slope = upper + (0.5 * v) * (1.0 - t * t) * (SCALE + (3.0 * SCALE * CUBE) * square)
    dpre = (back * slope).astype(jnp.bfloat16)
    spread_first[...] = jnp.dot(inputs_turned[...], dpre, preferred_element_type=jnp.float32)
    second_ref[...] = spread_second[pl.ds(shift, own), :]
    send_second_ref[...] = spread_second[pl.ds(other_shift, own), :].astype(jnp.bfloat16)
    first_ref[...] = spread_first[pl.ds(shift, own), :]
    send_first_ref[...] = spread_first[pl.ds(other_shift, own), :].astype(jnp.bfloat16)


def gradient(place, members, swap, errors, inputs, w_in, w_out, after=()):
    error_arrays, error_wheres = zip(*errors)
    input_arrays, input_wheres = zip(*inputs)
    depth, width = w_in.shape
    rows = sum(a.shape[0] for a in input_arrays)
    own = depth // members
    reach = max(m * own % 128 for m in range(members) if not m & swap) + (swap + 1) * own
    window = -(-reach // 128)
    tile = tile_of(width, 640)
    once = pl.Buffered(1)
    return call(
        functools.partial(
            gradient_kernel, (error_wheres, input_wheres), window, own, math.gcd(own, 128)
        ),
        "gradient",
        (place, *error_arrays, *input_arrays, w_in, w_out),
        [
            jax.ShapeDtypeStruct((own, width), jnp.float32),
            jax.ShapeDtypeStruct((own, width), jnp.float32),
            jax.ShapeDtypeStruct((own, width), jnp.bfloat16),
            jax.ShapeDtypeStruct((own, width), jnp.bfloat16),
        ],
        after,
        grid=(width // tile,),
        in_specs=[
            pl.BlockSpec(a.shape, whole, pipeline_mode=once)
            for a in (*error_arrays, *input_arrays)
        ]
        + [pl.BlockSpec((depth, tile), column), pl.BlockSpec((tile, depth), lambda n, s: (n, 0))],
        out_specs=[pl.BlockSpec((own, tile), column)] * 4,
        scratch_shapes=[
            pltpu.VMEM((rows, depth), jnp.bfloat16),
            pltpu.VMEM((rows, depth), jnp.bfloat16),
            pltpu.VMEM((window * 128, rows), jnp.bfloat16),
            pltpu.VMEM((window * 128, rows), jnp.bfloat16),
            pltpu.VMEM((window * 128, tile), jnp.float32),
            pltpu.VMEM((window * 128, tile), jnp.float32),
        ],
    )


def products_kernel(labels, fresh, place_ref, *refs):
    own = refs[0].shape[0]
    refs, (known_ref, out_ref, totals) = refs[:-3], refs[-3:]
    each = len(refs) // len(labels)
    slots = [refs[each * n : each * (n + 1)] for n in range(len(labels))]
    pairs = [(i, j) for i in range(len(slots) - fresh, len(slots)) for j in range(i + 1)]

    @pl.when(pl.program_id(0) == 0)
    def _():
        totals[...] = jnp.zeros_like(totals)

    def values(slot):
        return [ref[...].astype(jnp.float32) for ref in slot]

    for n, (i, j) in enumerate(pairs):
        a, b = values(slots[i]), values(slots[j])
        both = sum(u * v for u, v in zip(a, b))
        totals[n] += jnp.sum(both.reshape(own // 8, 8, -1), axis=0)

    @pl.when(pl.program_id(0) == pl.num_programs(0) - 1)
    def _():
        result = known_ref[...]
        row = lax.broadcasted_iota(jnp.int32, result.shape, 0)
        column = lax.broadcasted_iota(jnp.int32, result.shape, 1)
        for n, (i, j) in enumerate(pairs):
            i, j = (jnp.bitwise_xor(place_ref[MEMBER], labels[k]) for k in (i, j))
            here = ((row == i) & (column == j)) | ((row == j) & (column == i))
            result = result + jnp.where(here, jnp.sum(totals[n]), 0.0)
        out_ref[...] = result


def products(place, slots, labels, fresh, known, after=()):
    arrays = [a for slot in slots for a in slot]
    own, width = slots[0][0].shape
    tile = tile_of(width, 256)
    pairs = sum(len(slots) - n for n in range(fresh))
    return call(
        functools.partial(products_kernel, tuple(labels), fresh),
        "products",
        (place, *arrays, known),
        [jax.ShapeDtypeStruct(known.shape, jnp.float32)],
        after,
        grid=(width // tile,),
        in_specs=[pl.BlockSpec((a.shape[0], tile), lambda n, s: (0, n)) for a in arrays]
        + [pl.BlockSpec(known.shape, whole)],
        out_specs=[pl.BlockSpec(known.shape, whole)],
        scratch_shapes=[pltpu.VMEM((pairs, 8, tile), jnp.float32)],
    )[0]


def tree_weights(count, entry):
    def inner(a, b):
        total = 0.0
        for i, u in a.items():
            for j, v in b.items():
                total = total + u * v * entry(i, j)
        return total

    items = [{i: 1.0} for i in range(count)]
    while len(items) > 1:
        half = len(items) // 2
        merged = []
        for low, high in zip(items[:half], items[half:]):
            product = inner(low, high)
            scale_low = 1.0 - product / (2.0 * (jnp.maximum(inner(low, low), 0.0) + epsilon))
            scale_high = 1.0 - product / (2.0 * (jnp.maximum(inner(high, high), 0.0) + epsilon))
            joined = {i: u * scale_low for i, u in low.items()}
            joined.update({i: u * scale_high for i, u in high.items()})
            merged.append(joined)
        items = merged
    return [items[0][i] for i in range(count)]


def sum_kernel(place_ref, *refs):
    refs[-1][...] = sum(ref[...] for ref in refs[:-1])


def sum_of(place, parts):
    shape = parts[0].shape
    return call(
        sum_kernel,
        "sum_of",
        (place, *parts),
        [jax.ShapeDtypeStruct(shape, jnp.float32)],
        vmem=4 * 2**20,
        grid=(1,),
        in_specs=[pl.BlockSpec(shape, whole)] * len(parts),
        out_specs=[pl.BlockSpec(shape, whole)],
    )[0]


def merge_kernel(labels, place_ref, totals_ref, got_ref, *refs):
    refs, (first_ref, second_ref, weights_ref) = refs[:-3], refs[-3:]

    @pl.when(pl.program_id(0) == 0)
    def _():
        def entry(i, j):
            i, j = (jnp.bitwise_xor(place_ref[MEMBER], k) for k in (i, j))
            return totals_ref[i, j] + got_ref[i, j]

        for n, weight in enumerate(tree_weights(len(labels), entry)):
            weights_ref[n] = weight

    first = second = 0.0
    for n, label in enumerate(labels):
        weight = weights_ref[label]
        first = first + weight * refs[2 * n][...].astype(jnp.float32)
        second = second + weight * refs[2 * n + 1][...].astype(jnp.float32)
    first_ref[...] = first
    second_ref[...] = second


def merge(place, totals, got, slots, labels):
    own, width = slots[0][0].shape
    block = max(b for b in range(16, min(own, 32) + 1, 16) if own % b == 0)
    spec = pl.BlockSpec((block, width), lambda n, s: (n, 0))
    arrays = [a for slot in slots for a in slot]
    shape = jax.ShapeDtypeStruct((own, width), jnp.float32)
    return call(
        functools.partial(merge_kernel, tuple(labels)),
        "merge",
        (place, totals, got, *arrays),
        [shape, shape],
        vmem=16 * 2**20,
        grid=(own // block,),
        in_specs=[pl.BlockSpec(memory_space=pltpu.SMEM)] * 2 + [spec] * len(arrays),
        out_specs=[spec, spec],
        scratch_shapes=[pltpu.SMEM((len(slots),), jnp.float32)],
    )


def on_device(inputs, targets, w_in, w_out):
    row_count = inputs.shape[0]
    workers = lax.axis_size("dp")
    shards = lax.axis_size("tensor")
    levels = workers.bit_length() - 1
    shard_levels = shards.bit_length() - 1
    gathered = min(levels, gather_levels_limit)
    members = 2**gathered
    others = workers // members
    position = lax.axis_index("dp")
    shard = lax.axis_index("tensor")
    member = position // others

    def part_of(index):
        part = 0
        for bit in range(shard_levels):
            part = part * 2 + (index >> bit & 1)
        return part

    near = shard & 1
    part_rows = row_count // shards
    own = inputs.shape[1] // members
    swap = 1
    bits = [2**b for b in reversed(range(gathered)) if 2**b != swap]
    upper = member // swap % 2
    first_row = (member - upper * swap) * own
    place = jnp.stack(
        [
            first_row // 128,
            first_row % 128 + upper * swap * own,
            first_row % 128 + (1 - upper) * swap * own,
            member,
            near,
            1 - near,
            part_of(shard),
            part_of(shard) - near * (shards // 2),
        ]
    ).astype(jnp.int32)

    send, _ = forward(place, FAR, part_rows, inputs, w_in, w_out)
    got = from_mask(send, 0, 1)
    summed, own_part = forward(place, NEAR, part_rows, inputs, w_in, w_out)
    inputs_of = {bit: from_mask(own_part, bit * others, 0) for bit in bits}

    summed = summed + got
    most = 24.0 * 0.15625 * 0.078125 * inputs.shape[1] * w_in.shape[1] * shards
    scale = 2.0 ** math.ceil(math.log2(most / 65504.0))
    sums = [summed]
    for bit in range(1, shard_levels):
        rounded = (sum(sums) * (1.0 / scale)).astype(jnp.float16)
        sums.append(from_mask(rounded, 0, 2**bit).astype(jnp.float32) * scale)
    error, error_piece = error_half(
        place,
        part_rows,
        sum(sums[:-1]),
        sums[-1],
        targets,
        tuple(inputs_of.values()),
    )
    errors_of = {
        bit: from_mask(error_piece if bit == bits[0] else error, bit * others, 0) for bit in bits
    }

    def to_half(piece, *before):
        for bit in reversed(range(1, shard_levels)):
            got = ordered(from_mask(piece, 0, 2**bit), *before)
            piece = join(shard >> bit & 1, piece, got)
        return piece

    def both_halves(half):
        return [(half, NEAR), (from_mask(half, 0, 1), FAR)]

    slots, labels, known, sent, halves = [], [], [], [], {}
    totals = jnp.zeros((8, 128), jnp.float32)
    masks = [m for m in range(members) if not m & swap]
    for n, m in enumerate(masks):
        if n == 0:
            half = error
        elif m not in (bits[0], masks[-1]):
            half = errors_of[m] = ordered(errors_of[m], sent[0], *slots[1][:1])
            other_inputs = halves[m]
        elif m == bits[0]:
            before = [sent[-1], *slots[1]]
            errors_of[m] = ordered(errors_of[m], sent[0])
            for bit in bits[1:]:
                ready = ordered(errors_of[m], errors_of[bit])
                errors_of[m | bit] = from_mask(ready, bit * others, 0)
                before.append(errors_of[m | bit])
                ready = ordered(halves[m], errors_of[bit])
                halves[m | bit] = from_mask(ready, bit * others, 0)
            half = to_half(errors_of[m], *before)
            other_inputs = halves[m]
        else:
            half = to_half(ordered(errors_of[m], sent[-2]), sent[-1], *slots[2 * n - 3])
            other_inputs = ordered(halves[m], sent[-1])
        first, second, *send = gradient(
            place,
            members,
            swap,
            both_halves(half),
            both_halves(other_inputs) if n else [(inputs, None)],
            w_in,
            w_out,
            known[-2:-1],
        )
        if n == 0:
            for bit in bits:
                halves[bit] = to_half(inputs_of[bit], send[0], errors_of[bits[0]], *halves.values())
        sent.append(send[0])
        slots.append((first, second))
        labels.append(m)
        last = n == len(masks) - 1
        if last:
            totals = products(place, slots, labels, 1, totals)
        slots.append(tuple(from_mask(a, swap * others, 0) for a in send))
        labels.append(m ^ swap)
        if last:
            for k in range(2):
                totals = products(place, [slot[k : k + 1] for slot in slots], labels, 1, totals)
        else:
            totals = products(place, slots, labels, 2, totals)
        known.append(totals)

    rounds = [[(0, mask) for mask in range(1, shards)]]
    rounds.append([(m * others, 0) for m in range(2, members, 2)])
    for partners in rounds:
        totals = sum_of(place, [totals] + [from_mask(totals, *mask) for mask in partners])
    pieces = merge(place, totals, from_mask(totals, others, 0), slots, labels)

    for section in range(gathered, levels):
        upper_flag = position >> levels - 1 - section & 1
        keep_first, send_first = split_piece(pieces[0], upper_flag)
        keep_second, send_second = split_piece(pieces[1], upper_flag)
        got_first, got_second = from_partner((send_first, send_second), "dp", levels - 1 - section)
        pieces = combine(
            (keep_first, keep_second), (got_first, got_second), upper_flag, section, levels
        )
    return (pieces[0], pieces[1])


def solution(mesh):
    placed = (P("dp", None), P("dp", None), P(None, "tensor"), P("tensor", None))
    return jax.shard_map(
        on_device,
        mesh=mesh,
        in_specs=placed,
        out_specs=(P("dp", "tensor"), P("dp", "tensor")),
        check_vma=False,
    )
```

```python
import functools
import math

import jax
import jax.numpy as jnp
from jax import lax
from jax.experimental import pallas as pl
from jax.experimental.pallas import tpu as pltpu
from jax.sharding import PartitionSpec as P

epsilon = 1e-06
gather_levels_limit = 3
vmem_bytes = 36 * 2**20
vmem_most = 60 * 2**20


def from_partner(value, axis, distance):
    mask = 2**distance
    pairs = [(source, source ^ mask) for source in range(lax.axis_size(axis))]
    return lax.ppermute(value, axis, pairs)


def from_mask(value, dp_mask, tensor_mask):
    shards = lax.axis_size("tensor")
    mask = dp_mask * shards + tensor_mask
    pairs = [(source, source ^ mask) for source in range(lax.axis_size("dp") * shards)]
    return lax.ppermute(value, ("dp", "tensor"), pairs)


def ordered(value, *before):
    return lax.optimization_barrier((value, *before))[0]


def split_piece(piece, upper_flag):
    half = piece.shape[0] // 2
    keep = lax.dynamic_slice_in_dim(piece, upper_flag * half, half, 0)
    send = lax.dynamic_slice_in_dim(piece, (1 - upper_flag) * half, half, 0)
    return (keep, send)


def group_total(values, section, levels):
    summed = lax.psum(values, "tensor")
    for offset in range(section + 1):
        summed = summed + from_partner(summed, "dp", levels - 1 - offset)
    return summed


def combine(own, incoming, upper_flag, section, levels):
    product = jnp.sum(own[0] * incoming[0]) + jnp.sum(own[1] * incoming[1])
    norm_own = jnp.sum(own[0] * own[0]) + jnp.sum(own[1] * own[1])
    norm_incoming = jnp.sum(incoming[0] * incoming[0]) + jnp.sum(incoming[1] * incoming[1])
    is_upper = upper_flag == 1
    norm_low = jnp.where(is_upper, norm_incoming, norm_own)
    norm_high = jnp.where(is_upper, norm_own, norm_incoming)
    totals = group_total(jnp.stack([product, norm_low, norm_high]), section, levels)
    coef_low = 1.0 - totals[0] / (2.0 * (totals[1] + epsilon))
    coef_high = 1.0 - totals[0] / (2.0 * (totals[2] + epsilon))
    coef_own = jnp.where(is_upper, coef_high, coef_low)
    coef_incoming = jnp.where(is_upper, coef_low, coef_high)
    return (
        coef_own * own[0] + coef_incoming * incoming[0],
        coef_own * own[1] + coef_incoming * incoming[1],
    )


def tile_of(size, limit):
    return max(b for b in range(128, limit + 1, 128) if size % b == 0)


def contract(left, right, left_dim, right_dim):
    dims = (((left_dim,), (right_dim,)), ((), ()))
    return lax.dot_general(left, right, dims, preferred_element_type=jnp.float32)


def call(kernel, name, operands, shapes, after=(), vmem=vmem_bytes, **spec):
    spec["in_specs"] = [pl.BlockSpec(memory_space=pl.ANY)] * len(after) + spec["in_specs"]

    def body(place_ref, *refs):
        kernel(place_ref, *refs[len(after) :])

    return pl.pallas_call(
        body,
        grid_spec=pltpu.PrefetchScalarGridSpec(num_scalar_prefetch=1, **spec),
        out_shape=shapes,
        compiler_params=pltpu.CompilerParams(vmem_limit_bytes=vmem),
        cost_estimate=pl.CostEstimate(flops=1, bytes_accessed=1, transcendentals=0),
        name=name,
    )(operands[0], *after, *operands[1:])


WINDOW, SHIFT, OTHER_SHIFT, MEMBER, NEAR, FAR, PART, PIECE = range(8)


def row_start(place_ref, block, where):
    return 0 if where is None else pl.multiple_of(place_ref[where] * block.shape[0], 16)


def whole(n, s):
    return (0, 0)


def column(n, s):
    return (0, n)


SCALE = math.sqrt(2.0 / math.pi)
CUBE = 0.044715


def dot_of_halves(left, upper_ref, lower_ref):
    middle = upper_ref.shape[0]
    upper = jnp.dot(left[:, :middle], upper_ref[...], preferred_element_type=jnp.float32)
    return upper + jnp.dot(left[:, middle:], lower_ref[...], preferred_element_type=jnp.float32)


def forward_kernel(steps, place_ref, rows_ref, *refs):
    w_in_refs, w_out_refs, (out_ref, near_ref, part_ref, hidden) = refs[:2], refs[2:4], refs[4:]
    step = pl.program_id(0)
    half = out_ref.shape[0]
    far = pl.ds(row_start(place_ref, out_ref, FAR), half)
    tile = w_in_refs[0].shape[1]

    for n in range(steps):

        @pl.when(step == n)
        def _():
            v = dot_of_halves(rows_ref[...], *w_in_refs)
            t = jnp.tanh(v * (SCALE + (SCALE * CUBE) * (v * v)))
            hidden[:, n * tile : (n + 1) * tile] = (v * (0.5 + 0.5 * t)).astype(jnp.bfloat16)

    @pl.when(step == 0)
    def _():
        part_ref[...] = rows_ref[pl.ds(row_start(place_ref, part_ref, PART), part_ref.shape[0]), :]

    @pl.when(step == steps)
    def _():
        near_ref[...] = hidden[pl.ds(row_start(place_ref, out_ref, NEAR), half), :]

    @pl.when(step >= steps)
    def _():
        out_ref[...] = dot_of_halves(hidden[far, :], *w_out_refs)


def forward(place, part_rows, inputs, w_in, w_out):
    rows = inputs.shape[0]
    depth, width = w_in.shape
    tile, out_tile = tile_of(width, 640), tile_of(depth, 640)
    steps = width // tile
    last = lambda n: jnp.maximum(n - steps, 0)
    return call(
        functools.partial(forward_kernel, steps),
        "forward",
        (place, inputs, w_in, w_in, w_out, w_out),
        [
            jax.ShapeDtypeStruct((rows // 2, depth), jnp.float32),
            jax.ShapeDtypeStruct((rows // 2, width), jnp.bfloat16),
            jax.ShapeDtypeStruct((part_rows, depth), jnp.bfloat16),
        ],
        vmem=vmem_most,
        grid=(steps + depth // out_tile,),
        in_specs=[pl.BlockSpec((rows, depth), whole)]
        + [
            pl.BlockSpec((depth // 2, tile), lambda n, s, k=k: (k, jnp.minimum(n, steps - 1)))
            for k in range(2)
        ]
        + [
            pl.BlockSpec((width // 2, out_tile), lambda n, s, k=k: (k, last(n))) for k in range(2)
        ],
        out_specs=[
            pl.BlockSpec((rows // 2, out_tile), lambda n, s: (0, last(n))),
            pl.BlockSpec((rows // 2, width), whole),
            pl.BlockSpec((part_rows, depth), whole),
        ],
        scratch_shapes=[pltpu.VMEM((rows, width), jnp.bfloat16)],
    )


def product_kernel(place_ref, left_ref, right_ref, out_ref):
    out_ref[...] = jnp.dot(left_ref[...], right_ref[...], preferred_element_type=jnp.float32)


def product(place, left, right):
    rows, depth = left.shape
    width = right.shape[1]
    tile = tile_of(width, 640)
    return call(
        product_kernel,
        "product",
        (place, left, right),
        [jax.ShapeDtypeStruct((rows, width), jnp.float32)],
        grid=(width // tile,),
        in_specs=[pl.BlockSpec((rows, depth), whole), pl.BlockSpec((depth, tile), column)],
        out_specs=[pl.BlockSpec((rows, tile), column)],
    )[0]


def join_kernel(place_ref, own_ref, got_ref, out_ref):
    rows = own_ref.shape[0]
    out_ref[pl.ds(pl.multiple_of(place_ref[0] * rows, 16), rows), :] = own_ref[...]
    out_ref[pl.ds(pl.multiple_of((1 - place_ref[0]) * rows, 16), rows), :] = got_ref[...]


def join(flag, own, got):
    rows, depth = own.shape
    return call(
        join_kernel,
        "join",
        (flag.reshape(1), own, got),
        [jax.ShapeDtypeStruct((2 * rows, depth), own.dtype)],
        grid=(1,),
        in_specs=[pl.BlockSpec((rows, depth), whole)] * 2,
        out_specs=[pl.BlockSpec((2 * rows, depth), whole)],
    )[0]


def error_kernel(row_count, place_ref, own_ref, got_ref, targets_ref, half_ref, part_ref):
    out = own_ref[...] + got_ref[...]
    error = (out - targets_ref[...].astype(jnp.float32)) / row_count
    half_ref[...] = error.astype(jnp.bfloat16)
    rows = part_ref.shape[0]
    part_ref[...] = half_ref[pl.ds(pl.multiple_of(place_ref[PIECE] * rows, 16), rows), :]


def error_half(place, part_rows, own, got, targets, after):
    rows, depth = own.shape
    return call(
        functools.partial(error_kernel, targets.shape[0]),
        "error_half",
        (place, own, got, targets),
        [
            jax.ShapeDtypeStruct((rows, depth), jnp.bfloat16),
            jax.ShapeDtypeStruct((part_rows, depth), jnp.bfloat16),
        ],
        after,
        grid=(1,),
        in_specs=[
            pl.BlockSpec((rows, depth), whole),
            pl.BlockSpec((rows, depth), whole),
            pl.BlockSpec((rows, depth), lambda n, s: (s[NEAR], 0)),
        ],
        out_specs=[pl.BlockSpec((rows, depth), whole), pl.BlockSpec((part_rows, depth), whole)],
    )


def gradient_kernel(wheres, window, own, step_rows, place_ref, *refs):
    error_wheres, input_wheres = wheres
    refs = list(refs)

    def take(n):
        taken = refs[:n]
        del refs[:n]
        return taken

    error_refs, input_refs = take(len(error_wheres)), take(len(input_wheres))
    w_in_ref, w_out_ref, first_ref, second_ref, send_first_ref, send_second_ref = take(6)
    errors, inputs, inputs_turned, errors_turned, spread_first, spread_second = refs
    if len(input_refs) == 1:
        inputs = input_refs[0]

    @pl.when(pl.program_id(0) == 0)
    def _():
        for block, where in zip(error_refs, error_wheres):
            errors[pl.ds(row_start(place_ref, block, where), block.shape[0]), :] = block[...]
        if len(input_refs) > 1:
            for block, where in zip(input_refs, input_wheres):
                inputs[pl.ds(row_start(place_ref, block, where), block.shape[0]), :] = block[...]
        lane = pl.multiple_of(place_ref[WINDOW] * 128, 128)
        inputs_turned[...] = inputs[:, pl.ds(lane, window * 128)].T
        errors_turned[...] = errors[:, pl.ds(lane, window * 128)].T

    shift = pl.multiple_of(place_ref[SHIFT], step_rows)
    other_shift = pl.multiple_of(place_ref[OTHER_SHIFT], step_rows)
    v = jnp.dot(inputs[...], w_in_ref[...], preferred_element_type=jnp.float32)
    back = lax.dot_general(
        errors[...], w_out_ref[...], (((1,), (1,)), ((), ())), preferred_element_type=jnp.float32
    )
    square = v * v
    t = jnp.tanh(v * (SCALE + (SCALE * CUBE) * square))
    upper = 0.5 + 0.5 * t
    hidden = (v * upper).astype(jnp.bfloat16)
    spread_second[...] = jnp.dot(errors_turned[...], hidden, preferred_element_type=jnp.float32)
    slope = upper + (0.5 * v) * (1.0 - t * t) * (SCALE + (3.0 * SCALE * CUBE) * square)
    dpre = (back * slope).astype(jnp.bfloat16)
    spread_first[...] = jnp.dot(inputs_turned[...], dpre, preferred_element_type=jnp.float32)
    second_ref[...] = spread_second[pl.ds(shift, own), :]
    send_second_ref[...] = spread_second[pl.ds(other_shift, own), :].astype(jnp.bfloat16)
    first_ref[...] = spread_first[pl.ds(shift, own), :]
    send_first_ref[...] = spread_first[pl.ds(other_shift, own), :].astype(jnp.bfloat16)


def gradient(place, members, swap, errors, inputs, w_in, w_out, after=()):
    error_arrays, error_wheres = zip(*errors)
    input_arrays, input_wheres = zip(*inputs)
    depth, width = w_in.shape
    rows = sum(a.shape[0] for a in input_arrays)
    own = depth // members
    reach = max(m * own % 128 for m in range(members) if not m & swap) + (swap + 1) * own
    window = -(-reach // 128)
    tile = tile_of(width, 640)
    once = pl.Buffered(1)
    return call(
        functools.partial(
            gradient_kernel, (error_wheres, input_wheres), window, own, math.gcd(own, 128)
        ),
        "gradient",
        (place, *error_arrays, *input_arrays, w_in, w_out),
        [
            jax.ShapeDtypeStruct((own, width), jnp.float32),
            jax.ShapeDtypeStruct((own, width), jnp.float32),
            jax.ShapeDtypeStruct((own, width), jnp.bfloat16),
            jax.ShapeDtypeStruct((own, width), jnp.bfloat16),
        ],
        after,
        grid=(width // tile,),
        in_specs=[
            pl.BlockSpec(a.shape, whole, pipeline_mode=once)
            for a in (*error_arrays, *input_arrays)
        ]
        + [pl.BlockSpec((depth, tile), column), pl.BlockSpec((tile, depth), lambda n, s: (n, 0))],
        out_specs=[pl.BlockSpec((own, tile), column)] * 4,
        scratch_shapes=[
            pltpu.VMEM((rows, depth), jnp.bfloat16),
            pltpu.VMEM((rows, depth), jnp.bfloat16),
            pltpu.VMEM((window * 128, rows), jnp.bfloat16),
            pltpu.VMEM((window * 128, rows), jnp.bfloat16),
            pltpu.VMEM((window * 128, tile), jnp.float32),
            pltpu.VMEM((window * 128, tile), jnp.float32),
        ],
    )


def products_kernel(labels, fresh, place_ref, *refs):
    own = refs[0].shape[0]
    refs, (known_ref, out_ref, totals) = refs[:-3], refs[-3:]
    each = len(refs) // len(labels)
    slots = [refs[each * n : each * (n + 1)] for n in range(len(labels))]
    pairs = [(i, j) for i in range(len(slots) - fresh, len(slots)) for j in range(i + 1)]

    @pl.when(pl.program_id(0) == 0)
    def _():
        totals[...] = jnp.zeros_like(totals)

    def values(slot):
        return [ref[...].astype(jnp.float32) for ref in slot]

    for n, (i, j) in enumerate(pairs):
        a, b = values(slots[i]), values(slots[j])
        both = sum(u * v for u, v in zip(a, b))
        totals[n] += jnp.sum(both.reshape(own // 8, 8, -1), axis=0)

    @pl.when(pl.program_id(0) == pl.num_programs(0) - 1)
    def _():
        result = known_ref[...]
        row = lax.broadcasted_iota(jnp.int32, result.shape, 0)
        column = lax.broadcasted_iota(jnp.int32, result.shape, 1)
        for n, (i, j) in enumerate(pairs):
            i, j = (jnp.bitwise_xor(place_ref[MEMBER], labels[k]) for k in (i, j))
            here = ((row == i) & (column == j)) | ((row == j) & (column == i))
            result = result + jnp.where(here, jnp.sum(totals[n]), 0.0)
        out_ref[...] = result


def products(place, slots, labels, fresh, known, after=()):
    arrays = [a for slot in slots for a in slot]
    own, width = slots[0][0].shape
    tile = tile_of(width, 256)
    pairs = sum(len(slots) - n for n in range(fresh))
    return call(
        functools.partial(products_kernel, tuple(labels), fresh),
        "products",
        (place, *arrays, known),
        [jax.ShapeDtypeStruct(known.shape, jnp.float32)],
        after,
        grid=(width // tile,),
        in_specs=[pl.BlockSpec((a.shape[0], tile), lambda n, s: (0, n)) for a in arrays]
        + [pl.BlockSpec(known.shape, whole)],
        out_specs=[pl.BlockSpec(known.shape, whole)],
        scratch_shapes=[pltpu.VMEM((pairs, 8, tile), jnp.float32)],
    )[0]


def tree_weights(count, entry):
    def inner(a, b):
        total = 0.0
        for i, u in a.items():
            for j, v in b.items():
                total = total + u * v * entry(i, j)
        return total

    items = [{i: 1.0} for i in range(count)]
    while len(items) > 1:
        half = len(items) // 2
        merged = []
        for low, high in zip(items[:half], items[half:]):
            product = inner(low, high)
            scale_low = 1.0 - product / (2.0 * (jnp.maximum(inner(low, low), 0.0) + epsilon))
            scale_high = 1.0 - product / (2.0 * (jnp.maximum(inner(high, high), 0.0) + epsilon))
            joined = {i: u * scale_low for i, u in low.items()}
            joined.update({i: u * scale_high for i, u in high.items()})
            merged.append(joined)
        items = merged
    return [items[0][i] for i in range(count)]


def sum_kernel(place_ref, *refs):
    refs[-1][...] = sum(ref[...] for ref in refs[:-1])


def sum_of(place, parts):
    shape = parts[0].shape
    return call(
        sum_kernel,
        "sum_of",
        (place, *parts),
        [jax.ShapeDtypeStruct(shape, jnp.float32)],
        vmem=4 * 2**20,
        grid=(1,),
        in_specs=[pl.BlockSpec(shape, whole)] * len(parts),
        out_specs=[pl.BlockSpec(shape, whole)],
    )[0]


def merge_kernel(labels, place_ref, totals_ref, got_ref, *refs):
    refs, (first_ref, second_ref, weights_ref) = refs[:-3], refs[-3:]

    @pl.when(pl.program_id(0) == 0)
    def _():
        def entry(i, j):
            i, j = (jnp.bitwise_xor(place_ref[MEMBER], k) for k in (i, j))
            return totals_ref[i, j] + got_ref[i, j]

        for n, weight in enumerate(tree_weights(len(labels), entry)):
            weights_ref[n] = weight

    first = second = 0.0
    for n, label in enumerate(labels):
        weight = weights_ref[label]
        first = first + weight * refs[2 * n][...].astype(jnp.float32)
        second = second + weight * refs[2 * n + 1][...].astype(jnp.float32)
    first_ref[...] = first
    second_ref[...] = second


def merge(place, totals, got, slots, labels):
    own, width = slots[0][0].shape
    block = max(b for b in range(16, min(own, 32) + 1, 16) if own % b == 0)
    spec = pl.BlockSpec((block, width), lambda n, s: (n, 0))
    arrays = [a for slot in slots for a in slot]
    shape = jax.ShapeDtypeStruct((own, width), jnp.float32)
    return call(
        functools.partial(merge_kernel, tuple(labels)),
        "merge",
        (place, totals, got, *arrays),
        [shape, shape],
        vmem=16 * 2**20,
        grid=(own // block,),
        in_specs=[pl.BlockSpec(memory_space=pltpu.SMEM)] * 2 + [spec] * len(arrays),
        out_specs=[spec, spec],
        scratch_shapes=[pltpu.SMEM((len(slots),), jnp.float32)],
    )


def on_device(inputs, targets, w_in, w_out):
    row_count = inputs.shape[0]
    workers = lax.axis_size("dp")
    shards = lax.axis_size("tensor")
    levels = workers.bit_length() - 1
    shard_levels = shards.bit_length() - 1
    gathered = min(levels, gather_levels_limit)
    members = 2**gathered
    others = workers // members
    position = lax.axis_index("dp")
    shard = lax.axis_index("tensor")
    member = position // others

    def part_of(index):
        part = 0
        for bit in range(shard_levels):
            part = part * 2 + (index >> bit & 1)
        return part

    near = shard & 1
    part_rows = row_count // shards
    own = inputs.shape[1] // members
    swap = 1
    bits = [2**b for b in reversed(range(gathered)) if 2**b != swap]
    upper = member // swap % 2
    first_row = (member - upper * swap) * own
    place = jnp.stack(
        [
            first_row // 128,
            first_row % 128 + upper * swap * own,
            first_row % 128 + (1 - upper) * swap * own,
            member,
            near,
            1 - near,
            part_of(shard),
            part_of(shard) - near * (shards // 2),
        ]
    ).astype(jnp.int32)

    send, hidden_near, own_part = forward(place, part_rows, inputs, w_in, w_out)
    got = from_mask(send, 0, 1)
    inputs_of = {bit: from_mask(own_part, bit * others, 0) for bit in bits}

    summed = product(place, hidden_near, w_out) + got
    most = 24.0 * 0.15625 * 0.078125 * inputs.shape[1] * w_in.shape[1] * shards
    scale = 2.0 ** math.ceil(math.log2(most / 65504.0))
    sums = [summed]
    for bit in range(1, shard_levels):
        rounded = (sum(sums) * (1.0 / scale)).astype(jnp.float16)
        sums.append(from_mask(rounded, 0, 2**bit).astype(jnp.float32) * scale)
    error, error_piece = error_half(
        place,
        part_rows,
        sum(sums[:-1]),
        sums[-1],
        targets,
        tuple(inputs_of.values()),
    )
    errors_of = {
        bit: from_mask(error_piece if bit == bits[0] else error, bit * others, 0) for bit in bits
    }

    def to_half(piece, *before):
        for bit in reversed(range(1, shard_levels)):
            got = ordered(from_mask(piece, 0, 2**bit), *before)
            piece = join(shard >> bit & 1, piece, got)
        return piece

    def both_halves(half):
        return [(half, NEAR), (from_mask(half, 0, 1), FAR)]

    slots, labels, known, sent, halves = [], [], [], [], {}
    totals = jnp.zeros((8, 128), jnp.float32)
    masks = [m for m in range(members) if not m & swap]
    for n, m in enumerate(masks):
        if n == 0:
            half = error
        elif m not in (bits[0], masks[-1]):
            half = errors_of[m] = ordered(errors_of[m], sent[0], *slots[1][:1])
            other_inputs = halves[m]
        elif m == bits[0]:
            before = [sent[-1], *slots[1]]
            errors_of[m] = ordered(errors_of[m], sent[0])
            for bit in bits[1:]:
                ready = ordered(errors_of[m], errors_of[bit])
                errors_of[m | bit] = from_mask(ready, bit * others, 0)
                before.append(errors_of[m | bit])
                ready = ordered(halves[m], errors_of[bit])
                halves[m | bit] = from_mask(ready, bit * others, 0)
            half = to_half(errors_of[m], *before)
            other_inputs = halves[m]
        else:
            half = to_half(ordered(errors_of[m], sent[-2]), sent[-1], *slots[2 * n - 3])
            other_inputs = ordered(halves[m], sent[-1])
        first, second, *send = gradient(
            place,
            members,
            swap,
            both_halves(half),
            both_halves(other_inputs) if n else [(inputs, None)],
            w_in,
            w_out,
            known[-2:-1],
        )
        if n == 0:
            for bit in bits:
                halves[bit] = to_half(inputs_of[bit], send[0], errors_of[bits[0]], *halves.values())
        sent.append(send[0])
        slots.append((first, second))
        labels.append(m)
        last = n == len(masks) - 1
        if last:
            totals = products(place, slots, labels, 1, totals)
        slots.append(tuple(from_mask(a, swap * others, 0) for a in send))
        labels.append(m ^ swap)
        if last:
            for k in range(2):
                totals = products(place, [slot[k : k + 1] for slot in slots], labels, 1, totals)
        else:
            totals = products(place, slots, labels, 2, totals)
        known.append(totals)

    rounds = [[(0, mask) for mask in range(1, shards)]]
    rounds.append([(m * others, 0) for m in range(2, members, 2)])
    for partners in rounds:
        totals = sum_of(place, [totals] + [from_mask(totals, *mask) for mask in partners])
    pieces = merge(place, totals, from_mask(totals, others, 0), slots, labels)

    for section in range(gathered, levels):
        upper_flag = position >> levels - 1 - section & 1
        keep_first, send_first = split_piece(pieces[0], upper_flag)
        keep_second, send_second = split_piece(pieces[1], upper_flag)
        got_first, got_second = from_partner((send_first, send_second), "dp", levels - 1 - section)
        pieces = combine(
            (keep_first, keep_second), (got_first, got_second), upper_flag, section, levels
        )
    return (pieces[0], pieces[1])


def solution(mesh):
    placed = (P("dp", None), P("dp", None), P(None, "tensor"), P("tensor", None))
    return jax.shard_map(
        on_device,
        mesh=mesh,
        in_specs=placed,
        out_specs=(P("dp", "tensor"), P("dp", "tensor")),
        check_vma=False,
    )
```

```python
import functools
import math

import jax
import jax.numpy as jnp
from jax import lax
from jax.experimental import pallas as pl
from jax.experimental.pallas import tpu as pltpu
from jax.sharding import PartitionSpec as P

epsilon = 1e-06
gather_levels_limit = 3
vmem_bytes = 36 * 2**20
vmem_most = 60 * 2**20


def from_partner(value, axis, distance):
    mask = 2**distance
    pairs = [(source, source ^ mask) for source in range(lax.axis_size(axis))]
    return lax.ppermute(value, axis, pairs)


def from_mask(value, dp_mask, tensor_mask):
    shards = lax.axis_size("tensor")
    mask = dp_mask * shards + tensor_mask
    pairs = [(source, source ^ mask) for source in range(lax.axis_size("dp") * shards)]
    return lax.ppermute(value, ("dp", "tensor"), pairs)


def ordered(value, *before):
    return lax.optimization_barrier((value, *before))[0]


def split_piece(piece, upper_flag):
    half = piece.shape[0] // 2
    keep = lax.dynamic_slice_in_dim(piece, upper_flag * half, half, 0)
    send = lax.dynamic_slice_in_dim(piece, (1 - upper_flag) * half, half, 0)
    return (keep, send)


def group_total(values, section, levels):
    summed = lax.psum(values, "tensor")
    for offset in range(section + 1):
        summed = summed + from_partner(summed, "dp", levels - 1 - offset)
    return summed


def combine(own, incoming, upper_flag, section, levels):
    product = jnp.sum(own[0] * incoming[0]) + jnp.sum(own[1] * incoming[1])
    norm_own = jnp.sum(own[0] * own[0]) + jnp.sum(own[1] * own[1])
    norm_incoming = jnp.sum(incoming[0] * incoming[0]) + jnp.sum(incoming[1] * incoming[1])
    is_upper = upper_flag == 1
    norm_low = jnp.where(is_upper, norm_incoming, norm_own)
    norm_high = jnp.where(is_upper, norm_own, norm_incoming)
    totals = group_total(jnp.stack([product, norm_low, norm_high]), section, levels)
    coef_low = 1.0 - totals[0] / (2.0 * (totals[1] + epsilon))
    coef_high = 1.0 - totals[0] / (2.0 * (totals[2] + epsilon))
    coef_own = jnp.where(is_upper, coef_high, coef_low)
    coef_incoming = jnp.where(is_upper, coef_low, coef_high)
    return (
        coef_own * own[0] + coef_incoming * incoming[0],
        coef_own * own[1] + coef_incoming * incoming[1],
    )


def tile_of(size, limit):
    return max(b for b in range(128, limit + 1, 128) if size % b == 0)


def contract(left, right, left_dim, right_dim):
    dims = (((left_dim,), (right_dim,)), ((), ()))
    return lax.dot_general(left, right, dims, preferred_element_type=jnp.float32)


def call(kernel, name, operands, shapes, after=(), vmem=vmem_bytes, **spec):
    spec["in_specs"] = [pl.BlockSpec(memory_space=pl.ANY)] * len(after) + spec["in_specs"]

    def body(place_ref, *refs):
        kernel(place_ref, *refs[len(after) :])

    return pl.pallas_call(
        body,
        grid_spec=pltpu.PrefetchScalarGridSpec(num_scalar_prefetch=1, **spec),
        out_shape=shapes,
        compiler_params=pltpu.CompilerParams(vmem_limit_bytes=vmem),
        cost_estimate=pl.CostEstimate(flops=1, bytes_accessed=1, transcendentals=0),
        name=name,
    )(operands[0], *after, *operands[1:])


WINDOW, SHIFT, OTHER_SHIFT, MEMBER, NEAR, FAR, PART, PIECE = range(8)


def row_start(place_ref, block, where):
    return 0 if where is None else pl.multiple_of(place_ref[where] * block.shape[0], 16)


def whole(n, s):
    return (0, 0)


def column(n, s):
    return (0, n)


SCALE = math.sqrt(2.0 / math.pi)
CUBE = 0.044715


def forward_kernel(
    steps, place_ref, rows_ref, w_in_ref, w_out_ref, out_ref, near_ref, part_ref, hidden
):
    step = pl.program_id(0)
    half = out_ref.shape[0]
    far = pl.ds(row_start(place_ref, out_ref, FAR), half)
    tile = w_in_ref.shape[1]

    for n in range(steps):

        @pl.when(step == n)
        def _():
            v = jnp.dot(rows_ref[...], w_in_ref[...], preferred_element_type=jnp.float32)
            t = jnp.tanh(v * (SCALE + (SCALE * CUBE) * (v * v)))
            hidden[:, n * tile : (n + 1) * tile] = (v * (0.5 + 0.5 * t)).astype(jnp.bfloat16)

    @pl.when(step == 0)
    def _():
        part_ref[...] = rows_ref[pl.ds(row_start(place_ref, part_ref, PART), part_ref.shape[0]), :]

    @pl.when(step == steps)
    def _():
        near_ref[...] = hidden[pl.ds(row_start(place_ref, out_ref, NEAR), half), :]

    @pl.when(step >= steps)
    def _():
        out_ref[...] = jnp.dot(hidden[far, :], w_out_ref[...], preferred_element_type=jnp.float32)


def forward(place, part_rows, inputs, w_in, w_out):
    rows = inputs.shape[0]
    depth, width = w_in.shape
    tile, out_tile = tile_of(width, 256), tile_of(depth, 640)
    steps = width // tile
    last = lambda n: jnp.maximum(n - steps, 0)
    return call(
        functools.partial(forward_kernel, steps),
        "forward",
        (place, inputs, w_in, w_out),
        [
            jax.ShapeDtypeStruct((rows // 2, depth), jnp.float32),
            jax.ShapeDtypeStruct((rows // 2, width), jnp.bfloat16),
            jax.ShapeDtypeStruct((part_rows, depth), jnp.bfloat16),
        ],
        vmem=vmem_most,
        grid=(steps + depth // out_tile,),
        in_specs=[
            pl.BlockSpec((rows, depth), whole),
            pl.BlockSpec((depth, tile), lambda n, s: (0, jnp.minimum(n, steps - 1))),
            pl.BlockSpec((width, out_tile), lambda n, s: (0, last(n))),
        ],
        out_specs=[
            pl.BlockSpec((rows // 2, out_tile), lambda n, s: (0, last(n))),
            pl.BlockSpec((rows // 2, width), whole),
            pl.BlockSpec((part_rows, depth), whole),
        ],
        scratch_shapes=[pltpu.VMEM((rows, width), jnp.bfloat16)],
    )


def product_kernel(place_ref, left_ref, right_ref, out_ref):
    out_ref[...] = jnp.dot(left_ref[...], right_ref[...], preferred_element_type=jnp.float32)


def product(place, left, right):
    rows, depth = left.shape
    width = right.shape[1]
    tile = tile_of(width, 640)
    return call(
        product_kernel,
        "product",
        (place, left, right),
        [jax.ShapeDtypeStruct((rows, width), jnp.float32)],
        grid=(width // tile,),
        in_specs=[pl.BlockSpec((rows, depth), whole), pl.BlockSpec((depth, tile), column)],
        out_specs=[pl.BlockSpec((rows, tile), column)],
    )[0]


def join_kernel(place_ref, own_ref, got_ref, out_ref):
    rows = own_ref.shape[0]
    out_ref[pl.ds(pl.multiple_of(place_ref[0] * rows, 16), rows), :] = own_ref[...]
    out_ref[pl.ds(pl.multiple_of((1 - place_ref[0]) * rows, 16), rows), :] = got_ref[...]


def join(flag, own, got):
    rows, depth = own.shape
    return call(
        join_kernel,
        "join",
        (flag.reshape(1), own, got),
        [jax.ShapeDtypeStruct((2 * rows, depth), own.dtype)],
        grid=(1,),
        in_specs=[pl.BlockSpec((rows, depth), whole)] * 2,
        out_specs=[pl.BlockSpec((2 * rows, depth), whole)],
    )[0]


def error_kernel(row_count, place_ref, own_ref, got_ref, targets_ref, half_ref, part_ref):
    out = own_ref[...] + got_ref[...]
    error = (out - targets_ref[...].astype(jnp.float32)) / row_count
    half_ref[...] = error.astype(jnp.bfloat16)
    rows = part_ref.shape[0]
    part_ref[...] = half_ref[pl.ds(pl.multiple_of(place_ref[PIECE] * rows, 16), rows), :]


def error_half(place, part_rows, own, got, targets, after):
    rows, depth = own.shape
    return call(
        functools.partial(error_kernel, targets.shape[0]),
        "error_half",
        (place, own, got, targets),
        [
            jax.ShapeDtypeStruct((rows, depth), jnp.bfloat16),
            jax.ShapeDtypeStruct((part_rows, depth), jnp.bfloat16),
        ],
        after,
        grid=(1,),
        in_specs=[
            pl.BlockSpec((rows, depth), whole),
            pl.BlockSpec((rows, depth), whole),
            pl.BlockSpec((rows, depth), lambda n, s: (s[NEAR], 0)),
        ],
        out_specs=[pl.BlockSpec((rows, depth), whole), pl.BlockSpec((part_rows, depth), whole)],
    )


def gradient_kernel(wheres, window, own, step_rows, place_ref, *refs):
    error_wheres, input_wheres = wheres
    refs = list(refs)

    def take(n):
        taken = refs[:n]
        del refs[:n]
        return taken

    error_refs, input_refs = take(len(error_wheres)), take(len(input_wheres))
    w_in_ref, w_out_ref, first_ref, second_ref, send_first_ref, send_second_ref = take(6)
    errors, inputs, inputs_turned, errors_turned, spread_first, spread_second = refs
    if len(input_refs) == 1:
        inputs = input_refs[0]

    @pl.when(pl.program_id(0) == 0)
    def _():
        for block, where in zip(error_refs, error_wheres):
            errors[pl.ds(row_start(place_ref, block, where), block.shape[0]), :] = block[...]
        if len(input_refs) > 1:
            for block, where in zip(input_refs, input_wheres):
                inputs[pl.ds(row_start(place_ref, block, where), block.shape[0]), :] = block[...]
        lane = pl.multiple_of(place_ref[WINDOW] * 128, 128)
        inputs_turned[...] = inputs[:, pl.ds(lane, window * 128)].T
        errors_turned[...] = errors[:, pl.ds(lane, window * 128)].T

    shift = pl.multiple_of(place_ref[SHIFT], step_rows)
    other_shift = pl.multiple_of(place_ref[OTHER_SHIFT], step_rows)
    v = jnp.dot(inputs[...], w_in_ref[...], preferred_element_type=jnp.float32)
    back = lax.dot_general(
        errors[...], w_out_ref[...], (((1,), (1,)), ((), ())), preferred_element_type=jnp.float32
    )
    square = v * v
    t = jnp.tanh(v * (SCALE + (SCALE * CUBE) * square))
    upper = 0.5 + 0.5 * t
    hidden = (v * upper).astype(jnp.bfloat16)
    spread_second[...] = jnp.dot(errors_turned[...], hidden, preferred_element_type=jnp.float32)
    slope = upper + (0.5 * v) * (1.0 - t * t) * (SCALE + (3.0 * SCALE * CUBE) * square)
    dpre = (back * slope).astype(jnp.bfloat16)
    spread_first[...] = jnp.dot(inputs_turned[...], dpre, preferred_element_type=jnp.float32)
    second_ref[...] = spread_second[pl.ds(shift, own), :]
    send_second_ref[...] = spread_second[pl.ds(other_shift, own), :].astype(jnp.bfloat16)
    first_ref[...] = spread_first[pl.ds(shift, own), :]
    send_first_ref[...] = spread_first[pl.ds(other_shift, own), :].astype(jnp.bfloat16)


def gradient(place, members, swap, errors, inputs, w_in, w_out, after=()):
    error_arrays, error_wheres = zip(*errors)
    input_arrays, input_wheres = zip(*inputs)
    depth, width = w_in.shape
    rows = sum(a.shape[0] for a in input_arrays)
    own = depth // members
    reach = max(m * own % 128 for m in range(members) if not m & swap) + (swap + 1) * own
    window = -(-reach // 128)
    tile = tile_of(width, 640)
    once = pl.Buffered(1)
    return call(
        functools.partial(
            gradient_kernel, (error_wheres, input_wheres), window, own, math.gcd(own, 128)
        ),
        "gradient",
        (place, *error_arrays, *input_arrays, w_in, w_out),
        [
            jax.ShapeDtypeStruct((own, width), jnp.float32),
            jax.ShapeDtypeStruct((own, width), jnp.float32),
            jax.ShapeDtypeStruct((own, width), jnp.bfloat16),
            jax.ShapeDtypeStruct((own, width), jnp.bfloat16),
        ],
        after,
        grid=(width // tile,),
        in_specs=[
            pl.BlockSpec(a.shape, whole, pipeline_mode=once)
            for a in (*error_arrays, *input_arrays)
        ]
        + [pl.BlockSpec((depth, tile), column), pl.BlockSpec((tile, depth), lambda n, s: (n, 0))],
        out_specs=[pl.BlockSpec((own, tile), column)] * 4,
        scratch_shapes=[
            pltpu.VMEM((rows, depth), jnp.bfloat16),
            pltpu.VMEM((rows, depth), jnp.bfloat16),
            pltpu.VMEM((window * 128, rows), jnp.bfloat16),
            pltpu.VMEM((window * 128, rows), jnp.bfloat16),
            pltpu.VMEM((window * 128, tile), jnp.float32),
            pltpu.VMEM((window * 128, tile), jnp.float32),
        ],
    )


def products_kernel(labels, fresh, place_ref, *refs):
    own = refs[0].shape[0]
    refs, (known_ref, out_ref, totals) = refs[:-3], refs[-3:]
    each = len(refs) // len(labels)
    slots = [refs[each * n : each * (n + 1)] for n in range(len(labels))]
    pairs = [(i, j) for i in range(len(slots) - fresh, len(slots)) for j in range(i + 1)]

    @pl.when(pl.program_id(0) == 0)
    def _():
        totals[...] = jnp.zeros_like(totals)

    def values(slot):
        return [ref[...].astype(jnp.float32) for ref in slot]

    for n, (i, j) in enumerate(pairs):
        a, b = values(slots[i]), values(slots[j])
        both = sum(u * v for u, v in zip(a, b))
        totals[n] += jnp.sum(both.reshape(own // 8, 8, -1), axis=0)

    @pl.when(pl.program_id(0) == pl.num_programs(0) - 1)
    def _():
        result = known_ref[...]
        row = lax.broadcasted_iota(jnp.int32, result.shape, 0)
        column = lax.broadcasted_iota(jnp.int32, result.shape, 1)
        for n, (i, j) in enumerate(pairs):
            i, j = (jnp.bitwise_xor(place_ref[MEMBER], labels[k]) for k in (i, j))
            here = ((row == i) & (column == j)) | ((row == j) & (column == i))
            result = result + jnp.where(here, jnp.sum(totals[n]), 0.0)
        out_ref[...] = result


def products(place, slots, labels, fresh, known, after=()):
    arrays = [a for slot in slots for a in slot]
    own, width = slots[0][0].shape
    tile = tile_of(width, 256)
    pairs = sum(len(slots) - n for n in range(fresh))
    return call(
        functools.partial(products_kernel, tuple(labels), fresh),
        "products",
        (place, *arrays, known),
        [jax.ShapeDtypeStruct(known.shape, jnp.float32)],
        after,
        grid=(width // tile,),
        in_specs=[pl.BlockSpec((a.shape[0], tile), lambda n, s: (0, n)) for a in arrays]
        + [pl.BlockSpec(known.shape, whole)],
        out_specs=[pl.BlockSpec(known.shape, whole)],
        scratch_shapes=[pltpu.VMEM((pairs, 8, tile), jnp.float32)],
    )[0]


def tree_weights(count, entry):
    def inner(a, b):
        total = 0.0
        for i, u in a.items():
            for j, v in b.items():
                total = total + u * v * entry(i, j)
        return total

    items = [{i: 1.0} for i in range(count)]
    while len(items) > 1:
        half = len(items) // 2
        merged = []
        for low, high in zip(items[:half], items[half:]):
            product = inner(low, high)
            scale_low = 1.0 - product / (2.0 * (jnp.maximum(inner(low, low), 0.0) + epsilon))
            scale_high = 1.0 - product / (2.0 * (jnp.maximum(inner(high, high), 0.0) + epsilon))
            joined = {i: u * scale_low for i, u in low.items()}
            joined.update({i: u * scale_high for i, u in high.items()})
            merged.append(joined)
        items = merged
    return [items[0][i] for i in range(count)]


def sum_kernel(place_ref, *refs):
    refs[-1][...] = sum(ref[...] for ref in refs[:-1])


def sum_of(place, parts):
    shape = parts[0].shape
    return call(
        sum_kernel,
        "sum_of",
        (place, *parts),
        [jax.ShapeDtypeStruct(shape, jnp.float32)],
        vmem=4 * 2**20,
        grid=(1,),
        in_specs=[pl.BlockSpec(shape, whole)] * len(parts),
        out_specs=[pl.BlockSpec(shape, whole)],
    )[0]


def merge_kernel(labels, place_ref, totals_ref, got_ref, *refs):
    refs, (first_ref, second_ref, weights_ref) = refs[:-3], refs[-3:]

    @pl.when(pl.program_id(0) == 0)
    def _():
        def entry(i, j):
            i, j = (jnp.bitwise_xor(place_ref[MEMBER], k) for k in (i, j))
            return totals_ref[i, j] + got_ref[i, j]

        for n, weight in enumerate(tree_weights(len(labels), entry)):
            weights_ref[n] = weight

    first = second = 0.0
    for n, label in enumerate(labels):
        weight = weights_ref[label]
        first = first + weight * refs[2 * n][...].astype(jnp.float32)
        second = second + weight * refs[2 * n + 1][...].astype(jnp.float32)
    first_ref[...] = first
    second_ref[...] = second


def merge(place, totals, got, slots, labels):
    own, width = slots[0][0].shape
    block = max(b for b in range(16, min(own, 32) + 1, 16) if own % b == 0)
    spec = pl.BlockSpec((block, width), lambda n, s: (n, 0))
    arrays = [a for slot in slots for a in slot]
    shape = jax.ShapeDtypeStruct((own, width), jnp.float32)
    return call(
        functools.partial(merge_kernel, tuple(labels)),
        "merge",
        (place, totals, got, *arrays),
        [shape, shape],
        vmem=16 * 2**20,
        grid=(own // block,),
        in_specs=[pl.BlockSpec(memory_space=pltpu.SMEM)] * 2 + [spec] * len(arrays),
        out_specs=[spec, spec],
        scratch_shapes=[pltpu.SMEM((len(slots),), jnp.float32)],
    )


def on_device(inputs, targets, w_in, w_out):
    row_count = inputs.shape[0]
    workers = lax.axis_size("dp")
    shards = lax.axis_size("tensor")
    levels = workers.bit_length() - 1
    shard_levels = shards.bit_length() - 1
    gathered = min(levels, gather_levels_limit)
    members = 2**gathered
    others = workers // members
    position = lax.axis_index("dp")
    shard = lax.axis_index("tensor")
    member = position // others

    def part_of(index):
        part = 0
        for bit in range(shard_levels):
            part = part * 2 + (index >> bit & 1)
        return part

    near = shard & 1
    part_rows = row_count // shards
    own = inputs.shape[1] // members
    swap = 1
    bits = [2**b for b in reversed(range(gathered)) if 2**b != swap]
    upper = member // swap % 2
    first_row = (member - upper * swap) * own
    place = jnp.stack(
        [
            first_row // 128,
            first_row % 128 + upper * swap * own,
            first_row % 128 + (1 - upper) * swap * own,
            member,
            near,
            1 - near,
            part_of(shard),
            part_of(shard) - near * (shards // 2),
        ]
    ).astype(jnp.int32)

    send, hidden_near, own_part = forward(place, part_rows, inputs, w_in, w_out)
    got = from_mask(send, 0, 1)
    inputs_of = {bit: from_mask(own_part, bit * others, 0) for bit in bits}

    summed = product(place, hidden_near, w_out) + got
    most = 24.0 * 0.15625 * 0.078125 * inputs.shape[1] * w_in.shape[1] * shards
    scale = 2.0 ** math.ceil(math.log2(most / 65504.0))
    sums = [summed]
    for bit in range(1, shard_levels):
        rounded = (sum(sums) * (1.0 / scale)).astype(jnp.float16)
        sums.append(from_mask(rounded, 0, 2**bit).astype(jnp.float32) * scale)
    error, error_piece = error_half(
        place,
        part_rows,
        sum(sums[:-1]),
        sums[-1],
        targets,
        tuple(inputs_of.values()),
    )
    errors_of = {
        bit: from_mask(error_piece if bit == bits[0] else error, bit * others, 0) for bit in bits
    }

    def to_half(piece, *before):
        for bit in reversed(range(1, shard_levels)):
            got = ordered(from_mask(piece, 0, 2**bit), *before)
            piece = join(shard >> bit & 1, piece, got)
        return piece

    def both_halves(half):
        return [(half, NEAR), (from_mask(half, 0, 1), FAR)]

    slots, labels, known, sent, halves = [], [], [], [], {}
    totals = jnp.zeros((8, 128), jnp.float32)
    masks = [m for m in range(members) if not m & swap]
    for n, m in enumerate(masks):
        if n == 0:
            half = error
        elif m not in (bits[0], masks[-1]):
            half = errors_of[m] = ordered(errors_of[m], sent[0], *slots[1][:1])
            other_inputs = halves[m]
        elif m == bits[0]:
            before = [sent[-1], *slots[1]]
            errors_of[m] = ordered(errors_of[m], sent[0])
            for bit in bits[1:]:
                ready = ordered(errors_of[m], errors_of[bit])
                errors_of[m | bit] = from_mask(ready, bit * others, 0)
                before.append(errors_of[m | bit])
                ready = ordered(halves[m], errors_of[bit])
                halves[m | bit] = from_mask(ready, bit * others, 0)
            half = to_half(errors_of[m], *before)
            other_inputs = halves[m]
        else:
            half = to_half(ordered(errors_of[m], sent[-2]), sent[-1], *slots[2 * n - 3])
            other_inputs = ordered(halves[m], sent[-1])
        first, second, *send = gradient(
            place,
            members,
            swap,
            both_halves(half),
            both_halves(other_inputs) if n else [(inputs, None)],
            w_in,
            w_out,
            known[-2:-1],
        )
        if n == 0:
            for bit in bits:
                halves[bit] = to_half(inputs_of[bit], send[0], errors_of[bits[0]], *halves.values())
        sent.append(send[0])
        slots.append((first, second))
        labels.append(m)
        last = n == len(masks) - 1
        if last:
            totals = products(place, slots, labels, 1, totals)
        slots.append(tuple(from_mask(a, swap * others, 0) for a in send))
        labels.append(m ^ swap)
        if last:
            for k in range(2):
                totals = products(place, [slot[k : k + 1] for slot in slots], labels, 1, totals)
        else:
            totals = products(place, slots, labels, 2, totals)
        known.append(totals)

    rounds = [[(0, mask) for mask in range(1, shards)]]
    rounds.append([(m * others, 0) for m in range(2, members, 2)])
    for partners in rounds:
        totals = sum_of(place, [totals] + [from_mask(totals, *mask) for mask in partners])
    pieces = merge(place, totals, from_mask(totals, others, 0), slots, labels)

    for section in range(gathered, levels):
        upper_flag = position >> levels - 1 - section & 1
        keep_first, send_first = split_piece(pieces[0], upper_flag)
        keep_second, send_second = split_piece(pieces[1], upper_flag)
        got_first, got_second = from_partner((send_first, send_second), "dp", levels - 1 - section)
        pieces = combine(
            (keep_first, keep_second), (got_first, got_second), upper_flag, section, levels
        )
    return (pieces[0], pieces[1])


def solution(mesh):
    placed = (P("dp", None), P("dp", None), P(None, "tensor"), P("tensor", None))
    return jax.shard_map(
        on_device,
        mesh=mesh,
        in_specs=placed,
        out_specs=(P("dp", "tensor"), P("dp", "tensor")),
        check_vma=False,
    )
```

```python
import functools
import math

import jax
import jax.numpy as jnp
from jax import lax
from jax.experimental import pallas as pl
from jax.experimental.pallas import tpu as pltpu
from jax.sharding import PartitionSpec as P

epsilon = 1e-06
gather_levels_limit = 3
vmem_bytes = 36 * 2**20
vmem_most = 60 * 2**20


def from_partner(value, axis, distance):
    mask = 2**distance
    pairs = [(source, source ^ mask) for source in range(lax.axis_size(axis))]
    return lax.ppermute(value, axis, pairs)


def from_mask(value, dp_mask, tensor_mask):
    shards = lax.axis_size("tensor")
    mask = dp_mask * shards + tensor_mask
    pairs = [(source, source ^ mask) for source in range(lax.axis_size("dp") * shards)]
    return lax.ppermute(value, ("dp", "tensor"), pairs)


def ordered(value, *before):
    return lax.optimization_barrier((value, *before))[0]


def split_piece(piece, upper_flag):
    half = piece.shape[0] // 2
    keep = lax.dynamic_slice_in_dim(piece, upper_flag * half, half, 0)
    send = lax.dynamic_slice_in_dim(piece, (1 - upper_flag) * half, half, 0)
    return (keep, send)


def group_total(values, section, levels):
    summed = lax.psum(values, "tensor")
    for offset in range(section + 1):
        summed = summed + from_partner(summed, "dp", levels - 1 - offset)
    return summed


def combine(own, incoming, upper_flag, section, levels):
    product = jnp.sum(own[0] * incoming[0]) + jnp.sum(own[1] * incoming[1])
    norm_own = jnp.sum(own[0] * own[0]) + jnp.sum(own[1] * own[1])
    norm_incoming = jnp.sum(incoming[0] * incoming[0]) + jnp.sum(incoming[1] * incoming[1])
    is_upper = upper_flag == 1
    norm_low = jnp.where(is_upper, norm_incoming, norm_own)
    norm_high = jnp.where(is_upper, norm_own, norm_incoming)
    totals = group_total(jnp.stack([product, norm_low, norm_high]), section, levels)
    coef_low = 1.0 - totals[0] / (2.0 * (totals[1] + epsilon))
    coef_high = 1.0 - totals[0] / (2.0 * (totals[2] + epsilon))
    coef_own = jnp.where(is_upper, coef_high, coef_low)
    coef_incoming = jnp.where(is_upper, coef_low, coef_high)
    return (
        coef_own * own[0] + coef_incoming * incoming[0],
        coef_own * own[1] + coef_incoming * incoming[1],
    )


def tile_of(size, limit):
    return max(b for b in range(128, limit + 1, 128) if size % b == 0)


def contract(left, right, left_dim, right_dim):
    dims = (((left_dim,), (right_dim,)), ((), ()))
    return lax.dot_general(left, right, dims, preferred_element_type=jnp.float32)


def call(kernel, name, operands, shapes, after=(), vmem=vmem_bytes, **spec):
    spec["in_specs"] = [pl.BlockSpec(memory_space=pl.ANY)] * len(after) + spec["in_specs"]

    def body(place_ref, *refs):
        kernel(place_ref, *refs[len(after) :])

    return pl.pallas_call(
        body,
        grid_spec=pltpu.PrefetchScalarGridSpec(num_scalar_prefetch=1, **spec),
        out_shape=shapes,
        compiler_params=pltpu.CompilerParams(vmem_limit_bytes=vmem),
        cost_estimate=pl.CostEstimate(flops=1, bytes_accessed=1, transcendentals=0),
        name=name,
    )(operands[0], *after, *operands[1:])


WINDOW, SHIFT, OTHER_SHIFT, MEMBER, NEAR, FAR, PART, PIECE = range(8)


def row_start(place_ref, block, where):
    return 0 if where is None else pl.multiple_of(place_ref[where] * block.shape[0], 16)


def whole(n, s):
    return (0, 0)


def column(n, s):
    return (0, n)


SCALE = math.sqrt(2.0 / math.pi)
CUBE = 0.044715


def forward_kernel(
    steps, place_ref, rows_ref, w_in_ref, w_out_ref, out_ref, near_ref, part_ref, hidden
):
    step = pl.program_id(0)
    half = out_ref.shape[0]
    far = pl.ds(row_start(place_ref, out_ref, FAR), half)
    tile = w_in_ref.shape[1]

    for n in range(steps):

        @pl.when(step == n)
        def _():
            v = jnp.dot(rows_ref[...], w_in_ref[...], preferred_element_type=jnp.float32)
            t = jnp.tanh(v * (SCALE + (SCALE * CUBE) * (v * v)))
            hidden[:, n * tile : (n + 1) * tile] = (v * (0.5 + 0.5 * t)).astype(jnp.bfloat16)

    @pl.when(step == 0)
    def _():
        part_ref[...] = rows_ref[pl.ds(row_start(place_ref, part_ref, PART), part_ref.shape[0]), :]

    @pl.when(step == steps)
    def _():
        near_ref[...] = hidden[pl.ds(row_start(place_ref, out_ref, NEAR), half), :]

    @pl.when(step >= steps)
    def _():
        out_ref[...] = jnp.dot(hidden[far, :], w_out_ref[...], preferred_element_type=jnp.float32)


def forward(place, part_rows, inputs, w_in, w_out):
    rows = inputs.shape[0]
    depth, width = w_in.shape
    tile, out_tile = tile_of(width, 640), tile_of(depth, 640)
    steps = width // tile
    last = lambda n: jnp.maximum(n - steps, 0)
    return call(
        functools.partial(forward_kernel, steps),
        "forward",
        (place, inputs, w_in, w_out),
        [
            jax.ShapeDtypeStruct((rows // 2, depth), jnp.float32),
            jax.ShapeDtypeStruct((rows // 2, width), jnp.bfloat16),
            jax.ShapeDtypeStruct((part_rows, depth), jnp.bfloat16),
        ],
        vmem=vmem_most,
        grid=(steps + depth // out_tile,),
        in_specs=[
            pl.BlockSpec((rows, depth), whole),
            pl.BlockSpec((depth, tile), lambda n, s: (0, jnp.minimum(n, steps - 1))),
            pl.BlockSpec((width, out_tile), lambda n, s: (0, last(n))),
        ],
        out_specs=[
            pl.BlockSpec((rows // 2, out_tile), lambda n, s: (0, last(n))),
            pl.BlockSpec((rows // 2, width), whole),
            pl.BlockSpec((part_rows, depth), whole),
        ],
        scratch_shapes=[pltpu.VMEM((rows, width), jnp.bfloat16)],
    )


def product_kernel(place_ref, left_ref, right_ref, out_ref):
    out_ref[...] = jnp.dot(left_ref[...], right_ref[...], preferred_element_type=jnp.float32)


def product(place, left, right):
    rows, depth = left.shape
    width = right.shape[1]
    tile = tile_of(width, 640)
    return call(
        product_kernel,
        "product",
        (place, left, right),
        [jax.ShapeDtypeStruct((rows, width), jnp.float32)],
        vmem=vmem_most,
        grid=(width // tile,),
        in_specs=[pl.BlockSpec((rows, depth), whole), pl.BlockSpec((depth, tile), column)],
        out_specs=[pl.BlockSpec((rows, tile), column)],
    )[0]


def join_kernel(place_ref, own_ref, got_ref, out_ref):
    rows = own_ref.shape[0]
    out_ref[pl.ds(pl.multiple_of(place_ref[0] * rows, 16), rows), :] = own_ref[...]
    out_ref[pl.ds(pl.multiple_of((1 - place_ref[0]) * rows, 16), rows), :] = got_ref[...]


def join(flag, own, got):
    rows, depth = own.shape
    return call(
        join_kernel,
        "join",
        (flag.reshape(1), own, got),
        [jax.ShapeDtypeStruct((2 * rows, depth), own.dtype)],
        grid=(1,),
        in_specs=[pl.BlockSpec((rows, depth), whole)] * 2,
        out_specs=[pl.BlockSpec((2 * rows, depth), whole)],
    )[0]


def error_kernel(row_count, place_ref, own_ref, got_ref, targets_ref, half_ref, part_ref):
    out = own_ref[...] + got_ref[...]
    error = (out - targets_ref[...].astype(jnp.float32)) / row_count
    half_ref[...] = error.astype(jnp.bfloat16)
    rows = part_ref.shape[0]
    part_ref[...] = half_ref[pl.ds(pl.multiple_of(place_ref[PIECE] * rows, 16), rows), :]


def error_half(place, part_rows, own, got, targets, after):
    rows, depth = own.shape
    return call(
        functools.partial(error_kernel, targets.shape[0]),
        "error_half",
        (place, own, got, targets),
        [
            jax.ShapeDtypeStruct((rows, depth), jnp.bfloat16),
            jax.ShapeDtypeStruct((part_rows, depth), jnp.bfloat16),
        ],
        after,
        grid=(1,),
        in_specs=[
            pl.BlockSpec((rows, depth), whole),
            pl.BlockSpec((rows, depth), whole),
            pl.BlockSpec((rows, depth), lambda n, s: (s[NEAR], 0)),
        ],
        out_specs=[pl.BlockSpec((rows, depth), whole), pl.BlockSpec((part_rows, depth), whole)],
    )


def gradient_kernel(wheres, window, own, step_rows, place_ref, *refs):
    error_wheres, input_wheres = wheres
    refs = list(refs)

    def take(n):
        taken = refs[:n]
        del refs[:n]
        return taken

    error_refs, input_refs = take(len(error_wheres)), take(len(input_wheres))
    w_in_ref, w_out_ref, first_ref, second_ref, send_first_ref, send_second_ref = take(6)
    errors, inputs, inputs_turned, errors_turned, spread_first, spread_second = refs
    if len(input_refs) == 1:
        inputs = input_refs[0]

    @pl.when(pl.program_id(0) == 0)
    def _():
        for block, where in zip(error_refs, error_wheres):
            errors[pl.ds(row_start(place_ref, block, where), block.shape[0]), :] = block[...]
        if len(input_refs) > 1:
            for block, where in zip(input_refs, input_wheres):
                inputs[pl.ds(row_start(place_ref, block, where), block.shape[0]), :] = block[...]
        lane = pl.multiple_of(place_ref[WINDOW] * 128, 128)
        inputs_turned[...] = inputs[:, pl.ds(lane, window * 128)].T
        errors_turned[...] = errors[:, pl.ds(lane, window * 128)].T

    shift = pl.multiple_of(place_ref[SHIFT], step_rows)
    other_shift = pl.multiple_of(place_ref[OTHER_SHIFT], step_rows)
    v = jnp.dot(inputs[...], w_in_ref[...], preferred_element_type=jnp.float32)
    back = lax.dot_general(
        errors[...], w_out_ref[...], (((1,), (1,)), ((), ())), preferred_element_type=jnp.float32
    )
    square = v * v
    t = jnp.tanh(v * (SCALE + (SCALE * CUBE) * square))
    upper = 0.5 + 0.5 * t
    hidden = (v * upper).astype(jnp.bfloat16)
    spread_second[...] = jnp.dot(errors_turned[...], hidden, preferred_element_type=jnp.float32)
    slope = upper + (0.5 * v) * (1.0 - t * t) * (SCALE + (3.0 * SCALE * CUBE) * square)
    dpre = (back * slope).astype(jnp.bfloat16)
    spread_first[...] = jnp.dot(inputs_turned[...], dpre, preferred_element_type=jnp.float32)
    second_ref[...] = spread_second[pl.ds(shift, own), :]
    send_second_ref[...] = spread_second[pl.ds(other_shift, own), :].astype(jnp.bfloat16)
    first_ref[...] = spread_first[pl.ds(shift, own), :]
    send_first_ref[...] = spread_first[pl.ds(other_shift, own), :].astype(jnp.bfloat16)


def gradient(place, members, swap, errors, inputs, w_in, w_out, after=()):
    error_arrays, error_wheres = zip(*errors)
    input_arrays, input_wheres = zip(*inputs)
    depth, width = w_in.shape
    rows = sum(a.shape[0] for a in input_arrays)
    own = depth // members
    reach = max(m * own % 128 for m in range(members) if not m & swap) + (swap + 1) * own
    window = -(-reach // 128)
    tile = tile_of(width, 640)
    once = pl.Buffered(1)
    return call(
        functools.partial(
            gradient_kernel, (error_wheres, input_wheres), window, own, math.gcd(own, 128)
        ),
        "gradient",
        (place, *error_arrays, *input_arrays, w_in, w_out),
        [
            jax.ShapeDtypeStruct((own, width), jnp.float32),
            jax.ShapeDtypeStruct((own, width), jnp.float32),
            jax.ShapeDtypeStruct((own, width), jnp.bfloat16),
            jax.ShapeDtypeStruct((own, width), jnp.bfloat16),
        ],
        after,
        grid=(width // tile,),
        in_specs=[
            pl.BlockSpec(a.shape, whole, pipeline_mode=once)
            for a in (*error_arrays, *input_arrays)
        ]
        + [pl.BlockSpec((depth, tile), column), pl.BlockSpec((tile, depth), lambda n, s: (n, 0))],
        out_specs=[pl.BlockSpec((own, tile), column)] * 4,
        scratch_shapes=[
            pltpu.VMEM((rows, depth), jnp.bfloat16),
            pltpu.VMEM((rows, depth), jnp.bfloat16),
            pltpu.VMEM((window * 128, rows), jnp.bfloat16),
            pltpu.VMEM((window * 128, rows), jnp.bfloat16),
            pltpu.VMEM((window * 128, tile), jnp.float32),
            pltpu.VMEM((window * 128, tile), jnp.float32),
        ],
    )


def products_kernel(labels, fresh, place_ref, *refs):
    own = refs[0].shape[0]
    refs, (known_ref, out_ref, totals) = refs[:-3], refs[-3:]
    each = len(refs) // len(labels)
    slots = [refs[each * n : each * (n + 1)] for n in range(len(labels))]
    pairs = [(i, j) for i in range(len(slots) - fresh, len(slots)) for j in range(i + 1)]

    @pl.when(pl.program_id(0) == 0)
    def _():
        totals[...] = jnp.zeros_like(totals)

    def values(slot):
        return [ref[...].astype(jnp.float32) for ref in slot]

    for n, (i, j) in enumerate(pairs):
        a, b = values(slots[i]), values(slots[j])
        both = sum(u * v for u, v in zip(a, b))
        totals[n] += jnp.sum(both.reshape(own // 8, 8, -1), axis=0)

    @pl.when(pl.program_id(0) == pl.num_programs(0) - 1)
    def _():
        result = known_ref[...]
        row = lax.broadcasted_iota(jnp.int32, result.shape, 0)
        column = lax.broadcasted_iota(jnp.int32, result.shape, 1)
        for n, (i, j) in enumerate(pairs):
            i, j = (jnp.bitwise_xor(place_ref[MEMBER], labels[k]) for k in (i, j))
            here = ((row == i) & (column == j)) | ((row == j) & (column == i))
            result = result + jnp.where(here, jnp.sum(totals[n]), 0.0)
        out_ref[...] = result


def products(place, slots, labels, fresh, known, after=()):
    arrays = [a for slot in slots for a in slot]
    own, width = slots[0][0].shape
    tile = tile_of(width, 256)
    pairs = sum(len(slots) - n for n in range(fresh))
    return call(
        functools.partial(products_kernel, tuple(labels), fresh),
        "products",
        (place, *arrays, known),
        [jax.ShapeDtypeStruct(known.shape, jnp.float32)],
        after,
        grid=(width // tile,),
        in_specs=[pl.BlockSpec((a.shape[0], tile), lambda n, s: (0, n)) for a in arrays]
        + [pl.BlockSpec(known.shape, whole)],
        out_specs=[pl.BlockSpec(known.shape, whole)],
        scratch_shapes=[pltpu.VMEM((pairs, 8, tile), jnp.float32)],
    )[0]


def tree_weights(count, entry):
    def inner(a, b):
        total = 0.0
        for i, u in a.items():
            for j, v in b.items():
                total = total + u * v * entry(i, j)
        return total

    items = [{i: 1.0} for i in range(count)]
    while len(items) > 1:
        half = len(items) // 2
        merged = []
        for low, high in zip(items[:half], items[half:]):
            product = inner(low, high)
            scale_low = 1.0 - product / (2.0 * (jnp.maximum(inner(low, low), 0.0) + epsilon))
            scale_high = 1.0 - product / (2.0 * (jnp.maximum(inner(high, high), 0.0) + epsilon))
            joined = {i: u * scale_low for i, u in low.items()}
            joined.update({i: u * scale_high for i, u in high.items()})
            merged.append(joined)
        items = merged
    return [items[0][i] for i in range(count)]


def sum_kernel(place_ref, *refs):
    refs[-1][...] = sum(ref[...] for ref in refs[:-1])


def sum_of(place, parts):
    shape = parts[0].shape
    return call(
        sum_kernel,
        "sum_of",
        (place, *parts),
        [jax.ShapeDtypeStruct(shape, jnp.float32)],
        vmem=4 * 2**20,
        grid=(1,),
        in_specs=[pl.BlockSpec(shape, whole)] * len(parts),
        out_specs=[pl.BlockSpec(shape, whole)],
    )[0]


def merge_kernel(labels, place_ref, totals_ref, got_ref, *refs):
    refs, (first_ref, second_ref, weights_ref) = refs[:-3], refs[-3:]

    @pl.when(pl.program_id(0) == 0)
    def _():
        def entry(i, j):
            i, j = (jnp.bitwise_xor(place_ref[MEMBER], k) for k in (i, j))
            return totals_ref[i, j] + got_ref[i, j]

        for n, weight in enumerate(tree_weights(len(labels), entry)):
            weights_ref[n] = weight

    first = second = 0.0
    for n, label in enumerate(labels):
        weight = weights_ref[label]
        first = first + weight * refs[2 * n][...].astype(jnp.float32)
        second = second + weight * refs[2 * n + 1][...].astype(jnp.float32)
    first_ref[...] = first
    second_ref[...] = second


def merge(place, totals, got, slots, labels):
    own, width = slots[0][0].shape
    block = max(b for b in range(16, min(own, 32) + 1, 16) if own % b == 0)
    spec = pl.BlockSpec((block, width), lambda n, s: (n, 0))
    arrays = [a for slot in slots for a in slot]
    shape = jax.ShapeDtypeStruct((own, width), jnp.float32)
    return call(
        functools.partial(merge_kernel, tuple(labels)),
        "merge",
        (place, totals, got, *arrays),
        [shape, shape],
        vmem=16 * 2**20,
        grid=(own // block,),
        in_specs=[pl.BlockSpec(memory_space=pltpu.SMEM)] * 2 + [spec] * len(arrays),
        out_specs=[spec, spec],
        scratch_shapes=[pltpu.SMEM((len(slots),), jnp.float32)],
    )


def on_device(inputs, targets, w_in, w_out):
    row_count = inputs.shape[0]
    workers = lax.axis_size("dp")
    shards = lax.axis_size("tensor")
    levels = workers.bit_length() - 1
    shard_levels = shards.bit_length() - 1
    gathered = min(levels, gather_levels_limit)
    members = 2**gathered
    others = workers // members
    position = lax.axis_index("dp")
    shard = lax.axis_index("tensor")
    member = position // others

    def part_of(index):
        part = 0
        for bit in range(shard_levels):
            part = part * 2 + (index >> bit & 1)
        return part

    near = shard & 1
    part_rows = row_count // shards
    own = inputs.shape[1] // members
    swap = 1
    bits = [2**b for b in reversed(range(gathered)) if 2**b != swap]
    upper = member // swap % 2
    first_row = (member - upper * swap) * own
    place = jnp.stack(
        [
            first_row // 128,
            first_row % 128 + upper * swap * own,
            first_row % 128 + (1 - upper) * swap * own,
            member,
            near,
            1 - near,
            part_of(shard),
            part_of(shard) - near * (shards // 2),
        ]
    ).astype(jnp.int32)

    send, hidden_near, own_part = forward(place, part_rows, inputs, w_in, w_out)
    got = from_mask(send, 0, 1)
    inputs_of = {bit: from_mask(own_part, bit * others, 0) for bit in bits}

    summed = product(place, hidden_near, w_out) + got
    most = 24.0 * 0.15625 * 0.078125 * inputs.shape[1] * w_in.shape[1] * shards
    scale = 2.0 ** math.ceil(math.log2(most / 65504.0))
    sums = [summed]
    for bit in range(1, shard_levels):
        rounded = (sum(sums) * (1.0 / scale)).astype(jnp.float16)
        sums.append(from_mask(rounded, 0, 2**bit).astype(jnp.float32) * scale)
    error, error_piece = error_half(
        place,
        part_rows,
        sum(sums[:-1]),
        sums[-1],
        targets,
        tuple(inputs_of.values()),
    )
    errors_of = {
        bit: from_mask(error_piece if bit == bits[0] else error, bit * others, 0) for bit in bits
    }

    def to_half(piece, *before):
        for bit in reversed(range(1, shard_levels)):
            got = ordered(from_mask(piece, 0, 2**bit), *before)
            piece = join(shard >> bit & 1, piece, got)
        return piece

    def both_halves(half):
        return [(half, NEAR), (from_mask(half, 0, 1), FAR)]

    slots, labels, known, sent, halves = [], [], [], [], {}
    totals = jnp.zeros((8, 128), jnp.float32)
    masks = [m for m in range(members) if not m & swap]
    for n, m in enumerate(masks):
        if n == 0:
            half = error
        elif m not in (bits[0], masks[-1]):
            half = errors_of[m] = ordered(errors_of[m], sent[0], *slots[1][:1])
            other_inputs = halves[m]
        elif m == bits[0]:
            before = [sent[-1], *slots[1]]
            errors_of[m] = ordered(errors_of[m], sent[0])
            for bit in bits[1:]:
                ready = ordered(errors_of[m], errors_of[bit])
                errors_of[m | bit] = from_mask(ready, bit * others, 0)
                before.append(errors_of[m | bit])
                ready = ordered(halves[m], errors_of[bit])
                halves[m | bit] = from_mask(ready, bit * others, 0)
            half = to_half(errors_of[m], *before)
            other_inputs = halves[m]
        else:
            half = to_half(ordered(errors_of[m], sent[-2]), sent[-1], *slots[2 * n - 3])
            other_inputs = ordered(halves[m], sent[-1])
        first, second, *send = gradient(
            place,
            members,
            swap,
            both_halves(half),
            both_halves(other_inputs) if n else [(inputs, None)],
            w_in,
            w_out,
            known[-2:-1],
        )
        if n == 0:
            for bit in bits:
                halves[bit] = to_half(inputs_of[bit], send[0], errors_of[bits[0]], *halves.values())
        sent.append(send[0])
        slots.append((first, second))
        labels.append(m)
        last = n == len(masks) - 1
        if last:
            totals = products(place, slots, labels, 1, totals)
        slots.append(tuple(from_mask(a, swap * others, 0) for a in send))
        labels.append(m ^ swap)
        if last:
            for k in range(2):
                totals = products(place, [slot[k : k + 1] for slot in slots], labels, 1, totals)
        else:
            totals = products(place, slots, labels, 2, totals)
        known.append(totals)

    rounds = [[(0, mask) for mask in range(1, shards)]]
    rounds.append([(m * others, 0) for m in range(2, members, 2)])
    for partners in rounds:
        totals = sum_of(place, [totals] + [from_mask(totals, *mask) for mask in partners])
    pieces = merge(place, totals, from_mask(totals, others, 0), slots, labels)

    for section in range(gathered, levels):
        upper_flag = position >> levels - 1 - section & 1
        keep_first, send_first = split_piece(pieces[0], upper_flag)
        keep_second, send_second = split_piece(pieces[1], upper_flag)
        got_first, got_second = from_partner((send_first, send_second), "dp", levels - 1 - section)
        pieces = combine(
            (keep_first, keep_second), (got_first, got_second), upper_flag, section, levels
        )
    return (pieces[0], pieces[1])


def solution(mesh):
    placed = (P("dp", None), P("dp", None), P(None, "tensor"), P("tensor", None))
    return jax.shard_map(
        on_device,
        mesh=mesh,
        in_specs=placed,
        out_specs=(P("dp", "tensor"), P("dp", "tensor")),
        check_vma=False,
    )
```
